32 devices in a mesh: space: 8 (over z, x), sample: 4 (over y, core).
Axes of the slice: x: 2, y: 2, z: 4, core: 2. Of those that a mesh axis runs over, the one named last changes fastest.
Arguments:
- crops: bfloat16 [32, 16, 16, 1024], P('sample', None, 'space'), may hold values from -6 to 6
- first_kernel: bfloat16 [32, 16, 3, 3, 3], replicated, may hold values from -0.3125 to 0.3125
- second_kernel: bfloat16 [64, 32, 3, 3, 3], replicated, may hold values from -0.21875 to 0.21875
- out_grad: bfloat16 [32, 64, 4, 64], P(('sample', 'space')), may hold values from -0.15625 to 0.15625
Outputs:
- features_out: bfloat16 [32, 64, 4, 64], P(('sample', 'space'))
- first_grad: float32 [32, 16, 3, 3, 3], replicated
- second_grad: float32 [64, 32, 3, 3, 3], replicated
The draws below stay inside these ranges and needn't reach their ends.
All inputs are finite; a program needn't handle non-finite values.
Results may differ from the reference program's by a relative error of at most 0.012.
Values may be sent and summed in bfloat16 or wider, within the bound.
No kernel may reach another device: no remote copies, remote signals or barrier semaphores. Data moves between devices by JAX's collectives and lax.ppermute only.
A program may use at most 128 MiB of HBM per device.

```python
import jax
import jax.numpy as jnp
from jax import lax

C0 = 16
C1 = 32
C2 = 64
HEIGHT = 8
WIDTH = 128
SAMPLES = 32
DEPTH = 16


def level_of(stream_key, extent, shards, smallest, largest):
    def one(dim, blocks):
        steps = jax.random.uniform(jax.random.fold_in(jax.random.fold_in(stream_key, 6), dim), (blocks,), jnp.float32, smallest / len(shards), largest / len(shards))
        return jnp.repeat(jnp.exp(steps), extent[dim] // blocks).reshape((-1,) + (1,) * (len(extent) - dim - 1))

    level = one(*shards[0])
    for cut in shards[1:]:
        level = level * one(*cut)
    return level


def scatter_about(key, shape, deviation, reach, pieces=(), kind=jnp.bfloat16):
    drawn = jax.random.normal(key, shape, jnp.float32) * deviation
    if len(pieces) > 0:
        drawn = level_of(key, shape, pieces, -0.22, 0.18) * drawn
    return jnp.clip(drawn, min=-reach, max=reach).astype(kind)


def setup_inputs(seed: int = 0) -> dict:
    splits = jax.random.split(jax.random.key(seed), 5)
    return {
        "crops": scatter_about(splits[0], (SAMPLES, C0, DEPTH, HEIGHT * WIDTH), 1.0, 6.0, ((0, 4), (2, 8))),
        "first_kernel": scatter_about(splits[1], (C1, C0, 3, 3, 3), (C0 * 27) ** -0.5, 0.3125),
        "second_kernel": scatter_about(splits[2], (C2, C1, 3, 3, 3), (C1 * 27) ** -0.5, 0.21875),
        "out_grad": scatter_about(splits[3], (SAMPLES, C2, DEPTH // 4, HEIGHT * WIDTH // 16), ((SAMPLES * (DEPTH // 4) * (HEIGHT * WIDTH // 16)) ** -0.5), 0.15625, ((0, 32),)),
    }


def strided_conv(field, kernel):
    return lax.conv_general_dilated(field, kernel, (2, 2, 2), ((1, 0), (1, 0), (1, 0)), dimension_numbers=('NCDHW', 'OIDHW', 'NCDHW'), precision=lax.Precision.HIGHEST)

def silu_slope(value):
    sigma = jax.nn.sigmoid(value)
    return sigma * (1.0 + value * (1.0 - sigma))

def reference(crops, first_kernel, second_kernel, out_grad):
    kernel_one = first_kernel.astype(jnp.float32)
    kernel_two = second_kernel.astype(jnp.float32)

    def one_sample(carry, pair):
        sample, cotangent = pair
        field = sample.astype(jnp.float32).reshape(1, C0, DEPTH, HEIGHT, WIDTH)
        first_pre = strided_conv(field, kernel_one)
        first_act = lax.optimization_barrier(jax.nn.silu(first_pre).astype(jnp.bfloat16)).astype(jnp.float32)
        output, pullback = jax.vjp(strided_conv, first_act, kernel_two)
        grad_field = cotangent.astype(jnp.float32).reshape(1, C2, DEPTH // 4, HEIGHT // 4, WIDTH // 4)
        act_grad, kernel_two_grad = pullback(grad_field)
        act_grad = lax.optimization_barrier(act_grad.astype(jnp.bfloat16)).astype(jnp.float32)
        pre_grad = lax.optimization_barrier((act_grad * silu_slope(first_pre)).astype(jnp.bfloat16)).astype(jnp.float32)
        unused, pull_first = jax.vjp(lambda kernel: strided_conv(field, kernel), kernel_one)
        kernel_one_grad = pull_first(pre_grad)[0]
        result = output.astype(jnp.bfloat16).reshape(C2, DEPTH // 4, HEIGHT * WIDTH // 16)
        return ((carry[0] + kernel_one_grad, carry[1] + kernel_two_grad), result)
    start = (jnp.zeros((C1, C0, 3, 3, 3), jnp.float32), jnp.zeros((C2, C1, 3, 3, 3), jnp.float32))
    totals, features_out = lax.scan(one_sample, start, (crops, out_grad))
    return (features_out, totals[0], totals[1])
```

```python
import jax
import jax.numpy as jnp
from jax import lax
from jax.sharding import PartitionSpec as P

HEIGHT = 8
WIDTH = 128


def forward_conv(field, kernel, depth_pad):
    return lax.conv_general_dilated(
        field,
        kernel,
        (2, 2, 2),
        (depth_pad, (1, 0), (1, 0)),
        dimension_numbers=("NCDHW", "OIDHW", "NCDHW"),
        preferred_element_type=jnp.float32,
    )


def kernel_grad(field, cotangent, depth_pad):
    return lax.conv_general_dilated(
        field,
        cotangent,
        (1, 1, 1),
        (depth_pad, (1, 0), (1, 0)),
        rhs_dilation=(2, 2, 2),
        dimension_numbers=("CNDHW", "IODHW", "CNDHW"),
        preferred_element_type=jnp.float32,
    )


def input_grad(cotangent, kernel):
    flipped = kernel[:, :, ::-1, ::-1, ::-1]
    return lax.conv_general_dilated(
        cotangent,
        flipped,
        (1, 1, 1),
        ((1, 2), (1, 2), (1, 2)),
        lhs_dilation=(2, 2, 2),
        dimension_numbers=("NCDHW", "IODHW", "NCDHW"),
        preferred_element_type=jnp.float32,
    )


def silu_slope(value):
    sigma = jax.nn.sigmoid(value)
    return sigma * (1.0 + value * (1.0 - sigma))


def sum_everywhere(terms):
    axes = ("space", "sample")
    devices = lax.axis_size(axes)
    flat = [jnp.transpose(term, (2, 3, 4, 1, 0)) for term in terms]
    joined = jnp.concatenate([part.reshape(-1) for part in flat]).astype(jnp.bfloat16)
    lanes = 128
    rows = -(-joined.shape[0] // (devices * lanes))
    joined = jnp.pad(joined, (0, devices * rows * lanes - joined.shape[0]))
    blocks = joined.reshape(devices, rows, lanes)
    mine = lax.all_to_all(blocks, axes, split_axis=0, concat_axis=0, tiled=True)
    total = jnp.sum(mine.astype(jnp.float32), axis=0).astype(jnp.bfloat16)
    spread = jnp.broadcast_to(total[None], blocks.shape)
    whole = lax.all_to_all(spread, axes, split_axis=0, concat_axis=0, tiled=True)
    whole = whole.reshape(-1)
    out = []
    start = 0
    for part in flat:
        piece = whole[start:start + part.size].reshape(part.shape)
        out.append(jnp.transpose(piece, (4, 3, 0, 1, 2)).astype(jnp.float32))
        start += part.size
    return out


def body(crops, first_kernel, second_kernel, out_grad):
    local_samples, channels_in, planes, flat_cells = crops.shape
    whole_input = lax.all_to_all(crops, "space", split_axis=0, concat_axis=2, tiled=True)
    whole_input = whole_input.reshape(
        whole_input.shape[0], channels_in, whole_input.shape[2], HEIGHT, WIDTH
    )
    first_pre = forward_conv(whole_input, first_kernel, (1, 0))
    act_whole = jax.nn.silu(first_pre).astype(jnp.bfloat16)
    sample_count = act_whole.shape[0]
    second_pre = forward_conv(act_whole, second_kernel, (1, 0))
    features_out = second_pre.astype(jnp.bfloat16).reshape(out_grad.shape)
    cotangent = out_grad.reshape(
        sample_count, out_grad.shape[1], out_grad.shape[2], HEIGHT // 4, WIDTH // 4
    )
    second_grad = kernel_grad(act_whole, cotangent, (1, 0))
    act_grad = input_grad(cotangent, second_kernel).astype(jnp.bfloat16)
    pre_grad = (act_grad.astype(jnp.float32) * silu_slope(first_pre)).astype(jnp.bfloat16)
    first_grad = kernel_grad(whole_input, pre_grad, (1, 0))
    first_grad, second_grad = sum_everywhere((first_grad, second_grad))
    return (features_out, first_grad, second_grad)


def solution(mesh):
    placed = (P("sample", None, "space", None), P(), P(), P(("sample", "space"), None, None, None))
    return jax.shard_map(
        body,
        mesh=mesh,
        in_specs=placed,
        out_specs=(P(("sample", "space"), None, None, None), P(), P()),
        check_vma=False,
    )
```

```python
import jax
import jax.numpy as jnp
from jax import lax
from jax.experimental import pallas as pl
from jax.experimental.pallas import tpu as pltpu
from jax.sharding import PartitionSpec as P

HEIGHT = 8
WIDTH = 128
LANES = 128
VMEM_BYTES = 48 * 1024 * 1024


def iota(shape, dim):
    return lax.broadcasted_iota(jnp.int32, shape, dim)


def dot(left, right, dims=((1,), (0,))):
    return lax.dot_general(left, right, (dims, ((), ())), preferred_element_type=jnp.float32)


def ones_where(mask):
    return jnp.where(mask, 1.0, 0.0).astype(jnp.bfloat16)


def prepare_kernel(k1_ref, k2_ref, og_ref, pick_ref, k1t_ref, k2t_ref, up_ref, ogu_ref, ag_ref):
    channels_in, channels_mid = k1_ref.shape[3:]
    channels_out = k2_ref.shape[4]
    row, col = iota((2 * WIDTH, 2 * 64), 0), iota((2 * WIDTH, 2 * 64), 1)
    for aw in range(3):
        same = (row // WIDTH) == (col // 64)
        tap = (row % WIDTH) == 2 * (col % 64) + aw - 1
        pick_ref[:, aw * 128:(aw + 1) * 128] = ones_where(same & tap)
    shape = (9 * channels_in, channels_in * 2 * HEIGHT)
    row, col = iota(shape, 0), iota(shape, 1)
    ad, ah, i = row // (3 * channels_in), (row // channels_in) % 3, row % channels_in
    same = i == col // (2 * HEIGHT)
    h, d = (col // 2) % HEIGHT, col % 2
    taps = []
    for aw in range(3):
        parts = [k1_ref[a, b, aw] for a in range(3) for b in range(3)]
        taps.append(jnp.concatenate(parts, axis=0).astype(jnp.float32).T.astype(jnp.bfloat16))
    for following in range(2):
        plane = (ad == 0) & (d == 1) if following else (ad == d + 1)
        for hh in range(4):
            place = ones_where(same & plane & (h == 2 * hh + ah - 1))
            start = (following * 4 + hh) * channels_mid
            for aw in range(3):
                block = dot(taps[aw], place).astype(jnp.bfloat16)
                k1t_ref[start:start + channels_mid, aw * shape[1]:(aw + 1) * shape[1]] = block
    empty = jnp.zeros((channels_mid, channels_out), jnp.bfloat16)
    for ad in range(3):
        for aw in range(3):
            tap = [k2_ref[ad, ah, aw] for ah in range(3)]
            band = ((tap[1], empty), (tap[2], tap[0]), (empty, tap[1]), (empty, tap[2]))
            start = (ad * 3 + aw) * 2 * channels_out
            for hh in range(4):
                k2t_ref[hh * channels_mid:(hh + 1) * channels_mid, start:start + 2 * channels_out] = (
                    jnp.concatenate(band[hh], axis=1))
    row, col = iota((128, 512), 0), iota((128, 512), 1)
    groups = og_ref.shape[1] // 128
    for ad in range(3):
        for aw in range(3):
            t = ad * 3 + aw
            target = 128 * (row // 32) + 2 * (row % 32) + 64 * (ad - 1) + aw - 1
            valid = (row % 32 > 0) if aw == 0 else (row >= 0)
            up = ones_where((col == target) & valid)
            up_ref[t] = up
            for g in range(groups):
                value = dot(og_ref[:, g * 128:(g + 1) * 128], up)
                if ad == 0 and g + 1 < groups:
                    cross = ones_where((col == target + 512) & valid)
                    value = value + dot(og_ref[:, (g + 1) * 128:(g + 2) * 128], cross)
                ogu_ref[t * 128:(t + 1) * 128, g * 512:(g + 1) * 512] = value.astype(jnp.bfloat16)
    for g in range(groups):
        lanes = slice(g * 512, (g + 1) * 512)
        ag_ref[:, lanes] = dot(k2t_ref[...], ogu_ref[:, lanes]).astype(jnp.bfloat16)


def layer_kernel(x_ref, pick_ref, k1t_ref, ogu_ref, ag_ref, act_ref, terms_ref, y_scr, pg_scr):
    cells = ag_ref.shape[1]
    rows = 256
    for q in range(cells // 128):
        start = q * 2 * rows
        pair = jnp.concatenate([x_ref[start:start + rows, :], x_ref[start + rows:start + 2 * rows, :]], axis=1)
        y = dot(pair, pick_ref[...]).astype(jnp.bfloat16)
        for aw in range(3):
            y_scr[aw * rows:(aw + 1) * rows, q * 128:(q + 1) * 128] = y[:, aw * 128:(aw + 1) * 128]
    both = dot(k1t_ref[...], y_scr[...])
    lane = iota((128, cells), 1)
    from_last = jnp.where(lane < 64, 0.0, pltpu.roll(both[128:], 64, 1))
    pre = both[:128] + from_last
    sigma = jax.nn.sigmoid(pre)
    act = (pre * sigma).astype(jnp.bfloat16)
    act_ref[...] = act
    slope = sigma * (1.0 + pre * (1.0 - sigma))
    grad = (ag_ref[...].astype(jnp.float32) * slope).astype(jnp.bfloat16)
    pg_scr[:128, :] = grad
    to_last = pltpu.roll(grad.astype(jnp.float32), cells - 64, 1)
    pg_scr[128:, :] = jnp.where(lane < cells - 64, to_last, 0.0).astype(jnp.bfloat16)

    second = dot(act, ogu_ref[...], ((1,), (1,)))
    lane = iota((32, 128), 1)
    held = None
    for t in range(9):
        tile = second[:, t * 128:(t + 1) * 128]
        turned = pltpu.roll(tile, 64, 1)
        mixed = jnp.where(lane < 64, tile[0:32] + turned[64:96], turned[32:64] + tile[96:128])
        terms_ref[t * 32:(t + 1) * 32, :] = mixed.astype(jnp.bfloat16)
        if t % 2 == 0:
            held = jnp.where(lane < 64, turned[32:64], 0.0)
        else:
            held = jnp.where(lane < 64, held, tile[32:64])
        if t % 2 == 1 or t == 8:
            start = 288 + (t // 2) * 32
            terms_ref[start:start + 32, :] = held.astype(jnp.bfloat16)

    first = dot(y_scr[...], pg_scr[...], ((1,), (1,)))
    shape = (rows, 256)
    row, col = iota(shape, 0), iota(shape, 1)
    h, hh, block = (row // 2) % HEIGHT, (col // 32) % 4, (col // 32) % 4
    rank, index = iota((48, rows), 0), iota((48, rows), 1)
    depth = rank // 16
    wanted = jnp.where(depth == 0, 1, depth - 1)
    gather = ones_where((rank % 16 == index // 16) & (wanted == index % 2))
    for aw in range(3):
        tile = first[aw * rows:(aw + 1) * rows]
        packed = jnp.zeros(shape, jnp.float32)
        for ah in range(3):
            kept = jnp.where(h == 2 * hh + ah - 1, tile, 0.0)
            halves = []
            for half in (kept[:, :128], kept[:, 128:]):
                half = half + pltpu.roll(half, 64, 1)
                halves.append(half + pltpu.roll(half, 32, 1))
            packed = jnp.where(block == ah, jnp.concatenate(halves, axis=1), packed)
        high = packed.astype(jnp.bfloat16)
        low = (packed - high.astype(jnp.float32)).astype(jnp.bfloat16)
        total = dot(gather, high) + dot(gather, low)
        start = 448 + aw * 48
        terms_ref[start:start + 16, :] = total[:16, 128:].astype(jnp.bfloat16)
        terms_ref[start + 16:start + 48, :] = total[16:, :128].astype(jnp.bfloat16)
    rest = terms_ref.shape[0] - 592
    terms_ref[592:, :] = jnp.zeros((rest, 128), jnp.bfloat16)


def features_kernel(act_ref, k2t_ref, up_ref, out_ref):
    groups = out_ref.shape[1] // 128
    for g in range(groups):
        total = jnp.zeros((128, 128), jnp.float32)
        for t in range(9):
            up = up_ref[t]
            wide = act_ref[:, g * 512:(g + 1) * 512]
            taken = dot(wide, up, ((1,), (1,)))
            if t < 3 and g > 0:
                last = act_ref[:, (g - 1) * 512:g * 512]
                row, col = iota((128, 512), 0), iota((128, 512), 1)
                target = 512 + 2 * row - 64 + t - 1
                cross = ones_where((col == target) & (row < 32) & ((row > 0) if t == 0 else (row >= 0)))
                taken = taken + dot(last, cross, ((1,), (1,)))
            band = k2t_ref[:, t * 128:(t + 1) * 128]
            total = total + dot(band, taken.astype(jnp.bfloat16), ((0,), (0,)))
        out_ref[:, g * 128:(g + 1) * 128] = total.astype(jnp.bfloat16)


def add_kernel(mine_ref, out_ref):
    total = jnp.sum(mine_ref[...].astype(jnp.float32), axis=0).astype(jnp.bfloat16)
    out_ref[...] = jnp.broadcast_to(total[None], out_ref.shape)


def unpack_kernel(whole_ref, first_ref, second_ref):
    for ad in range(3):
        for aw in range(3):
            t = ad * 3 + aw
            pair = whole_ref[t * 32:(t + 1) * 32, :].astype(jnp.float32)
            second_ref[ad, 1, aw] = pair[:, :64]
            second_ref[ad, 2, aw] = pair[:, 64:]
            start = 288 + (t // 2) * 32
            lone = whole_ref[start:start + 32, :].astype(jnp.float32)
            second_ref[ad, 0, aw] = lone[:, :64] if t % 2 == 0 else lone[:, 64:]
            start = 448 + aw * 48 + ad * 16
            tile = whole_ref[start:start + 16, :].astype(jnp.float32)
            for ah in range(3):
                first_ref[ad, ah, aw] = tile[:, ah * 32:(ah + 1) * 32]


def call(kernel, outs, args, scratch=(), flops=0):
    whole = pl.BlockSpec(memory_space=pltpu.VMEM)
    size = sum(a.size * a.dtype.itemsize for a in list(args) + list(outs))
    return pl.pallas_call(
        kernel,
        out_shape=tuple(outs),
        in_specs=[whole] * len(args),
        out_specs=(whole,) * len(outs),
        scratch_shapes=list(scratch),
        compiler_params=pltpu.CompilerParams(vmem_limit_bytes=VMEM_BYTES),
        cost_estimate=pl.CostEstimate(flops=flops, bytes_accessed=size, transcendentals=0),
    )(*args)


def array(shape, dtype=jnp.bfloat16):
    return jax.ShapeDtypeStruct(shape, dtype)


def prepare(first_kernel, second_kernel, out_grad):
    c1, c0 = first_kernel.shape[:2]
    c2 = second_kernel.shape[0]
    planes = out_grad.shape[2]
    cells = planes * 2 * 64
    k1 = jnp.transpose(first_kernel, (2, 3, 4, 1, 0))
    k2 = jnp.transpose(second_kernel, (2, 3, 4, 1, 0))
    og = out_grad.reshape(c2, planes, 2, 32).transpose(2, 0, 1, 3).reshape(2 * c2, planes * 32)
    outs = [
        array((256, 384)),
        array((2 * 4 * c1, 3 * c0 * 16)),
        array((4 * c1, 9 * 2 * c2)),
        array((9, 128, 512)),
        array((9 * 2 * c2, cells)),
        array((4 * c1, cells)),
    ]
    return call(prepare_kernel, outs, (k1, k2, og), flops=2 * 128 * 1152 * cells * 2)


def body(crops, first_kernel, second_kernel, out_grad):
    axes = ("space", "sample")
    devices = lax.axis_size(axes)
    channels_out, planes = out_grad.shape[1:3]
    whole_input = lax.all_to_all(crops, "space", split_axis=0, concat_axis=0, tiled=True)
    pick, k1t, k2t, up, ogu, act_grad = prepare(first_kernel, second_kernel, out_grad)
    sources, channels_in, two, flat_cells = whole_input.shape
    x = whole_input.reshape(sources, channels_in, two, HEIGHT, WIDTH).transpose(0, 1, 3, 2, 4)
    x = x.reshape(sources * channels_in * two * HEIGHT, WIDTH)
    cells = act_grad.shape[1]
    rows = -(-592 // (devices * 8)) * 8
    act, terms = call(
        layer_kernel,
        [array((128, cells)), array((devices * rows, LANES))],
        (x, pick, k1t, ogu, act_grad),
        scratch=[pltpu.VMEM((768, cells), jnp.bfloat16), pltpu.VMEM((256, cells), jnp.bfloat16)],
        flops=2 * 128 * 4096 * cells,
    )
    blocks = terms.reshape(devices, rows, LANES)
    mine = lax.all_to_all(blocks, axes, split_axis=0, concat_axis=0, tiled=True)
    (features,) = call(
        features_kernel, [array((2 * channels_out, planes * 32))], (act, k2t, up), flops=2 * 128 * 1152 * cells
    )
    features = features.reshape(2, channels_out, planes, 32).transpose(1, 2, 0, 3).reshape(out_grad.shape)
    (spread,) = call(add_kernel, [array(blocks.shape)], (mine,))
    whole = lax.all_to_all(spread, axes, split_axis=0, concat_axis=0, tiled=True)
    first, second = call(
        unpack_kernel,
        [
            array((3, 3, 3) + first_kernel.shape[1::-1], jnp.float32),
            array((3, 3, 3) + second_kernel.shape[1::-1], jnp.float32),
        ],
        (whole.reshape(devices * rows, LANES),),
    )
    return (features, jnp.transpose(first, (4, 3, 0, 1, 2)), jnp.transpose(second, (4, 3, 0, 1, 2)))


def solution(mesh):
    placed = (P("sample", None, "space", None), P(), P(), P(("sample", "space"), None, None, None))
    return jax.shard_map(
        body,
        mesh=mesh,
        in_specs=placed,
        out_specs=(P(("sample", "space"), None, None, None), P(), P()),
        check_vma=False,
    )
```

```python
import functools

import jax
import jax.numpy as jnp
from jax import lax
from jax.experimental import pallas as pl
from jax.experimental.pallas import tpu as pltpu
from jax.sharding import PartitionSpec as P

HEIGHT = 8
WIDTH = 128
LANES = 128
VMEM_BYTES = 16 * 1024 * 1024
TERM_ROWS = 576


def iota(shape, dim):
    return lax.broadcasted_iota(jnp.int32, shape, dim)


def dot(left, right, dims=((1,), (0,))):
    return lax.dot_general(left, right, (dims, ((), ())), preferred_element_type=jnp.float32)


def ones_where(mask):
    return jnp.where(mask, 1.0, 0.0).astype(jnp.bfloat16)


def prepare_kernel(k1_ref, k2_ref, og_ref, pick_ref, k1t_ref, k2t_ref, up_ref, ogu_ref, ag_ref):
    channels_in, channels_mid = k1_ref.shape[3:]
    channels_out = k2_ref.shape[4]
    row, col = iota((2 * WIDTH, 2 * 64), 0), iota((2 * WIDTH, 2 * 64), 1)
    for aw in range(3):
        same = (row // WIDTH) == (col // 64)
        tap = (row % WIDTH) == 2 * (col % 64) + aw - 1
        pick_ref[:, aw * 128:(aw + 1) * 128] = ones_where(same & tap)
    shape = (9 * channels_in, channels_in * 2 * HEIGHT)
    row, col = iota(shape, 0), iota(shape, 1)
    ad, ah, i = row // (3 * channels_in), (row // channels_in) % 3, row % channels_in
    same = i == col // (2 * HEIGHT)
    h, d = (col // 2) % HEIGHT, col % 2
    taps = []
    for aw in range(3):
        parts = [k1_ref[a, b, aw] for a in range(3) for b in range(3)]
        taps.append(jnp.concatenate(parts, axis=0).astype(jnp.float32).T.astype(jnp.bfloat16))
    for following in range(2):
        plane = (ad == 0) & (d == 1) if following else (ad == d + 1)
        for hh in range(4):
            place = ones_where(same & plane & (h == 2 * hh + ah - 1))
            start = (following * 4 + hh) * channels_mid
            for aw in range(3):
                block = dot(taps[aw], place).astype(jnp.bfloat16)
                k1t_ref[start:start + channels_mid, aw * shape[1]:(aw + 1) * shape[1]] = block
    empty = jnp.zeros((channels_mid, channels_out), jnp.bfloat16)
    for ad in range(3):
        for aw in range(3):
            tap = [k2_ref[ad, ah, aw] for ah in range(3)]
            band = ((tap[1], empty), (tap[2], tap[0]), (empty, tap[1]), (empty, tap[2]))
            start = (ad * 3 + aw) * 2 * channels_out
            for hh in range(4):
                k2t_ref[hh * channels_mid:(hh + 1) * channels_mid, start:start + 2 * channels_out] = (
                    jnp.concatenate(band[hh], axis=1))
    row, col = iota((128, 512), 0), iota((128, 512), 1)
    groups = og_ref.shape[1] // 128
    for ad in range(3):
        for aw in range(3):
            t = ad * 3 + aw
            target = 128 * (row // 32) + 2 * (row % 32) + 64 * (ad - 1) + aw - 1
            valid = (row % 32 > 0) if aw == 0 else (row >= 0)
            up = ones_where((col == target) & valid)
            up_ref[t] = up
            for g in range(groups):
                value = dot(og_ref[:, g * 128:(g + 1) * 128], up)
                if ad == 0 and g + 1 < groups:
                    cross = ones_where((col == target + 512) & valid)
                    value = value + dot(og_ref[:, (g + 1) * 128:(g + 2) * 128], cross)
                ogu_ref[t * 128:(t + 1) * 128, g * 512:(g + 1) * 512] = value.astype(jnp.bfloat16)
    for g in range(groups):
        lanes = slice(g * 512, (g + 1) * 512)
        ag_ref[:, lanes] = dot(k2t_ref[...], ogu_ref[:, lanes]).astype(jnp.bfloat16)


def layer_kernel(x_ref, pick_ref, k1t_ref, ogu_ref, ag_ref, act_ref, terms_ref, y_scr, pg_scr):
    cells = ag_ref.shape[1]
    rows = 256
    for q in range(cells // 128):
        start = q * 2 * rows
        pair = jnp.concatenate([x_ref[start:start + rows, :], x_ref[start + rows:start + 2 * rows, :]], axis=1)
        y = dot(pair, pick_ref[...]).astype(jnp.bfloat16)
        for aw in range(3):
            y_scr[aw * rows:(aw + 1) * rows, q * 128:(q + 1) * 128] = y[:, aw * 128:(aw + 1) * 128]
    both = dot(k1t_ref[...], y_scr[...])
    lane = iota((128, cells), 1)
    from_last = jnp.where(lane < 64, 0.0, pltpu.roll(both[128:], 64, 1))
    pre = both[:128] + from_last
    sigma = jax.nn.sigmoid(pre)
    act = (pre * sigma).astype(jnp.bfloat16)
    act_ref[...] = act
    slope = sigma * (1.0 + pre * (1.0 - sigma))
    grad = (ag_ref[...].astype(jnp.float32) * slope).astype(jnp.bfloat16)
    pg_scr[:128, :] = grad
    to_last = pltpu.roll(grad.astype(jnp.float32), cells - 64, 1)
    pg_scr[128:, :] = jnp.where(lane < cells - 64, to_last, 0.0).astype(jnp.bfloat16)

    second = dot(act, ogu_ref[...], ((1,), (1,)))
    lane = iota((32, 128), 1)
    held = None
    for t in range(9):
        tile = second[:, t * 128:(t + 1) * 128]
        turned = pltpu.roll(tile, 64, 1)
        mixed = jnp.where(lane < 64, tile[0:32] + turned[64:96], turned[32:64] + tile[96:128])
        terms_ref[t * 32:(t + 1) * 32, :] = mixed.astype(jnp.bfloat16)
        if t % 2 == 0:
            held = jnp.where(lane < 64, turned[32:64], 0.0)
        else:
            held = jnp.where(lane < 64, held, tile[32:64])
        if t % 2 == 1:
            start = 288 + (t // 2) * 32
            terms_ref[start:start + 32, :] = held.astype(jnp.bfloat16)
    terms_ref[416:432, :] = jnp.where(lane[:16] < 64, held[:16], pltpu.roll(held[16:], 64, 1)).astype(jnp.bfloat16)

    first = dot(y_scr[...], pg_scr[...], ((1,), (1,)))
    shape = (rows, 256)
    row, col = iota(shape, 0), iota(shape, 1)
    h, hh, block = (row // 2) % HEIGHT, (col // 32) % 4, (col // 32) % 4
    rank, index = iota((48, rows), 0), iota((48, rows), 1)
    depth = rank // 16
    wanted = jnp.where(depth == 0, 1, depth - 1)
    gather = ones_where((rank % 16 == index // 16) & (wanted == index % 2))
    for aw in range(3):
        tile = first[aw * rows:(aw + 1) * rows]
        packed = jnp.zeros(shape, jnp.float32)
        for ah in range(3):
            kept = jnp.where(h == 2 * hh + ah - 1, tile, 0.0)
            halves = []
            for half in (kept[:, :128], kept[:, 128:]):
                half = half + pltpu.roll(half, 64, 1)
                halves.append(half + pltpu.roll(half, 32, 1))
            packed = jnp.where(block == ah, jnp.concatenate(halves, axis=1), packed)
        high = packed.astype(jnp.bfloat16)
        low = (packed - high.astype(jnp.float32)).astype(jnp.bfloat16)
        total = dot(gather, high) + dot(gather, low)
        start = 432 + aw * 48
        terms_ref[start:start + 16, :] = total[:16, 128:].astype(jnp.bfloat16)
        terms_ref[start + 16:start + 48, :] = total[16:, :128].astype(jnp.bfloat16)
    rest = terms_ref.shape[0] - TERM_ROWS
    if rest > 0:
        terms_ref[TERM_ROWS:, :] = jnp.zeros((rest, 128), jnp.bfloat16)


def features_kernel(act_ref, k2t_ref, up_ref, out_ref):
    groups = out_ref.shape[1] // 128
    for g in range(groups):
        total = jnp.zeros((128, 128), jnp.float32)
        for t in range(9):
            up = up_ref[t]
            wide = act_ref[:, g * 512:(g + 1) * 512]
            taken = dot(wide, up, ((1,), (1,)))
            if t < 3 and g > 0:
                last = act_ref[:, (g - 1) * 512:g * 512]
                row, col = iota((128, 512), 0), iota((128, 512), 1)
                target = 512 + 2 * row - 64 + t - 1
                cross = ones_where((col == target) & (row < 32) & ((row > 0) if t == 0 else (row >= 0)))
                taken = taken + dot(last, cross, ((1,), (1,)))
            band = k2t_ref[:, t * 128:(t + 1) * 128]
            total = total + dot(band, taken.astype(jnp.bfloat16), ((0,), (0,)))
        out_ref[:, g * 128:(g + 1) * 128] = total.astype(jnp.bfloat16)


def add_kernel(rows, mine_ref, out_ref):
    count = mine_ref.shape[0]
    held = -(-rows // 16) * 16
    to = ones_where(iota((held, count), 0) == iota((held, count), 1) % rows)
    back = ones_where(iota((count, held), 0) % rows == iota((count, held), 1))
    total = dot(to, mine_ref[...]).astype(jnp.bfloat16)
    out_ref[...] = dot(back, total).astype(jnp.bfloat16)


def unpack_kernel(whole_ref, first_ref, second_ref):
    for ad in range(3):
        for aw in range(3):
            t = ad * 3 + aw
            pair = whole_ref[t * 32:(t + 1) * 32, :].astype(jnp.float32)
            second_ref[ad, 1, aw] = pair[:, :64]
            second_ref[ad, 2, aw] = pair[:, 64:]
            if t == 8:
                lone = whole_ref[416:432, :].astype(jnp.float32)
                second_ref[ad, 0, aw] = jnp.concatenate([lone[:, :64], lone[:, 64:]], axis=0)
            else:
                start = 288 + (t // 2) * 32
                lone = whole_ref[start:start + 32, :].astype(jnp.float32)
                second_ref[ad, 0, aw] = lone[:, :64] if t % 2 == 0 else lone[:, 64:]
            start = 432 + aw * 48 + ad * 16
            tile = whole_ref[start:start + 16, :].astype(jnp.float32)
            for ah in range(3):
                first_ref[ad, ah, aw] = tile[:, ah * 32:(ah + 1) * 32]


def call(kernel, outs, args, scratch=(), flops=0):
    whole = pl.BlockSpec(memory_space=pltpu.VMEM)
    size = sum(a.size * a.dtype.itemsize for a in list(args) + list(outs))
    return pl.pallas_call(
        kernel,
        out_shape=tuple(outs),
        in_specs=[whole] * len(args),
        out_specs=(whole,) * len(outs),
        scratch_shapes=list(scratch),
        compiler_params=pltpu.CompilerParams(vmem_limit_bytes=VMEM_BYTES),
        cost_estimate=pl.CostEstimate(flops=flops, bytes_accessed=size, transcendentals=0),
    )(*args)


def array(shape, dtype=jnp.bfloat16):
    return jax.ShapeDtypeStruct(shape, dtype)


def prepare(first_kernel, second_kernel, out_grad):
    c1, c0 = first_kernel.shape[:2]
    c2 = second_kernel.shape[0]
    planes = out_grad.shape[2]
    cells = planes * 2 * 64
    k1 = jnp.transpose(first_kernel, (2, 3, 4, 1, 0))
    k2 = jnp.transpose(second_kernel, (2, 3, 4, 1, 0))
    og = out_grad.reshape(c2, planes, 2, 32).transpose(2, 0, 1, 3).reshape(2 * c2, planes * 32)
    outs = [
        array((256, 384)),
        array((2 * 4 * c1, 3 * c0 * 16)),
        array((4 * c1, 9 * 2 * c2)),
        array((9, 128, 512)),
        array((9 * 2 * c2, cells)),
        array((4 * c1, cells)),
    ]
    return call(prepare_kernel, outs, (k1, k2, og), flops=2 * 128 * 1152 * cells * 2)


def body(crops, first_kernel, second_kernel, out_grad):
    axes = ("space", "sample")
    devices = lax.axis_size(axes)
    channels_out, planes = out_grad.shape[1:3]
    whole_input = lax.all_to_all(crops, "space", split_axis=0, concat_axis=0, tiled=True)
    pick, k1t, k2t, up, ogu, act_grad = prepare(first_kernel, second_kernel, out_grad)
    sources, channels_in, two, flat_cells = whole_input.shape
    x = whole_input.reshape(sources, channels_in, two, HEIGHT, WIDTH).transpose(0, 1, 3, 2, 4)
    x = x.reshape(sources * channels_in * two * HEIGHT, WIDTH)
    cells = act_grad.shape[1]
    rows = -(-TERM_ROWS // (devices * 2)) * 2
    act, terms = call(
        layer_kernel,
        [array((128, cells)), array((devices * rows, LANES))],
        (x, pick, k1t, ogu, act_grad),
        scratch=[pltpu.VMEM((768, cells), jnp.bfloat16), pltpu.VMEM((256, cells), jnp.bfloat16)],
        flops=2 * 128 * 4096 * cells,
    )
    blocks = terms.reshape(devices, rows // 2, 2, LANES)
    mine = lax.all_to_all(blocks, axes, split_axis=0, concat_axis=0, tiled=True)
    (features,) = call(
        features_kernel, [array((2 * channels_out, planes * 32))], (act, k2t, up), flops=2 * 128 * 1152 * cells
    )
    features = features.reshape(2, channels_out, planes, 32).transpose(1, 2, 0, 3).reshape(out_grad.shape)
    add = functools.partial(add_kernel, rows)
    (spread,) = call(add, [array(terms.shape)], (mine.reshape(terms.shape),))
    spread = spread.reshape(blocks.shape)
    whole = lax.all_to_all(spread, axes, split_axis=0, concat_axis=0, tiled=True)
    first, second = call(
        unpack_kernel,
        [
            array((3, 3, 3) + first_kernel.shape[1::-1], jnp.float32),
            array((3, 3, 3) + second_kernel.shape[1::-1], jnp.float32),
        ],
        (whole.reshape(terms.shape),),
    )
    return (features, jnp.transpose(first, (4, 3, 0, 1, 2)), jnp.transpose(second, (4, 3, 0, 1, 2)))


def solution(mesh):
    placed = (P("sample", None, "space", None), P(), P(), P(("sample", "space"), None, None, None))
    return jax.shard_map(
        body,
        mesh=mesh,
        in_specs=placed,
        out_specs=(P(("sample", "space"), None, None, None), P(), P()),
        check_vma=False,
    )
```

```python
import functools

import jax
import jax.numpy as jnp
from jax import lax
from jax.experimental import pallas as pl
from jax.experimental.pallas import tpu as pltpu
from jax.sharding import PartitionSpec as P

HEIGHT = 8
WIDTH = 128
LANES = 128
VMEM_BYTES = 16 * 1024 * 1024
TERM_ROWS = 576


def iota(shape, dim):
    return lax.broadcasted_iota(jnp.int32, shape, dim)


def dot(left, right, dims=((1,), (0,))):
    return lax.dot_general(left, right, (dims, ((), ())), preferred_element_type=jnp.float32)


def ones_where(mask):
    return jnp.where(mask, 1.0, 0.0).astype(jnp.bfloat16)


def band_of_second(k2_ref, k2t_ref):
    channels_mid, channels_out = k2_ref.shape[3:]
    empty = jnp.zeros((channels_mid, channels_out), jnp.bfloat16)
    for ad in range(3):
        for aw in range(3):
            tap = [k2_ref[ad, ah, aw] for ah in range(3)]
            band = ((tap[1], empty), (tap[2], tap[0]), (empty, tap[1]), (empty, tap[2]))
            start = (ad * 3 + aw) * 2 * channels_out
            for hh in range(4):
                k2t_ref[hh * channels_mid:(hh + 1) * channels_mid, start:start + 2 * channels_out] = (
                    jnp.concatenate(band[hh], axis=1))


def upsampling(ad, aw, beyond=0):
    row, col = iota((128, 512), 0), iota((128, 512), 1)
    target = 128 * (row // 32) + 2 * (row % 32) + 64 * (ad - 1) + aw - 1 + 128 * beyond
    keep = col == target
    if aw == 0:
        keep = keep & (row % 32 > 0)
    return ones_where(keep)


def prepare_kernel(k1_ref, k2_ref, og_ref, pick_ref, k1t_ref, ogu_ref, ag_ref, k2t_ref):
    channels_in, channels_mid = k1_ref.shape[3:]
    row, col = iota((2 * WIDTH, 2 * 64), 0), iota((2 * WIDTH, 2 * 64), 1)
    for aw in range(3):
        same = (row // WIDTH) == (col // 64)
        tap = (row % WIDTH) == 2 * (col % 64) + aw - 1
        pick_ref[:, aw * 128:(aw + 1) * 128] = ones_where(same & tap)
    shape = (9 * channels_in, channels_in * 2 * HEIGHT)
    row, col = iota(shape, 0), iota(shape, 1)
    ad, ah, i = row // (3 * channels_in), (row // channels_in) % 3, row % channels_in
    same = i == col // (2 * HEIGHT)
    h, d = (col // 2) % HEIGHT, col % 2
    taps = []
    for aw in range(3):
        parts = [k1_ref[a, b, aw] for a in range(3) for b in range(3)]
        taps.append(jnp.concatenate(parts, axis=0).astype(jnp.float32).T.astype(jnp.bfloat16))
    for following in range(2):
        plane = (ad == 0) & (d == 1) if following else (ad == d + 1)
        for hh in range(4):
            place = ones_where(same & plane & (h == 2 * hh + ah - 1))
            start = (following * 4 + hh) * channels_mid
            for aw in range(3):
                block = dot(taps[aw], place).astype(jnp.bfloat16)
                k1t_ref[start:start + channels_mid, aw * shape[1]:(aw + 1) * shape[1]] = block
    band_of_second(k2_ref, k2t_ref)
    groups = og_ref.shape[1] // 128
    for ad in range(3):
        for aw in range(3):
            t = ad * 3 + aw
            up = upsampling(ad, aw)
            for g in range(groups):
                value = dot(og_ref[:, g * 128:(g + 1) * 128], up)
                if ad == 0 and g + 1 < groups:
                    value = value + dot(og_ref[:, (g + 1) * 128:(g + 2) * 128], upsampling(ad, aw, 4))
                ogu_ref[t * 128:(t + 1) * 128, g * 512:(g + 1) * 512] = value.astype(jnp.bfloat16)
    for g in range(groups):
        lanes = slice(g * 512, (g + 1) * 512)
        ag_ref[:, lanes] = dot(k2t_ref[...], ogu_ref[:, lanes]).astype(jnp.bfloat16)


def layer_kernel(x_ref, pick_ref, k1t_ref, ogu_ref, ag_ref, act_ref, terms_ref, y_scr, pg_scr):
    cells = ag_ref.shape[1]
    rows = 256
    for q in range(cells // 128):
        start = q * 2 * rows
        pair = jnp.concatenate([x_ref[start:start + rows, :], x_ref[start + rows:start + 2 * rows, :]], axis=1)
        y = dot(pair, pick_ref[...]).astype(jnp.bfloat16)
        for aw in range(3):
            y_scr[aw * rows:(aw + 1) * rows, q * 128:(q + 1) * 128] = y[:, aw * 128:(aw + 1) * 128]
    both = dot(k1t_ref[...], y_scr[...])
    lane = iota((128, cells), 1)
    from_last = jnp.where(lane < 64, 0.0, pltpu.roll(both[128:], 64, 1))
    pre = both[:128] + from_last
    sigma = jax.nn.sigmoid(pre)
    act = (pre * sigma).astype(jnp.bfloat16)
    act_ref[...] = act
    slope = sigma * (1.0 + pre * (1.0 - sigma))
    grad = (ag_ref[...].astype(jnp.float32) * slope).astype(jnp.bfloat16)
    pg_scr[:128, :] = grad
    to_last = pltpu.roll(grad.astype(jnp.float32), cells - 64, 1)
    pg_scr[128:, :] = jnp.where(lane < cells - 64, to_last, 0.0).astype(jnp.bfloat16)

    second = dot(act, ogu_ref[...], ((1,), (1,)))
    lane = iota((32, 128), 1)
    held = None
    for t in range(9):
        tile = second[:, t * 128:(t + 1) * 128]
        turned = pltpu.roll(tile, 64, 1)
        mixed = jnp.where(lane < 64, tile[0:32] + turned[64:96], turned[32:64] + tile[96:128])
        terms_ref[t * 32:(t + 1) * 32, :] = mixed.astype(jnp.bfloat16)
        if t % 2 == 0:
            held = jnp.where(lane < 64, turned[32:64], 0.0)
        else:
            held = jnp.where(lane < 64, held, tile[32:64])
        if t % 2 == 1:
            start = 288 + (t // 2) * 32
            terms_ref[start:start + 32, :] = held.astype(jnp.bfloat16)
    terms_ref[416:432, :] = jnp.where(lane[:16] < 64, held[:16], pltpu.roll(held[16:], 64, 1)).astype(jnp.bfloat16)

    first = dot(y_scr[...], pg_scr[...], ((1,), (1,)))
    shape = (rows, 256)
    row, col = iota(shape, 0), iota(shape, 1)
    h, hh, block = (row // 2) % HEIGHT, (col // 32) % 4, (col // 32) % 4
    rank, index = iota((48, rows), 0), iota((48, rows), 1)
    depth = rank // 16
    wanted = jnp.where(depth == 0, 1, depth - 1)
    gather = ones_where((rank % 16 == index // 16) & (wanted == index % 2))
    for aw in range(3):
        tile = first[aw * rows:(aw + 1) * rows]
        packed = jnp.zeros(shape, jnp.float32)
        for ah in range(3):
            kept = jnp.where(h == 2 * hh + ah - 1, tile, 0.0)
            halves = []
            for half in (kept[:, :128], kept[:, 128:]):
                half = half + pltpu.roll(half, 64, 1)
                halves.append(half + pltpu.roll(half, 32, 1))
            packed = jnp.where(block == ah, jnp.concatenate(halves, axis=1), packed)
        high = packed.astype(jnp.bfloat16)
        low = (packed - high.astype(jnp.float32)).astype(jnp.bfloat16)
        total = dot(gather, high) + dot(gather, low)
        start = 432 + aw * 48
        terms_ref[start:start + 16, :] = total[:16, 128:].astype(jnp.bfloat16)
        terms_ref[start + 16:start + 48, :] = total[16:, :128].astype(jnp.bfloat16)
    rest = terms_ref.shape[0] - TERM_ROWS
    if rest > 0:
        terms_ref[TERM_ROWS:, :] = jnp.zeros((rest, 128), jnp.bfloat16)


def features_kernel(act_ref, k2_ref, out_ref, k2t_ref):
    band_of_second(k2_ref, k2t_ref)
    groups = out_ref.shape[1] // 128
    for g in range(groups):
        total = jnp.zeros((128, 128), jnp.float32)
        for t in range(9):
            taken = dot(act_ref[:, g * 512:(g + 1) * 512], upsampling(t // 3, t % 3), ((1,), (1,)))
            if t < 3 and g > 0:
                last = act_ref[:, (g - 1) * 512:g * 512]
                taken = taken + dot(last, upsampling(0, t, 4), ((1,), (1,)))
            band = k2t_ref[:, t * 128:(t + 1) * 128]
            total = total + dot(band, taken.astype(jnp.bfloat16), ((0,), (0,)))
        out_ref[:, g * 128:(g + 1) * 128] = total.astype(jnp.bfloat16)


def add_kernel(rows, mine_ref, out_ref):
    count = mine_ref.shape[0]
    held = -(-rows // 16) * 16
    to = ones_where(iota((held, count), 0) == iota((held, count), 1) % rows)
    back = ones_where(iota((count, held), 0) % rows == iota((count, held), 1))
    total = dot(to, mine_ref[...]).astype(jnp.bfloat16)
    out_ref[...] = dot(back, total).astype(jnp.bfloat16)


def unpack_kernel(whole_ref, first_ref, second_ref):
    for ad in range(3):
        for aw in range(3):
            t = ad * 3 + aw
            pair = whole_ref[t * 32:(t + 1) * 32, :].astype(jnp.float32)
            second_ref[ad, 1, aw] = pair[:, :64]
            second_ref[ad, 2, aw] = pair[:, 64:]
            if t == 8:
                lone = whole_ref[416:432, :].astype(jnp.float32)
                second_ref[ad, 0, aw] = jnp.concatenate([lone[:, :64], lone[:, 64:]], axis=0)
            else:
                start = 288 + (t // 2) * 32
                lone = whole_ref[start:start + 32, :].astype(jnp.float32)
                second_ref[ad, 0, aw] = lone[:, :64] if t % 2 == 0 else lone[:, 64:]
            start = 432 + aw * 48 + ad * 16
            tile = whole_ref[start:start + 16, :].astype(jnp.float32)
            for ah in range(3):
                first_ref[ad, ah, aw] = tile[:, ah * 32:(ah + 1) * 32]


def call(kernel, outs, args, scratch=(), flops=0):
    whole = pl.BlockSpec(memory_space=pltpu.VMEM)
    size = sum(a.size * a.dtype.itemsize for a in list(args) + list(outs))
    return pl.pallas_call(
        kernel,
        out_shape=tuple(outs),
        in_specs=[whole] * len(args),
        out_specs=(whole,) * len(outs),
        scratch_shapes=list(scratch),
        compiler_params=pltpu.CompilerParams(vmem_limit_bytes=VMEM_BYTES),
        cost_estimate=pl.CostEstimate(flops=flops, bytes_accessed=size, transcendentals=0),
    )(*args)


def array(shape, dtype=jnp.bfloat16):
    return jax.ShapeDtypeStruct(shape, dtype)


def by_tap(kernel):
    return jnp.transpose(kernel, (2, 3, 4, 1, 0))


def prepare(k1, k2, out_grad):
    c0, c1 = k1.shape[3:]
    c2 = k2.shape[4]
    planes = out_grad.shape[2]
    cells = planes * 2 * 64
    og = out_grad.reshape(c2, planes, 2, 32).transpose(2, 0, 1, 3).reshape(2 * c2, planes * 32)
    outs = [
        array((256, 384)),
        array((2 * 4 * c1, 3 * c0 * 16)),
        array((9 * 2 * c2, cells)),
        array((4 * c1, cells)),
    ]
    scratch = [pltpu.VMEM((4 * c1, 9 * 2 * c2), jnp.bfloat16)]
    return call(prepare_kernel, outs, (k1, k2, og), scratch, flops=2 * 128 * 1152 * cells * 2)


def body(crops, first_kernel, second_kernel, out_grad):
    axes = ("space", "sample")
    devices = lax.axis_size(axes)
    channels_out, planes = out_grad.shape[1:3]
    arrived = lax.all_to_all(crops, "space", split_axis=0, concat_axis=0, tiled=True)
    sources, channels_in, two, flat_cells = arrived.shape
    x = arrived.reshape(sources, channels_in, two, HEIGHT, WIDTH).transpose(0, 1, 3, 2, 4)
    x = x.reshape(sources * channels_in * two * HEIGHT, WIDTH)
    k1, k2 = by_tap(first_kernel), by_tap(second_kernel)
    pick, k1t, ogu, act_grad = prepare(k1, k2, out_grad)
    cells = act_grad.shape[1]
    rows = -(-TERM_ROWS // (devices * 2)) * 2
    act, terms = call(
        layer_kernel,
        [array((128, cells)), array((devices * rows, LANES))],
        (x, pick, k1t, ogu, act_grad),
        scratch=[pltpu.VMEM((768, cells), jnp.bfloat16), pltpu.VMEM((256, cells), jnp.bfloat16)],
        flops=2 * 128 * 4096 * cells,
    )
    blocks = terms.reshape(devices, rows // 2, 2, LANES)
    mine = lax.all_to_all(blocks, axes, split_axis=0, concat_axis=0, tiled=True)
    (features,) = call(
        features_kernel,
        [array((2 * channels_out, planes * 32))],
        (act, k2),
        scratch=[pltpu.VMEM((128, 1152), jnp.bfloat16)],
        flops=2 * 128 * 1152 * cells,
    )
    features = features.reshape(2, channels_out, planes, 32).transpose(1, 2, 0, 3).reshape(out_grad.shape)
    add = functools.partial(add_kernel, rows)
    (spread,) = call(add, [array(terms.shape)], (mine.reshape(terms.shape),))
    spread = spread.reshape(blocks.shape)
    whole = lax.all_to_all(spread, axes, split_axis=0, concat_axis=0, tiled=True)
    first, second = call(
        unpack_kernel,
        [
            array((3, 3, 3) + first_kernel.shape[1::-1], jnp.float32),
            array((3, 3, 3) + second_kernel.shape[1::-1], jnp.float32),
        ],
        (whole.reshape(terms.shape),),
    )
    return (features, jnp.transpose(first, (4, 3, 0, 1, 2)), jnp.transpose(second, (4, 3, 0, 1, 2)))


def solution(mesh):
    placed = (P("sample", None, "space", None), P(), P(), P(("sample", "space"), None, None, None))
    return jax.shard_map(
        body,
        mesh=mesh,
        in_specs=placed,
        out_specs=(P(("sample", "space"), None, None, None), P(), P()),
        check_vma=False,
    )
```

```python
import functools

import jax
import jax.numpy as jnp
from jax import lax
from jax.experimental import pallas as pl
from jax.experimental.pallas import tpu as pltpu
from jax.sharding import PartitionSpec as P

HEIGHT = 8
WIDTH = 128
LANES = 128
VMEM_BYTES = 16 * 1024 * 1024
TERM_ROWS = 576


def iota(shape, dim):
    return lax.broadcasted_iota(jnp.int32, shape, dim)


def dot(left, right, dims=((1,), (0,))):
    return lax.dot_general(left, right, (dims, ((), ())), preferred_element_type=jnp.float32)


def ones_where(mask):
    return jnp.where(mask, 1.0, 0.0).astype(jnp.bfloat16)


def band_of_second(k2_ref, k2t_ref):
    channels_mid, channels_out = k2_ref.shape[3:]
    empty = jnp.zeros((channels_mid, channels_out), jnp.bfloat16)
    for ad in range(3):
        for aw in range(3):
            tap = [k2_ref[ad, ah, aw] for ah in range(3)]
            band = ((tap[1], empty), (tap[2], tap[0]), (empty, tap[1]), (empty, tap[2]))
            start = (ad * 3 + aw) * 2 * channels_out
            for hh in range(4):
                k2t_ref[hh * channels_mid:(hh + 1) * channels_mid, start:start + 2 * channels_out] = (
                    jnp.concatenate(band[hh], axis=1))


def upsampling(ad, aw, beyond=0):
    row, col = iota((128, 512), 0), iota((128, 512), 1)
    target = 128 * (row // 32) + 2 * (row % 32) + 64 * (ad - 1) + aw - 1 + 128 * beyond
    keep = col == target
    if aw == 0:
        keep = keep & (row % 32 > 0)
    return ones_where(keep)


def prepare_kernel(k1_ref, k2_ref, og_ref, pick_ref, k1t_ref, ogu_ref, ag_ref, k2t_ref):
    channels_in, channels_mid = k1_ref.shape[3:]
    row, col = iota((2 * WIDTH, 2 * 64), 0), iota((2 * WIDTH, 2 * 64), 1)
    for aw in range(3):
        same = (row // WIDTH) == (col // 64)
        tap = (row % WIDTH) == 2 * (col % 64) + aw - 1
        pick_ref[:, aw * 128:(aw + 1) * 128] = ones_where(same & tap)
    shape = (9 * channels_in, channels_in * 2 * HEIGHT)
    row, col = iota(shape, 0), iota(shape, 1)
    ad, ah, i = row // (3 * channels_in), (row // channels_in) % 3, row % channels_in
    same = i == col // (2 * HEIGHT)
    h, d = (col // 2) % HEIGHT, col % 2
    taps = []
    for aw in range(3):
        parts = [k1_ref[a, b, aw] for a in range(3) for b in range(3)]
        taps.append(jnp.concatenate(parts, axis=0).astype(jnp.float32).T.astype(jnp.bfloat16))
    for following in range(2):
        plane = (ad == 0) & (d == 1) if following else (ad == d + 1)
        for hh in range(4):
            place = ones_where(same & plane & (h == 2 * hh + ah - 1))
            start = (following * 4 + hh) * channels_mid
            for aw in range(3):
                block = dot(taps[aw], place).astype(jnp.bfloat16)
                k1t_ref[start:start + channels_mid, aw * shape[1]:(aw + 1) * shape[1]] = block
    band_of_second(k2_ref, k2t_ref)
    groups = og_ref.shape[1] // 128
    for ad in range(3):
        for aw in range(3):
            t = ad * 3 + aw
            up = upsampling(ad, aw)
            for g in range(groups):
                value = dot(og_ref[:, g * 128:(g + 1) * 128], up)
                if ad == 0 and g + 1 < groups:
                    value = value + dot(og_ref[:, (g + 1) * 128:(g + 2) * 128], upsampling(ad, aw, 4))
                ogu_ref[t * 128:(t + 1) * 128, g * 512:(g + 1) * 512] = value.astype(jnp.bfloat16)
    for g in range(groups):
        lanes = slice(g * 512, (g + 1) * 512)
        ag_ref[:, lanes] = dot(k2t_ref[...], ogu_ref[:, lanes]).astype(jnp.bfloat16)


def rotate_kernel(position_ref, crops_ref, *outs_and_sems):
    outs, sems = outs_and_sems[:-1], outs_and_sems[-1]
    count = len(outs)
    copies = []
    for step in range(count):
        block = lax.rem(position_ref[0] + step, count)
        copies.append(pltpu.make_async_copy(crops_ref.at[block], outs[step], sems.at[step]))
        copies[-1].start()
    for copy in copies:
        copy.wait()


def layer_kernel(position_ref, *refs):
    cells = refs[-6].shape[1]
    blocks = cells // 64
    pick_ref, k1t_ref, ogu_ref, ag_ref, act_ref, terms_ref, y_scr, pg_scr, x_ref = refs[blocks:]
    rows = 256
    for step in range(blocks):
        source = lax.rem(position_ref[0] - step + blocks, blocks)
        x_ref[pl.ds(pl.multiple_of(source * rows, rows), rows), :] = refs[step][...]
    for q in range(cells // 128):
        start = q * 2 * rows
        pair = jnp.concatenate([x_ref[start:start + rows, :], x_ref[start + rows:start + 2 * rows, :]], axis=1)
        y = dot(pair, pick_ref[...]).astype(jnp.bfloat16)
        for aw in range(3):
            y_scr[aw * rows:(aw + 1) * rows, q * 128:(q + 1) * 128] = y[:, aw * 128:(aw + 1) * 128]
    both = dot(k1t_ref[...], y_scr[...])
    lane = iota((128, cells), 1)
    from_last = jnp.where(lane < 64, 0.0, pltpu.roll(both[128:], 64, 1))
    pre = both[:128] + from_last
    sigma = jax.nn.sigmoid(pre)
    act = (pre * sigma).astype(jnp.bfloat16)
    act_ref[...] = act
    slope = sigma * (1.0 + pre * (1.0 - sigma))
    grad = (ag_ref[...].astype(jnp.float32) * slope).astype(jnp.bfloat16)
    pg_scr[:128, :] = grad
    to_last = pltpu.roll(grad.astype(jnp.float32), cells - 64, 1)
    pg_scr[128:, :] = jnp.where(lane < cells - 64, to_last, 0.0).astype(jnp.bfloat16)

    second = dot(act, ogu_ref[...], ((1,), (1,)))
    lane = iota((32, 128), 1)
    held = None
    for t in range(9):
        tile = second[:, t * 128:(t + 1) * 128]
        turned = pltpu.roll(tile, 64, 1)
        mixed = jnp.where(lane < 64, tile[0:32] + turned[64:96], turned[32:64] + tile[96:128])
        terms_ref[t * 32:(t + 1) * 32, :] = mixed.astype(jnp.bfloat16)
        if t % 2 == 0:
            held = jnp.where(lane < 64, turned[32:64], 0.0)
        else:
            held = jnp.where(lane < 64, held, tile[32:64])
        if t % 2 == 1:
            start = 288 + (t // 2) * 32
            terms_ref[start:start + 32, :] = held.astype(jnp.bfloat16)
    terms_ref[416:432, :] = jnp.where(lane[:16] < 64, held[:16], pltpu.roll(held[16:], 64, 1)).astype(jnp.bfloat16)

    first = dot(y_scr[...], pg_scr[...], ((1,), (1,)))
    shape = (rows, 256)
    row, col = iota(shape, 0), iota(shape, 1)
    h, hh, block = (row // 2) % HEIGHT, (col // 32) % 4, (col // 32) % 4
    rank, index = iota((48, rows), 0), iota((48, rows), 1)
    depth = rank // 16
    wanted = jnp.where(depth == 0, 1, depth - 1)
    gather = ones_where((rank % 16 == index // 16) & (wanted == index % 2))
    for aw in range(3):
        tile = first[aw * rows:(aw + 1) * rows]
        packed = jnp.zeros(shape, jnp.float32)
        for ah in range(3):
            kept = jnp.where(h == 2 * hh + ah - 1, tile, 0.0)
            halves = []
            for half in (kept[:, :128], kept[:, 128:]):
                half = half + pltpu.roll(half, 64, 1)
                halves.append(half + pltpu.roll(half, 32, 1))
            packed = jnp.where(block == ah, jnp.concatenate(halves, axis=1), packed)
        high = packed.astype(jnp.bfloat16)
        low = (packed - high.astype(jnp.float32)).astype(jnp.bfloat16)
        total = dot(gather, high) + dot(gather, low)
        start = 432 + aw * 48
        terms_ref[start:start + 16, :] = total[:16, 128:].astype(jnp.bfloat16)
        terms_ref[start + 16:start + 48, :] = total[16:, :128].astype(jnp.bfloat16)
    rest = terms_ref.shape[0] - TERM_ROWS
    if rest > 0:
        terms_ref[TERM_ROWS:, :] = jnp.zeros((rest, 128), jnp.bfloat16)


def features_kernel(act_ref, k2_ref, out_ref, k2t_ref):
    band_of_second(k2_ref, k2t_ref)
    groups = out_ref.shape[1] // 128
    for g in range(groups):
        total = jnp.zeros((128, 128), jnp.float32)
        for t in range(9):
            taken = dot(act_ref[:, g * 512:(g + 1) * 512], upsampling(t // 3, t % 3), ((1,), (1,)))
            if t < 3 and g > 0:
                last = act_ref[:, (g - 1) * 512:g * 512]
                taken = taken + dot(last, upsampling(0, t, 4), ((1,), (1,)))
            band = k2t_ref[:, t * 128:(t + 1) * 128]
            total = total + dot(band, taken.astype(jnp.bfloat16), ((0,), (0,)))
        out_ref[:, g * 128:(g + 1) * 128] = total.astype(jnp.bfloat16)


def add_kernel(rows, mine_ref, out_ref):
    count = mine_ref.shape[0]
    held = -(-rows // 16) * 16
    to = ones_where(iota((held, count), 0) == iota((held, count), 1) % rows)
    back = ones_where(iota((count, held), 0) % rows == iota((count, held), 1))
    total = dot(to, mine_ref[...]).astype(jnp.bfloat16)
    out_ref[...] = dot(back, total).astype(jnp.bfloat16)


def unpack_kernel(whole_ref, first_ref, second_ref):
    for ad in range(3):
        for aw in range(3):
            t = ad * 3 + aw
            pair = whole_ref[t * 32:(t + 1) * 32, :].astype(jnp.float32)
            second_ref[ad, 1, aw] = pair[:, :64]
            second_ref[ad, 2, aw] = pair[:, 64:]
            if t == 8:
                lone = whole_ref[416:432, :].astype(jnp.float32)
                second_ref[ad, 0, aw] = jnp.concatenate([lone[:, :64], lone[:, 64:]], axis=0)
            else:
                start = 288 + (t // 2) * 32
                lone = whole_ref[start:start + 32, :].astype(jnp.float32)
                second_ref[ad, 0, aw] = lone[:, :64] if t % 2 == 0 else lone[:, 64:]
            start = 432 + aw * 48 + ad * 16
            tile = whole_ref[start:start + 16, :].astype(jnp.float32)
            for ah in range(3):
                first_ref[ad, ah, aw] = tile[:, ah * 32:(ah + 1) * 32]


def call(kernel, outs, args, scratch=(), flops=0):
    whole = pl.BlockSpec(memory_space=pltpu.VMEM)
    scalar = pl.BlockSpec(memory_space=pltpu.SMEM)
    size = sum(a.size * a.dtype.itemsize for a in list(args) + list(outs))
    return pl.pallas_call(
        kernel,
        out_shape=tuple(outs),
        in_specs=[scalar if a.dtype == jnp.int32 else whole for a in args],
        out_specs=(whole,) * len(outs),
        scratch_shapes=list(scratch),
        compiler_params=pltpu.CompilerParams(vmem_limit_bytes=VMEM_BYTES),
        cost_estimate=pl.CostEstimate(flops=flops, bytes_accessed=size, transcendentals=0),
    )(*args)


def array(shape, dtype=jnp.bfloat16):
    return jax.ShapeDtypeStruct(shape, dtype)


def by_tap(kernel):
    return jnp.transpose(kernel, (2, 3, 4, 1, 0))


def prepare(k1, k2, out_grad):
    c0, c1 = k1.shape[3:]
    c2 = k2.shape[4]
    planes = out_grad.shape[2]
    cells = planes * 2 * 64
    og = out_grad.reshape(c2, planes, 2, 32).transpose(2, 0, 1, 3).reshape(2 * c2, planes * 32)
    outs = [
        array((256, 384)),
        array((2 * 4 * c1, 3 * c0 * 16)),
        array((9 * 2 * c2, cells)),
        array((4 * c1, cells)),
    ]
    scratch = [pltpu.VMEM((4 * c1, 9 * 2 * c2), jnp.bfloat16)]
    return call(prepare_kernel, outs, (k1, k2, og), scratch, flops=2 * 128 * 1152 * cells * 2)


def body(crops, first_kernel, second_kernel, out_grad):
    axes = ("space", "sample")
    devices = lax.axis_size(axes)
    channels_out, planes = out_grad.shape[1:3]
    space = lax.axis_size("space")
    position = lax.axis_index("space").astype(jnp.int32).reshape(1)
    smem, anywhere, vmem = (pl.BlockSpec(memory_space=m) for m in (pltpu.SMEM, pl.ANY, pltpu.VMEM))
    rotated = pl.pallas_call(
        rotate_kernel,
        out_shape=(array(crops.shape[1:]),) * space,
        in_specs=[smem, anywhere],
        out_specs=(vmem,) * space,
        scratch_shapes=[pltpu.SemaphoreType.DMA((space,))],
        compiler_params=pltpu.CompilerParams(vmem_limit_bytes=VMEM_BYTES),
    )(position, crops)
    arrived = [rotated[0]]
    for step in range(1, space):
        pairs = [(source, (source + step) % space) for source in range(space)]
        arrived.append(lax.ppermute(rotated[step], "space", pairs))
    x = []
    for block in arrived:
        channels_in, two, flat_cells = block.shape
        block = block.reshape(channels_in, two, HEIGHT, WIDTH).transpose(0, 2, 1, 3)
        x.append(block.reshape(channels_in * two * HEIGHT, WIDTH))
    k1, k2 = by_tap(first_kernel), by_tap(second_kernel)
    pick, k1t, ogu, act_grad = prepare(k1, k2, out_grad)
    cells = act_grad.shape[1]
    rows = -(-TERM_ROWS // (devices * 2)) * 2
    act, terms = call(
        layer_kernel,
        [array((128, cells)), array((devices * rows, LANES))],
        (position, *x, pick, k1t, ogu, act_grad),
        scratch=[pltpu.VMEM((768, cells), jnp.bfloat16), pltpu.VMEM((256, cells), jnp.bfloat16), pltpu.VMEM((4 * cells, 128), jnp.bfloat16)],
        flops=2 * 128 * 4096 * cells,
    )
    blocks = terms.reshape(devices, rows // 2, 2, LANES)
    mine = lax.all_to_all(blocks, axes, split_axis=0, concat_axis=0, tiled=True)
    (features,) = call(
        features_kernel,
        [array((2 * channels_out, planes * 32))],
        (act, k2),
        scratch=[pltpu.VMEM((128, 1152), jnp.bfloat16)],
        flops=2 * 128 * 1152 * cells,
    )
    features = features.reshape(2, channels_out, planes, 32).transpose(1, 2, 0, 3).reshape(out_grad.shape)
    add = functools.partial(add_kernel, rows)
    (spread,) = call(add, [array(terms.shape)], (mine.reshape(terms.shape),))
    spread = spread.reshape(blocks.shape)
    whole = lax.all_to_all(spread, axes, split_axis=0, concat_axis=0, tiled=True)
    first, second = call(
        unpack_kernel,
        [
            array((3, 3, 3) + first_kernel.shape[1::-1], jnp.float32),
            array((3, 3, 3) + second_kernel.shape[1::-1], jnp.float32),
        ],
        (whole.reshape(terms.shape),),
    )
    return (features, jnp.transpose(first, (4, 3, 0, 1, 2)), jnp.transpose(second, (4, 3, 0, 1, 2)))


def solution(mesh):
    placed = (P("sample", None, "space", None), P(), P(), P(("sample", "space"), None, None, None))
    return jax.shard_map(
        body,
        mesh=mesh,
        in_specs=placed,
        out_specs=(P(("sample", "space"), None, None, None), P(), P()),
        check_vma=False,
    )
```

```python
import functools

import jax
import jax.numpy as jnp
from jax import lax
from jax.experimental import pallas as pl
from jax.experimental.pallas import tpu as pltpu
from jax.sharding import PartitionSpec as P

HEIGHT = 8
WIDTH = 128
LANES = 128
VMEM_BYTES = 16 * 1024 * 1024
TERM_ROWS = 576


def iota(shape, dim):
    return lax.broadcasted_iota(jnp.int32, shape, dim)


def dot(left, right, dims=((1,), (0,))):
    return lax.dot_general(left, right, (dims, ((), ())), preferred_element_type=jnp.float32)


def ones_where(mask):
    return jnp.where(mask, 1.0, 0.0).astype(jnp.bfloat16)


def band_of_second(k2_ref, k2t_ref):
    channels_mid, channels_out = k2_ref.shape[3:]
    empty = jnp.zeros((channels_mid, channels_out), jnp.bfloat16)
    for ad in range(3):
        for aw in range(3):
            tap = [k2_ref[ad, ah, aw] for ah in range(3)]
            band = ((tap[1], empty), (tap[2], tap[0]), (empty, tap[1]), (empty, tap[2]))
            start = (ad * 3 + aw) * 2 * channels_out
            for hh in range(4):
                k2t_ref[hh * channels_mid:(hh + 1) * channels_mid, start:start + 2 * channels_out] = (
                    jnp.concatenate(band[hh], axis=1))


def upsampling(ad, aw, beyond=0):
    row, col = iota((128, 512), 0), iota((128, 512), 1)
    target = ((row >> 5) << 7) + ((row & 31) << 1) + (64 * (ad - 1) + aw - 1 + 128 * beyond)
    keep = col == target
    if aw == 0:
        keep = keep & ((row & 31) > 0)
    return ones_where(keep)


def prepare_kernel(k1_ref, k2_ref, og_ref, pick_ref, k1t_ref, ogu_ref, ag_ref, k2t_ref):
    channels_in, channels_mid = k1_ref.shape[3:]
    row, col = iota((2 * WIDTH, 2 * 64), 0), iota((2 * WIDTH, 2 * 64), 1)
    for aw in range(3):
        same = (row >> 7) == (col >> 6)
        tap = (row & 127) == 2 * (col & 63) + aw - 1
        pick_ref[:, aw * 128:(aw + 1) * 128] = ones_where(same & tap)
    shape = (9 * channels_in, channels_in * 2 * HEIGHT)
    row, col = iota(shape, 0), iota(shape, 1)
    tap = row >> 4
    ad = jnp.where(tap >= 6, 2, jnp.where(tap >= 3, 1, 0))
    ah, i = tap - 3 * ad, row & 15
    same = i == col >> 4
    h, d = (col >> 1) & 7, col & 1
    taps = []
    for aw in range(3):
        parts = [k1_ref[a, b, aw] for a in range(3) for b in range(3)]
        taps.append(jnp.concatenate(parts, axis=0).astype(jnp.float32).T.astype(jnp.bfloat16))
    for following in range(2):
        plane = (ad == 0) & (d == 1) if following else (ad == d + 1)
        for hh in range(4):
            place = ones_where(same & plane & (h == 2 * hh + ah - 1))
            start = (following * 4 + hh) * channels_mid
            for aw in range(3):
                block = dot(taps[aw], place).astype(jnp.bfloat16)
                k1t_ref[start:start + channels_mid, aw * shape[1]:(aw + 1) * shape[1]] = block
    band_of_second(k2_ref, k2t_ref)
    groups = og_ref.shape[1] // 128
    for ad in range(3):
        for aw in range(3):
            t = ad * 3 + aw
            up = upsampling(ad, aw)
            for g in range(groups):
                value = dot(og_ref[:, g * 128:(g + 1) * 128], up)
                if ad == 0 and g + 1 < groups:
                    value = value + dot(og_ref[:, (g + 1) * 128:(g + 2) * 128], upsampling(ad, aw, 4))
                ogu_ref[t * 128:(t + 1) * 128, g * 512:(g + 1) * 512] = value.astype(jnp.bfloat16)
    for g in range(groups):
        lanes = slice(g * 512, (g + 1) * 512)
        ag_ref[:, lanes] = dot(k2t_ref[...], ogu_ref[:, lanes]).astype(jnp.bfloat16)


def layer_kernel(steps, position_ref, *refs):
    cells = refs[-6].shape[1]
    blocks = cells // 64
    pick_ref, k1t_ref, ogu_ref, ag_ref, act_ref, terms_ref, y_scr, pg_scr, x_ref = refs[blocks:]
    rows = 256
    for place, step in enumerate(steps):
        source = lax.bitwise_xor(position_ref[0], jnp.int32(step))
        x_ref[pl.ds(pl.multiple_of(source * rows, rows), rows), :] = refs[place][...]
    for q in range(cells // 128):
        start = q * 2 * rows
        pair = jnp.concatenate([x_ref[start:start + rows, :], x_ref[start + rows:start + 2 * rows, :]], axis=1)
        y = dot(pair, pick_ref[...]).astype(jnp.bfloat16)
        for aw in range(3):
            y_scr[aw * rows:(aw + 1) * rows, q * 128:(q + 1) * 128] = y[:, aw * 128:(aw + 1) * 128]
    both = dot(k1t_ref[...], y_scr[...])
    lane = iota((128, cells), 1)
    from_last = jnp.where(lane < 64, 0.0, pltpu.roll(both[128:], 64, 1))
    pre = both[:128] + from_last
    sigma = jax.nn.sigmoid(pre)
    act = (pre * sigma).astype(jnp.bfloat16)
    act_ref[...] = act
    slope = sigma * (1.0 + pre * (1.0 - sigma))
    grad = (ag_ref[...].astype(jnp.float32) * slope).astype(jnp.bfloat16)
    pg_scr[:128, :] = grad
    to_last = pltpu.roll(grad.astype(jnp.float32), cells - 64, 1)
    pg_scr[128:, :] = jnp.where(lane < cells - 64, to_last, 0.0).astype(jnp.bfloat16)

    second = dot(act, ogu_ref[...], ((1,), (1,)))
    lane = iota((32, 128), 1)
    held = None
    for t in range(9):
        tile = second[:, t * 128:(t + 1) * 128]
        turned = pltpu.roll(tile, 64, 1)
        mixed = jnp.where(lane < 64, tile[0:32] + turned[64:96], turned[32:64] + tile[96:128])
        terms_ref[t * 32:(t + 1) * 32, :] = mixed.astype(jnp.bfloat16)
        if t % 2 == 0:
            held = jnp.where(lane < 64, turned[32:64], 0.0)
        else:
            held = jnp.where(lane < 64, held, tile[32:64])
        if t % 2 == 1:
            start = 288 + (t // 2) * 32
            terms_ref[start:start + 32, :] = held.astype(jnp.bfloat16)
    terms_ref[416:432, :] = jnp.where(lane[:16] < 64, held[:16], pltpu.roll(held[16:], 64, 1)).astype(jnp.bfloat16)

    first = dot(y_scr[...], pg_scr[...], ((1,), (1,)))
    shape = (rows, 256)
    row, col = iota(shape, 0), iota(shape, 1)
    h, hh = (row >> 1) & 7, (col >> 5) & 3
    rank, index = iota((48, rows), 0), iota((48, rows), 1)
    depth = rank >> 4
    wanted = jnp.where(depth == 0, 1, depth - 1)
    gather = ones_where(((rank & 15) == index >> 4) & (wanted == index & 1))
    for aw in range(3):
        tile = first[aw * rows:(aw + 1) * rows]
        packed = jnp.zeros(shape, jnp.float32)
        for ah in range(3):
            kept = jnp.where(h == 2 * hh + ah - 1, tile, 0.0)
            halves = []
            for half in (kept[:, :128], kept[:, 128:]):
                half = half + pltpu.roll(half, 64, 1)
                halves.append(half + pltpu.roll(half, 32, 1))
            packed = jnp.where(hh == ah, jnp.concatenate(halves, axis=1), packed)
        high = packed.astype(jnp.bfloat16)
        low = (packed - high.astype(jnp.float32)).astype(jnp.bfloat16)
        total = dot(gather, high) + dot(gather, low)
        start = 432 + aw * 48
        terms_ref[start:start + 16, :] = total[:16, 128:].astype(jnp.bfloat16)
        terms_ref[start + 16:start + 48, :] = total[16:, :128].astype(jnp.bfloat16)
    rest = terms_ref.shape[0] - TERM_ROWS
    if rest > 0:
        terms_ref[TERM_ROWS:, :] = jnp.zeros((rest, 128), jnp.bfloat16)


def features_kernel(act_ref, k2_ref, out_ref, k2t_ref):
    band_of_second(k2_ref, k2t_ref)
    groups = out_ref.shape[1] // 128
    for g in range(groups):
        total = jnp.zeros((128, 128), jnp.float32)
        for t in range(9):
            taken = dot(act_ref[:, g * 512:(g + 1) * 512], upsampling(t // 3, t % 3), ((1,), (1,)))
            if t < 3 and g > 0:
                last = act_ref[:, (g - 1) * 512:g * 512]
                taken = taken + dot(last, upsampling(0, t, 4), ((1,), (1,)))
            band = k2t_ref[:, t * 128:(t + 1) * 128]
            total = total + dot(band, taken.astype(jnp.bfloat16), ((0,), (0,)))
        out_ref[:, g * 128:(g + 1) * 128] = total.astype(jnp.bfloat16)


def place_in_block(shape, dim, size):
    index = iota(shape, dim)
    block = jnp.floor((index.astype(jnp.float32) + 0.5) * (1.0 / size))
    return index - size * block.astype(jnp.int32)


def add_kernel(rows, mine_ref, out_ref):
    count = mine_ref.shape[0]
    held = -(-rows // 16) * 16
    to = ones_where(iota((held, count), 0) == place_in_block((held, count), 1, rows))
    back = ones_where(place_in_block((count, held), 0, rows) == iota((count, held), 1))
    total = dot(to, mine_ref[...]).astype(jnp.bfloat16)
    out_ref[...] = dot(back, total).astype(jnp.bfloat16)


def unpack_kernel(whole_ref, first_ref, second_ref):
    for ad in range(3):
        for aw in range(3):
            t = ad * 3 + aw
            pair = whole_ref[t * 32:(t + 1) * 32, :].astype(jnp.float32)
            second_ref[ad, 1, aw] = pair[:, :64]
            second_ref[ad, 2, aw] = pair[:, 64:]
            if t == 8:
                lone = whole_ref[416:432, :].astype(jnp.float32)
                second_ref[ad, 0, aw] = jnp.concatenate([lone[:, :64], lone[:, 64:]], axis=0)
            else:
                start = 288 + (t // 2) * 32
                lone = whole_ref[start:start + 32, :].astype(jnp.float32)
                second_ref[ad, 0, aw] = lone[:, :64] if t % 2 == 0 else lone[:, 64:]
            start = 432 + aw * 48 + ad * 16
            tile = whole_ref[start:start + 16, :].astype(jnp.float32)
            for ah in range(3):
                first_ref[ad, ah, aw] = tile[:, ah * 32:(ah + 1) * 32]


def call(kernel, outs, args, scratch=(), flops=0):
    whole = pl.BlockSpec(memory_space=pltpu.VMEM)
    scalar = pl.BlockSpec(memory_space=pltpu.SMEM)
    size = sum(a.size * a.dtype.itemsize for a in list(args) + list(outs))
    return pl.pallas_call(
        kernel,
        out_shape=tuple(outs),
        in_specs=[scalar if a.dtype == jnp.int32 else whole for a in args],
        out_specs=(whole,) * len(outs),
        scratch_shapes=list(scratch),
        compiler_params=pltpu.CompilerParams(vmem_limit_bytes=VMEM_BYTES),
        cost_estimate=pl.CostEstimate(flops=flops, bytes_accessed=size, transcendentals=0),
    )(*args)


def array(shape, dtype=jnp.bfloat16):
    return jax.ShapeDtypeStruct(shape, dtype)


def by_tap(kernel):
    return jnp.transpose(kernel, (2, 3, 4, 1, 0))


def prepare(k1, k2, out_grad):
    c0, c1 = k1.shape[3:]
    c2 = k2.shape[4]
    planes = out_grad.shape[2]
    cells = planes * 2 * 64
    og = out_grad.reshape(c2, planes, 2, 32).transpose(2, 0, 1, 3).reshape(2 * c2, planes * 32)
    outs = [
        array((256, 384)),
        array((2 * 4 * c1, 3 * c0 * 16)),
        array((9 * 2 * c2, cells)),
        array((4 * c1, cells)),
    ]
    scratch = [pltpu.VMEM((4 * c1, 9 * 2 * c2), jnp.bfloat16)]
    return call(prepare_kernel, outs, (k1, k2, og), scratch, flops=2 * 128 * 1152 * cells * 2)


def body(crops, first_kernel, second_kernel, out_grad):
    axes = ("space", "sample")
    devices = lax.axis_size(axes)
    channels_out, planes = out_grad.shape[1:3]
    space = lax.axis_size("space")
    assert space & (space - 1) == 0
    position = lax.axis_index("space").astype(jnp.int32)
    steps = sorted(range(space), key=lambda step: -step.bit_length())
    k1, k2 = by_tap(first_kernel), by_tap(second_kernel)
    x = []
    for step in steps:
        block = lax.dynamic_index_in_dim(crops, position ^ step, 0, keepdims=False)
        if step > 0:
            block = lax.ppermute(block, "space", [(source, source ^ step) for source in range(space)])
        channels_in, two, flat_cells = block.shape
        block = block.reshape(channels_in, two, HEIGHT, WIDTH).transpose(0, 2, 1, 3)
        x.append(block.reshape(channels_in * two * HEIGHT, WIDTH))
    pick, k1t, ogu, act_grad = prepare(k1, k2, out_grad)
    cells = act_grad.shape[1]
    rows = -(-TERM_ROWS // (devices * 2)) * 2
    act, terms = call(
        functools.partial(layer_kernel, steps),
        [array((128, cells)), array((devices * rows, LANES))],
        (position.reshape(1), *x, pick, k1t, ogu, act_grad),
        scratch=[pltpu.VMEM((768, cells), jnp.bfloat16), pltpu.VMEM((256, cells), jnp.bfloat16), pltpu.VMEM((4 * cells, 128), jnp.bfloat16)],
        flops=2 * 128 * 4096 * cells,
    )
    blocks = terms.reshape(devices, rows // 2, 2, LANES)
    mine = lax.all_to_all(blocks, axes, split_axis=0, concat_axis=0, tiled=True)
    (features,) = call(
        features_kernel,
        [array((2 * channels_out, planes * 32))],
        (act, k2),
        scratch=[pltpu.VMEM((128, 1152), jnp.bfloat16)],
        flops=2 * 128 * 1152 * cells,
    )
    features = features.reshape(2, channels_out, planes, 32).transpose(1, 2, 0, 3).reshape(out_grad.shape)
    add = functools.partial(add_kernel, rows)
    (spread,) = call(add, [array(terms.shape)], (mine.reshape(terms.shape),))
    spread = spread.reshape(blocks.shape)
    whole = lax.all_to_all(spread, axes, split_axis=0, concat_axis=0, tiled=True)
    first, second = call(
        unpack_kernel,
        [
            array((3, 3, 3) + first_kernel.shape[1::-1], jnp.float32),
            array((3, 3, 3) + second_kernel.shape[1::-1], jnp.float32),
        ],
        (whole.reshape(terms.shape),),
    )
    return (features, jnp.transpose(first, (4, 3, 0, 1, 2)), jnp.transpose(second, (4, 3, 0, 1, 2)))


def solution(mesh):
    placed = (P("sample", None, "space", None), P(), P(), P(("sample", "space"), None, None, None))
    return jax.shard_map(
        body,
        mesh=mesh,
        in_specs=placed,
        out_specs=(P(("sample", "space"), None, None, None), P(), P()),
        check_vma=False,
    )
```

```python
import functools

import jax
import jax.numpy as jnp
from jax import lax
from jax.experimental import pallas as pl
from jax.experimental.pallas import tpu as pltpu
from jax.sharding import PartitionSpec as P

HEIGHT = 8
WIDTH = 128
LANES = 128
VMEM_BYTES = 16 * 1024 * 1024
TERM_ROWS = 576


def iota(shape, dim):
    return lax.broadcasted_iota(jnp.int32, shape, dim)


def dot(left, right, dims=((1,), (0,))):
    return lax.dot_general(left, right, (dims, ((), ())), preferred_element_type=jnp.float32)


def ones_where(mask):
    return jnp.where(mask, 1.0, 0.0).astype(jnp.bfloat16)


def band_of_second(k2_ref, k2t_ref):
    channels_mid, channels_out = k2_ref.shape[3:]
    empty = jnp.zeros((channels_mid, channels_out), jnp.bfloat16)
    for ad in range(3):
        for aw in range(3):
            tap = [k2_ref[ad, ah, aw] for ah in range(3)]
            band = ((tap[1], empty), (tap[2], tap[0]), (empty, tap[1]), (empty, tap[2]))
            start = (ad * 3 + aw) * 2 * channels_out
            for hh in range(4):
                k2t_ref[hh * channels_mid:(hh + 1) * channels_mid, start:start + 2 * channels_out] = (
                    jnp.concatenate(band[hh], axis=1))


def upsampling(ad, aw, beyond=0):
    row, col = iota((128, 512), 0), iota((128, 512), 1)
    target = ((row >> 5) << 7) + ((row & 31) << 1) + (64 * (ad - 1) + aw - 1 + 128 * beyond)
    keep = col == target
    if aw == 0:
        keep = keep & ((row & 31) > 0)
    return ones_where(keep)


def prepare_kernel(k1_ref, k2_ref, og_ref, pick_ref, k1t_ref, ogu_ref, ag_ref, k2t_ref):
    channels_in, channels_mid = k1_ref.shape[3:]
    row, col = iota((2 * WIDTH, 2 * 64), 0), iota((2 * WIDTH, 2 * 64), 1)
    for aw in range(3):
        same = (row >> 7) == (col >> 6)
        tap = (row & 127) == 2 * (col & 63) + aw - 1
        pick_ref[:, aw * 128:(aw + 1) * 128] = ones_where(same & tap)
    shape = (9 * channels_in, channels_in * 2 * HEIGHT)
    row, col = iota(shape, 0), iota(shape, 1)
    tap = row >> 4
    ad = jnp.where(tap >= 6, 2, jnp.where(tap >= 3, 1, 0))
    ah, i = tap - 3 * ad, row & 15
    same = i == col >> 4
    h, d = (col >> 1) & 7, col & 1
    taps = []
    for aw in range(3):
        parts = [k1_ref[a, b, aw] for a in range(3) for b in range(3)]
        taps.append(jnp.concatenate(parts, axis=0).astype(jnp.float32).T.astype(jnp.bfloat16))
    for following in range(2):
        plane = (ad == 0) & (d == 1) if following else (ad == d + 1)
        for hh in range(4):
            place = ones_where(same & plane & (h == 2 * hh + ah - 1))
            start = (following * 4 + hh) * channels_mid
            for aw in range(3):
                block = dot(taps[aw], place).astype(jnp.bfloat16)
                k1t_ref[start:start + channels_mid, aw * shape[1]:(aw + 1) * shape[1]] = block
    band_of_second(k2_ref, k2t_ref)
    groups = og_ref.shape[1] // 128
    for ad in range(3):
        for aw in range(3):
            t = ad * 3 + aw
            up = upsampling(ad, aw)
            for g in range(groups):
                value = dot(og_ref[:, g * 128:(g + 1) * 128], up)
                if ad == 0 and g + 1 < groups:
                    value = value + dot(og_ref[:, (g + 1) * 128:(g + 2) * 128], upsampling(ad, aw, 4))
                ogu_ref[t * 128:(t + 1) * 128, g * 512:(g + 1) * 512] = value.astype(jnp.bfloat16)
    for g in range(groups):
        lanes = slice(g * 512, (g + 1) * 512)
        ag_ref[:, lanes] = dot(k2t_ref[...], ogu_ref[:, lanes]).astype(jnp.bfloat16)


def layer_kernel(steps, position_ref, *refs):
    cells = refs[-6].shape[1]
    blocks = cells // 64
    pick_ref, k1t_ref, ogu_ref, ag_ref, act_ref, terms_ref, y_scr, pg_scr, x_ref = refs[blocks:]
    rows = 256
    for place, step in enumerate(steps):
        source = lax.bitwise_xor(position_ref[0], jnp.int32(step))
        x_ref[pl.ds(pl.multiple_of(source * rows, rows), rows), :] = refs[place][...]
    for q in range(cells // 128):
        start = q * 2 * rows
        pair = jnp.concatenate([x_ref[start:start + rows, :], x_ref[start + rows:start + 2 * rows, :]], axis=1)
        y = dot(pair, pick_ref[...]).astype(jnp.bfloat16)
        for aw in range(3):
            y_scr[aw * rows:(aw + 1) * rows, q * 128:(q + 1) * 128] = y[:, aw * 128:(aw + 1) * 128]
    both = dot(k1t_ref[...], y_scr[...])
    lane = iota((128, cells), 1)
    from_last = jnp.where(lane < 64, 0.0, pltpu.roll(both[128:], 64, 1))
    pre = both[:128] + from_last
    sigma = jax.nn.sigmoid(pre)
    act = (pre * sigma).astype(jnp.bfloat16)
    act_ref[...] = act
    slope = sigma * (1.0 + pre * (1.0 - sigma))
    grad = (ag_ref[...].astype(jnp.float32) * slope).astype(jnp.bfloat16)
    pg_scr[:128, :] = grad
    to_last = pltpu.roll(grad.astype(jnp.float32), cells - 64, 1)
    pg_scr[128:, :] = jnp.where(lane < cells - 64, to_last, 0.0).astype(jnp.bfloat16)

    second = dot(act, ogu_ref[...], ((1,), (1,)))
    lane = iota((32, 128), 1)
    held = None
    for t in range(9):
        tile = second[:, t * 128:(t + 1) * 128]
        turned = pltpu.roll(tile, 64, 1)
        mixed = jnp.where(lane < 64, tile[0:32] + turned[64:96], turned[32:64] + tile[96:128])
        terms_ref[t * 32:(t + 1) * 32, :] = mixed.astype(jnp.bfloat16)
        if t % 2 == 0:
            held = jnp.where(lane < 64, turned[32:64], 0.0)
        else:
            held = jnp.where(lane < 64, held, tile[32:64])
        if t % 2 == 1:
            start = 288 + (t // 2) * 32
            terms_ref[start:start + 32, :] = held.astype(jnp.bfloat16)
    terms_ref[416:432, :] = jnp.where(lane[:16] < 64, held[:16], pltpu.roll(held[16:], 64, 1)).astype(jnp.bfloat16)

    first = dot(y_scr[...], pg_scr[...], ((1,), (1,)))
    shape = (rows, 256)
    row, col = iota(shape, 0), iota(shape, 1)
    h, hh = (row >> 1) & 7, (col >> 5) & 3
    rank, index = iota((48, rows), 0), iota((48, rows), 1)
    depth = rank >> 4
    wanted = jnp.where(depth == 0, 1, depth - 1)
    gather = ones_where(((rank & 15) == index >> 4) & (wanted == index & 1))
    for aw in range(3):
        tile = first[aw * rows:(aw + 1) * rows]
        packed = jnp.zeros(shape, jnp.float32)
        for ah in range(3):
            kept = jnp.where(h == 2 * hh + ah - 1, tile, 0.0)
            halves = []
            for half in (kept[:, :128], kept[:, 128:]):
                half = half + pltpu.roll(half, 64, 1)
                halves.append(half + pltpu.roll(half, 32, 1))
            packed = jnp.where(hh == ah, jnp.concatenate(halves, axis=1), packed)
        high = packed.astype(jnp.bfloat16)
        low = (packed - high.astype(jnp.float32)).astype(jnp.bfloat16)
        total = dot(gather, high) + dot(gather, low)
        start = 432 + aw * 48
        terms_ref[start:start + 16, :] = total[:16, 128:].astype(jnp.bfloat16)
        terms_ref[start + 16:start + 48, :] = total[16:, :128].astype(jnp.bfloat16)
    rest = terms_ref.shape[0] - TERM_ROWS
    if rest > 0:
        terms_ref[TERM_ROWS:, :] = jnp.zeros((rest, 128), jnp.bfloat16)


def features_kernel(act_ref, k2_ref, out_ref, k2t_ref):
    band_of_second(k2_ref, k2t_ref)
    groups = out_ref.shape[1] // 128
    for g in range(groups):
        total = jnp.zeros((128, 128), jnp.float32)
        for t in range(9):
            taken = dot(act_ref[:, g * 512:(g + 1) * 512], upsampling(t // 3, t % 3), ((1,), (1,)))
            if t < 3 and g > 0:
                last = act_ref[:, (g - 1) * 512:g * 512]
                taken = taken + dot(last, upsampling(0, t, 4), ((1,), (1,)))
            band = k2t_ref[:, t * 128:(t + 1) * 128]
            total = total + dot(band, taken.astype(jnp.bfloat16), ((0,), (0,)))
        out_ref[:, g * 128:(g + 1) * 128] = total.astype(jnp.bfloat16)


def place_in_block(shape, dim, size):
    index = iota(shape, dim)
    block = jnp.floor((index.astype(jnp.float32) + 0.5) * (1.0 / size))
    return index - size * block.astype(jnp.int32)


def add_kernel(rows, mine_ref, out_ref):
    count = mine_ref.shape[0]
    held = -(-rows // 16) * 16
    to = ones_where(iota((held, count), 0) == place_in_block((held, count), 1, rows))
    back = ones_where(place_in_block((count, held), 0, rows) == iota((count, held), 1))
    total = dot(to, mine_ref[...]).astype(jnp.bfloat16)
    out_ref[...] = dot(back, total).astype(jnp.bfloat16)


def unpack_kernel(whole_ref, first_ref, second_ref):
    for ad in range(3):
        for aw in range(3):
            t = ad * 3 + aw
            pair = whole_ref[t * 32:(t + 1) * 32, :].astype(jnp.float32)
            second_ref[ad, 1, aw] = pair[:, :64]
            second_ref[ad, 2, aw] = pair[:, 64:]
            if t == 8:
                lone = whole_ref[416:432, :].astype(jnp.float32)
                second_ref[ad, 0, aw] = jnp.concatenate([lone[:, :64], lone[:, 64:]], axis=0)
            else:
                start = 288 + (t // 2) * 32
                lone = whole_ref[start:start + 32, :].astype(jnp.float32)
                second_ref[ad, 0, aw] = lone[:, :64] if t % 2 == 0 else lone[:, 64:]
            start = 432 + aw * 48 + ad * 16
            tile = whole_ref[start:start + 16, :].astype(jnp.float32)
            for ah in range(3):
                first_ref[ad, ah, aw] = tile[:, ah * 32:(ah + 1) * 32]


def call(kernel, outs, args, scratch=(), flops=0):
    whole = pl.BlockSpec(memory_space=pltpu.VMEM)
    scalar = pl.BlockSpec(memory_space=pltpu.SMEM)
    size = sum(a.size * a.dtype.itemsize for a in list(args) + list(outs))
    return pl.pallas_call(
        kernel,
        out_shape=tuple(outs),
        in_specs=[scalar if a.dtype == jnp.int32 else whole for a in args],
        out_specs=(whole,) * len(outs),
        scratch_shapes=list(scratch),
        compiler_params=pltpu.CompilerParams(vmem_limit_bytes=VMEM_BYTES),
        cost_estimate=pl.CostEstimate(flops=flops, bytes_accessed=size, transcendentals=0),
    )(*args)


def array(shape, dtype=jnp.bfloat16):
    return jax.ShapeDtypeStruct(shape, dtype)


def by_tap(kernel):
    return jnp.transpose(kernel, (2, 3, 4, 1, 0))


def prepare(k1, k2, out_grad):
    c0, c1 = k1.shape[3:]
    c2 = k2.shape[4]
    planes = out_grad.shape[2]
    cells = planes * 2 * 64
    og = out_grad.reshape(c2, planes, 2, 32).transpose(2, 0, 1, 3).reshape(2 * c2, planes * 32)
    outs = [
        array((256, 384)),
        array((2 * 4 * c1, 3 * c0 * 16)),
        array((9 * 2 * c2, cells)),
        array((4 * c1, cells)),
    ]
    scratch = [pltpu.VMEM((4 * c1, 9 * 2 * c2), jnp.bfloat16)]
    return call(prepare_kernel, outs, (k1, k2, og), scratch, flops=2 * 128 * 1152 * cells * 2)


def body(crops, first_kernel, second_kernel, out_grad):
    axes = ("space", "sample")
    devices = lax.axis_size(axes)
    channels_out, planes = out_grad.shape[1:3]
    space = lax.axis_size("space")
    assert space & (space - 1) == 0
    position = lax.axis_index("space").astype(jnp.int32)
    wanted = sorted(range(1, space), key=lambda step: -step.bit_length())
    steps = [0] + wanted[-2:0:-1] + [wanted[-1], wanted[0]]
    k1, k2 = by_tap(first_kernel), by_tap(second_kernel)
    x = []
    for step in steps:
        block = lax.dynamic_index_in_dim(crops, position ^ step, 0, keepdims=False)
        if step > 0:
            block = lax.ppermute(block, "space", [(source, source ^ step) for source in range(space)])
        channels_in, two, flat_cells = block.shape
        block = block.reshape(channels_in, two, HEIGHT, WIDTH).transpose(0, 2, 1, 3)
        x.append(block.reshape(channels_in * two * HEIGHT, WIDTH))
    pick, k1t, ogu, act_grad = prepare(k1, k2, out_grad)
    cells = act_grad.shape[1]
    rows = -(-TERM_ROWS // (devices * 2)) * 2
    act, terms = call(
        functools.partial(layer_kernel, steps),
        [array((128, cells)), array((devices * rows, LANES))],
        (position.reshape(1), *x, pick, k1t, ogu, act_grad),
        scratch=[pltpu.VMEM((768, cells), jnp.bfloat16), pltpu.VMEM((256, cells), jnp.bfloat16), pltpu.VMEM((4 * cells, 128), jnp.bfloat16)],
        flops=2 * 128 * 4096 * cells,
    )
    blocks = terms.reshape(devices, rows // 2, 2, LANES)
    mine = lax.all_to_all(blocks, axes, split_axis=0, concat_axis=0, tiled=True)
    (features,) = call(
        features_kernel,
        [array((2 * channels_out, planes * 32))],
        (act, k2),
        scratch=[pltpu.VMEM((128, 1152), jnp.bfloat16)],
        flops=2 * 128 * 1152 * cells,
    )
    features = features.reshape(2, channels_out, planes, 32).transpose(1, 2, 0, 3).reshape(out_grad.shape)
    add = functools.partial(add_kernel, rows)
    (spread,) = call(add, [array(terms.shape)], (mine.reshape(terms.shape),))
    spread = spread.reshape(blocks.shape)
    whole = lax.all_to_all(spread, axes, split_axis=0, concat_axis=0, tiled=True)
    first, second = call(
        unpack_kernel,
        [
            array((3, 3, 3) + first_kernel.shape[1::-1], jnp.float32),
            array((3, 3, 3) + second_kernel.shape[1::-1], jnp.float32),
        ],
        (whole.reshape(terms.shape),),
    )
    return (features, jnp.transpose(first, (4, 3, 0, 1, 2)), jnp.transpose(second, (4, 3, 0, 1, 2)))


def solution(mesh):
    placed = (P("sample", None, "space", None), P(), P(), P(("sample", "space"), None, None, None))
    return jax.shard_map(
        body,
        mesh=mesh,
        in_specs=placed,
        out_specs=(P(("sample", "space"), None, None, None), P(), P()),
        check_vma=False,
    )
```

```python
import functools

import jax
import jax.numpy as jnp
from jax import lax
from jax.experimental import pallas as pl
from jax.experimental.pallas import tpu as pltpu
from jax.sharding import PartitionSpec as P

HEIGHT = 8
WIDTH = 128
LANES = 128
VMEM_BYTES = 16 * 1024 * 1024
TERM_ROWS = 576


def iota(shape, dim):
    return lax.broadcasted_iota(jnp.int32, shape, dim)


def dot(left, right, dims=((1,), (0,))):
    return lax.dot_general(left, right, (dims, ((), ())), preferred_element_type=jnp.float32)


def ones_where(mask):
    return jnp.where(mask, 1.0, 0.0).astype(jnp.bfloat16)


def band_of_second(k2_ref, k2t_ref):
    channels_mid, channels_out = k2_ref.shape[3:]
    empty = jnp.zeros((channels_mid, channels_out), jnp.bfloat16)
    for ad in range(3):
        for aw in range(3):
            tap = [k2_ref[ad, ah, aw] for ah in range(3)]
            band = ((tap[1], empty), (tap[2], tap[0]), (empty, tap[1]), (empty, tap[2]))
            start = (ad * 3 + aw) * 2 * channels_out
            for hh in range(4):
                k2t_ref[hh * channels_mid:(hh + 1) * channels_mid, start:start + 2 * channels_out] = (
                    jnp.concatenate(band[hh], axis=1))


def upsampling(ad, aw):
    row, col = iota((128, 512), 0), iota((128, 512), 1)
    keep = col == ((row >> 5) << 7) + ((row & 31) << 1) + ((0 if ad == 1 else 64) + aw - 1)
    if aw == 0:
        keep = keep & ((row & 31) > 0)
    return ones_where(keep)


def prepare_kernel(steps, position_ref, k1_ref, k2_ref, *refs):
    flat_refs = refs[:len(steps)]
    pick_ref, k1m_ref, k1f_ref, ogu_ref, ag_ref, k2t_ref, og_ref = refs[len(steps):]
    channels_in, channels_mid = k1_ref.shape[3:]
    row, col = iota((2 * WIDTH, 2 * 64), 0), iota((2 * WIDTH, 2 * 64), 1)
    for aw in range(3):
        same = (row >> 7) == (col >> 6)
        tap = (row & 127) == 2 * (col & 63) + aw - 1
        pick_ref[:, aw * 128:(aw + 1) * 128] = ones_where(same & tap)
    taps = []
    for aw in range(3):
        parts = [k1_ref[a, b, aw] for a in range(3) for b in range(3)]
        taps.append(jnp.concatenate(parts, axis=0).astype(jnp.float32).T.astype(jnp.bfloat16))
    row, col = iota((9 * channels_in, 256), 0), iota((9 * channels_in, 256), 1)
    tap = row >> 4
    ad = jnp.where(tap >= 6, 2, jnp.where(tap >= 3, 1, 0))
    ah, i = tap - 3 * ad, row & 15
    pair = (i == col >> 4) & (ad == (col & 1) + 1)
    before_col = iota((9 * channels_in, 128), 1)
    before = (i[:, :128] == (before_col & 15)) & (ad[:, :128] == 0)
    for hh in range(4):
        rows = slice(hh * channels_mid, (hh + 1) * channels_mid)
        place = ones_where(pair & (((col >> 1) & 7) == 2 * hh + ah - 1))
        place_before = ones_where(before & ((before_col >> 4) == 2 * hh + ah[:, :128] - 1))
        for aw in range(3):
            k1m_ref[rows, aw * 256:(aw + 1) * 256] = dot(taps[aw], place).astype(jnp.bfloat16)
            k1f_ref[rows, aw * 128:(aw + 1) * 128] = dot(taps[aw], place_before).astype(jnp.bfloat16)
    band_of_second(k2_ref, k2t_ref)
    wide = og_ref.shape[2]
    row, col = iota((64, wide), 0), iota((64, wide), 1)
    pair_index = position_ref[0] >> 1
    turned = [None, None]
    for place, step in enumerate(steps):
        j = lax.bitwise_xor(pair_index, jnp.int32(step))
        for hhh in range(2):
            spread = ones_where(((row >> 5) == hhh) & (col == (row & 31) + j * 32))
            value = dot(flat_refs[place][...], spread)
            turned[hhh] = value if turned[hhh] is None else turned[hhh] + value
    for plane in range(2):
        for hhh in range(2):
            og_ref[plane, hhh * 64:(hhh + 1) * 64, :] = (
                turned[hhh][plane * 64:(plane + 1) * 64].astype(jnp.bfloat16))
    groups = wide // 128
    for ad in range(3):
        for aw in range(3):
            t = ad * 3 + aw
            up = upsampling(ad, aw)
            for g in range(groups):
                value = dot(og_ref[1 if ad == 0 else 0, :, g * 128:(g + 1) * 128], up)
                ogu_ref[t * 128:(t + 1) * 128, g * 512:(g + 1) * 512] = value.astype(jnp.bfloat16)
    for g in range(groups):
        lanes = slice(g * 512, (g + 1) * 512)
        ag_ref[:, lanes] = dot(k2t_ref[...], ogu_ref[:, lanes]).astype(jnp.bfloat16)


def packed_by_height(tile, h, hh):
    packed = jnp.zeros(tile.shape, jnp.float32)
    for ah in range(3):
        kept = jnp.where(h == 2 * hh + ah - 1, tile, 0.0)
        kept = kept + pltpu.roll(kept, 64, 1)
        kept = kept + pltpu.roll(kept, 32, 1)
        packed = jnp.where(hh == ah, kept, packed)
    return packed


def sum_rows(chosen, value):
    high = value.astype(jnp.bfloat16)
    low = (value - high.astype(jnp.float32)).astype(jnp.bfloat16)
    return dot(chosen, high) + dot(chosen, low)


def halo_kernel(own_ref, send_ref, own_out_ref, send_out_ref):
    chosen = odd_plane()
    for source, out in ((own_ref, own_out_ref), (send_ref, send_out_ref)):
        for j in range(source.shape[0] // 256):
            out[j * 128:(j + 1) * 128, :] = dot(chosen, source[j * 256:(j + 1) * 256, :]).astype(jnp.bfloat16)


def odd_plane():
    row, col = iota((128, 256), 0), iota((128, 256), 1)
    return ones_where(((row >> 4) == ((col >> 1) & 7)) & ((row & 15) == (col >> 4)) & ((col & 1) == 1))


def layer_kernel(position_ref, own_ref, got_ref, halo0_ref, halo1_ref, pick_ref, k1m_ref, k1f_ref, ogu_ref, ag_ref,
                 act_ref, terms_ref, y_scr, yf_scr):
    cells = ag_ref.shape[1]
    samples = cells // 128
    parity = position_ref[0] & 1
    chosen = odd_plane()
    for j in range(samples):
        lanes = slice(j * 128, (j + 1) * 128)
        own, got = own_ref[j * 256:(j + 1) * 256, :], got_ref[j * 256:(j + 1) * 256, :]
        lower, upper = jnp.where(parity == 0, own, got), jnp.where(parity == 0, got, own)
        y = dot(jnp.concatenate([lower, upper], axis=1), pick_ref[...]).astype(jnp.bfloat16)
        for aw in range(3):
            y_scr[aw * 256:(aw + 1) * 256, lanes] = y[:, aw * 128:(aw + 1) * 128]
        between = dot(chosen, lower).astype(jnp.bfloat16)
        rows = slice(j * 128, (j + 1) * 128)
        halo = jnp.where(parity == 0, halo0_ref[rows, :], halo1_ref[rows, :])
        y = dot(jnp.concatenate([halo, between], axis=1), pick_ref[...]).astype(jnp.bfloat16)
        for aw in range(3):
            yf_scr[aw * 128:(aw + 1) * 128, lanes] = y[:, aw * 128:(aw + 1) * 128]
    pre = dot(k1m_ref[...], y_scr[...]) + dot(k1f_ref[...], yf_scr[...])
    sigma = jax.nn.sigmoid(pre)
    act = (pre * sigma).astype(jnp.bfloat16)
    act_ref[...] = act
    slope = sigma * (1.0 + pre * (1.0 - sigma))
    grad = (ag_ref[...].astype(jnp.float32) * slope).astype(jnp.bfloat16)

    second = dot(act, ogu_ref[...], ((1,), (1,)))
    lane = iota((32, 128), 1)
    held = None
    for t in range(9):
        tile = second[:, t * 128:(t + 1) * 128]
        turned = pltpu.roll(tile, 64, 1)
        mixed = jnp.where(lane < 64, tile[0:32] + turned[64:96], turned[32:64] + tile[96:128])
        terms_ref[t * 32:(t + 1) * 32, :] = mixed.astype(jnp.bfloat16)
        if t % 2 == 0:
            held = jnp.where(lane < 64, turned[32:64], 0.0)
        else:
            held = jnp.where(lane < 64, held, tile[32:64])
            start = 288 + (t // 2) * 32
            terms_ref[start:start + 32, :] = held.astype(jnp.bfloat16)
    terms_ref[416:432, :] = jnp.where(lane[:16] < 64, held[:16], pltpu.roll(held[16:], 64, 1)).astype(jnp.bfloat16)

    first = dot(y_scr[...], grad, ((1,), (1,)))
    before = dot(yf_scr[...], grad, ((1,), (1,)))
    row, hh = iota((256, 128), 0), iota((256, 128), 1) >> 5
    rank, index = iota((32, 256), 0), iota((32, 256), 1)
    chosen = ones_where(((rank & 15) == index >> 4) & ((rank >> 4) == (index & 1)))
    rank, index = iota((16, 128), 0), iota((16, 128), 1)
    chosen_before = ones_where(rank == (index & 15))
    for aw in range(3):
        start = 432 + aw * 48
        tile = packed_by_height(before[aw * 128:(aw + 1) * 128], row[:128] >> 4, hh[:128])
        terms_ref[start:start + 16, :] = sum_rows(chosen_before, tile).astype(jnp.bfloat16)
        tile = packed_by_height(first[aw * 256:(aw + 1) * 256], (row >> 1) & 7, hh)
        terms_ref[start + 16:start + 48, :] = sum_rows(chosen, tile).astype(jnp.bfloat16)
    rest = terms_ref.shape[0] - TERM_ROWS
    if rest > 0:
        terms_ref[TERM_ROWS:, :] = jnp.zeros((rest, 128), jnp.bfloat16)


def features_kernel(act_ref, k2_ref, out_ref, k2t_ref):
    band_of_second(k2_ref, k2t_ref)
    row, col = iota((512, 512), 0), iota((512, 512), 1)
    order = ones_where(col == (((row >> 5) & 3) << 7) + ((row >> 7) << 5) + (row & 31))
    for g in range(out_ref.shape[0] // 4):
        share = [jnp.zeros((128, 128), jnp.float32) for _ in range(2)]
        for t in range(9):
            taken = dot(act_ref[:, g * 512:(g + 1) * 512], upsampling(t // 3, t % 3), ((1,), (1,)))
            band = k2t_ref[:, t * 128:(t + 1) * 128]
            later = 1 if t < 3 else 0
            share[later] = share[later] + dot(band, taken.astype(jnp.bfloat16), ((0,), (0,)))
        parts = [share[later][hhh * 64:(hhh + 1) * 64] for later in range(2) for hhh in range(2)]
        mixed = dot(jnp.concatenate(parts, axis=1).astype(jnp.bfloat16), order).astype(jnp.bfloat16)
        for j in range(4):
            out_ref[4 * g + j] = mixed[:, j * 128:(j + 1) * 128]


def join_kernel(steps, position_ref, *refs):
    shares, out_ref, held = refs[:len(steps)], refs[-2], refs[-1]
    pair_index = position_ref[0] >> 1
    for place, step in enumerate(steps):
        held[lax.bitwise_xor(pair_index, jnp.int32(step))] = shares[place][...].astype(jnp.float32)
    for plane in range(len(steps)):
        total = held[plane][:, :64]
        if plane > 0:
            total = total + held[plane - 1][:, 64:]
        out_ref[plane] = total.astype(jnp.bfloat16)


def place_in_block(shape, dim, size):
    index = iota(shape, dim)
    block = jnp.floor((index.astype(jnp.float32) + 0.5) * (1.0 / size))
    return index - size * block.astype(jnp.int32)


def add_kernel(rows, mine_ref, out_ref):
    count = mine_ref.shape[0]
    held = -(-rows // 16) * 16
    to = ones_where(iota((held, count), 0) == place_in_block((held, count), 1, rows))
    back = ones_where(place_in_block((count, held), 0, rows) == iota((count, held), 1))
    total = dot(to, mine_ref[...]).astype(jnp.bfloat16)
    out_ref[...] = dot(back, total).astype(jnp.bfloat16)


def unpack_kernel(whole_ref, first_ref, second_ref):
    for ad in range(3):
        for aw in range(3):
            t = ad * 3 + aw
            pair = whole_ref[t * 32:(t + 1) * 32, :].astype(jnp.float32)
            second_ref[ad, 1, aw] = pair[:, :64]
            second_ref[ad, 2, aw] = pair[:, 64:]
            if t == 8:
                lone = whole_ref[416:432, :].astype(jnp.float32)
                second_ref[ad, 0, aw] = jnp.concatenate([lone[:, :64], lone[:, 64:]], axis=0)
            else:
                start = 288 + (t // 2) * 32
                lone = whole_ref[start:start + 32, :].astype(jnp.float32)
                second_ref[ad, 0, aw] = lone[:, :64] if t % 2 == 0 else lone[:, 64:]
            start = 432 + aw * 48 + ad * 16
            tile = whole_ref[start:start + 16, :].astype(jnp.float32)
            for ah in range(3):
                first_ref[ad, ah, aw] = tile[:, ah * 32:(ah + 1) * 32]


def call(kernel, outs, args, scratch=(), flops=0):
    whole = pl.BlockSpec(memory_space=pltpu.VMEM)
    scalar = pl.BlockSpec(memory_space=pltpu.SMEM)
    size = sum(a.size * a.dtype.itemsize for a in list(args) + list(outs))
    return pl.pallas_call(
        kernel,
        out_shape=tuple(outs),
        in_specs=[scalar if a.dtype == jnp.int32 else whole for a in args],
        out_specs=(whole,) * len(outs),
        scratch_shapes=[pltpu.VMEM(shape, dtype) for shape, dtype in scratch],
        compiler_params=pltpu.CompilerParams(vmem_limit_bytes=VMEM_BYTES),
        cost_estimate=pl.CostEstimate(flops=flops, bytes_accessed=size, transcendentals=0),
    )(*args)


def array(shape, dtype=jnp.bfloat16):
    return jax.ShapeDtypeStruct(shape, dtype)


def by_tap(kernel):
    return jnp.transpose(kernel, (2, 3, 4, 1, 0))


def as_rows(block):
    samples, channels, two, flat_cells = block.shape
    block = block.reshape(samples, channels, two, HEIGHT, WIDTH).transpose(0, 1, 3, 2, 4)
    return block.reshape(samples * channels * two * HEIGHT, WIDTH)


def swap(block, space, step):
    if step == 0:
        return block
    return lax.ppermute(block, "space", [(source, source ^ step) for source in range(space)])


def body(crops, first_kernel, second_kernel, out_grad):
    axes = ("space", "sample")
    devices = lax.axis_size(axes)
    space = lax.axis_size("space")
    assert space & (space - 1) == 0 and space >= 8
    samples, channels_in, two, flat_cells = crops.shape
    channels_out, planes = out_grad.shape[1:3]
    pairs = space // 2
    cells = pairs * 128
    position = lax.axis_index("space").astype(jnp.int32)
    parity, pair_index = position & 1, position >> 1
    scalar = position.reshape(1)
    steps = list(range(pairs))
    k1, k2 = by_tap(first_kernel), by_tap(second_kernel)

    by_parity = crops.reshape(pairs, 2, channels_in, two, flat_cells)
    own = lax.dynamic_index_in_dim(by_parity, parity, 1, keepdims=False)
    send = lax.dynamic_index_in_dim(by_parity, parity ^ 1, 1, keepdims=False)
    got = swap(send, space, 1)
    halo_to_odd, halo_to_even = call(
        halo_kernel, [array((pairs * 128, 128))] * 2, (as_rows(own), as_rows(send)), flops=2 * 256 * 128 * 1024
    )
    halo = []
    for to, block in enumerate((halo_to_even, halo_to_odd)):
        upward = [(2 * z + 1, 2 * z + 2 + to) for z in range(pairs - 1)]
        halo.append(lax.ppermute(block, "space", upward))
    by_plane = jnp.pad(jnp.transpose(out_grad[0], (1, 0, 2)), ((0, 1), (0, 0), (0, 0)))
    flat = []
    for step in steps:
        two_planes = lax.dynamic_slice_in_dim(by_plane, pair_index ^ step, 2, 0)
        flat.append(swap(two_planes.reshape(2 * channels_out, -1), space, 2 * step))

    pick, k1m, k1f, ogu, act_grad = call(
        functools.partial(prepare_kernel, steps),
        [array((256, 384)), array((128, 768)), array((128, 384)), array((1152, cells)), array((128, cells))],
        (scalar, k1, k2, *flat),
        scratch=[((128, 1152), jnp.bfloat16), ((2, 128, pairs * 32), jnp.bfloat16)],
        flops=2 * 128 * 1152 * cells * 2,
    )
    rows = -(-TERM_ROWS // (devices * 2)) * 2
    act, terms = call(
        layer_kernel,
        [array((128, cells)), array((devices * rows, LANES))],
        (scalar, as_rows(own), as_rows(got), *halo, pick, k1m, k1f, ogu, act_grad),
        scratch=[((768, cells), jnp.bfloat16), ((384, cells), jnp.bfloat16)],
        flops=2 * 128 * 4096 * cells,
    )
    blocks = terms.reshape(devices, rows // 2, 2, LANES)
    mine = lax.all_to_all(blocks, axes, split_axis=0, concat_axis=0, tiled=True)
    add = functools.partial(add_kernel, rows)
    (spread,) = call(add, [array(terms.shape)], (mine.reshape(terms.shape),))
    spread, act = lax.optimization_barrier((spread.reshape(blocks.shape), act))
    whole = lax.all_to_all(spread, axes, split_axis=0, concat_axis=0, tiled=True)
    first, second = call(
        unpack_kernel,
        [
            array((3, 3, 3) + first_kernel.shape[1::-1], jnp.float32),
            array((3, 3, 3) + second_kernel.shape[1::-1], jnp.float32),
        ],
        (whole.reshape(terms.shape),),
    )

    (shares,) = call(
        features_kernel,
        [array((pairs, channels_out, LANES))],
        (act, k2),
        scratch=[((128, 1152), jnp.bfloat16)],
        flops=2 * 128 * 1152 * cells,
    )
    arrived = []
    for step in steps:
        share = lax.dynamic_index_in_dim(shares, pair_index ^ step, 0, keepdims=False)
        arrived.append(swap(share, space, 2 * step))
    (features,) = call(
        functools.partial(join_kernel, steps),
        [array((planes, channels_out, 64))],
        (scalar, *arrived),
        scratch=[((planes, channels_out, LANES), jnp.float32)],
    )
    features = jnp.transpose(features, (1, 0, 2)).reshape(out_grad.shape)
    return (features, jnp.transpose(first, (4, 3, 0, 1, 2)), jnp.transpose(second, (4, 3, 0, 1, 2)))


def solution(mesh):
    placed = (P("sample", None, "space", None), P(), P(), P(("sample", "space"), None, None, None))
    return jax.shard_map(
        body,
        mesh=mesh,
        in_specs=placed,
        out_specs=(P(("sample", "space"), None, None, None), P(), P()),
        check_vma=False,
    )
```

```python
import functools

import jax
import jax.numpy as jnp
from jax import lax
from jax.experimental import pallas as pl
from jax.experimental.pallas import tpu as pltpu
from jax.sharding import PartitionSpec as P

HEIGHT = 8
WIDTH = 128
LANES = 128
VMEM_BYTES = 16 * 1024 * 1024
TERM_ROWS = 576


def iota(shape, dim):
    return lax.broadcasted_iota(jnp.int32, shape, dim)


def dot(left, right, dims=((1,), (0,))):
    return lax.dot_general(left, right, (dims, ((), ())), preferred_element_type=jnp.float32)


def ones_where(mask):
    return jnp.where(mask, 1.0, 0.0).astype(jnp.bfloat16)


def band_of_second(k2_ref, k2t_ref):
    channels_mid, channels_out = k2_ref.shape[3:]
    empty = jnp.zeros((channels_mid, channels_out), jnp.bfloat16)
    for ad in range(3):
        for aw in range(3):
            tap = [k2_ref[ad, ah, aw] for ah in range(3)]
            band = ((tap[1], empty), (tap[2], tap[0]), (empty, tap[1]), (empty, tap[2]))
            start = (ad * 3 + aw) * 2 * channels_out
            for hh in range(4):
                k2t_ref[hh * channels_mid:(hh + 1) * channels_mid, start:start + 2 * channels_out] = (
                    jnp.concatenate(band[hh], axis=1))


def upsampling(ad, aw):
    row, col = iota((128, 512), 0), iota((128, 512), 1)
    keep = col == ((row >> 5) << 7) + ((row & 31) << 1) + ((0 if ad == 1 else 64) + aw - 1)
    if aw == 0:
        keep = keep & ((row & 31) > 0)
    return ones_where(keep)


def prepare_kernel(steps, position_ref, k1_ref, k2_ref, *refs):
    flat_refs = refs[:len(steps)]
    pick_ref, k1m_ref, k1f_ref, ogu_ref, ag_ref, k2t_ref, og_ref = refs[len(steps):]
    channels_in, channels_mid = k1_ref.shape[3:]
    row, col = iota((2 * WIDTH, 2 * 64), 0), iota((2 * WIDTH, 2 * 64), 1)
    for aw in range(3):
        same = (row >> 7) == (col >> 6)
        tap = (row & 127) == 2 * (col & 63) + aw - 1
        pick_ref[:, aw * 128:(aw + 1) * 128] = ones_where(same & tap)
    taps = []
    for aw in range(3):
        parts = [k1_ref[a, b, aw] for a in range(3) for b in range(3)]
        taps.append(jnp.concatenate(parts, axis=0).astype(jnp.float32).T.astype(jnp.bfloat16))
    row, col = iota((9 * channels_in, 256), 0), iota((9 * channels_in, 256), 1)
    tap = row >> 4
    ad = jnp.where(tap >= 6, 2, jnp.where(tap >= 3, 1, 0))
    ah, i = tap - 3 * ad, row & 15
    pair = (i == col >> 4) & (ad == (col & 1) + 1)
    before_col = iota((9 * channels_in, 128), 1)
    before = (i[:, :128] == (before_col & 15)) & (ad[:, :128] == 0)
    for hh in range(4):
        rows = slice(hh * channels_mid, (hh + 1) * channels_mid)
        place = ones_where(pair & (((col >> 1) & 7) == 2 * hh + ah - 1))
        place_before = ones_where(before & ((before_col >> 4) == 2 * hh + ah[:, :128] - 1))
        for aw in range(3):
            k1m_ref[rows, aw * 256:(aw + 1) * 256] = dot(taps[aw], place).astype(jnp.bfloat16)
            k1f_ref[rows, aw * 128:(aw + 1) * 128] = dot(taps[aw], place_before).astype(jnp.bfloat16)
    band_of_second(k2_ref, k2t_ref)
    wide = og_ref.shape[2]
    row, col = iota((64, wide), 0), iota((64, wide), 1)
    pair_index = position_ref[0] >> 1
    turned = [None, None]
    for place, step in enumerate(steps):
        j = lax.bitwise_xor(pair_index, jnp.int32(step))
        for hhh in range(2):
            spread = ones_where(((row >> 5) == hhh) & (col == (row & 31) + j * 32))
            value = dot(flat_refs[place][...], spread)
            turned[hhh] = value if turned[hhh] is None else turned[hhh] + value
    for plane in range(2):
        for hhh in range(2):
            og_ref[plane, hhh * 64:(hhh + 1) * 64, :] = (
                turned[hhh][plane * 64:(plane + 1) * 64].astype(jnp.bfloat16))
    groups = wide // 128
    for ad in range(3):
        for aw in range(3):
            t = ad * 3 + aw
            up = upsampling(ad, aw)
            for g in range(groups):
                value = dot(og_ref[1 if ad == 0 else 0, :, g * 128:(g + 1) * 128], up)
                ogu_ref[t * 128:(t + 1) * 128, g * 512:(g + 1) * 512] = value.astype(jnp.bfloat16)
    for g in range(groups):
        lanes = slice(g * 512, (g + 1) * 512)
        ag_ref[:, lanes] = dot(k2t_ref[...], ogu_ref[:, lanes]).astype(jnp.bfloat16)


def packed_by_height(tile, h, hh):
    packed = jnp.zeros(tile.shape, jnp.float32)
    for ah in range(3):
        kept = jnp.where(h == 2 * hh + ah - 1, tile, 0.0)
        kept = kept + pltpu.roll(kept, 64, 1)
        kept = kept + pltpu.roll(kept, 32, 1)
        packed = jnp.where(hh == ah, kept, packed)
    return packed


def sum_rows(chosen, value):
    high = value.astype(jnp.bfloat16)
    low = (value - high.astype(jnp.float32)).astype(jnp.bfloat16)
    return dot(chosen, high) + dot(chosen, low)


def halo_kernel(own_ref, send_ref, own_out_ref, send_out_ref):
    chosen = odd_plane()
    for source, out in ((own_ref, own_out_ref), (send_ref, send_out_ref)):
        for j in range(source.shape[0] // 256):
            out[j * 128:(j + 1) * 128, :] = dot(chosen, source[j * 256:(j + 1) * 256, :]).astype(jnp.bfloat16)


def odd_plane():
    row, col = iota((128, 256), 0), iota((128, 256), 1)
    return ones_where(((row >> 4) == ((col >> 1) & 7)) & ((row & 15) == (col >> 4)) & ((col & 1) == 1))


def layer_kernel(position_ref, own_ref, got_ref, halo0_ref, halo1_ref, pick_ref, k1m_ref, k1f_ref, ogu_ref, ag_ref,
                 act_ref, terms_ref, y_scr, yf_scr):
    cells = ag_ref.shape[1]
    samples = cells // 128
    parity = position_ref[0] & 1
    chosen = odd_plane()
    for j in range(samples):
        lanes = slice(j * 128, (j + 1) * 128)
        own, got = own_ref[j * 256:(j + 1) * 256, :], got_ref[j * 256:(j + 1) * 256, :]
        lower, upper = jnp.where(parity == 0, own, got), jnp.where(parity == 0, got, own)
        y = dot(jnp.concatenate([lower, upper], axis=1), pick_ref[...]).astype(jnp.bfloat16)
        for aw in range(3):
            y_scr[aw * 256:(aw + 1) * 256, lanes] = y[:, aw * 128:(aw + 1) * 128]
        between = dot(chosen, lower).astype(jnp.bfloat16)
        rows = slice(j * 128, (j + 1) * 128)
        halo = jnp.where(parity == 0, halo0_ref[rows, :], halo1_ref[rows, :])
        y = dot(jnp.concatenate([halo, between], axis=1), pick_ref[...]).astype(jnp.bfloat16)
        for aw in range(3):
            yf_scr[aw * 128:(aw + 1) * 128, lanes] = y[:, aw * 128:(aw + 1) * 128]
    pre = dot(k1m_ref[...], y_scr[...]) + dot(k1f_ref[...], yf_scr[...])
    sigma = jax.nn.sigmoid(pre)
    act = (pre * sigma).astype(jnp.bfloat16)
    act_ref[...] = act
    slope = sigma * (1.0 + pre * (1.0 - sigma))
    grad = (ag_ref[...].astype(jnp.float32) * slope).astype(jnp.bfloat16)

    second = dot(act, ogu_ref[...], ((1,), (1,)))
    lane = iota((32, 128), 1)
    held = None
    for t in range(9):
        tile = second[:, t * 128:(t + 1) * 128]
        turned = pltpu.roll(tile, 64, 1)
        mixed = jnp.where(lane < 64, tile[0:32] + turned[64:96], turned[32:64] + tile[96:128])
        terms_ref[t * 32:(t + 1) * 32, :] = mixed.astype(jnp.bfloat16)
        if t % 2 == 0:
            held = jnp.where(lane < 64, turned[32:64], 0.0)
        else:
            held = jnp.where(lane < 64, held, tile[32:64])
            start = 288 + (t // 2) * 32
            terms_ref[start:start + 32, :] = held.astype(jnp.bfloat16)
    terms_ref[416:432, :] = jnp.where(lane[:16] < 64, held[:16], pltpu.roll(held[16:], 64, 1)).astype(jnp.bfloat16)

    first = dot(y_scr[...], grad, ((1,), (1,)))
    before = dot(yf_scr[...], grad, ((1,), (1,)))
    row, hh = iota((256, 128), 0), iota((256, 128), 1) >> 5
    rank, index = iota((32, 256), 0), iota((32, 256), 1)
    chosen = ones_where(((rank & 15) == index >> 4) & ((rank >> 4) == (index & 1)))
    rank, index = iota((16, 128), 0), iota((16, 128), 1)
    chosen_before = ones_where(rank == (index & 15))
    for aw in range(3):
        start = 432 + aw * 48
        tile = packed_by_height(before[aw * 128:(aw + 1) * 128], row[:128] >> 4, hh[:128])
        terms_ref[start:start + 16, :] = sum_rows(chosen_before, tile).astype(jnp.bfloat16)
        tile = packed_by_height(first[aw * 256:(aw + 1) * 256], (row >> 1) & 7, hh)
        terms_ref[start + 16:start + 48, :] = sum_rows(chosen, tile).astype(jnp.bfloat16)
    rest = terms_ref.shape[0] - TERM_ROWS
    if rest > 0:
        terms_ref[TERM_ROWS:, :] = jnp.zeros((rest, 128), jnp.bfloat16)


def features_kernel(act_ref, k2_ref, out_ref, k2t_ref):
    band_of_second(k2_ref, k2t_ref)
    row, col = iota((512, 512), 0), iota((512, 512), 1)
    order = ones_where(col == (((row >> 5) & 3) << 7) + ((row >> 7) << 5) + (row & 31))
    for g in range(out_ref.shape[0] // 4):
        share = [jnp.zeros((128, 128), jnp.float32) for _ in range(2)]
        for t in range(9):
            taken = dot(act_ref[:, g * 512:(g + 1) * 512], upsampling(t // 3, t % 3), ((1,), (1,)))
            band = k2t_ref[:, t * 128:(t + 1) * 128]
            later = 1 if t < 3 else 0
            share[later] = share[later] + dot(band, taken.astype(jnp.bfloat16), ((0,), (0,)))
        parts = [share[later][hhh * 64:(hhh + 1) * 64] for later in range(2) for hhh in range(2)]
        mixed = dot(jnp.concatenate(parts, axis=1).astype(jnp.bfloat16), order).astype(jnp.bfloat16)
        for j in range(4):
            out_ref[4 * g + j] = mixed[:, j * 128:(j + 1) * 128]


def join_kernel(steps, position_ref, *refs):
    shares, out_ref, held = refs[:len(steps)], refs[-2], refs[-1]
    pair_index = position_ref[0] >> 1
    for place, step in enumerate(steps):
        held[lax.bitwise_xor(pair_index, jnp.int32(step))] = shares[place][...].astype(jnp.float32)
    for plane in range(len(steps)):
        total = held[plane][:, :64]
        if plane > 0:
            total = total + held[plane - 1][:, 64:]
        out_ref[plane] = total.astype(jnp.bfloat16)


def place_in_block(shape, dim, size):
    index = iota(shape, dim)
    block = jnp.floor((index.astype(jnp.float32) + 0.5) * (1.0 / size))
    return index - size * block.astype(jnp.int32)


def add_kernel(rows, mine_ref, out_ref):
    count = mine_ref.shape[0]
    held = -(-rows // 16) * 16
    to = ones_where(iota((held, count), 0) == place_in_block((held, count), 1, rows))
    back = ones_where(place_in_block((count, held), 0, rows) == iota((count, held), 1))
    total = dot(to, mine_ref[...]).astype(jnp.bfloat16)
    out_ref[...] = dot(back, total).astype(jnp.bfloat16)


def unpack_kernel(whole_ref, first_ref, second_ref):
    for ad in range(3):
        for aw in range(3):
            t = ad * 3 + aw
            pair = whole_ref[t * 32:(t + 1) * 32, :].astype(jnp.float32)
            second_ref[ad, 1, aw] = pair[:, :64]
            second_ref[ad, 2, aw] = pair[:, 64:]
            if t == 8:
                lone = whole_ref[416:432, :].astype(jnp.float32)
                second_ref[ad, 0, aw] = jnp.concatenate([lone[:, :64], lone[:, 64:]], axis=0)
            else:
                start = 288 + (t // 2) * 32
                lone = whole_ref[start:start + 32, :].astype(jnp.float32)
                second_ref[ad, 0, aw] = lone[:, :64] if t % 2 == 0 else lone[:, 64:]
            start = 432 + aw * 48 + ad * 16
            tile = whole_ref[start:start + 16, :].astype(jnp.float32)
            for ah in range(3):
                first_ref[ad, ah, aw] = tile[:, ah * 32:(ah + 1) * 32]


def call(kernel, outs, args, scratch=(), flops=0):
    whole = pl.BlockSpec(memory_space=pltpu.VMEM)
    scalar = pl.BlockSpec(memory_space=pltpu.SMEM)
    size = sum(a.size * a.dtype.itemsize for a in list(args) + list(outs))
    return pl.pallas_call(
        kernel,
        out_shape=tuple(outs),
        in_specs=[scalar if a.dtype == jnp.int32 else whole for a in args],
        out_specs=(whole,) * len(outs),
        scratch_shapes=[pltpu.VMEM(shape, dtype) for shape, dtype in scratch],
        compiler_params=pltpu.CompilerParams(vmem_limit_bytes=VMEM_BYTES),
        cost_estimate=pl.CostEstimate(flops=flops, bytes_accessed=size, transcendentals=0),
    )(*args)


def array(shape, dtype=jnp.bfloat16):
    return jax.ShapeDtypeStruct(shape, dtype)


def by_tap(kernel):
    return jnp.transpose(kernel, (2, 3, 4, 1, 0))


def as_rows(block):
    samples, channels, two, flat_cells = block.shape
    block = block.reshape(samples, channels, two, HEIGHT, WIDTH).transpose(0, 1, 3, 2, 4)
    return block.reshape(samples * channels * two * HEIGHT, WIDTH)


def swap(block, space, step):
    if step == 0:
        return block
    return lax.ppermute(block, "space", [(source, source ^ step) for source in range(space)])


def body(crops, first_kernel, second_kernel, out_grad):
    axes = ("space", "sample")
    devices = lax.axis_size(axes)
    space = lax.axis_size("space")
    assert space & (space - 1) == 0 and space >= 8
    samples, channels_in, two, flat_cells = crops.shape
    channels_out, planes = out_grad.shape[1:3]
    pairs = space // 2
    cells = pairs * 128
    position = lax.axis_index("space").astype(jnp.int32)
    parity, pair_index = position & 1, position >> 1
    scalar = position.reshape(1)
    steps = list(range(pairs))
    k1, k2 = by_tap(first_kernel), by_tap(second_kernel)

    by_parity = crops.reshape(pairs, 2, channels_in, two, flat_cells)
    own = lax.dynamic_index_in_dim(by_parity, parity, 1, keepdims=False)
    send = lax.dynamic_index_in_dim(by_parity, parity ^ 1, 1, keepdims=False)
    got = swap(send, space, 1)
    by_plane = jnp.pad(jnp.transpose(out_grad[0], (1, 0, 2)), ((0, 1), (0, 0), (0, 0)))
    flat = []
    for step in steps:
        two_planes = lax.dynamic_slice_in_dim(by_plane, pair_index ^ step, 2, 0)
        flat.append(swap(two_planes.reshape(2 * channels_out, -1), space, 2 * step))

    own_now, send_now, flat = lax.optimization_barrier((own, send, flat))
    halo_to_odd, halo_to_even = call(
        halo_kernel, [array((pairs * 128, 128))] * 2, (as_rows(own_now), as_rows(send_now)), flops=2 * 256 * 128 * 1024
    )
    halo = []
    for to, block in enumerate((halo_to_even, halo_to_odd)):
        upward = [(2 * z + 1, 2 * z + 2 + to) for z in range(pairs - 1)]
        halo.append(lax.ppermute(block, "space", upward))
    pick, k1m, k1f, ogu, act_grad = call(
        functools.partial(prepare_kernel, steps),
        [array((256, 384)), array((128, 768)), array((128, 384)), array((1152, cells)), array((128, cells))],
        (scalar, k1, k2, *flat),
        scratch=[((128, 1152), jnp.bfloat16), ((2, 128, pairs * 32), jnp.bfloat16)],
        flops=2 * 128 * 1152 * cells * 2,
    )
    rows = -(-TERM_ROWS // (devices * 2)) * 2
    act, terms = call(
        layer_kernel,
        [array((128, cells)), array((devices * rows, LANES))],
        (scalar, as_rows(own), as_rows(got), *halo, pick, k1m, k1f, ogu, act_grad),
        scratch=[((768, cells), jnp.bfloat16), ((384, cells), jnp.bfloat16)],
        flops=2 * 128 * 4096 * cells,
    )
    blocks = terms.reshape(devices, rows // 2, 2, LANES)
    mine = lax.all_to_all(blocks, axes, split_axis=0, concat_axis=0, tiled=True)
    (shares,) = call(
        features_kernel,
        [array((pairs, channels_out, LANES))],
        (act, k2),
        scratch=[((128, 1152), jnp.bfloat16)],
        flops=2 * 128 * 1152 * cells,
    )
    mine, shares = lax.optimization_barrier((mine, shares))
    add = functools.partial(add_kernel, rows)
    (spread,) = call(add, [array(terms.shape)], (mine.reshape(terms.shape),))
    spread = spread.reshape(blocks.shape)
    whole = lax.all_to_all(spread, axes, split_axis=0, concat_axis=0, tiled=True)
    first, second = call(
        unpack_kernel,
        [
            array((3, 3, 3) + first_kernel.shape[1::-1], jnp.float32),
            array((3, 3, 3) + second_kernel.shape[1::-1], jnp.float32),
        ],
        (whole.reshape(terms.shape),),
    )

    arrived = []
    for step in steps:
        share = lax.dynamic_index_in_dim(shares, pair_index ^ step, 0, keepdims=False)
        arrived.append(swap(share, space, 2 * step))
    (features,) = call(
        functools.partial(join_kernel, steps),
        [array((planes, channels_out, 64))],
        (scalar, *arrived),
        scratch=[((planes, channels_out, LANES), jnp.float32)],
    )
    features = jnp.transpose(features, (1, 0, 2)).reshape(out_grad.shape)
    return (features, jnp.transpose(first, (4, 3, 0, 1, 2)), jnp.transpose(second, (4, 3, 0, 1, 2)))


def solution(mesh):
    placed = (P("sample", None, "space", None), P(), P(), P(("sample", "space"), None, None, None))
    return jax.shard_map(
        body,
        mesh=mesh,
        in_specs=placed,
        out_specs=(P(("sample", "space"), None, None, None), P(), P()),
        check_vma=False,
    )
```

```python
import functools

import jax
import jax.numpy as jnp
from jax import lax
from jax.experimental import pallas as pl
from jax.experimental.pallas import tpu as pltpu
from jax.sharding import PartitionSpec as P

HEIGHT = 8
WIDTH = 128
LANES = 128
VMEM_BYTES = 16 * 1024 * 1024
TERM_ROWS = 576


def iota(shape, dim):
    return lax.broadcasted_iota(jnp.int32, shape, dim)


def dot(left, right, dims=((1,), (0,))):
    return lax.dot_general(left, right, (dims, ((), ())), preferred_element_type=jnp.float32)


def ones_where(mask):
    return jnp.where(mask, 1.0, 0.0).astype(jnp.bfloat16)


def band_of_second(k2_ref, k2t_ref):
    channels_mid, channels_out = k2_ref.shape[3:]
    empty = jnp.zeros((channels_mid, channels_out), jnp.bfloat16)
    for ad in range(3):
        for aw in range(3):
            tap = [k2_ref[ad, ah, aw] for ah in range(3)]
            band = ((tap[1], empty), (tap[2], tap[0]), (empty, tap[1]), (empty, tap[2]))
            start = (ad * 3 + aw) * 2 * channels_out
            for hh in range(4):
                k2t_ref[hh * channels_mid:(hh + 1) * channels_mid, start:start + 2 * channels_out] = (
                    jnp.concatenate(band[hh], axis=1))


def upsampling(ad, aw):
    row, col = iota((128, 512), 0), iota((128, 512), 1)
    keep = col == ((row >> 5) << 7) + ((row & 31) << 1) + ((0 if ad == 1 else 64) + aw - 1)
    if aw == 0:
        keep = keep & ((row & 31) > 0)
    return ones_where(keep)


def prepare_kernel(half_ref, k1_ref, k2_ref, flat0_ref, flat1_ref, pick_ref, k1m_ref, k1f_ref, ogu_ref, ag_ref,
                   k2t_ref, og_ref):
    channels_in, channels_mid = k1_ref.shape[3:]
    row, col = iota((2 * WIDTH, 2 * 64), 0), iota((2 * WIDTH, 2 * 64), 1)
    for aw in range(3):
        same = (row >> 7) == (col >> 6)
        tap = (row & 127) == 2 * (col & 63) + aw - 1
        pick_ref[:, aw * 128:(aw + 1) * 128] = ones_where(same & tap)
    taps = []
    for aw in range(3):
        parts = [k1_ref[a, b, aw] for a in range(3) for b in range(3)]
        taps.append(jnp.concatenate(parts, axis=0).astype(jnp.float32).T.astype(jnp.bfloat16))
    row, col = iota((9 * channels_in, 256), 0), iota((9 * channels_in, 256), 1)
    tap = row >> 4
    ad = jnp.where(tap >= 6, 2, jnp.where(tap >= 3, 1, 0))
    ah, i = tap - 3 * ad, row & 15
    pair = (i == col >> 4) & (ad == (col & 1) + 1)
    before_col = iota((9 * channels_in, 128), 1)
    before = (i[:, :128] == (before_col & 15)) & (ad[:, :128] == 0)
    for hh in range(4):
        rows = slice(hh * channels_mid, (hh + 1) * channels_mid)
        place = ones_where(pair & (((col >> 1) & 7) == 2 * hh + ah - 1))
        place_before = ones_where(before & ((before_col >> 4) == 2 * hh + ah[:, :128] - 1))
        for aw in range(3):
            k1m_ref[rows, aw * 256:(aw + 1) * 256] = dot(taps[aw], place).astype(jnp.bfloat16)
            k1f_ref[rows, aw * 128:(aw + 1) * 128] = dot(taps[aw], place_before).astype(jnp.bfloat16)
    band_of_second(k2_ref, k2t_ref)
    wide = og_ref.shape[2]
    count = wide // 64
    row, col = iota((64, wide), 0), iota((64, wide), 1)
    for later in range(2):
        for hhh in range(2):
            value = jnp.zeros((64, wide), jnp.float32)
            for place, flat_ref in enumerate((flat0_ref, flat1_ref)):
                m = lax.bitwise_xor(half_ref[0], jnp.int32(place))
                for q in range(count):
                    spread = ones_where(((row >> 5) == hhh) & (col == (row & 31) + (m * count + q) * 32))
                    plane = q + later
                    value = value + dot(flat_ref[plane * 64:(plane + 1) * 64, :], spread)
            og_ref[later, hhh * 64:(hhh + 1) * 64, :] = value.astype(jnp.bfloat16)
    groups = wide // 128
    for ad in range(3):
        for aw in range(3):
            t = ad * 3 + aw
            up = upsampling(ad, aw)
            for g in range(groups):
                value = dot(og_ref[1 if ad == 0 else 0, :, g * 128:(g + 1) * 128], up)
                ogu_ref[t * 128:(t + 1) * 128, g * 512:(g + 1) * 512] = value.astype(jnp.bfloat16)
    for g in range(groups):
        lanes = slice(g * 512, (g + 1) * 512)
        ag_ref[:, lanes] = dot(k2t_ref[...], ogu_ref[:, lanes]).astype(jnp.bfloat16)


def packed_by_height(tile, h, hh):
    packed = jnp.zeros(tile.shape, jnp.float32)
    for ah in range(3):
        kept = jnp.where(h == 2 * hh + ah - 1, tile, 0.0)
        kept = kept + pltpu.roll(kept, 64, 1)
        kept = kept + pltpu.roll(kept, 32, 1)
        packed = jnp.where(hh == ah, kept, packed)
    return packed


def sum_rows(chosen, value):
    high = value.astype(jnp.bfloat16)
    low = (value - high.astype(jnp.float32)).astype(jnp.bfloat16)
    return dot(chosen, high) + dot(chosen, low)


def halo_kernel(x_ref, out_ref):
    chosen = odd_plane()
    start = x_ref.shape[0] - 512
    for m in range(2):
        rows = slice(start + m * 256, start + (m + 1) * 256)
        out_ref[m * 128:(m + 1) * 128, :] = dot(chosen, x_ref[rows, :]).astype(jnp.bfloat16)


def odd_plane():
    row, col = iota((128, 256), 0), iota((128, 256), 1)
    return ones_where(((row >> 4) == ((col >> 1) & 7)) & ((row & 15) == (col >> 4)) & ((col & 1) == 1))


def layer_kernel(x_ref, halo_ref, pick_ref, k1m_ref, k1f_ref, ogu_ref, ag_ref, act_ref, terms_ref, y_scr, yf_scr):
    cells = ag_ref.shape[1]
    count = cells // 256
    chosen = odd_plane()
    for m in range(2):
        before = halo_ref[m * 128:(m + 1) * 128, :]
        for q in range(count):
            block = m * count + q
            lanes = slice(block * 128, (block + 1) * 128)
            start = (4 * q + m) * 256
            lower, upper = x_ref[start:start + 256, :], x_ref[start + 512:start + 768, :]
            y = dot(jnp.concatenate([lower, upper], axis=1), pick_ref[...]).astype(jnp.bfloat16)
            for aw in range(3):
                y_scr[aw * 256:(aw + 1) * 256, lanes] = y[:, aw * 128:(aw + 1) * 128]
            between = dot(chosen, lower).astype(jnp.bfloat16)
            y = dot(jnp.concatenate([before, between], axis=1), pick_ref[...]).astype(jnp.bfloat16)
            for aw in range(3):
                yf_scr[aw * 128:(aw + 1) * 128, lanes] = y[:, aw * 128:(aw + 1) * 128]
            if q + 1 < count:
                before = dot(chosen, upper).astype(jnp.bfloat16)
    pre = dot(k1m_ref[...], y_scr[...]) + dot(k1f_ref[...], yf_scr[...])
    sigma = jax.nn.sigmoid(pre)
    act = (pre * sigma).astype(jnp.bfloat16)
    act_ref[...] = act
    slope = sigma * (1.0 + pre * (1.0 - sigma))
    grad = (ag_ref[...].astype(jnp.float32) * slope).astype(jnp.bfloat16)

    second = dot(act, ogu_ref[...], ((1,), (1,)))
    lane = iota((32, 128), 1)
    held = None
    for t in range(9):
        tile = second[:, t * 128:(t + 1) * 128]
        turned = pltpu.roll(tile, 64, 1)
        mixed = jnp.where(lane < 64, tile[0:32] + turned[64:96], turned[32:64] + tile[96:128])
        terms_ref[t * 32:(t + 1) * 32, :] = mixed.astype(jnp.bfloat16)
        if t % 2 == 0:
            held = jnp.where(lane < 64, turned[32:64], 0.0)
        else:
            held = jnp.where(lane < 64, held, tile[32:64])
            start = 288 + (t // 2) * 32
            terms_ref[start:start + 32, :] = held.astype(jnp.bfloat16)
    terms_ref[416:432, :] = jnp.where(lane[:16] < 64, held[:16], pltpu.roll(held[16:], 64, 1)).astype(jnp.bfloat16)

    first = dot(y_scr[...], grad, ((1,), (1,)))
    before = dot(yf_scr[...], grad, ((1,), (1,)))
    row, hh = iota((256, 128), 0), iota((256, 128), 1) >> 5
    rank, index = iota((32, 256), 0), iota((32, 256), 1)
    chosen = ones_where(((rank & 15) == index >> 4) & ((rank >> 4) == (index & 1)))
    rank, index = iota((16, 128), 0), iota((16, 128), 1)
    chosen_before = ones_where(rank == (index & 15))
    for aw in range(3):
        start = 432 + aw * 48
        tile = packed_by_height(before[aw * 128:(aw + 1) * 128], row[:128] >> 4, hh[:128])
        terms_ref[start:start + 16, :] = sum_rows(chosen_before, tile).astype(jnp.bfloat16)
        tile = packed_by_height(first[aw * 256:(aw + 1) * 256], (row >> 1) & 7, hh)
        terms_ref[start + 16:start + 48, :] = sum_rows(chosen, tile).astype(jnp.bfloat16)
    rest = terms_ref.shape[0] - TERM_ROWS
    if rest > 0:
        terms_ref[TERM_ROWS:, :] = jnp.zeros((rest, 128), jnp.bfloat16)


def features_kernel(act_ref, k2_ref, out_ref, k2t_ref):
    band_of_second(k2_ref, k2t_ref)
    groups = act_ref.shape[1] // 512
    count = groups * 2
    span = out_ref.shape[2]
    row, col = iota((512, 2 * span), 0), iota((512, 2 * span), 1)
    later, hhh, www = row >> 8, (row >> 7) & 1, row & 31
    total = jnp.zeros((64, 2 * span), jnp.float32)
    for g in range(groups):
        share = [jnp.zeros((128, 128), jnp.float32) for _ in range(2)]
        for t in range(9):
            taken = dot(act_ref[:, g * 512:(g + 1) * 512], upsampling(t // 3, t % 3), ((1,), (1,)))
            band = k2t_ref[:, t * 128:(t + 1) * 128]
            place = 1 if t < 3 else 0
            share[place] = share[place] + dot(band, taken.astype(jnp.bfloat16), ((0,), (0,)))
        parts = [share[place][side * 64:(side + 1) * 64] for place in range(2) for side in range(2)]
        block = ((row >> 5) & 3) + 4 * g
        m = jnp.where(block >= count, 1, 0)
        q = block - m * count
        order = ones_where(col == m * span + (q + later) * 64 + hhh * 32 + www)
        total = total + dot(jnp.concatenate(parts, axis=1).astype(jnp.bfloat16), order)
    for m in range(2):
        out_ref[m] = total[:, m * span:(m + 1) * span].astype(jnp.bfloat16)


def join_kernel(parity_ref, share0_ref, share1_ref, out_ref):
    first = share0_ref[...].astype(jnp.float32)
    second = share1_ref[...].astype(jnp.float32)
    even = parity_ref[0] == 0
    low, high = jnp.where(even, first, second), jnp.where(even, second, first)
    planes = out_ref.shape[0]
    count = planes // 2
    for plane in range(planes):
        if plane < count:
            total = low[:, plane * 64:(plane + 1) * 64]
        else:
            total = high[:, (plane - count) * 64:(plane - count + 1) * 64]
        if plane == count:
            total = total + low[:, plane * 64:(plane + 1) * 64]
        out_ref[plane] = total.astype(jnp.bfloat16)


def place_in_block(shape, dim, size):
    index = iota(shape, dim)
    block = jnp.floor((index.astype(jnp.float32) + 0.5) * (1.0 / size))
    return index - size * block.astype(jnp.int32)


def add_kernel(rows, mine_ref, out_ref):
    count = mine_ref.shape[0]
    held = -(-rows // 16) * 16
    to = ones_where(iota((held, count), 0) == place_in_block((held, count), 1, rows))
    back = ones_where(place_in_block((count, held), 0, rows) == iota((count, held), 1))
    total = dot(to, mine_ref[...]).astype(jnp.bfloat16)
    out_ref[...] = dot(back, total).astype(jnp.bfloat16)


def unpack_kernel(whole_ref, first_ref, second_ref):
    for ad in range(3):
        for aw in range(3):
            t = ad * 3 + aw
            pair = whole_ref[t * 32:(t + 1) * 32, :].astype(jnp.float32)
            second_ref[ad, 1, aw] = pair[:, :64]
            second_ref[ad, 2, aw] = pair[:, 64:]
            if t == 8:
                lone = whole_ref[416:432, :].astype(jnp.float32)
                second_ref[ad, 0, aw] = jnp.concatenate([lone[:, :64], lone[:, 64:]], axis=0)
            else:
                start = 288 + (t // 2) * 32
                lone = whole_ref[start:start + 32, :].astype(jnp.float32)
                second_ref[ad, 0, aw] = lone[:, :64] if t % 2 == 0 else lone[:, 64:]
            start = 432 + aw * 48 + ad * 16
            tile = whole_ref[start:start + 16, :].astype(jnp.float32)
            for ah in range(3):
                first_ref[ad, ah, aw] = tile[:, ah * 32:(ah + 1) * 32]


def call(kernel, outs, args, scratch=(), flops=0):
    whole = pl.BlockSpec(memory_space=pltpu.VMEM)
    scalar = pl.BlockSpec(memory_space=pltpu.SMEM)
    size = sum(a.size * a.dtype.itemsize for a in list(args) + list(outs))
    return pl.pallas_call(
        kernel,
        out_shape=tuple(outs),
        in_specs=[scalar if a.dtype == jnp.int32 else whole for a in args],
        out_specs=(whole,) * len(outs),
        scratch_shapes=[pltpu.VMEM(shape, dtype) for shape, dtype in scratch],
        compiler_params=pltpu.CompilerParams(vmem_limit_bytes=VMEM_BYTES),
        cost_estimate=pl.CostEstimate(flops=flops, bytes_accessed=size, transcendentals=0),
    )(*args)


def array(shape, dtype=jnp.bfloat16):
    return jax.ShapeDtypeStruct(shape, dtype)


def by_tap(kernel):
    return jnp.transpose(kernel, (2, 3, 4, 1, 0))


def as_rows(block):
    samples, channels, two, flat_cells = block.shape
    block = block.reshape(samples, channels, two, HEIGHT, WIDTH).transpose(0, 1, 3, 2, 4)
    return block.reshape(samples * channels * two * HEIGHT, WIDTH)


def body(crops, first_kernel, second_kernel, out_grad):
    axes = ("space", "sample")
    devices = lax.axis_size(axes)
    space = lax.axis_size("space")
    channels_out, planes = out_grad.shape[1:3]
    size = space // 2
    count = size // 2
    cells = size * 128
    position = lax.axis_index("space").astype(jnp.int32)
    half, parity = jnp.where(position >= size, 1, 0).astype(jnp.int32), position & 1
    k1, k2 = by_tap(first_kernel), by_tap(second_kernel)

    halves = [list(range(size)), list(range(size, space))]
    x = lax.all_to_all(crops, "space", split_axis=0, concat_axis=0, axis_index_groups=halves, tiled=True)
    x = as_rows(x)
    owner_to_worker = [[(n, (n >> 1) + size * ((n & 1) ^ other)) for n in range(space)] for other in range(2)]
    by_plane = jnp.pad(jnp.transpose(out_grad[0], (1, 0, 2)), ((0, 1), (0, 0), (0, 0)))
    flat = []
    for other in range(2):
        some = lax.dynamic_slice_in_dim(by_plane, (parity ^ other) * count, count + 1, 0)
        flat.append(lax.ppermute(some.reshape((count + 1) * channels_out, -1), "space", owner_to_worker[other]))
    pick, k1m, k1f, ogu, act_grad = call(
        prepare_kernel,
        [array((256, 384)), array((128, 768)), array((128, 384)), array((1152, cells)), array((128, cells))],
        (half.reshape(1), k1, k2, *flat),
        scratch=[((128, 1152), jnp.bfloat16), ((2, 128, size * 32), jnp.bfloat16)],
        flops=2 * 128 * 1152 * cells * 2,
    )
    x, pick, k1m, k1f, ogu, act_grad = lax.optimization_barrier((x, pick, k1m, k1f, ogu, act_grad))
    (halo,) = call(halo_kernel, [array((256, 128))], (x,), flops=2 * 256 * 256 * 128)
    halo = lax.ppermute(halo, "space", [(n, n + size) for n in range(size)])

    rows = -(-TERM_ROWS // (devices * 2)) * 2
    act, terms = call(
        layer_kernel,
        [array((128, cells)), array((devices * rows, LANES))],
        (x, halo, pick, k1m, k1f, ogu, act_grad),
        scratch=[((768, cells), jnp.bfloat16), ((384, cells), jnp.bfloat16)],
        flops=2 * 128 * 4096 * cells,
    )
    blocks = terms.reshape(devices, rows // 2, 2, LANES)
    mine = lax.all_to_all(blocks, axes, split_axis=0, concat_axis=0, tiled=True)
    span = -(-(count + 1) * 64 // LANES) * LANES
    (shares,) = call(
        features_kernel,
        [array((2, channels_out, span))],
        (act, k2),
        scratch=[((128, 1152), jnp.bfloat16)],
        flops=2 * 128 * 1152 * cells,
    )
    mine, shares = lax.optimization_barrier((mine, shares))
    add = functools.partial(add_kernel, rows)
    (spread,) = call(add, [array(terms.shape)], (mine.reshape(terms.shape),))
    spread = spread.reshape(blocks.shape)
    whole = lax.all_to_all(spread, axes, split_axis=0, concat_axis=0, tiled=True)
    first, second = call(
        unpack_kernel,
        [
            array((3, 3, 3) + first_kernel.shape[1::-1], jnp.float32),
            array((3, 3, 3) + second_kernel.shape[1::-1], jnp.float32),
        ],
        (whole.reshape(terms.shape),),
    )
    arrived = []
    for other in range(2):
        share = lax.dynamic_index_in_dim(shares, half ^ other, 0, keepdims=False)
        back = [(worker, owner) for owner, worker in owner_to_worker[other]]
        arrived.append(lax.ppermute(share, "space", back))
    (features,) = call(
        join_kernel,
        [array((planes, channels_out, 64))],
        (parity.reshape(1), *arrived),
    )
    features = jnp.transpose(features, (1, 0, 2)).reshape(out_grad.shape)
    return (features, jnp.transpose(first, (4, 3, 0, 1, 2)), jnp.transpose(second, (4, 3, 0, 1, 2)))


def solution(mesh):
    placed = (P("sample", None, "space", None), P(), P(), P(("sample", "space"), None, None, None))
    return jax.shard_map(
        body,
        mesh=mesh,
        in_specs=placed,
        out_specs=(P(("sample", "space"), None, None, None), P(), P()),
        check_vma=False,
    )
```

```python
import functools
import math

import jax
import jax.numpy as jnp
from jax import lax
from jax.experimental import pallas as pl
from jax.experimental.pallas import tpu as pltpu
from jax.sharding import PartitionSpec as P

HEIGHT = 8
WIDTH = 128
LANES = 128
VMEM_BYTES = 16 * 1024 * 1024
TERM_ROWS = 576


def iota(shape, dim):
    return lax.broadcasted_iota(jnp.int32, shape, dim)


def dot(left, right, dims=((1,), (0,))):
    return lax.dot_general(left, right, (dims, ((), ())), preferred_element_type=jnp.float32)


def ones_where(mask):
    return jnp.where(mask, 1.0, 0.0).astype(jnp.bfloat16)


def band_of_second(k2_ref, k2t_ref):
    channels_mid, channels_out = k2_ref.shape[3:]
    empty = jnp.zeros((channels_mid, channels_out), jnp.bfloat16)
    for ad in range(3):
        for aw in range(3):
            tap = [k2_ref[ad, ah, aw] for ah in range(3)]
            band = ((tap[1], empty), (tap[2], tap[0]), (empty, tap[1]), (empty, tap[2]))
            start = (ad * 3 + aw) * 2 * channels_out
            for hh in range(4):
                k2t_ref[hh * channels_mid:(hh + 1) * channels_mid, start:start + 2 * channels_out] = (
                    jnp.concatenate(band[hh], axis=1))


def upsampling(ad, aw, beyond=0):
    row, col = iota((128, 512), 0), iota((128, 512), 1)
    target = ((row >> 5) << 7) + ((row & 31) << 1) + (64 * (ad - 1) + aw - 1 + 128 * beyond)
    keep = col == target
    if aw == 0:
        keep = keep & ((row & 31) > 0)
    return ones_where(keep)


def prepare_kernel(k1_ref, k2_ref, og_ref, pick_ref, k1t_ref, ogt_ref, ag_ref, k2t_ref, ogu_ref):
    channels_in, channels_mid = k1_ref.shape[3:]
    row, col = iota((2 * WIDTH, 2 * 64), 0), iota((2 * WIDTH, 2 * 64), 1)
    for aw in range(3):
        same = (row >> 7) == (col >> 6)
        tap = (row & 127) == 2 * (col & 63) + aw - 1
        pick_ref[:, aw * 128:(aw + 1) * 128] = ones_where(same & tap)
    shape = (9 * channels_in, channels_in * 2 * HEIGHT)
    row, col = iota(shape, 0), iota(shape, 1)
    tap = row >> 4
    ad = jnp.where(tap >= 6, 2, jnp.where(tap >= 3, 1, 0))
    ah, i = tap - 3 * ad, row & 15
    same = i == col >> 4
    h, d = (col >> 1) & 7, col & 1
    taps = []
    for aw in range(3):
        parts = [k1_ref[a, b, aw] for a in range(3) for b in range(3)]
        taps.append(jnp.concatenate(parts, axis=0).astype(jnp.float32).T.astype(jnp.bfloat16))
    for following in range(2):
        plane = (ad == 0) & (d == 1) if following else (ad == d + 1)
        for hh in range(4):
            place = ones_where(same & plane & (h == 2 * hh + ah - 1))
            start = (following * 4 + hh) * channels_mid
            for aw in range(3):
                block = dot(taps[aw], place).astype(jnp.bfloat16)
                k1t_ref[start:start + channels_mid, aw * shape[1]:(aw + 1) * shape[1]] = block
    band_of_second(k2_ref, k2t_ref)
    groups = og_ref.shape[1] // 128
    for ad in range(3):
        for aw in range(3):
            t = ad * 3 + aw
            up = upsampling(ad, aw)
            for g in range(groups):
                value = dot(og_ref[:, g * 128:(g + 1) * 128], up)
                if ad == 0 and g + 1 < groups:
                    value = value + dot(og_ref[:, (g + 1) * 128:(g + 2) * 128], upsampling(ad, aw, 4))
                ogu_ref[t * 128:(t + 1) * 128, g * 512:(g + 1) * 512] = value.astype(jnp.bfloat16)
                ogt_ref[g * 512:(g + 1) * 512, t * 128:(t + 1) * 128] = value.T.astype(jnp.bfloat16)
    for g in range(groups):
        lanes = slice(g * 512, (g + 1) * 512)
        ag_ref[:, lanes] = dot(k2t_ref[...], ogu_ref[:, lanes]).astype(jnp.bfloat16)


def layer_kernel(steps, position_ref, *refs):
    cells = refs[-6].shape[1]
    blocks = cells // 64
    pick_ref, k1t_ref, ogt_ref, ag_ref, act_ref, terms_ref, y_scr, pg_scr, x_ref = refs[blocks:]
    rows = 256
    for place, step in enumerate(steps):
        source = lax.bitwise_xor(position_ref[0], jnp.int32(step))
        x_ref[pl.ds(pl.multiple_of(source * rows, rows), rows), :] = refs[place][...]
    for q in range(cells // 128):
        start = q * 2 * rows
        pair = jnp.concatenate([x_ref[start:start + rows, :], x_ref[start + rows:start + 2 * rows, :]], axis=1)
        y = dot(pair, pick_ref[...]).astype(jnp.bfloat16)
        for aw in range(3):
            y_scr[aw * rows:(aw + 1) * rows, q * 128:(q + 1) * 128] = y[:, aw * 128:(aw + 1) * 128]
    both = dot(k1t_ref[...], y_scr[...])
    lane = iota((128, cells), 1)
    from_last = jnp.where(lane < 64, 0.0, pltpu.roll(both[128:], 64, 1))
    pre = both[:128] + from_last
    sigma = jax.nn.sigmoid(pre)
    act = (pre * sigma).astype(jnp.bfloat16)
    act_ref[...] = act
    slope = sigma * (1.0 + pre * (1.0 - sigma))
    grad = (ag_ref[...].astype(jnp.float32) * slope).astype(jnp.bfloat16)
    pg_scr[:128, :] = grad
    to_last = pltpu.roll(grad.astype(jnp.float32), cells - 64, 1)
    pg_scr[128:, :] = jnp.where(lane < cells - 64, to_last, 0.0).astype(jnp.bfloat16)

    second = dot(act, ogt_ref[...])
    lane = iota((32, 128), 1)
    held = None
    for t in range(9):
        tile = second[:, t * 128:(t + 1) * 128]
        turned = pltpu.roll(tile, 64, 1)
        mixed = jnp.where(lane < 64, tile[0:32] + turned[64:96], turned[32:64] + tile[96:128])
        terms_ref[t * 32:(t + 1) * 32, :] = mixed.astype(jnp.bfloat16)
        if t % 2 == 0:
            held = jnp.where(lane < 64, turned[32:64], 0.0)
        else:
            held = jnp.where(lane < 64, held, tile[32:64])
        if t % 2 == 1:
            start = 288 + (t // 2) * 32
            terms_ref[start:start + 32, :] = held.astype(jnp.bfloat16)
    terms_ref[416:432, :] = jnp.where(lane[:16] < 64, held[:16], pltpu.roll(held[16:], 64, 1)).astype(jnp.bfloat16)

    first = dot(y_scr[...], pg_scr[...], ((1,), (1,)))
    shape = (rows, 256)
    row, col = iota(shape, 0), iota(shape, 1)
    h, hh = (row >> 1) & 7, (col >> 5) & 3
    rank, index = iota((48, rows), 0), iota((48, rows), 1)
    depth = rank >> 4
    wanted = jnp.where(depth == 0, 1, depth - 1)
    gather = ones_where(((rank & 15) == index >> 4) & (wanted == index & 1))
    for aw in range(3):
        tile = first[aw * rows:(aw + 1) * rows]
        packed = jnp.zeros(shape, jnp.float32)
        for ah in range(3):
            kept = jnp.where(h == 2 * hh + ah - 1, tile, 0.0)
            halves = []
            for half in (kept[:, :128], kept[:, 128:]):
                half = half + pltpu.roll(half, 64, 1)
                halves.append(half + pltpu.roll(half, 32, 1))
            packed = jnp.where(hh == ah, jnp.concatenate(halves, axis=1), packed)
        high = packed.astype(jnp.bfloat16)
        low = (packed - high.astype(jnp.float32)).astype(jnp.bfloat16)
        total = dot(gather, high) + dot(gather, low)
        start = 432 + aw * 48
        terms_ref[start:start + 16, :] = total[:16, 128:].astype(jnp.bfloat16)
        terms_ref[start + 16:start + 48, :] = total[16:, :128].astype(jnp.bfloat16)
    rest = terms_ref.shape[0] - TERM_ROWS
    if rest > 0:
        terms_ref[TERM_ROWS:, :] = jnp.zeros((rest, 128), jnp.bfloat16)


def features_kernel(act_ref, k2_ref, out_ref, k2t_ref):
    band_of_second(k2_ref, k2t_ref)
    groups = out_ref.shape[1] // 128
    for g in range(groups):
        total = jnp.zeros((128, 128), jnp.float32)
        for t in range(9):
            taken = dot(act_ref[:, g * 512:(g + 1) * 512], upsampling(t // 3, t % 3), ((1,), (1,)))
            if t < 3 and g > 0:
                last = act_ref[:, (g - 1) * 512:g * 512]
                taken = taken + dot(last, upsampling(0, t, 4), ((1,), (1,)))
            band = k2t_ref[:, t * 128:(t + 1) * 128]
            total = total + dot(band, taken.astype(jnp.bfloat16), ((0,), (0,)))
        out_ref[:, g * 128:(g + 1) * 128] = total.astype(jnp.bfloat16)


def add_kernel(rows, mine_ref, out_ref):
    count = mine_ref.shape[0]
    unit = rows * 16 // math.gcd(rows, 16)
    total = mine_ref[0:unit, :].astype(jnp.float32)
    for start in range(unit, count, unit):
        total = total + mine_ref[start:start + unit, :].astype(jnp.float32)
    if unit % (2 * rows) == 0 and (unit // 2) % 8 == 0:
        total = total[:unit // 2] + total[unit // 2:]
    parts = [total[start:start + rows] for start in range(0, total.shape[0], rows)]
    total = functools.reduce(jnp.add, parts)
    spread = jnp.concatenate([total] * (unit // rows), axis=0).astype(jnp.bfloat16)
    for start in range(0, count, unit):
        out_ref[start:start + unit, :] = spread


def unpack_kernel(whole_ref, first_ref, second_ref):
    for ad in range(3):
        for aw in range(3):
            t = ad * 3 + aw
            pair = whole_ref[t * 32:(t + 1) * 32, :].astype(jnp.float32)
            second_ref[ad, 1, aw] = pair[:, :64]
            second_ref[ad, 2, aw] = pair[:, 64:]
            if t == 8:
                lone = whole_ref[416:432, :].astype(jnp.float32)
                second_ref[ad, 0, aw] = jnp.concatenate([lone[:, :64], lone[:, 64:]], axis=0)
            else:
                start = 288 + (t // 2) * 32
                lone = whole_ref[start:start + 32, :].astype(jnp.float32)
                second_ref[ad, 0, aw] = lone[:, :64] if t % 2 == 0 else lone[:, 64:]
            start = 432 + aw * 48 + ad * 16
            tile = whole_ref[start:start + 16, :].astype(jnp.float32)
            for ah in range(3):
                first_ref[ad, ah, aw] = tile[:, ah * 32:(ah + 1) * 32]


def call(kernel, outs, args, scratch=(), flops=0):
    whole = pl.BlockSpec(memory_space=pltpu.VMEM)
    scalar = pl.BlockSpec(memory_space=pltpu.SMEM)
    size = sum(a.size * a.dtype.itemsize for a in list(args) + list(outs))
    return pl.pallas_call(
        kernel,
        out_shape=tuple(outs),
        in_specs=[scalar if a.dtype == jnp.int32 else whole for a in args],
        out_specs=(whole,) * len(outs),
        scratch_shapes=list(scratch),
        compiler_params=pltpu.CompilerParams(vmem_limit_bytes=VMEM_BYTES),
        cost_estimate=pl.CostEstimate(flops=flops, bytes_accessed=size, transcendentals=0),
    )(*args)


def array(shape, dtype=jnp.bfloat16):
    return jax.ShapeDtypeStruct(shape, dtype)


def by_tap(kernel):
    return jnp.transpose(kernel, (2, 3, 4, 1, 0))


def prepare(k1, k2, out_grad):
    c0, c1 = k1.shape[3:]
    c2 = k2.shape[4]
    planes = out_grad.shape[2]
    cells = planes * 2 * 64
    og = out_grad.reshape(c2, planes, 2, 32).transpose(2, 0, 1, 3).reshape(2 * c2, planes * 32)
    outs = [
        array((256, 384)),
        array((2 * 4 * c1, 3 * c0 * 16)),
        array((cells, 9 * 2 * c2)),
        array((4 * c1, cells)),
    ]
    scratch = [pltpu.VMEM((4 * c1, 9 * 2 * c2), jnp.bfloat16), pltpu.VMEM((9 * 2 * c2, cells), jnp.bfloat16)]
    return call(prepare_kernel, outs, (k1, k2, og), scratch, flops=2 * 128 * 1152 * cells * 2)


def body(crops, first_kernel, second_kernel, out_grad):
    axes = ("space", "sample")
    devices = lax.axis_size(axes)
    channels_out, planes = out_grad.shape[1:3]
    space = lax.axis_size("space")
    assert space & (space - 1) == 0
    position = lax.axis_index("space").astype(jnp.int32)
    wanted = sorted(range(1, space), key=lambda step: -step.bit_length())
    steps = [0] + wanted[::-1]
    k1, k2 = by_tap(first_kernel), by_tap(second_kernel)
    x = []
    early = [lax.dynamic_index_in_dim(crops, position ^ step, 0, keepdims=False) for step in wanted[:2]]
    rest, early = lax.optimization_barrier((crops, early))
    for step in steps:
        if step in wanted[:2]:
            block = early[wanted.index(step)]
        else:
            block = lax.dynamic_index_in_dim(rest, position ^ step, 0, keepdims=False)
        if step > 0:
            block = lax.ppermute(block, "space", [(source, source ^ step) for source in range(space)])
        channels_in, two, flat_cells = block.shape
        block = block.reshape(channels_in, two, HEIGHT, WIDTH).transpose(0, 2, 1, 3)
        x.append(block.reshape(channels_in * two * HEIGHT, WIDTH))
    pick, k1t, ogt, act_grad = prepare(k1, k2, out_grad)
    cells = act_grad.shape[1]
    rows = -(-TERM_ROWS // (devices * 2)) * 2
    act, terms = call(
        functools.partial(layer_kernel, steps),
        [array((128, cells)), array((devices * rows, LANES))],
        (position.reshape(1), *x, pick, k1t, ogt, act_grad),
        scratch=[pltpu.VMEM((768, cells), jnp.bfloat16), pltpu.VMEM((256, cells), jnp.bfloat16), pltpu.VMEM((4 * cells, 128), jnp.bfloat16)],
        flops=2 * 128 * 4096 * cells,
    )
    blocks = terms.reshape(devices, rows // 2, 2, LANES)
    mine = lax.all_to_all(blocks, axes, split_axis=0, concat_axis=0, tiled=True)
    (features,) = call(
        features_kernel,
        [array((2 * channels_out, planes * 32))],
        (act, k2),
        scratch=[pltpu.VMEM((128, 1152), jnp.bfloat16)],
        flops=2 * 128 * 1152 * cells,
    )
    features = features.reshape(2, channels_out, planes, 32).transpose(1, 2, 0, 3).reshape(out_grad.shape)
    add = functools.partial(add_kernel, rows)
    (spread,) = call(add, [array(terms.shape)], (mine.reshape(terms.shape),))
    spread = spread.reshape(blocks.shape)
    whole = lax.all_to_all(spread, axes, split_axis=0, concat_axis=0, tiled=True)
    first, second = call(
        unpack_kernel,
        [
            array((3, 3, 3) + first_kernel.shape[1::-1], jnp.float32),
            array((3, 3, 3) + second_kernel.shape[1::-1], jnp.float32),
        ],
        (whole.reshape(terms.shape),),
    )
    return (features, jnp.transpose(first, (4, 3, 0, 1, 2)), jnp.transpose(second, (4, 3, 0, 1, 2)))


def solution(mesh):
    placed = (P("sample", None, "space", None), P(), P(), P(("sample", "space"), None, None, None))
    return jax.shard_map(
        body,
        mesh=mesh,
        in_specs=placed,
        out_specs=(P(("sample", "space"), None, None, None), P(), P()),
        check_vma=False,
    )
```

```python
import functools
import math

import jax
import jax.numpy as jnp
from jax import lax
from jax.experimental import pallas as pl
from jax.experimental.pallas import tpu as pltpu
from jax.sharding import PartitionSpec as P

HEIGHT = 8
WIDTH = 128
LANES = 128
VMEM_BYTES = 16 * 1024 * 1024
TERM_ROWS = 576


def iota(shape, dim):
    return lax.broadcasted_iota(jnp.int32, shape, dim)


def dot(left, right, dims=((1,), (0,))):
    return lax.dot_general(left, right, (dims, ((), ())), preferred_element_type=jnp.float32)


def ones_where(mask):
    return jnp.where(mask, 1.0, 0.0).astype(jnp.bfloat16)


def band_of_second(k2_ref, k2t_ref):
    channels_mid, channels_out = k2_ref.shape[3:]
    empty = jnp.zeros((channels_mid, channels_out), jnp.bfloat16)
    for ad in range(3):
        for aw in range(3):
            tap = [k2_ref[ad, ah, aw] for ah in range(3)]
            band = ((tap[1], empty), (tap[2], tap[0]), (empty, tap[1]), (empty, tap[2]))
            start = (ad * 3 + aw) * 2 * channels_out
            for hh in range(4):
                k2t_ref[hh * channels_mid:(hh + 1) * channels_mid, start:start + 2 * channels_out] = (
                    jnp.concatenate(band[hh], axis=1))


def upsampling(ad, aw, beyond=0):
    row, col = iota((128, 512), 0), iota((128, 512), 1)
    target = ((row >> 5) << 7) + ((row & 31) << 1) + (64 * (ad - 1) + aw - 1 + 128 * beyond)
    keep = col == target
    if aw == 0:
        keep = keep & ((row & 31) > 0)
    return ones_where(keep)


def prepare_kernel(k1_ref, k2_ref, og_ref, pick_ref, k1t_ref, ogt_ref, ag_ref, k2t_ref, ogu_ref):
    channels_in, channels_mid = k1_ref.shape[3:]
    row, col = iota((2 * WIDTH, 2 * 64), 0), iota((2 * WIDTH, 2 * 64), 1)
    for aw in range(3):
        same = (row >> 7) == (col >> 6)
        tap = (row & 127) == 2 * (col & 63) + aw - 1
        pick_ref[:, aw * 128:(aw + 1) * 128] = ones_where(same & tap)
    shape = (9 * channels_in, channels_in * 2 * HEIGHT)
    row, col = iota(shape, 0), iota(shape, 1)
    tap = row >> 4
    ad = jnp.where(tap >= 6, 2, jnp.where(tap >= 3, 1, 0))
    ah, i = tap - 3 * ad, row & 15
    same = i == col >> 4
    h, d = (col >> 1) & 7, col & 1
    taps = []
    for aw in range(3):
        parts = [k1_ref[a, b, aw] for a in range(3) for b in range(3)]
        taps.append(jnp.concatenate(parts, axis=0).astype(jnp.float32).T.astype(jnp.bfloat16))
    for following in range(2):
        plane = (ad == 0) & (d == 1) if following else (ad == d + 1)
        for hh in range(4):
            place = ones_where(same & plane & (h == 2 * hh + ah - 1))
            start = (following * 4 + hh) * channels_mid
            for aw in range(3):
                block = dot(taps[aw], place).astype(jnp.bfloat16)
                k1t_ref[start:start + channels_mid, aw * shape[1]:(aw + 1) * shape[1]] = block
    band_of_second(k2_ref, k2t_ref)
    groups = og_ref.shape[1] // 128
    for ad in range(3):
        for aw in range(3):
            t = ad * 3 + aw
            up = upsampling(ad, aw)
            for g in range(groups):
                value = dot(og_ref[:, g * 128:(g + 1) * 128], up)
                if ad == 0 and g + 1 < groups:
                    value = value + dot(og_ref[:, (g + 1) * 128:(g + 2) * 128], upsampling(ad, aw, 4))
                ogu_ref[t * 128:(t + 1) * 128, g * 512:(g + 1) * 512] = value.astype(jnp.bfloat16)
                ogt_ref[g * 512:(g + 1) * 512, t * 128:(t + 1) * 128] = value.T.astype(jnp.bfloat16)
    for g in range(groups):
        lanes = slice(g * 512, (g + 1) * 512)
        ag_ref[:, lanes] = dot(k2t_ref[...], ogu_ref[:, lanes]).astype(jnp.bfloat16)


def layer_kernel(steps, position_ref, *refs):
    cells = refs[-6].shape[1]
    blocks = cells // 64
    pick_ref, k1t_ref, ogt_ref, ag_ref, act_ref, terms_ref, y_scr, pg_scr, x_ref = refs[blocks:]
    rows = 256
    for place, step in enumerate(steps):
        source = lax.bitwise_xor(position_ref[0], jnp.int32(step))
        x_ref[pl.ds(pl.multiple_of(source * rows, rows), rows), :] = refs[place][...]
    for q in range(cells // 128):
        start = q * 2 * rows
        pair = jnp.concatenate([x_ref[start:start + rows, :], x_ref[start + rows:start + 2 * rows, :]], axis=1)
        y = dot(pair, pick_ref[...]).astype(jnp.bfloat16)
        for aw in range(3):
            y_scr[aw * rows:(aw + 1) * rows, q * 128:(q + 1) * 128] = y[:, aw * 128:(aw + 1) * 128]
    both = dot(k1t_ref[...], y_scr[...])
    lane = iota((128, cells), 1)
    from_last = jnp.where(lane < 64, 0.0, pltpu.roll(both[128:], 64, 1))
    pre = both[:128] + from_last
    sigma = jax.nn.sigmoid(pre)
    act = (pre * sigma).astype(jnp.bfloat16)
    act_ref[...] = act
    slope = sigma * (1.0 + pre * (1.0 - sigma))
    grad = (ag_ref[...].astype(jnp.float32) * slope).astype(jnp.bfloat16)
    pg_scr[:128, :] = grad
    to_last = pltpu.roll(grad.astype(jnp.float32), cells - 64, 1)
    pg_scr[128:, :] = jnp.where(lane < cells - 64, to_last, 0.0).astype(jnp.bfloat16)

    second = dot(act, ogt_ref[...])
    lane = iota((32, 128), 1)
    held = None
    for t in range(9):
        tile = second[:, t * 128:(t + 1) * 128]
        turned = pltpu.roll(tile, 64, 1)
        mixed = jnp.where(lane < 64, tile[0:32] + turned[64:96], turned[32:64] + tile[96:128])
        terms_ref[t * 32:(t + 1) * 32, :] = mixed.astype(jnp.bfloat16)
        if t % 2 == 0:
            held = jnp.where(lane < 64, turned[32:64], 0.0)
        else:
            held = jnp.where(lane < 64, held, tile[32:64])
        if t % 2 == 1:
            start = 288 + (t // 2) * 32
            terms_ref[start:start + 32, :] = held.astype(jnp.bfloat16)
    terms_ref[416:432, :] = jnp.where(lane[:16] < 64, held[:16], pltpu.roll(held[16:], 64, 1)).astype(jnp.bfloat16)

    first = dot(y_scr[...], pg_scr[...], ((1,), (1,))).astype(jnp.bfloat16)
    shape = (rows, 256)
    h, hh = (iota(shape, 0) >> 1) & 7, (iota(shape, 1) >> 5) & 3
    even, odd = ones_where((h >> 1) == hh), ones_where(((h & 1) == 1) & ((h + 1) >> 1 == hh))
    rank, index = iota((64, rows), 0), iota((64, rows), 1)
    same = ((rank & 15) == index >> 4) & (((rank >> 4) & 1) == (index & 1))
    later_taps = ones_where(same & ((rank >> 5) == ((index >> 1) & 1)))
    first_tap = ones_where(same[:32] & (((index[:32] >> 1) & 1) == 1))
    lane = iota((16, 128), 1)
    for aw in range(3):
        tile = first[aw * rows:(aw + 1) * rows]
        total = jnp.concatenate([dot(first_tap, tile * odd), dot(later_taps, tile * even)], axis=0)
        start = 432 + aw * 48
        for ad in range(3):
            side = slice(128, 256) if ad == 0 else slice(0, 128)
            d = 0 if ad == 1 else 1
            packed = None
            for ah in range(3):
                part = total[ah * 32 + d * 16:ah * 32 + d * 16 + 16, side]
                part = part + pltpu.roll(part, 64, 1)
                part = part + pltpu.roll(part, 32, 1)
                packed = part if packed is None else jnp.where(lane >= ah * 32, part, packed)
            terms_ref[start + ad * 16:start + (ad + 1) * 16, :] = packed.astype(jnp.bfloat16)
    rest = terms_ref.shape[0] - TERM_ROWS
    if rest > 0:
        terms_ref[TERM_ROWS:, :] = jnp.zeros((rest, 128), jnp.bfloat16)


def features_kernel(act_ref, k2_ref, out_ref, k2t_ref):
    band_of_second(k2_ref, k2t_ref)
    groups = out_ref.shape[1] // 128
    for g in range(groups):
        total = jnp.zeros((128, 128), jnp.float32)
        for t in range(9):
            taken = dot(act_ref[:, g * 512:(g + 1) * 512], upsampling(t // 3, t % 3), ((1,), (1,)))
            if t < 3 and g > 0:
                last = act_ref[:, (g - 1) * 512:g * 512]
                taken = taken + dot(last, upsampling(0, t, 4), ((1,), (1,)))
            band = k2t_ref[:, t * 128:(t + 1) * 128]
            total = total + dot(band, taken.astype(jnp.bfloat16), ((0,), (0,)))
        out_ref[:, g * 128:(g + 1) * 128] = total.astype(jnp.bfloat16)


def add_kernel(rows, mine_ref, out_ref):
    count = mine_ref.shape[0]
    unit = rows * 16 // math.gcd(rows, 16)
    total = mine_ref[0:unit, :].astype(jnp.float32)
    for start in range(unit, count, unit):
        total = total + mine_ref[start:start + unit, :].astype(jnp.float32)
    if unit % (2 * rows) == 0 and (unit // 2) % 8 == 0:
        total = total[:unit // 2] + total[unit // 2:]
    parts = [total[start:start + rows] for start in range(0, total.shape[0], rows)]
    total = functools.reduce(jnp.add, parts)
    spread = jnp.concatenate([total] * (unit // rows), axis=0).astype(jnp.bfloat16)
    for start in range(0, count, unit):
        out_ref[start:start + unit, :] = spread


def unpack_kernel(whole_ref, first_ref, second_ref):
    for ad in range(3):
        for aw in range(3):
            t = ad * 3 + aw
            pair = whole_ref[t * 32:(t + 1) * 32, :].astype(jnp.float32)
            second_ref[ad, 1, aw] = pair[:, :64]
            second_ref[ad, 2, aw] = pair[:, 64:]
            if t == 8:
                lone = whole_ref[416:432, :].astype(jnp.float32)
                second_ref[ad, 0, aw] = jnp.concatenate([lone[:, :64], lone[:, 64:]], axis=0)
            else:
                start = 288 + (t // 2) * 32
                lone = whole_ref[start:start + 32, :].astype(jnp.float32)
                second_ref[ad, 0, aw] = lone[:, :64] if t % 2 == 0 else lone[:, 64:]
            start = 432 + aw * 48 + ad * 16
            tile = whole_ref[start:start + 16, :].astype(jnp.float32)
            for ah in range(3):
                first_ref[ad, ah, aw] = tile[:, ah * 32:(ah + 1) * 32]


def call(kernel, outs, args, scratch=(), flops=0):
    whole = pl.BlockSpec(memory_space=pltpu.VMEM)
    scalar = pl.BlockSpec(memory_space=pltpu.SMEM)
    size = sum(a.size * a.dtype.itemsize for a in list(args) + list(outs))
    return pl.pallas_call(
        kernel,
        out_shape=tuple(outs),
        in_specs=[scalar if a.dtype == jnp.int32 else whole for a in args],
        out_specs=(whole,) * len(outs),
        scratch_shapes=list(scratch),
        compiler_params=pltpu.CompilerParams(vmem_limit_bytes=VMEM_BYTES),
        cost_estimate=pl.CostEstimate(flops=flops, bytes_accessed=size, transcendentals=0),
    )(*args)


def array(shape, dtype=jnp.bfloat16):
    return jax.ShapeDtypeStruct(shape, dtype)


def by_tap(kernel):
    return jnp.transpose(kernel, (2, 3, 4, 1, 0))


def prepare(k1, k2, out_grad):
    c0, c1 = k1.shape[3:]
    c2 = k2.shape[4]
    planes = out_grad.shape[2]
    cells = planes * 2 * 64
    og = out_grad.reshape(c2, planes, 2, 32).transpose(2, 0, 1, 3).reshape(2 * c2, planes * 32)
    outs = [
        array((256, 384)),
        array((2 * 4 * c1, 3 * c0 * 16)),
        array((cells, 9 * 2 * c2)),
        array((4 * c1, cells)),
    ]
    scratch = [pltpu.VMEM((4 * c1, 9 * 2 * c2), jnp.bfloat16), pltpu.VMEM((9 * 2 * c2, cells), jnp.bfloat16)]
    return call(prepare_kernel, outs, (k1, k2, og), scratch, flops=2 * 128 * 1152 * cells * 2)


def body(crops, first_kernel, second_kernel, out_grad):
    axes = ("space", "sample")
    devices = lax.axis_size(axes)
    channels_out, planes = out_grad.shape[1:3]
    space = lax.axis_size("space")
    assert space & (space - 1) == 0
    position = lax.axis_index("space").astype(jnp.int32)
    wanted = sorted(range(1, space), key=lambda step: -step.bit_length())
    steps = [0] + wanted[::-1]
    k1, k2 = by_tap(first_kernel), by_tap(second_kernel)
    x = []
    far = wanted[:space // 2]
    early = [lax.dynamic_index_in_dim(crops, position ^ step, 0, keepdims=False) for step in far]
    rest, early = lax.optimization_barrier((crops, early))
    for step in steps:
        if step in far:
            block = early[far.index(step)]
        else:
            block = lax.dynamic_index_in_dim(rest, position ^ step, 0, keepdims=False)
        if step > 0:
            block = lax.ppermute(block, "space", [(source, source ^ step) for source in range(space)])
        channels_in, two, flat_cells = block.shape
        block = block.reshape(channels_in, two, HEIGHT, WIDTH).transpose(0, 2, 1, 3)
        x.append(block.reshape(channels_in * two * HEIGHT, WIDTH))
    pick, k1t, ogt, act_grad = prepare(k1, k2, out_grad)
    cells = act_grad.shape[1]
    rows = -(-TERM_ROWS // (devices * 2)) * 2
    act, terms = call(
        functools.partial(layer_kernel, steps),
        [array((128, cells)), array((devices * rows, LANES))],
        (position.reshape(1), *x, pick, k1t, ogt, act_grad),
        scratch=[pltpu.VMEM((768, cells), jnp.bfloat16), pltpu.VMEM((256, cells), jnp.bfloat16), pltpu.VMEM((4 * cells, 128), jnp.bfloat16)],
        flops=2 * 128 * 4096 * cells,
    )
    blocks = terms.reshape(devices, rows // 2, 2, LANES)
    mine = lax.all_to_all(blocks, axes, split_axis=0, concat_axis=0, tiled=True)
    (features,) = call(
        features_kernel,
        [array((2 * channels_out, planes * 32))],
        (act, k2),
        scratch=[pltpu.VMEM((128, 1152), jnp.bfloat16)],
        flops=2 * 128 * 1152 * cells,
    )
    features = features.reshape(2, channels_out, planes, 32).transpose(1, 2, 0, 3).reshape(out_grad.shape)
    add = functools.partial(add_kernel, rows)
    (spread,) = call(add, [array(terms.shape)], (mine.reshape(terms.shape),))
    spread = spread.reshape(blocks.shape)
    whole = lax.all_to_all(spread, axes, split_axis=0, concat_axis=0, tiled=True)
    first, second = call(
        unpack_kernel,
        [
            array((3, 3, 3) + first_kernel.shape[1::-1], jnp.float32),
            array((3, 3, 3) + second_kernel.shape[1::-1], jnp.float32),
        ],
        (whole.reshape(terms.shape),),
    )
    return (features, jnp.transpose(first, (4, 3, 0, 1, 2)), jnp.transpose(second, (4, 3, 0, 1, 2)))


def solution(mesh):
    placed = (P("sample", None, "space", None), P(), P(), P(("sample", "space"), None, None, None))
    return jax.shard_map(
        body,
        mesh=mesh,
        in_specs=placed,
        out_specs=(P(("sample", "space"), None, None, None), P(), P()),
        check_vma=False,
    )
```

```python
import functools
import math

import jax
import jax.numpy as jnp
from jax import lax
from jax.experimental import pallas as pl
from jax.experimental.pallas import tpu as pltpu
from jax.sharding import PartitionSpec as P

HEIGHT = 8
WIDTH = 128
LANES = 128
VMEM_BYTES = 16 * 1024 * 1024
TERM_ROWS = 576


def iota(shape, dim):
    return lax.broadcasted_iota(jnp.int32, shape, dim)


def dot(left, right, dims=((1,), (0,))):
    return lax.dot_general(left, right, (dims, ((), ())), preferred_element_type=jnp.float32)


def ones_where(mask):
    return jnp.where(mask, 1.0, 0.0).astype(jnp.bfloat16)


def band_of_second(k2_ref, k2t_ref):
    channels_mid, channels_out = k2_ref.shape[3:]
    empty = jnp.zeros((channels_mid, channels_out), jnp.bfloat16)
    for ad in range(3):
        for aw in range(3):
            tap = [k2_ref[ad, ah, aw] for ah in range(3)]
            band = ((tap[1], empty), (tap[2], tap[0]), (empty, tap[1]), (empty, tap[2]))
            start = (ad * 3 + aw) * 2 * channels_out
            for hh in range(4):
                k2t_ref[hh * channels_mid:(hh + 1) * channels_mid, start:start + 2 * channels_out] = (
                    jnp.concatenate(band[hh], axis=1))


def upsampling(ad, aw, beyond=0):
    row, col = iota((128, 512), 0), iota((128, 512), 1)
    target = ((row >> 5) << 7) + ((row & 31) << 1) + (64 * (ad - 1) + aw - 1 + 128 * beyond)
    keep = col == target
    if aw == 0:
        keep = keep & ((row & 31) > 0)
    return ones_where(keep)


def prepare_kernel(k1_ref, k2_ref, og_ref, pick_ref, k1t_ref, ogt_ref, ag_ref, k2t_ref, ogu_ref):
    channels_in, channels_mid = k1_ref.shape[3:]
    row, col = iota((2 * WIDTH, 2 * 64), 0), iota((2 * WIDTH, 2 * 64), 1)
    for aw in range(3):
        same = (row >> 7) == (col >> 6)
        tap = (row & 127) == 2 * (col & 63) + aw - 1
        pick_ref[:, aw * 128:(aw + 1) * 128] = ones_where(same & tap)
    shape = (9 * channels_in, channels_in * 2 * HEIGHT)
    row, col = iota(shape, 0), iota(shape, 1)
    tap = row >> 4
    ad = jnp.where(tap >= 6, 2, jnp.where(tap >= 3, 1, 0))
    ah, i = tap - 3 * ad, row & 15
    same = i == col >> 4
    h, d = (col >> 1) & 7, col & 1
    taps = []
    for aw in range(3):
        parts = [k1_ref[a, b, aw] for a in range(3) for b in range(3)]
        taps.append(jnp.concatenate(parts, axis=0).astype(jnp.float32).T.astype(jnp.bfloat16))
    for following in range(2):
        plane = (ad == 0) & (d == 1) if following else (ad == d + 1)
        for hh in range(4):
            place = ones_where(same & plane & (h == 2 * hh + ah - 1))
            start = (following * 4 + hh) * channels_mid
            for aw in range(3):
                block = dot(taps[aw], place).astype(jnp.bfloat16)
                k1t_ref[start:start + channels_mid, aw * shape[1]:(aw + 1) * shape[1]] = block
    band_of_second(k2_ref, k2t_ref)
    groups = og_ref.shape[1] // 128
    for ad in range(3):
        for aw in range(3):
            t = ad * 3 + aw
            up = upsampling(ad, aw)
            for g in range(groups):
                value = dot(og_ref[:, g * 128:(g + 1) * 128], up)
                if ad == 0 and g + 1 < groups:
                    value = value + dot(og_ref[:, (g + 1) * 128:(g + 2) * 128], upsampling(ad, aw, 4))
                ogu_ref[t * 128:(t + 1) * 128, g * 512:(g + 1) * 512] = value.astype(jnp.bfloat16)
                ogt_ref[g * 512:(g + 1) * 512, t * 128:(t + 1) * 128] = value.T.astype(jnp.bfloat16)
    for g in range(groups):
        lanes = slice(g * 512, (g + 1) * 512)
        ag_ref[:, lanes] = dot(k2t_ref[...], ogu_ref[:, lanes]).astype(jnp.bfloat16)


def layer_kernel(steps, position_ref, *refs):
    cells = refs[-6].shape[1]
    blocks = cells // 64
    pick_ref, k1t_ref, ogt_ref, ag_ref, act_ref, terms_ref, y_scr, pg_scr, x_ref = refs[blocks:]
    rows = 256
    for place, step in enumerate(steps):
        source = lax.bitwise_xor(position_ref[0], jnp.int32(step))
        x_ref[pl.ds(pl.multiple_of(source * rows, rows), rows), :] = refs[place][...]
    for q in range(cells // 128):
        start = q * 2 * rows
        pair = jnp.concatenate([x_ref[start:start + rows, :], x_ref[start + rows:start + 2 * rows, :]], axis=1)
        y = dot(pair, pick_ref[...]).astype(jnp.bfloat16)
        for aw in range(3):
            y_scr[aw * rows:(aw + 1) * rows, q * 128:(q + 1) * 128] = y[:, aw * 128:(aw + 1) * 128]
    both = dot(k1t_ref[...], y_scr[...])
    lane = iota((128, cells), 1)
    from_last = jnp.where(lane < 64, 0.0, pltpu.roll(both[128:], 64, 1))
    pre = both[:128] + from_last
    sigma = jax.nn.sigmoid(pre)
    act = (pre * sigma).astype(jnp.bfloat16)
    act_ref[...] = act
    slope = sigma * (1.0 + pre * (1.0 - sigma))
    grad = (ag_ref[...].astype(jnp.float32) * slope).astype(jnp.bfloat16)
    pg_scr[:128, :] = grad
    to_last = pltpu.roll(grad.astype(jnp.float32), cells - 64, 1)
    pg_scr[128:, :] = jnp.where(lane < cells - 64, to_last, 0.0).astype(jnp.bfloat16)

    second = dot(act, ogt_ref[...])
    lane = iota((32, 128), 1)
    held = None
    for t in range(9):
        tile = second[:, t * 128:(t + 1) * 128]
        turned = pltpu.roll(tile, 64, 1)
        mixed = jnp.where(lane < 64, tile[0:32] + turned[64:96], turned[32:64] + tile[96:128])
        terms_ref[t * 32:(t + 1) * 32, :] = mixed.astype(jnp.bfloat16)
        if t % 2 == 0:
            held = jnp.where(lane < 64, turned[32:64], 0.0)
        else:
            held = jnp.where(lane < 64, held, tile[32:64])
        if t % 2 == 1:
            start = 288 + (t // 2) * 32
            terms_ref[start:start + 32, :] = held.astype(jnp.bfloat16)
    terms_ref[416:432, :] = jnp.where(lane[:16] < 64, held[:16], pltpu.roll(held[16:], 64, 1)).astype(jnp.bfloat16)

    first = dot(y_scr[...], pg_scr[...], ((1,), (1,))).astype(jnp.bfloat16)
    shape = (rows, 256)
    h, hh = (iota(shape, 0) >> 1) & 7, (iota(shape, 1) >> 5) & 3
    even, odd = ones_where((h >> 1) == hh), ones_where(((h & 1) == 1) & ((h + 1) >> 1 == hh))
    rank, index = iota((64, rows), 0), iota((64, rows), 1)
    same = ((rank & 15) == index >> 4) & (((rank >> 4) & 1) == (index & 1))
    later_taps = ones_where(same & ((rank >> 5) == ((index >> 1) & 1)))
    first_tap = ones_where(same[:32] & (((index[:32] >> 1) & 1) == 1))
    lane = iota((16, 128), 1)
    for aw in range(3):
        tile = first[aw * rows:(aw + 1) * rows]
        total = jnp.concatenate([dot(first_tap, tile * odd), dot(later_taps, tile * even)], axis=0)
        start = 432 + aw * 48
        for ad in range(3):
            side = slice(128, 256) if ad == 0 else slice(0, 128)
            d = 0 if ad == 1 else 1
            packed = None
            for ah in range(3):
                part = total[ah * 32 + d * 16:ah * 32 + d * 16 + 16, side]
                part = part + pltpu.roll(part, 64, 1)
                part = part + pltpu.roll(part, 32, 1)
                packed = part if packed is None else jnp.where(lane >= ah * 32, part, packed)
            terms_ref[start + ad * 16:start + (ad + 1) * 16, :] = packed.astype(jnp.bfloat16)
    rest = terms_ref.shape[0] - TERM_ROWS
    if rest > 0:
        terms_ref[TERM_ROWS:, :] = jnp.zeros((rest, 128), jnp.bfloat16)


def features_kernel(act_ref, k2_ref, out_ref, k2t_ref):
    band_of_second(k2_ref, k2t_ref)
    groups = out_ref.shape[1] // 128
    for g in range(groups):
        total = jnp.zeros((128, 128), jnp.float32)
        for t in range(9):
            taken = dot(act_ref[:, g * 512:(g + 1) * 512], upsampling(t // 3, t % 3), ((1,), (1,)))
            if t < 3 and g > 0:
                last = act_ref[:, (g - 1) * 512:g * 512]
                taken = taken + dot(last, upsampling(0, t, 4), ((1,), (1,)))
            band = k2t_ref[:, t * 128:(t + 1) * 128]
            total = total + dot(band, taken.astype(jnp.bfloat16), ((0,), (0,)))
        out_ref[:, g * 128:(g + 1) * 128] = total.astype(jnp.bfloat16)


def add_kernel(rows, mine_ref, out_ref):
    count = mine_ref.shape[0]
    unit = rows * 16 // math.gcd(rows, 16)
    total = mine_ref[0:unit, :].astype(jnp.float32)
    for start in range(unit, count, unit):
        total = total + mine_ref[start:start + unit, :].astype(jnp.float32)
    if unit % (2 * rows) == 0 and (unit // 2) % 8 == 0:
        total = total[:unit // 2] + total[unit // 2:]
    parts = [total[start:start + rows] for start in range(0, total.shape[0], rows)]
    total = functools.reduce(jnp.add, parts)
    spread = jnp.concatenate([total] * (unit // rows), axis=0).astype(jnp.bfloat16)
    for start in range(0, count, unit):
        out_ref[start:start + unit, :] = spread


def unpack_kernel(whole_ref, first_ref, second_ref, first_scr, second_scr, sems):
    copies = []
    for ad in range(3):
        for aw in range(3):
            t = ad * 3 + aw
            pair = whole_ref[t * 32:(t + 1) * 32, :].astype(jnp.float32)
            second_scr[ad, 1, aw] = pair[:, :64]
            second_scr[ad, 2, aw] = pair[:, 64:]
            if t == 8:
                lone = whole_ref[416:432, :].astype(jnp.float32)
                second_scr[ad, 0, aw] = jnp.concatenate([lone[:, :64], lone[:, 64:]], axis=0)
            else:
                start = 288 + (t // 2) * 32
                lone = whole_ref[start:start + 32, :].astype(jnp.float32)
                second_scr[ad, 0, aw] = lone[:, :64] if t % 2 == 0 else lone[:, 64:]
        copies.append(pltpu.make_async_copy(second_scr.at[ad], second_ref.at[ad], sems.at[0, ad]))
        copies[-1].start()
    for ad in range(3):
        for aw in range(3):
            start = 432 + aw * 48 + ad * 16
            tile = whole_ref[start:start + 16, :].astype(jnp.float32)
            for ah in range(3):
                first_scr[ad, ah, aw] = tile[:, ah * 32:(ah + 1) * 32]
        copies.append(pltpu.make_async_copy(first_scr.at[ad], first_ref.at[ad], sems.at[1, ad]))
        copies[-1].start()
    for copy in copies:
        copy.wait()


def call(kernel, outs, args, scratch=(), flops=0):
    whole = pl.BlockSpec(memory_space=pltpu.VMEM)
    scalar = pl.BlockSpec(memory_space=pltpu.SMEM)
    size = sum(a.size * a.dtype.itemsize for a in list(args) + list(outs))
    return pl.pallas_call(
        kernel,
        out_shape=tuple(outs),
        in_specs=[scalar if a.dtype == jnp.int32 else whole for a in args],
        out_specs=(whole,) * len(outs),
        scratch_shapes=list(scratch),
        compiler_params=pltpu.CompilerParams(vmem_limit_bytes=VMEM_BYTES),
        cost_estimate=pl.CostEstimate(flops=flops, bytes_accessed=size, transcendentals=0),
    )(*args)


def array(shape, dtype=jnp.bfloat16):
    return jax.ShapeDtypeStruct(shape, dtype)


def by_tap(kernel):
    return jnp.transpose(kernel, (2, 3, 4, 1, 0))


def prepare(k1, k2, out_grad):
    c0, c1 = k1.shape[3:]
    c2 = k2.shape[4]
    planes = out_grad.shape[2]
    cells = planes * 2 * 64
    og = out_grad.reshape(c2, planes, 2, 32).transpose(2, 0, 1, 3).reshape(2 * c2, planes * 32)
    outs = [
        array((256, 384)),
        array((2 * 4 * c1, 3 * c0 * 16)),
        array((cells, 9 * 2 * c2)),
        array((4 * c1, cells)),
    ]
    scratch = [pltpu.VMEM((4 * c1, 9 * 2 * c2), jnp.bfloat16), pltpu.VMEM((9 * 2 * c2, cells), jnp.bfloat16)]
    return call(prepare_kernel, outs, (k1, k2, og), scratch, flops=2 * 128 * 1152 * cells * 2)


def body(crops, first_kernel, second_kernel, out_grad):
    axes = ("space", "sample")
    devices = lax.axis_size(axes)
    channels_out, planes = out_grad.shape[1:3]
    space = lax.axis_size("space")
    assert space & (space - 1) == 0
    position = lax.axis_index("space").astype(jnp.int32)
    wanted = sorted(range(1, space), key=lambda step: -step.bit_length())
    steps = [0] + wanted[::-1]
    k1, k2 = by_tap(first_kernel), by_tap(second_kernel)
    x = []
    far = wanted[:space // 2]
    early = [lax.dynamic_index_in_dim(crops, position ^ step, 0, keepdims=False) for step in far]
    rest, early = lax.optimization_barrier((crops, early))
    for step in steps:
        if step in far:
            block = early[far.index(step)]
        else:
            block = lax.dynamic_index_in_dim(rest, position ^ step, 0, keepdims=False)
        if step > 0:
            block = lax.ppermute(block, "space", [(source, source ^ step) for source in range(space)])
        channels_in, two, flat_cells = block.shape
        block = block.reshape(channels_in, two, HEIGHT, WIDTH).transpose(0, 2, 1, 3)
        x.append(block.reshape(channels_in * two * HEIGHT, WIDTH))
    pick, k1t, ogt, act_grad = prepare(k1, k2, out_grad)
    cells = act_grad.shape[1]
    rows = -(-TERM_ROWS // (devices * 2)) * 2
    act, terms = call(
        functools.partial(layer_kernel, steps),
        [array((128, cells)), array((devices * rows, LANES))],
        (position.reshape(1), *x, pick, k1t, ogt, act_grad),
        scratch=[pltpu.VMEM((768, cells), jnp.bfloat16), pltpu.VMEM((256, cells), jnp.bfloat16), pltpu.VMEM((4 * cells, 128), jnp.bfloat16)],
        flops=2 * 128 * 4096 * cells,
    )
    blocks = terms.reshape(devices, rows // 2, 2, LANES)
    mine = lax.all_to_all(blocks, axes, split_axis=0, concat_axis=0, tiled=True)
    (features,) = call(
        features_kernel,
        [array((2 * channels_out, planes * 32))],
        (act, k2),
        scratch=[pltpu.VMEM((128, 1152), jnp.bfloat16)],
        flops=2 * 128 * 1152 * cells,
    )
    features = features.reshape(2, channels_out, planes, 32).transpose(1, 2, 0, 3).reshape(out_grad.shape)
    add = functools.partial(add_kernel, rows)
    (spread,) = call(add, [array(terms.shape)], (mine.reshape(terms.shape),))
    spread = spread.reshape(blocks.shape)
    whole = lax.all_to_all(spread, axes, split_axis=0, concat_axis=0, tiled=True)
    shapes = [(3, 3, 3) + kernel.shape[1::-1] for kernel in (first_kernel, second_kernel)]
    first, second = pl.pallas_call(
        unpack_kernel,
        out_shape=[array(shape, jnp.float32) for shape in shapes],
        in_specs=[pl.BlockSpec(memory_space=pltpu.VMEM)],
        out_specs=[pl.BlockSpec(memory_space=pl.ANY)] * 2,
        scratch_shapes=[pltpu.VMEM(shape, jnp.float32) for shape in shapes] + [pltpu.SemaphoreType.DMA((2, 3))],
        compiler_params=pltpu.CompilerParams(vmem_limit_bytes=VMEM_BYTES),
    )(whole.reshape(terms.shape))
    return (features, jnp.transpose(first, (4, 3, 0, 1, 2)), jnp.transpose(second, (4, 3, 0, 1, 2)))


def solution(mesh):
    placed = (P("sample", None, "space", None), P(), P(), P(("sample", "space"), None, None, None))
    return jax.shard_map(
        body,
        mesh=mesh,
        in_specs=placed,
        out_specs=(P(("sample", "space"), None, None, None), P(), P()),
        check_vma=False,
    )
```

```python
import functools
import math

import jax
import jax.numpy as jnp
from jax import lax
from jax.experimental import pallas as pl
from jax.experimental.pallas import tpu as pltpu
from jax.sharding import PartitionSpec as P

HEIGHT = 8
WIDTH = 128
LANES = 128
VMEM_BYTES = 16 * 1024 * 1024
TERM_ROWS = 576


def iota(shape, dim):
    return lax.broadcasted_iota(jnp.int32, shape, dim)


def dot(left, right, dims=((1,), (0,))):
    return lax.dot_general(left, right, (dims, ((), ())), preferred_element_type=jnp.float32)


def ones_where(mask):
    return jnp.where(mask, 1.0, 0.0).astype(jnp.bfloat16)


def band_of_second(k2_ref, k2t_ref):
    channels_mid, channels_out = k2_ref.shape[3:]
    empty = jnp.zeros((channels_mid, channels_out), jnp.bfloat16)
    for ad in range(3):
        for aw in range(3):
            tap = [k2_ref[ad, ah, aw] for ah in range(3)]
            band = ((tap[1], empty), (tap[2], tap[0]), (empty, tap[1]), (empty, tap[2]))
            start = (ad * 3 + aw) * 2 * channels_out
            for hh in range(4):
                k2t_ref[hh * channels_mid:(hh + 1) * channels_mid, start:start + 2 * channels_out] = (
                    jnp.concatenate(band[hh], axis=1))


def upsampling(ad, aw):
    row, col = iota((128, 512), 0), iota((128, 512), 1)
    keep = col == ((row >> 5) << 7) + ((row & 31) << 1) + ((0 if ad == 1 else 64) + aw - 1)
    if aw == 0:
        keep = keep & ((row & 31) > 0)
    return ones_where(keep)


def prepare_kernel(half_ref, k1_ref, k2_ref, flat0_ref, flat1_ref, pick_ref, k1m_ref, k1f_ref, ogt_ref, ag_ref,
                   k2t_ref, og_ref, ogu_ref):
    channels_in, channels_mid = k1_ref.shape[3:]
    row, col = iota((2 * WIDTH, 2 * 64), 0), iota((2 * WIDTH, 2 * 64), 1)
    for aw in range(3):
        same = (row >> 7) == (col >> 6)
        tap = (row & 127) == 2 * (col & 63) + aw - 1
        pick_ref[:, aw * 128:(aw + 1) * 128] = ones_where(same & tap)
    taps = []
    for aw in range(3):
        parts = [k1_ref[a, b, aw] for a in range(3) for b in range(3)]
        taps.append(jnp.concatenate(parts, axis=0).astype(jnp.float32).T.astype(jnp.bfloat16))
    row, col = iota((9 * channels_in, 256), 0), iota((9 * channels_in, 256), 1)
    tap = row >> 4
    ad = jnp.where(tap >= 6, 2, jnp.where(tap >= 3, 1, 0))
    ah, i = tap - 3 * ad, row & 15
    pair = (i == col >> 4) & (ad == (col & 1) + 1)
    before_col = iota((9 * channels_in, 128), 1)
    before = (i[:, :128] == (before_col & 15)) & (ad[:, :128] == 0)
    for hh in range(4):
        rows = slice(hh * channels_mid, (hh + 1) * channels_mid)
        place = ones_where(pair & (((col >> 1) & 7) == 2 * hh + ah - 1))
        place_before = ones_where(before & ((before_col >> 4) == 2 * hh + ah[:, :128] - 1))
        for aw in range(3):
            k1m_ref[rows, aw * 256:(aw + 1) * 256] = dot(taps[aw], place).astype(jnp.bfloat16)
            k1f_ref[rows, aw * 128:(aw + 1) * 128] = dot(taps[aw], place_before).astype(jnp.bfloat16)
    band_of_second(k2_ref, k2t_ref)
    wide = og_ref.shape[2]
    count = wide // 64
    row, col = iota((64, wide), 0), iota((64, wide), 1)
    for later in range(2):
        for hhh in range(2):
            value = jnp.zeros((64, wide), jnp.float32)
            for place, flat_ref in enumerate((flat0_ref, flat1_ref)):
                m = lax.bitwise_xor(half_ref[0], jnp.int32(place))
                for q in range(count):
                    spread = ones_where(((row >> 5) == hhh) & (col == (row & 31) + (m * count + q) * 32))
                    plane = q + later
                    value = value + dot(flat_ref[plane * 64:(plane + 1) * 64, :], spread)
            og_ref[later, hhh * 64:(hhh + 1) * 64, :] = value.astype(jnp.bfloat16)
    groups = wide // 128
    for ad in range(3):
        for aw in range(3):
            t = ad * 3 + aw
            up = upsampling(ad, aw)
            for g in range(groups):
                value = dot(og_ref[1 if ad == 0 else 0, :, g * 128:(g + 1) * 128], up)
                ogu_ref[t * 128:(t + 1) * 128, g * 512:(g + 1) * 512] = value.astype(jnp.bfloat16)
                ogt_ref[g * 512:(g + 1) * 512, t * 128:(t + 1) * 128] = value.T.astype(jnp.bfloat16)
    for g in range(groups):
        lanes = slice(g * 512, (g + 1) * 512)
        ag_ref[:, lanes] = dot(k2t_ref[...], ogu_ref[:, lanes]).astype(jnp.bfloat16)


def halo_kernel(*refs):
    count = len(refs) // 2
    chosen = odd_plane()
    for source, out in zip(refs[:count], refs[count:]):
        for m in range(2):
            out[m * 128:(m + 1) * 128, :] = dot(chosen, source[m * 256:(m + 1) * 256, :]).astype(jnp.bfloat16)


def odd_plane():
    row, col = iota((128, 256), 0), iota((128, 256), 1)
    return ones_where(((row >> 4) == ((col >> 1) & 7)) & ((row & 15) == (col >> 4)) & ((col & 1) == 1))


def layer_kernel(steps, place_ref, *refs):
    size = len(steps)
    halo_refs = refs[size:2 * size]
    pick_ref, k1m_ref, k1f_ref, ogt_ref, ag_ref, act_ref, terms_ref, y_scr, yf_scr, x_ref = refs[2 * size:]
    count = size // 2
    for block, step in enumerate(steps):
        source = lax.bitwise_xor(place_ref[0], jnp.int32(step))
        x_ref[pl.ds(pl.multiple_of(source * 512, 512), 512), :] = refs[block][...]
    chosen = odd_plane()
    for m in range(2):
        before = functools.reduce(jnp.add, [ref[m * 128:(m + 1) * 128, :] for ref in halo_refs])
        for q in range(count):
            block = m * count + q
            lanes = slice(block * 128, (block + 1) * 128)
            start = (4 * q + m) * 256
            lower, upper = x_ref[start:start + 256, :], x_ref[start + 512:start + 768, :]
            y = dot(jnp.concatenate([lower, upper], axis=1), pick_ref[...]).astype(jnp.bfloat16)
            for aw in range(3):
                y_scr[aw * 256:(aw + 1) * 256, lanes] = y[:, aw * 128:(aw + 1) * 128]
            between = dot(chosen, lower).astype(jnp.bfloat16)
            y = dot(jnp.concatenate([before, between], axis=1), pick_ref[...]).astype(jnp.bfloat16)
            for aw in range(3):
                yf_scr[aw * 128:(aw + 1) * 128, lanes] = y[:, aw * 128:(aw + 1) * 128]
            if q + 1 < count:
                before = dot(chosen, upper).astype(jnp.bfloat16)
    pre = dot(k1m_ref[...], y_scr[...]) + dot(k1f_ref[...], yf_scr[...])
    sigma = jax.nn.sigmoid(pre)
    act = (pre * sigma).astype(jnp.bfloat16)
    act_ref[...] = act
    slope = sigma * (1.0 + pre * (1.0 - sigma))
    grad = (ag_ref[...].astype(jnp.float32) * slope).astype(jnp.bfloat16)

    second = dot(act, ogt_ref[...])
    lane = iota((32, 128), 1)
    held = None
    for t in range(9):
        tile = second[:, t * 128:(t + 1) * 128]
        turned = pltpu.roll(tile, 64, 1)
        mixed = jnp.where(lane < 64, tile[0:32] + turned[64:96], turned[32:64] + tile[96:128])
        terms_ref[t * 32:(t + 1) * 32, :] = mixed.astype(jnp.bfloat16)
        if t % 2 == 0:
            held = jnp.where(lane < 64, turned[32:64], 0.0)
        else:
            held = jnp.where(lane < 64, held, tile[32:64])
            start = 288 + (t // 2) * 32
            terms_ref[start:start + 32, :] = held.astype(jnp.bfloat16)
    terms_ref[416:432, :] = jnp.where(lane[:16] < 64, held[:16], pltpu.roll(held[16:], 64, 1)).astype(jnp.bfloat16)

    first = dot(y_scr[...], grad, ((1,), (1,))).astype(jnp.bfloat16)
    before = dot(yf_scr[...], grad, ((1,), (1,))).astype(jnp.bfloat16)
    h, hh = (iota((256, 128), 0) >> 1) & 7, iota((256, 128), 1) >> 5
    even, odd = ones_where((h >> 1) == hh), ones_where(((h & 1) == 1) & ((h + 1) >> 1 == hh))
    rank, index = iota((64, 256), 0), iota((64, 256), 1)
    same = ((rank & 15) == index >> 4) & (((rank >> 4) & 1) == (index & 1))
    later_taps = ones_where(same & ((rank >> 5) == ((index >> 1) & 1)))
    first_tap = ones_where(same[:32] & (((index[:32] >> 1) & 1) == 1))
    h, hh = iota((128, 128), 0) >> 4, iota((128, 128), 1) >> 5
    even_before, odd_before = ones_where((h >> 1) == hh), ones_where(((h & 1) == 1) & ((h + 1) >> 1 == hh))
    rank, index = iota((32, 128), 0), iota((32, 128), 1)
    same = (rank & 15) == (index & 15)
    later_before = ones_where(same & ((rank >> 4) == ((index >> 4) & 1)))
    first_before = ones_where(same[:16] & (((index[:16] >> 4) & 1) == 1))
    lane = iota((48, 128), 1)
    for aw in range(3):
        tile, tile_before = first[aw * 256:(aw + 1) * 256], before[aw * 128:(aw + 1) * 128]
        low, high = dot(first_tap, tile * odd), dot(later_taps, tile * even)
        low_before, high_before = dot(first_before, tile_before * odd_before), dot(later_before, tile_before * even_before)
        parts = [
            jnp.concatenate([low_before, low], axis=0),
            jnp.concatenate([high_before[:16], high[:32]], axis=0),
            jnp.concatenate([high_before[16:], high[32:]], axis=0),
        ]
        packed = None
        for ah, part in enumerate(parts):
            part = part + pltpu.roll(part, 64, 1)
            part = part + pltpu.roll(part, 32, 1)
            packed = part if packed is None else jnp.where(lane >= ah * 32, part, packed)
        terms_ref[432 + aw * 48:480 + aw * 48, :] = packed.astype(jnp.bfloat16)
    rest = terms_ref.shape[0] - TERM_ROWS
    if rest > 0:
        terms_ref[TERM_ROWS:, :] = jnp.zeros((rest, 128), jnp.bfloat16)


def features_kernel(act_ref, k2_ref, out_ref, k2t_ref):
    band_of_second(k2_ref, k2t_ref)
    groups = act_ref.shape[1] // 512
    count = groups * 2
    span = out_ref.shape[2]
    row, col = iota((512, 2 * span), 0), iota((512, 2 * span), 1)
    later, hhh, www = row >> 8, (row >> 7) & 1, row & 31
    total = jnp.zeros((64, 2 * span), jnp.float32)
    for g in range(groups):
        share = [jnp.zeros((128, 128), jnp.float32) for _ in range(2)]
        for t in range(9):
            taken = dot(act_ref[:, g * 512:(g + 1) * 512], upsampling(t // 3, t % 3), ((1,), (1,)))
            band = k2t_ref[:, t * 128:(t + 1) * 128]
            place = 1 if t < 3 else 0
            share[place] = share[place] + dot(band, taken.astype(jnp.bfloat16), ((0,), (0,)))
        parts = [share[place][side * 64:(side + 1) * 64] for place in range(2) for side in range(2)]
        block = ((row >> 5) & 3) + 4 * g
        m = jnp.where(block >= count, 1, 0)
        q = block - m * count
        order = ones_where(col == m * span + (q + later) * 64 + hhh * 32 + www)
        total = total + dot(jnp.concatenate(parts, axis=1).astype(jnp.bfloat16), order)
    for m in range(2):
        out_ref[m] = total[:, m * span:(m + 1) * span].astype(jnp.bfloat16)


def join_kernel(half_ref, share0_ref, share1_ref, out_ref):
    first = share0_ref[...].astype(jnp.float32)
    second = share1_ref[...].astype(jnp.float32)
    lower = half_ref[0] == 0
    low, high = jnp.where(lower, first, second), jnp.where(lower, second, first)
    planes = out_ref.shape[0]
    count = planes // 2
    for plane in range(planes):
        if plane < count:
            total = low[:, plane * 64:(plane + 1) * 64]
        else:
            total = high[:, (plane - count) * 64:(plane - count + 1) * 64]
        if plane == count:
            total = total + low[:, plane * 64:(plane + 1) * 64]
        out_ref[plane] = total.astype(jnp.bfloat16)


def add_kernel(rows, mine_ref, out_ref):
    count = mine_ref.shape[0]
    unit = rows * 16 // math.gcd(rows, 16)
    total = mine_ref[0:unit, :].astype(jnp.float32)
    for start in range(unit, count, unit):
        total = total + mine_ref[start:start + unit, :].astype(jnp.float32)
    if unit % (2 * rows) == 0 and (unit // 2) % 8 == 0:
        total = total[:unit // 2] + total[unit // 2:]
    parts = [total[start:start + rows] for start in range(0, total.shape[0], rows)]
    total = functools.reduce(jnp.add, parts)
    spread = jnp.concatenate([total] * (unit // rows), axis=0).astype(jnp.bfloat16)
    for start in range(0, count, unit):
        out_ref[start:start + unit, :] = spread


def unpack_kernel(whole_ref, first_ref, second_ref, first_scr, second_scr, sems):
    copies = []
    for ad in range(3):
        for aw in range(3):
            t = ad * 3 + aw
            pair = whole_ref[t * 32:(t + 1) * 32, :].astype(jnp.float32)
            second_scr[ad, 1, aw] = pair[:, :64]
            second_scr[ad, 2, aw] = pair[:, 64:]
            if t == 8:
                lone = whole_ref[416:432, :].astype(jnp.float32)
                second_scr[ad, 0, aw] = jnp.concatenate([lone[:, :64], lone[:, 64:]], axis=0)
            else:
                start = 288 + (t // 2) * 32
                lone = whole_ref[start:start + 32, :].astype(jnp.float32)
                second_scr[ad, 0, aw] = lone[:, :64] if t % 2 == 0 else lone[:, 64:]
        copies.append(pltpu.make_async_copy(second_scr.at[ad], second_ref.at[ad], sems.at[0, ad]))
        copies[-1].start()
    for ad in range(3):
        for aw in range(3):
            start = 432 + aw * 48 + ad * 16
            tile = whole_ref[start:start + 16, :].astype(jnp.float32)
            for ah in range(3):
                first_scr[ad, ah, aw] = tile[:, ah * 32:(ah + 1) * 32]
        copies.append(pltpu.make_async_copy(first_scr.at[ad], first_ref.at[ad], sems.at[1, ad]))
        copies[-1].start()
    for copy in copies:
        copy.wait()


def call(kernel, outs, args, scratch=(), flops=0):
    whole = pl.BlockSpec(memory_space=pltpu.VMEM)
    scalar = pl.BlockSpec(memory_space=pltpu.SMEM)
    size = sum(a.size * a.dtype.itemsize for a in list(args) + list(outs))
    return pl.pallas_call(
        kernel,
        out_shape=tuple(outs),
        in_specs=[scalar if a.dtype == jnp.int32 else whole for a in args],
        out_specs=(whole,) * len(outs),
        scratch_shapes=[pltpu.VMEM(shape, dtype) for shape, dtype in scratch],
        compiler_params=pltpu.CompilerParams(vmem_limit_bytes=VMEM_BYTES),
        cost_estimate=pl.CostEstimate(flops=flops, bytes_accessed=size, transcendentals=0),
    )(*args)


def array(shape, dtype=jnp.bfloat16):
    return jax.ShapeDtypeStruct(shape, dtype)


def by_tap(kernel):
    return jnp.transpose(kernel, (2, 3, 4, 1, 0))


def as_rows(block):
    samples, channels, two, flat_cells = block.shape
    block = block.reshape(samples, channels, two, HEIGHT, WIDTH).transpose(0, 1, 3, 2, 4)
    return block.reshape(samples * channels * two * HEIGHT, WIDTH)


def swap(block, space, step):
    return lax.ppermute(block, "space", [(source, source ^ step) for source in range(space)])


def body(crops, first_kernel, second_kernel, out_grad):
    axes = ("space", "sample")
    devices = lax.axis_size(axes)
    space = lax.axis_size("space")
    channels_out, planes = out_grad.shape[1:3]
    size = space // 2
    count = size // 2
    cells = size * 128
    assert space & (space - 1) == 0 and space >= 8
    position = lax.axis_index("space").astype(jnp.int32)
    place, half = position & (size - 1), jnp.where(position >= size, 1, 0).astype(jnp.int32)
    steps = list(range(size))
    k1, k2 = by_tap(first_kernel), by_tap(second_kernel)

    by_place = crops.reshape((2, size) + crops.shape[1:])
    send = [lax.dynamic_index_in_dim(by_place, place ^ step, 1, keepdims=False) for step in steps]
    cotangent, send = lax.optimization_barrier((out_grad, send))
    by_plane = jnp.pad(jnp.transpose(cotangent[0], (1, 0, 2)), ((0, 1), (0, 0), (0, 0)))
    flat = []
    for other in range(2):
        some = lax.dynamic_slice_in_dim(by_plane, (half ^ other) * count, count + 1, 0)
        flat.append(some.reshape((count + 1) * channels_out, -1))
    x = [as_rows(send[step] if step == 0 else swap(send[step], space, step)) for step in steps]
    send_now, flat = lax.optimization_barrier((send, flat))
    flat = [flat[0], swap(flat[1], space, size)]
    halo = call(
        halo_kernel, [array((256, 128))] * size, [as_rows(block) for block in send_now], flops=2 * 256 * 256 * 128
    )
    halo = [lax.ppermute(halo[step], "space", [(size - 1, size + ((size - 1) ^ step))]) for step in steps]
    pick, k1m, k1f, ogt, act_grad = call(
        prepare_kernel,
        [array((256, 384)), array((128, 768)), array((128, 384)), array((cells, 1152)), array((128, cells))],
        (half.reshape(1), k1, k2, *flat),
        scratch=[((128, 1152), jnp.bfloat16), ((2, 128, size * 32), jnp.bfloat16), ((1152, cells), jnp.bfloat16)],
        flops=2 * 128 * 1152 * cells * 2,
    )

    rows = -(-TERM_ROWS // (devices * 2)) * 2
    act, terms = call(
        functools.partial(layer_kernel, steps),
        [array((128, cells)), array((devices * rows, LANES))],
        (place.reshape(1), *x, *halo, pick, k1m, k1f, ogt, act_grad),
        scratch=[((768, cells), jnp.bfloat16), ((384, cells), jnp.bfloat16), ((4 * cells, 128), jnp.bfloat16)],
        flops=2 * 128 * 4096 * cells,
    )
    blocks = terms.reshape(devices, rows // 2, 2, LANES)
    mine = lax.all_to_all(blocks, axes, split_axis=0, concat_axis=0, tiled=True)
    (spread,) = call(functools.partial(add_kernel, rows), [array(terms.shape)], (mine.reshape(terms.shape),))
    spread = spread.reshape(blocks.shape)
    whole = lax.all_to_all(spread, axes, split_axis=0, concat_axis=0, tiled=True)
    shapes = [(3, 3, 3) + kernel.shape[1::-1] for kernel in (first_kernel, second_kernel)]
    first, second = pl.pallas_call(
        unpack_kernel,
        out_shape=[array(shape, jnp.float32) for shape in shapes],
        in_specs=[pl.BlockSpec(memory_space=pltpu.VMEM)],
        out_specs=[pl.BlockSpec(memory_space=pl.ANY)] * 2,
        scratch_shapes=[pltpu.VMEM(shape, jnp.float32) for shape in shapes] + [pltpu.SemaphoreType.DMA((2, 3))],
        compiler_params=pltpu.CompilerParams(vmem_limit_bytes=VMEM_BYTES),
    )(whole.reshape(terms.shape))

    act, unused = lax.optimization_barrier((act, spread))
    span = -(-(count + 1) * 64 // LANES) * LANES
    (shares,) = call(
        features_kernel,
        [array((2, channels_out, span))],
        (act, k2),
        scratch=[((128, 1152), jnp.bfloat16)],
        flops=2 * 128 * 1152 * cells,
    )
    kept, given = [lax.dynamic_index_in_dim(shares, half ^ other, 0, keepdims=False) for other in range(2)]
    (features,) = call(
        join_kernel,
        [array((planes, channels_out, 64))],
        (half.reshape(1), kept, swap(given, space, size)),
    )
    features = jnp.transpose(features, (1, 0, 2)).reshape(out_grad.shape)
    return (features, jnp.transpose(first, (4, 3, 0, 1, 2)), jnp.transpose(second, (4, 3, 0, 1, 2)))


def solution(mesh):
    placed = (P("sample", None, "space", None), P(), P(), P(("sample", "space"), None, None, None))
    return jax.shard_map(
        body,
        mesh=mesh,
        in_specs=placed,
        out_specs=(P(("sample", "space"), None, None, None), P(), P()),
        check_vma=False,
    )
```

```python
import functools
import math

import jax
import jax.numpy as jnp
from jax import lax
from jax.experimental import pallas as pl
from jax.experimental.pallas import tpu as pltpu
from jax.sharding import PartitionSpec as P

HEIGHT = 8
WIDTH = 128
LANES = 128
VMEM_BYTES = 16 * 1024 * 1024
TERM_ROWS = 576


def iota(shape, dim):
    return lax.broadcasted_iota(jnp.int32, shape, dim)


def dot(left, right, dims=((1,), (0,))):
    return lax.dot_general(left, right, (dims, ((), ())), preferred_element_type=jnp.float32)


def ones_where(mask):
    return jnp.where(mask, 1.0, 0.0).astype(jnp.bfloat16)


def band_of_second(k2_ref, k2t_ref):
    channels_mid, channels_out = k2_ref.shape[3:]
    empty = jnp.zeros((channels_mid, channels_out), jnp.bfloat16)
    for ad in range(3):
        for aw in range(3):
            tap = [k2_ref[ad, ah, aw] for ah in range(3)]
            band = ((tap[1], empty), (tap[2], tap[0]), (empty, tap[1]), (empty, tap[2]))
            start = (ad * 3 + aw) * 2 * channels_out
            for hh in range(4):
                k2t_ref[hh * channels_mid:(hh + 1) * channels_mid, start:start + 2 * channels_out] = (
                    jnp.concatenate(band[hh], axis=1))


def upsampling(ad, aw, beyond=0):
    row, col = iota((128, 512), 0), iota((128, 512), 1)
    target = ((row >> 5) << 7) + ((row & 31) << 1) + (64 * (ad - 1) + aw - 1 + 128 * beyond)
    keep = col == target
    if aw == 0:
        keep = keep & ((row & 31) > 0)
    return ones_where(keep)


def prepare_kernel(k1_ref, k2_ref, og_ref, pick_ref, k1t_ref, ogt_ref, ag_ref, k2t_ref, ogu_ref):
    channels_in, channels_mid = k1_ref.shape[3:]
    row, col = iota((2 * WIDTH, 2 * 64), 0), iota((2 * WIDTH, 2 * 64), 1)
    for aw in range(3):
        same = (row >> 7) == (col >> 6)
        tap = (row & 127) == 2 * (col & 63) + aw - 1
        pick_ref[:, aw * 128:(aw + 1) * 128] = ones_where(same & tap)
    shape = (9 * channels_in, channels_in * 2 * HEIGHT)
    row, col = iota(shape, 0), iota(shape, 1)
    tap = row >> 4
    ad = jnp.where(tap >= 6, 2, jnp.where(tap >= 3, 1, 0))
    ah, i = tap - 3 * ad, row & 15
    same = i == col >> 4
    h, d = (col >> 1) & 7, col & 1
    taps = []
    for aw in range(3):
        parts = [k1_ref[a, b, aw] for a in range(3) for b in range(3)]
        taps.append(jnp.concatenate(parts, axis=0).astype(jnp.float32).T.astype(jnp.bfloat16))
    for following in range(2):
        plane = (ad == 0) & (d == 1) if following else (ad == d + 1)
        for hh in range(4):
            place = ones_where(same & plane & (h == 2 * hh + ah - 1))
            start = (following * 4 + hh) * channels_mid
            for aw in range(3):
                block = dot(taps[aw], place).astype(jnp.bfloat16)
                k1t_ref[start:start + channels_mid, aw * shape[1]:(aw + 1) * shape[1]] = block
    band_of_second(k2_ref, k2t_ref)
    groups = og_ref.shape[1] // 128
    for ad in range(3):
        for aw in range(3):
            t = ad * 3 + aw
            up = upsampling(ad, aw)
            for g in range(groups):
                value = dot(og_ref[:, g * 128:(g + 1) * 128], up)
                if ad == 0 and g + 1 < groups:
                    value = value + dot(og_ref[:, (g + 1) * 128:(g + 2) * 128], upsampling(ad, aw, 4))
                ogu_ref[t * 128:(t + 1) * 128, g * 512:(g + 1) * 512] = value.astype(jnp.bfloat16)
                ogt_ref[g * 512:(g + 1) * 512, t * 128:(t + 1) * 128] = value.T.astype(jnp.bfloat16)
    for g in range(groups):
        lanes = slice(g * 512, (g + 1) * 512)
        ag_ref[:, lanes] = dot(k2t_ref[...], ogu_ref[:, lanes]).astype(jnp.bfloat16)


def layer_kernel(steps, position_ref, *refs):
    cells = refs[-6].shape[1]
    blocks = cells // 64
    pick_ref, k1t_ref, ogt_ref, ag_ref, act_ref, terms_ref, y_scr, pg_scr, x_ref = refs[blocks:]
    rows = 256
    for place, step in enumerate(steps):
        source = lax.bitwise_xor(position_ref[0], jnp.int32(step))
        x_ref[pl.ds(pl.multiple_of(source * rows, rows), rows), :] = refs[place][...]
    for q in range(cells // 128):
        start = q * 2 * rows
        pair = jnp.concatenate([x_ref[start:start + rows, :], x_ref[start + rows:start + 2 * rows, :]], axis=1)
        y = dot(pair, pick_ref[...]).astype(jnp.bfloat16)
        for aw in range(3):
            y_scr[aw * rows:(aw + 1) * rows, q * 128:(q + 1) * 128] = y[:, aw * 128:(aw + 1) * 128]
    both = dot(k1t_ref[...], y_scr[...])
    lane = iota((128, cells), 1)
    from_last = jnp.where(lane < 64, 0.0, pltpu.roll(both[128:], 64, 1))
    pre = both[:128] + from_last
    sigma = jax.nn.sigmoid(pre)
    act = (pre * sigma).astype(jnp.bfloat16)
    act_ref[...] = act
    slope = sigma * (1.0 + pre * (1.0 - sigma))
    grad = (ag_ref[...].astype(jnp.float32) * slope).astype(jnp.bfloat16)
    pg_scr[:128, :] = grad
    to_last = pltpu.roll(grad.astype(jnp.float32), cells - 64, 1)
    pg_scr[128:, :] = jnp.where(lane < cells - 64, to_last, 0.0).astype(jnp.bfloat16)

    second = dot(act, ogt_ref[...])
    lane = iota((32, 128), 1)
    held = None
    for t in range(9):
        tile = second[:, t * 128:(t + 1) * 128]
        turned = pltpu.roll(tile, 64, 1)
        mixed = jnp.where(lane < 64, tile[0:32] + turned[64:96], turned[32:64] + tile[96:128])
        terms_ref[t * 32:(t + 1) * 32, :] = mixed.astype(jnp.bfloat16)
        if t % 2 == 0:
            held = jnp.where(lane < 64, turned[32:64], 0.0)
        else:
            held = jnp.where(lane < 64, held, tile[32:64])
        if t % 2 == 1:
            start = 288 + (t // 2) * 32
            terms_ref[start:start + 32, :] = held.astype(jnp.bfloat16)
    terms_ref[416:432, :] = jnp.where(lane[:16] < 64, held[:16], pltpu.roll(held[16:], 64, 1)).astype(jnp.bfloat16)

    first = dot(y_scr[...], pg_scr[...], ((1,), (1,))).astype(jnp.bfloat16)
    shape = (rows, 256)
    h, hh = (iota(shape, 0) >> 1) & 7, (iota(shape, 1) >> 5) & 3
    even, odd = ones_where((h >> 1) == hh), ones_where(((h & 1) == 1) & ((h + 1) >> 1 == hh))
    rank, index = iota((64, rows), 0), iota((64, rows), 1)
    same = ((rank & 15) == index >> 4) & (((rank >> 4) & 1) == (index & 1))
    later_taps = ones_where(same & ((rank >> 5) == ((index >> 1) & 1)))
    first_tap = ones_where(same[:32] & (((index[:32] >> 1) & 1) == 1))
    lane = iota((16, 128), 1)
    for aw in range(3):
        tile = first[aw * rows:(aw + 1) * rows]
        total = jnp.concatenate([dot(first_tap, tile * odd), dot(later_taps, tile * even)], axis=0)
        start = 432 + aw * 48
        for ad in range(3):
            side = slice(128, 256) if ad == 0 else slice(0, 128)
            d = 0 if ad == 1 else 1
            packed = None
            for ah in range(3):
                part = total[ah * 32 + d * 16:ah * 32 + d * 16 + 16, side]
                part = part + pltpu.roll(part, 64, 1)
                part = part + pltpu.roll(part, 32, 1)
                packed = part if packed is None else jnp.where(lane >= ah * 32, part, packed)
            terms_ref[start + ad * 16:start + (ad + 1) * 16, :] = packed.astype(jnp.bfloat16)
    rest = terms_ref.shape[0] - TERM_ROWS
    if rest > 0:
        terms_ref[TERM_ROWS:, :] = jnp.zeros((rest, 128), jnp.bfloat16)


def features_kernel(act_ref, k2_ref, out_ref, k2t_ref):
    band_of_second(k2_ref, k2t_ref)
    groups = out_ref.shape[1] // 128
    for g in range(groups):
        total = jnp.zeros((128, 128), jnp.float32)
        for t in range(9):
            taken = dot(act_ref[:, g * 512:(g + 1) * 512], upsampling(t // 3, t % 3), ((1,), (1,)))
            if t < 3 and g > 0:
                last = act_ref[:, (g - 1) * 512:g * 512]
                taken = taken + dot(last, upsampling(0, t, 4), ((1,), (1,)))
            band = k2t_ref[:, t * 128:(t + 1) * 128]
            total = total + dot(band, taken.astype(jnp.bfloat16), ((0,), (0,)))
        out_ref[:, g * 128:(g + 1) * 128] = total.astype(jnp.bfloat16)


def add_kernel(rows, mine_ref, out_ref):
    count = mine_ref.shape[0]
    unit = rows * 16 // math.gcd(rows, 16)
    total = mine_ref[0:unit, :].astype(jnp.float32)
    for start in range(unit, count, unit):
        total = total + mine_ref[start:start + unit, :].astype(jnp.float32)
    if unit % (2 * rows) == 0 and (unit // 2) % 8 == 0:
        total = total[:unit // 2] + total[unit // 2:]
    parts = [total[start:start + rows] for start in range(0, total.shape[0], rows)]
    total = functools.reduce(jnp.add, parts)
    spread = jnp.concatenate([total] * (unit // rows), axis=0).astype(jnp.bfloat16)
    for start in range(0, count, unit):
        out_ref[start:start + unit, :] = spread


def unpack_kernel(whole_ref, first_ref, second_ref, first_scr, second_scr, sems):
    copies = []
    for ad in range(3):
        for aw in range(3):
            t = ad * 3 + aw
            pair = whole_ref[t * 32:(t + 1) * 32, :].astype(jnp.float32)
            second_scr[ad, 1, aw] = pair[:, :64]
            second_scr[ad, 2, aw] = pair[:, 64:]
            if t == 8:
                lone = whole_ref[416:432, :].astype(jnp.float32)
                second_scr[ad, 0, aw] = jnp.concatenate([lone[:, :64], lone[:, 64:]], axis=0)
            else:
                start = 288 + (t // 2) * 32
                lone = whole_ref[start:start + 32, :].astype(jnp.float32)
                second_scr[ad, 0, aw] = lone[:, :64] if t % 2 == 0 else lone[:, 64:]
        copies.append(pltpu.make_async_copy(second_scr.at[ad], second_ref.at[ad], sems.at[0, ad]))
        copies[-1].start()
    for ad in range(3):
        for aw in range(3):
            start = 432 + aw * 48 + ad * 16
            tile = whole_ref[start:start + 16, :].astype(jnp.float32)
            for ah in range(3):
                first_scr[ad, ah, aw] = tile[:, ah * 32:(ah + 1) * 32]
        copies.append(pltpu.make_async_copy(first_scr.at[ad], first_ref.at[ad], sems.at[1, ad]))
        copies[-1].start()
    for copy in copies:
        copy.wait()


def call(kernel, outs, args, scratch=(), flops=0):
    whole = pl.BlockSpec(memory_space=pltpu.VMEM)
    scalar = pl.BlockSpec(memory_space=pltpu.SMEM)
    size = sum(math.prod(a.shape) * a.dtype.itemsize for a in list(args) + list(outs))
    return pl.pallas_call(
        kernel,
        out_shape=tuple(outs),
        in_specs=[scalar if a.dtype == jnp.int32 else whole for a in args],
        out_specs=(whole,) * len(outs),
        scratch_shapes=list(scratch),
        compiler_params=pltpu.CompilerParams(vmem_limit_bytes=VMEM_BYTES),
        cost_estimate=pl.CostEstimate(flops=flops, bytes_accessed=size, transcendentals=0),
    )(*args)


def array(shape, dtype=jnp.bfloat16):
    return jax.ShapeDtypeStruct(shape, dtype)


def by_tap(kernel):
    return jnp.transpose(kernel, (2, 3, 4, 1, 0))


def prepare(k1, k2, out_grad):
    c0, c1 = k1.shape[3:]
    c2 = k2.shape[4]
    planes = out_grad.shape[2]
    cells = planes * 2 * 64
    og = out_grad.reshape(c2, planes, 2, 32).transpose(2, 0, 1, 3).reshape(2 * c2, planes * 32)
    outs = [
        array((256, 384)),
        array((2 * 4 * c1, 3 * c0 * 16)),
        array((cells, 9 * 2 * c2)),
        array((4 * c1, cells)),
    ]
    scratch = [pltpu.VMEM((4 * c1, 9 * 2 * c2), jnp.bfloat16), pltpu.VMEM((9 * 2 * c2, cells), jnp.bfloat16)]
    return call(prepare_kernel, outs, (k1, k2, og), scratch, flops=2 * 128 * 1152 * cells * 2)


def body(crops, first_kernel, second_kernel, out_grad):
    axes = ("space", "sample")
    devices = lax.axis_size(axes)
    channels_out, planes = out_grad.shape[1:3]
    space = lax.axis_size("space")
    assert space & (space - 1) == 0
    position = lax.axis_index("space").astype(jnp.int32)
    wanted = sorted(range(1, space), key=lambda step: -step.bit_length())
    steps = [0] + wanted[::-1]
    k1, k2 = by_tap(first_kernel), by_tap(second_kernel)
    x = []
    far = wanted[:space // 2]
    early = [lax.dynamic_index_in_dim(crops, position ^ step, 0, keepdims=False) for step in far]
    rest, early = lax.optimization_barrier((crops, early))
    for step in steps:
        if step in far:
            block = early[far.index(step)]
        else:
            block = lax.dynamic_index_in_dim(rest, position ^ step, 0, keepdims=False)
        if step > 0:
            block = lax.ppermute(block, "space", [(source, source ^ step) for source in range(space)])
        channels_in, two, flat_cells = block.shape
        block = block.reshape(channels_in, two, HEIGHT, WIDTH).transpose(0, 2, 1, 3)
        x.append(block.reshape(channels_in * two * HEIGHT, WIDTH))
    pick, k1t, ogt, act_grad = prepare(k1, k2, out_grad)
    cells = act_grad.shape[1]
    rows = -(-TERM_ROWS // (devices * 2)) * 2
    act, terms = call(
        functools.partial(layer_kernel, steps),
        [array((128, cells)), array((devices * rows, LANES))],
        (position.reshape(1), *x, pick, k1t, ogt, act_grad),
        scratch=[pltpu.VMEM((768, cells), jnp.bfloat16), pltpu.VMEM((256, cells), jnp.bfloat16), pltpu.VMEM((4 * cells, 128), jnp.bfloat16)],
        flops=2 * 128 * 4096 * cells,
    )
    blocks = terms.reshape(devices, rows // 2, 2, LANES)
    mine = lax.all_to_all(blocks, axes, split_axis=0, concat_axis=0, tiled=True)
    (features,) = call(
        features_kernel,
        [array((2 * channels_out, planes * 32))],
        (act, k2),
        scratch=[pltpu.VMEM((128, 1152), jnp.bfloat16)],
        flops=2 * 128 * 1152 * cells,
    )
    features = features.reshape(2, channels_out, planes, 32).transpose(1, 2, 0, 3).reshape(out_grad.shape)
    add = functools.partial(add_kernel, rows)
    (spread,) = call(add, [pltpu.VMEM(terms.shape, jnp.bfloat16)], (mine.reshape(terms.shape),))
    spread = spread.reshape(blocks.shape)
    whole = lax.all_to_all(spread, axes, split_axis=0, concat_axis=0, tiled=True)
    shapes = [(3, 3, 3) + kernel.shape[1::-1] for kernel in (first_kernel, second_kernel)]
    first, second = pl.pallas_call(
        unpack_kernel,
        out_shape=[array(shape, jnp.float32) for shape in shapes],
        in_specs=[pl.BlockSpec(memory_space=pltpu.VMEM)],
        out_specs=[pl.BlockSpec(memory_space=pl.ANY)] * 2,
        scratch_shapes=[pltpu.VMEM(shape, jnp.float32) for shape in shapes] + [pltpu.SemaphoreType.DMA((2, 3))],
        compiler_params=pltpu.CompilerParams(vmem_limit_bytes=VMEM_BYTES),
    )(whole.reshape(terms.shape))
    return (features, jnp.transpose(first, (4, 3, 0, 1, 2)), jnp.transpose(second, (4, 3, 0, 1, 2)))


def solution(mesh):
    placed = (P("sample", None, "space", None), P(), P(), P(("sample", "space"), None, None, None))
    return jax.shard_map(
        body,
        mesh=mesh,
        in_specs=placed,
        out_specs=(P(("sample", "space"), None, None, None), P(), P()),
        check_vma=False,
    )
```

```python
import functools
import math

import jax
import jax.numpy as jnp
from jax import lax
from jax.experimental import pallas as pl
from jax.experimental.pallas import tpu as pltpu
from jax.sharding import PartitionSpec as P

HEIGHT = 8
WIDTH = 128
LANES = 128
VMEM_BYTES = 16 * 1024 * 1024
TERM_ROWS = 576


def iota(shape, dim):
    return lax.broadcasted_iota(jnp.int32, shape, dim)


def dot(left, right, dims=((1,), (0,))):
    return lax.dot_general(left, right, (dims, ((), ())), preferred_element_type=jnp.float32)


def ones_where(mask):
    return jnp.where(mask, 1.0, 0.0).astype(jnp.bfloat16)


def band_of_second(k2_ref, k2t_ref):
    channels_mid, channels_out = k2_ref.shape[3:]
    empty = jnp.zeros((channels_mid, channels_out), jnp.bfloat16)
    for ad in range(3):
        for aw in range(3):
            tap = [k2_ref[ad, ah, aw] for ah in range(3)]
            band = ((tap[1], empty), (tap[2], tap[0]), (empty, tap[1]), (empty, tap[2]))
            start = (ad * 3 + aw) * 2 * channels_out
            for hh in range(4):
                k2t_ref[hh * channels_mid:(hh + 1) * channels_mid, start:start + 2 * channels_out] = (
                    jnp.concatenate(band[hh], axis=1))


def upsampling(ad, aw, beyond=0):
    row, col = iota((128, 512), 0), iota((128, 512), 1)
    target = ((row >> 5) << 7) + ((row & 31) << 1) + (64 * (ad - 1) + aw - 1 + 128 * beyond)
    keep = col == target
    if aw == 0:
        keep = keep & ((row & 31) > 0)
    return ones_where(keep)


def prepare_kernel(k1_ref, k2_ref, og_ref, pick_ref, k1t_ref, ogt_ref, ag_ref, k2t_ref, ogu_ref):
    channels_in, channels_mid = k1_ref.shape[3:]
    row, col = iota((2 * WIDTH, 2 * 64), 0), iota((2 * WIDTH, 2 * 64), 1)
    for aw in range(3):
        same = (row >> 7) == (col >> 6)
        tap = (row & 127) == 2 * (col & 63) + aw - 1
        pick_ref[:, aw * 128:(aw + 1) * 128] = ones_where(same & tap)
    shape = (9 * channels_in, channels_in * 2 * HEIGHT)
    row, col = iota(shape, 0), iota(shape, 1)
    tap = row >> 4
    ad = jnp.where(tap >= 6, 2, jnp.where(tap >= 3, 1, 0))
    ah, i = tap - 3 * ad, row & 15
    same = i == col >> 4
    h, d = (col >> 1) & 7, col & 1
    taps = []
    for aw in range(3):
        parts = [k1_ref[a, b, aw] for a in range(3) for b in range(3)]
        taps.append(jnp.concatenate(parts, axis=0).astype(jnp.float32).T.astype(jnp.bfloat16))
    for following in range(2):
        plane = (ad == 0) & (d == 1) if following else (ad == d + 1)
        for hh in range(4):
            place = ones_where(same & plane & (h == 2 * hh + ah - 1))
            start = (following * 4 + hh) * channels_mid
            for aw in range(3):
                block = dot(taps[aw], place).astype(jnp.bfloat16)
                k1t_ref[start:start + channels_mid, aw * shape[1]:(aw + 1) * shape[1]] = block
    band_of_second(k2_ref, k2t_ref)
    groups = og_ref.shape[1] // 128
    for ad in range(3):
        for aw in range(3):
            t = ad * 3 + aw
            up = upsampling(ad, aw)
            for g in range(groups):
                value = dot(og_ref[:, g * 128:(g + 1) * 128], up)
                if ad == 0 and g + 1 < groups:
                    value = value + dot(og_ref[:, (g + 1) * 128:(g + 2) * 128], upsampling(ad, aw, 4))
                ogu_ref[t * 128:(t + 1) * 128, g * 512:(g + 1) * 512] = value.astype(jnp.bfloat16)
                ogt_ref[g * 512:(g + 1) * 512, t * 128:(t + 1) * 128] = value.T.astype(jnp.bfloat16)
    for g in range(groups):
        lanes = slice(g * 512, (g + 1) * 512)
        ag_ref[:, lanes] = dot(k2t_ref[...], ogu_ref[:, lanes]).astype(jnp.bfloat16)


def layer_kernel(steps, position_ref, *refs):
    cells = refs[-6].shape[1]
    blocks = cells // 64
    pick_ref, k1t_ref, ogt_ref, ag_ref, act_ref, terms_ref, y_scr, pg_scr, x_ref = refs[blocks:]
    rows = 256
    for place, step in enumerate(steps):
        source = lax.bitwise_xor(position_ref[0], jnp.int32(step))
        x_ref[pl.ds(pl.multiple_of(source * rows, rows), rows), :] = refs[place][...]
    for q in range(cells // 128):
        start = q * 2 * rows
        pair = jnp.concatenate([x_ref[start:start + rows, :], x_ref[start + rows:start + 2 * rows, :]], axis=1)
        y = dot(pair, pick_ref[...]).astype(jnp.bfloat16)
        for aw in range(3):
            y_scr[aw * rows:(aw + 1) * rows, q * 128:(q + 1) * 128] = y[:, aw * 128:(aw + 1) * 128]
    both = dot(k1t_ref[...], y_scr[...])
    lane = iota((128, cells), 1)
    from_last = jnp.where(lane < 64, 0.0, pltpu.roll(both[128:], 64, 1))
    pre = both[:128] + from_last
    sigma = jax.nn.sigmoid(pre)
    act = (pre * sigma).astype(jnp.bfloat16)
    act_ref[...] = act
    slope = sigma * (1.0 + pre * (1.0 - sigma))
    grad = (ag_ref[...].astype(jnp.float32) * slope).astype(jnp.bfloat16)
    pg_scr[:128, :] = grad
    to_last = pltpu.roll(grad.astype(jnp.float32), cells - 64, 1)
    pg_scr[128:, :] = jnp.where(lane < cells - 64, to_last, 0.0).astype(jnp.bfloat16)

    second = dot(act, ogt_ref[...])
    lane = iota((32, 128), 1)
    held = None
    for t in range(9):
        tile = second[:, t * 128:(t + 1) * 128]
        turned = pltpu.roll(tile, 64, 1)
        mixed = jnp.where(lane < 64, tile[0:32] + turned[64:96], turned[32:64] + tile[96:128])
        terms_ref[t * 32:(t + 1) * 32, :] = mixed.astype(jnp.bfloat16)
        if t % 2 == 0:
            held = jnp.where(lane < 64, turned[32:64], 0.0)
        else:
            held = jnp.where(lane < 64, held, tile[32:64])
        if t % 2 == 1:
            start = 288 + (t // 2) * 32
            terms_ref[start:start + 32, :] = held.astype(jnp.bfloat16)
    terms_ref[416:432, :] = jnp.where(lane[:16] < 64, held[:16], pltpu.roll(held[16:], 64, 1)).astype(jnp.bfloat16)

    first = dot(y_scr[...], pg_scr[...], ((1,), (1,))).astype(jnp.bfloat16)
    shape = (rows, 256)
    h, hh = (iota(shape, 0) >> 1) & 7, (iota(shape, 1) >> 5) & 3
    even, odd = ones_where((h >> 1) == hh), ones_where(((h & 1) == 1) & ((h + 1) >> 1 == hh))
    rank, index = iota((64, rows), 0), iota((64, rows), 1)
    same = ((rank & 15) == index >> 4) & (((rank >> 4) & 1) == (index & 1))
    later_taps = ones_where(same & ((rank >> 5) == ((index >> 1) & 1)))
    first_tap = ones_where(same[:32] & (((index[:32] >> 1) & 1) == 1))
    lane = iota((16, 128), 1)
    for aw in range(3):
        tile = first[aw * rows:(aw + 1) * rows]
        total = jnp.concatenate([dot(first_tap, tile * odd), dot(later_taps, tile * even)], axis=0)
        start = 432 + aw * 48
        for ad in range(3):
            side = slice(128, 256) if ad == 0 else slice(0, 128)
            d = 0 if ad == 1 else 1
            packed = None
            for ah in range(3):
                part = total[ah * 32 + d * 16:ah * 32 + d * 16 + 16, side]
                part = part + pltpu.roll(part, 64, 1)
                part = part + pltpu.roll(part, 32, 1)
                packed = part if packed is None else jnp.where(lane >= ah * 32, part, packed)
            terms_ref[start + ad * 16:start + (ad + 1) * 16, :] = packed.astype(jnp.bfloat16)
    rest = terms_ref.shape[0] - TERM_ROWS
    if rest > 0:
        terms_ref[TERM_ROWS:, :] = jnp.zeros((rest, 128), jnp.bfloat16)


def features_kernel(act_ref, k2_ref, out_ref, k2t_ref):
    band_of_second(k2_ref, k2t_ref)
    groups = out_ref.shape[1] // 128
    for g in range(groups):
        total = jnp.zeros((128, 128), jnp.float32)
        for t in range(9):
            taken = dot(act_ref[:, g * 512:(g + 1) * 512], upsampling(t // 3, t % 3), ((1,), (1,)))
            if t < 3 and g > 0:
                last = act_ref[:, (g - 1) * 512:g * 512]
                taken = taken + dot(last, upsampling(0, t, 4), ((1,), (1,)))
            band = k2t_ref[:, t * 128:(t + 1) * 128]
            total = total + dot(band, taken.astype(jnp.bfloat16), ((0,), (0,)))
        out_ref[:, g * 128:(g + 1) * 128] = total.astype(jnp.bfloat16)


def add_kernel(rows, mine_ref, out_ref):
    count = mine_ref.shape[0]
    unit = rows * 16 // math.gcd(rows, 16)
    total = mine_ref[0:unit, :].astype(jnp.float32)
    for start in range(unit, count, unit):
        total = total + mine_ref[start:start + unit, :].astype(jnp.float32)
    if unit % (2 * rows) == 0 and (unit // 2) % 8 == 0:
        total = total[:unit // 2] + total[unit // 2:]
    parts = [total[start:start + rows] for start in range(0, total.shape[0], rows)]
    total = functools.reduce(jnp.add, parts)
    spread = jnp.concatenate([total] * (unit // rows), axis=0).astype(jnp.bfloat16)
    for start in range(0, count, unit):
        out_ref[start:start + unit, :] = spread


def unpack_kernel(whole_ref, first_ref, second_ref, first_scr, second_scr, sems):
    copies = []
    for ad in range(3):
        for aw in range(3):
            t = ad * 3 + aw
            pair = whole_ref[t * 32:(t + 1) * 32, :].astype(jnp.float32)
            second_scr[ad, 1, aw] = pair[:, :64]
            second_scr[ad, 2, aw] = pair[:, 64:]
            if t == 8:
                lone = whole_ref[416:432, :].astype(jnp.float32)
                second_scr[ad, 0, aw] = jnp.concatenate([lone[:, :64], lone[:, 64:]], axis=0)
            else:
                start = 288 + (t // 2) * 32
                lone = whole_ref[start:start + 32, :].astype(jnp.float32)
                second_scr[ad, 0, aw] = lone[:, :64] if t % 2 == 0 else lone[:, 64:]
        copies.append(pltpu.make_async_copy(second_scr.at[ad], second_ref.at[ad], sems.at[0, ad]))
        copies[-1].start()
    for ad in range(3):
        for aw in range(3):
            start = 432 + aw * 48 + ad * 16
            tile = whole_ref[start:start + 16, :].astype(jnp.float32)
            for ah in range(3):
                first_scr[ad, ah, aw] = tile[:, ah * 32:(ah + 1) * 32]
        copies.append(pltpu.make_async_copy(first_scr.at[ad], first_ref.at[ad], sems.at[1, ad]))
        copies[-1].start()
    for copy in copies:
        copy.wait()


def call(kernel, outs, args, scratch=(), flops=0):
    whole = pl.BlockSpec(memory_space=pltpu.VMEM)
    scalar = pl.BlockSpec(memory_space=pltpu.SMEM)
    size = sum(a.size * a.dtype.itemsize for a in list(args) + list(outs))
    return pl.pallas_call(
        kernel,
        out_shape=tuple(outs),
        in_specs=[scalar if a.dtype == jnp.int32 else whole for a in args],
        out_specs=(whole,) * len(outs),
        scratch_shapes=list(scratch),
        compiler_params=pltpu.CompilerParams(vmem_limit_bytes=VMEM_BYTES),
        cost_estimate=pl.CostEstimate(flops=flops, bytes_accessed=size, transcendentals=0),
    )(*args)


def array(shape, dtype=jnp.bfloat16):
    return jax.ShapeDtypeStruct(shape, dtype)


def by_tap(kernel):
    return jnp.transpose(kernel, (2, 3, 4, 1, 0))


def prepare(k1, k2, out_grad):
    c0, c1 = k1.shape[3:]
    c2 = k2.shape[4]
    planes = out_grad.shape[2]
    cells = planes * 2 * 64
    og = out_grad.reshape(c2, planes, 2, 32).transpose(2, 0, 1, 3).reshape(2 * c2, planes * 32)
    outs = [
        array((256, 384)),
        array((2 * 4 * c1, 3 * c0 * 16)),
        array((cells, 9 * 2 * c2)),
        array((4 * c1, cells)),
    ]
    scratch = [pltpu.VMEM((4 * c1, 9 * 2 * c2), jnp.bfloat16), pltpu.VMEM((9 * 2 * c2, cells), jnp.bfloat16)]
    return call(prepare_kernel, outs, (k1, k2, og), scratch, flops=2 * 128 * 1152 * cells * 2)


def body(crops, first_kernel, second_kernel, out_grad):
    axes = ("space", "sample")
    devices = lax.axis_size(axes)
    channels_out, planes = out_grad.shape[1:3]
    space = lax.axis_size("space")
    assert space & (space - 1) == 0
    position = lax.axis_index("space").astype(jnp.int32)
    across, near = range(space - 1, space // 2 - 1, -1), range(1, space // 2)
    order = [step for two in zip(across, near) for step in two] + [space // 2]
    early, late = order[:space // 2], order[space // 2:]
    steps = [0] + late[::-1] + early
    k1, k2 = by_tap(first_kernel), by_tap(second_kernel)
    x = []
    cut = [lax.dynamic_index_in_dim(crops, position ^ step, 0, keepdims=False) for step in early]
    rest, cut = lax.optimization_barrier((crops, cut))
    for step in steps:
        if step in early:
            block = cut[early.index(step)]
        else:
            block = lax.dynamic_index_in_dim(rest, position ^ step, 0, keepdims=False)
        if step > 0:
            block = lax.ppermute(block, "space", [(source, source ^ step) for source in range(space)])
        channels_in, two, flat_cells = block.shape
        block = block.reshape(channels_in, two, HEIGHT, WIDTH).transpose(0, 2, 1, 3)
        x.append(block.reshape(channels_in * two * HEIGHT, WIDTH))
    pick, k1t, ogt, act_grad = prepare(k1, k2, out_grad)
    cells = act_grad.shape[1]
    rows = -(-TERM_ROWS // (devices * 2)) * 2
    act, terms = call(
        functools.partial(layer_kernel, steps),
        [array((128, cells)), array((devices * rows, LANES))],
        (position.reshape(1), *x, pick, k1t, ogt, act_grad),
        scratch=[pltpu.VMEM((768, cells), jnp.bfloat16), pltpu.VMEM((256, cells), jnp.bfloat16), pltpu.VMEM((4 * cells, 128), jnp.bfloat16)],
        flops=2 * 128 * 4096 * cells,
    )
    blocks = terms.reshape(devices, rows // 2, 2, LANES)
    mine = lax.all_to_all(blocks, axes, split_axis=0, concat_axis=0, tiled=True)
    (features,) = call(
        features_kernel,
        [array((2 * channels_out, planes * 32))],
        (act, k2),
        scratch=[pltpu.VMEM((128, 1152), jnp.bfloat16)],
        flops=2 * 128 * 1152 * cells,
    )
    features = features.reshape(2, channels_out, planes, 32).transpose(1, 2, 0, 3).reshape(out_grad.shape)
    add = functools.partial(add_kernel, rows)
    (spread,) = call(add, [array(terms.shape)], (mine.reshape(terms.shape),))
    spread = spread.reshape(blocks.shape)
    whole = lax.all_to_all(spread, axes, split_axis=0, concat_axis=0, tiled=True)
    shapes = [(3, 3, 3) + kernel.shape[1::-1] for kernel in (first_kernel, second_kernel)]
    first, second = pl.pallas_call(
        unpack_kernel,
        out_shape=[array(shape, jnp.float32) for shape in shapes],
        in_specs=[pl.BlockSpec(memory_space=pltpu.VMEM)],
        out_specs=[pl.BlockSpec(memory_space=pl.ANY)] * 2,
        scratch_shapes=[pltpu.VMEM(shape, jnp.float32) for shape in shapes] + [pltpu.SemaphoreType.DMA((2, 3))],
        compiler_params=pltpu.CompilerParams(vmem_limit_bytes=VMEM_BYTES),
    )(whole.reshape(terms.shape))
    return (features, jnp.transpose(first, (4, 3, 0, 1, 2)), jnp.transpose(second, (4, 3, 0, 1, 2)))


def solution(mesh):
    placed = (P("sample", None, "space", None), P(), P(), P(("sample", "space"), None, None, None))
    return jax.shard_map(
        body,
        mesh=mesh,
        in_specs=placed,
        out_specs=(P(("sample", "space"), None, None, None), P(), P()),
        check_vma=False,
    )
```

```python
import functools
import math

import jax
import jax.numpy as jnp
from jax import lax
from jax.experimental import pallas as pl
from jax.experimental.pallas import tpu as pltpu
from jax.sharding import PartitionSpec as P

HEIGHT = 8
WIDTH = 128
LANES = 128
VMEM_BYTES = 16 * 1024 * 1024
TERM_ROWS = 576


def iota(shape, dim):
    return lax.broadcasted_iota(jnp.int32, shape, dim)


def dot(left, right, dims=((1,), (0,))):
    return lax.dot_general(left, right, (dims, ((), ())), preferred_element_type=jnp.float32)


def ones_where(mask):
    return jnp.where(mask, 1.0, 0.0).astype(jnp.bfloat16)


def band_of_second(k2_ref, k2t_ref):
    channels_mid, channels_out = k2_ref.shape[3:]
    empty = jnp.zeros((channels_mid, channels_out), jnp.bfloat16)
    for ad in range(3):
        for aw in range(3):
            tap = [k2_ref[ad, ah, aw] for ah in range(3)]
            band = ((tap[1], empty), (tap[2], tap[0]), (empty, tap[1]), (empty, tap[2]))
            start = (ad * 3 + aw) * 2 * channels_out
            for hh in range(4):
                k2t_ref[hh * channels_mid:(hh + 1) * channels_mid, start:start + 2 * channels_out] = (
                    jnp.concatenate(band[hh], axis=1))


def upsampling(ad, aw, beyond=0):
    row, col = iota((128, 512), 0), iota((128, 512), 1)
    target = ((row >> 5) << 7) + ((row & 31) << 1) + (64 * (ad - 1) + aw - 1 + 128 * beyond)
    keep = col == target
    if aw == 0:
        keep = keep & ((row & 31) > 0)
    return ones_where(keep)


def prepare_kernel(k1_ref, k2_ref, og_ref, pick_ref, k1t_ref, ogt_ref, ag_ref, k2t_ref, ogu_ref):
    channels_in, channels_mid = k1_ref.shape[3:]
    row, col = iota((2 * WIDTH, 2 * 64), 0), iota((2 * WIDTH, 2 * 64), 1)
    for aw in range(3):
        same = (row >> 7) == (col >> 6)
        tap = (row & 127) == 2 * (col & 63) + aw - 1
        pick_ref[:, aw * 128:(aw + 1) * 128] = ones_where(same & tap)
    shape = (9 * channels_in, channels_in * 2 * HEIGHT)
    row, col = iota(shape, 0), iota(shape, 1)
    tap = row >> 4
    ad = jnp.where(tap >= 6, 2, jnp.where(tap >= 3, 1, 0))
    ah, i = tap - 3 * ad, row & 15
    same = i == col >> 4
    h, d = (col >> 1) & 7, col & 1
    taps = []
    for aw in range(3):
        parts = [k1_ref[a, b, aw] for a in range(3) for b in range(3)]
        taps.append(jnp.concatenate(parts, axis=0).astype(jnp.float32).T.astype(jnp.bfloat16))
    for following in range(2):
        plane = (ad == 0) & (d == 1) if following else (ad == d + 1)
        for hh in range(4):
            place = ones_where(same & plane & (h == 2 * hh + ah - 1))
            start = (following * 4 + hh) * channels_mid
            for aw in range(3):
                block = dot(taps[aw], place).astype(jnp.bfloat16)
                k1t_ref[start:start + channels_mid, aw * shape[1]:(aw + 1) * shape[1]] = block
    band_of_second(k2_ref, k2t_ref)
    groups = og_ref.shape[1] // 128
    for ad in range(3):
        for aw in range(3):
            t = ad * 3 + aw
            up = upsampling(ad, aw)
            for g in range(groups):
                value = dot(og_ref[:, g * 128:(g + 1) * 128], up)
                if ad == 0 and g + 1 < groups:
                    value = value + dot(og_ref[:, (g + 1) * 128:(g + 2) * 128], upsampling(ad, aw, 4))
                ogu_ref[t * 128:(t + 1) * 128, g * 512:(g + 1) * 512] = value.astype(jnp.bfloat16)
                ogt_ref[g * 512:(g + 1) * 512, t * 128:(t + 1) * 128] = value.T.astype(jnp.bfloat16)
    for g in range(groups):
        lanes = slice(g * 512, (g + 1) * 512)
        ag_ref[:, lanes] = dot(k2t_ref[...], ogu_ref[:, lanes]).astype(jnp.bfloat16)


def layer_kernel(source_ref, *refs):
    cells = refs[-6].shape[1]
    blocks = cells // 64
    pick_ref, k1t_ref, ogt_ref, ag_ref, act_ref, terms_ref, y_scr, pg_scr, x_ref = refs[blocks:]
    rows = 256
    for place in range(blocks):
        source = source_ref[place]
        x_ref[pl.ds(pl.multiple_of(source * rows, rows), rows), :] = refs[place][...]
    for q in range(cells // 128):
        start = q * 2 * rows
        pair = jnp.concatenate([x_ref[start:start + rows, :], x_ref[start + rows:start + 2 * rows, :]], axis=1)
        y = dot(pair, pick_ref[...]).astype(jnp.bfloat16)
        for aw in range(3):
            y_scr[aw * rows:(aw + 1) * rows, q * 128:(q + 1) * 128] = y[:, aw * 128:(aw + 1) * 128]
    both = dot(k1t_ref[...], y_scr[...])
    lane = iota((128, cells), 1)
    from_last = jnp.where(lane < 64, 0.0, pltpu.roll(both[128:], 64, 1))
    pre = both[:128] + from_last
    sigma = jax.nn.sigmoid(pre)
    act = (pre * sigma).astype(jnp.bfloat16)
    act_ref[...] = act
    slope = sigma * (1.0 + pre * (1.0 - sigma))
    grad = (ag_ref[...].astype(jnp.float32) * slope).astype(jnp.bfloat16)
    pg_scr[:128, :] = grad
    to_last = pltpu.roll(grad.astype(jnp.float32), cells - 64, 1)
    pg_scr[128:, :] = jnp.where(lane < cells - 64, to_last, 0.0).astype(jnp.bfloat16)

    second = dot(act, ogt_ref[...])
    lane = iota((32, 128), 1)
    held = None
    for t in range(9):
        tile = second[:, t * 128:(t + 1) * 128]
        turned = pltpu.roll(tile, 64, 1)
        mixed = jnp.where(lane < 64, tile[0:32] + turned[64:96], turned[32:64] + tile[96:128])
        terms_ref[t * 32:(t + 1) * 32, :] = mixed.astype(jnp.bfloat16)
        if t % 2 == 0:
            held = jnp.where(lane < 64, turned[32:64], 0.0)
        else:
            held = jnp.where(lane < 64, held, tile[32:64])
        if t % 2 == 1:
            start = 288 + (t // 2) * 32
            terms_ref[start:start + 32, :] = held.astype(jnp.bfloat16)
    terms_ref[416:432, :] = jnp.where(lane[:16] < 64, held[:16], pltpu.roll(held[16:], 64, 1)).astype(jnp.bfloat16)

    first = dot(y_scr[...], pg_scr[...], ((1,), (1,))).astype(jnp.bfloat16)
    shape = (rows, 256)
    h, hh = (iota(shape, 0) >> 1) & 7, (iota(shape, 1) >> 5) & 3
    even, odd = ones_where((h >> 1) == hh), ones_where(((h & 1) == 1) & ((h + 1) >> 1 == hh))
    rank, index = iota((64, rows), 0), iota((64, rows), 1)
    same = ((rank & 15) == index >> 4) & (((rank >> 4) & 1) == (index & 1))
    later_taps = ones_where(same & ((rank >> 5) == ((index >> 1) & 1)))
    first_tap = ones_where(same[:32] & (((index[:32] >> 1) & 1) == 1))
    lane = iota((16, 128), 1)
    for aw in range(3):
        tile = first[aw * rows:(aw + 1) * rows]
        total = jnp.concatenate([dot(first_tap, tile * odd), dot(later_taps, tile * even)], axis=0)
        start = 432 + aw * 48
        for ad in range(3):
            side = slice(128, 256) if ad == 0 else slice(0, 128)
            d = 0 if ad == 1 else 1
            packed = None
            for ah in range(3):
                part = total[ah * 32 + d * 16:ah * 32 + d * 16 + 16, side]
                part = part + pltpu.roll(part, 64, 1)
                part = part + pltpu.roll(part, 32, 1)
                packed = part if packed is None else jnp.where(lane >= ah * 32, part, packed)
            terms_ref[start + ad * 16:start + (ad + 1) * 16, :] = packed.astype(jnp.bfloat16)
    rest = terms_ref.shape[0] - TERM_ROWS
    if rest > 0:
        terms_ref[TERM_ROWS:, :] = jnp.zeros((rest, 128), jnp.bfloat16)


def features_kernel(act_ref, k2_ref, out_ref, k2t_ref):
    band_of_second(k2_ref, k2t_ref)
    groups = out_ref.shape[1] // 128
    for g in range(groups):
        total = jnp.zeros((128, 128), jnp.float32)
        for t in range(9):
            taken = dot(act_ref[:, g * 512:(g + 1) * 512], upsampling(t // 3, t % 3), ((1,), (1,)))
            if t < 3 and g > 0:
                last = act_ref[:, (g - 1) * 512:g * 512]
                taken = taken + dot(last, upsampling(0, t, 4), ((1,), (1,)))
            band = k2t_ref[:, t * 128:(t + 1) * 128]
            total = total + dot(band, taken.astype(jnp.bfloat16), ((0,), (0,)))
        out_ref[:, g * 128:(g + 1) * 128] = total.astype(jnp.bfloat16)


def add_kernel(rows, mine_ref, out_ref):
    count = mine_ref.shape[0]
    unit = rows * 16 // math.gcd(rows, 16)
    total = mine_ref[0:unit, :].astype(jnp.float32)
    for start in range(unit, count, unit):
        total = total + mine_ref[start:start + unit, :].astype(jnp.float32)
    if unit % (2 * rows) == 0 and (unit // 2) % 8 == 0:
        total = total[:unit // 2] + total[unit // 2:]
    parts = [total[start:start + rows] for start in range(0, total.shape[0], rows)]
    total = functools.reduce(jnp.add, parts)
    spread = jnp.concatenate([total] * (unit // rows), axis=0).astype(jnp.bfloat16)
    for start in range(0, count, unit):
        out_ref[start:start + unit, :] = spread


def unpack_kernel(whole_ref, first_ref, second_ref, first_scr, second_scr, sems):
    copies = []
    for ad in range(3):
        for aw in range(3):
            t = ad * 3 + aw
            pair = whole_ref[t * 32:(t + 1) * 32, :].astype(jnp.float32)
            second_scr[ad, 1, aw] = pair[:, :64]
            second_scr[ad, 2, aw] = pair[:, 64:]
            if t == 8:
                lone = whole_ref[416:432, :].astype(jnp.float32)
                second_scr[ad, 0, aw] = jnp.concatenate([lone[:, :64], lone[:, 64:]], axis=0)
            else:
                start = 288 + (t // 2) * 32
                lone = whole_ref[start:start + 32, :].astype(jnp.float32)
                second_scr[ad, 0, aw] = lone[:, :64] if t % 2 == 0 else lone[:, 64:]
        copies.append(pltpu.make_async_copy(second_scr.at[ad], second_ref.at[ad], sems.at[0, ad]))
        copies[-1].start()
    for ad in range(3):
        for aw in range(3):
            start = 432 + aw * 48 + ad * 16
            tile = whole_ref[start:start + 16, :].astype(jnp.float32)
            for ah in range(3):
                first_scr[ad, ah, aw] = tile[:, ah * 32:(ah + 1) * 32]
        copies.append(pltpu.make_async_copy(first_scr.at[ad], first_ref.at[ad], sems.at[1, ad]))
        copies[-1].start()
    for copy in copies:
        copy.wait()


def call(kernel, outs, args, scratch=(), flops=0):
    whole = pl.BlockSpec(memory_space=pltpu.VMEM)
    scalar = pl.BlockSpec(memory_space=pltpu.SMEM)
    size = sum(a.size * a.dtype.itemsize for a in list(args) + list(outs))
    return pl.pallas_call(
        kernel,
        out_shape=tuple(outs),
        in_specs=[scalar if a.dtype == jnp.int32 else whole for a in args],
        out_specs=(whole,) * len(outs),
        scratch_shapes=list(scratch),
        compiler_params=pltpu.CompilerParams(vmem_limit_bytes=VMEM_BYTES),
        cost_estimate=pl.CostEstimate(flops=flops, bytes_accessed=size, transcendentals=0),
    )(*args)


def array(shape, dtype=jnp.bfloat16):
    return jax.ShapeDtypeStruct(shape, dtype)


def by_tap(kernel):
    return jnp.transpose(kernel, (2, 3, 4, 1, 0))


def prepare(k1, k2, out_grad):
    c0, c1 = k1.shape[3:]
    c2 = k2.shape[4]
    planes = out_grad.shape[2]
    cells = planes * 2 * 64
    og = out_grad.reshape(c2, planes, 2, 32).transpose(2, 0, 1, 3).reshape(2 * c2, planes * 32)
    outs = [
        array((256, 384)),
        array((2 * 4 * c1, 3 * c0 * 16)),
        array((cells, 9 * 2 * c2)),
        array((4 * c1, cells)),
    ]
    scratch = [pltpu.VMEM((4 * c1, 9 * 2 * c2), jnp.bfloat16), pltpu.VMEM((9 * 2 * c2, cells), jnp.bfloat16)]
    return call(prepare_kernel, outs, (k1, k2, og), scratch, flops=2 * 128 * 1152 * cells * 2)


def body(crops, first_kernel, second_kernel, out_grad):
    axes = ("space", "sample")
    devices = lax.axis_size(axes)
    channels_out, planes = out_grad.shape[1:3]
    space = lax.axis_size("space")
    assert space & (space - 1) == 0
    position = lax.axis_index("space").astype(jnp.int32)
    across, near = range(space - 1, space // 2 - 1, -1), range(1, space // 2)
    order = [two for pair in zip(across, near) for two in (pair, pair[::-1])] + [(space // 2, space // 2)]
    early, late = order[:space // 2], order[space // 2:]
    steps = [(0, 0)] + late[::-1] + early
    samples = lax.axis_size("sample")
    second_core = lax.axis_index("sample") % 2 == 1
    sources = {step: position ^ jnp.where(second_core, step[1], step[0]).astype(jnp.int32) for step in steps}
    k1, k2 = by_tap(first_kernel), by_tap(second_kernel)
    x = []
    cut = [lax.dynamic_index_in_dim(crops, sources[step], 0, keepdims=False) for step in early]
    rest, cut = lax.optimization_barrier((crops, cut))
    for step in steps:
        if step in early:
            block = cut[early.index(step)]
        else:
            block = lax.dynamic_index_in_dim(rest, sources[step], 0, keepdims=False)
        if step[0] > 0:
            pairs = [
                (source * samples + n, (source ^ step[n % 2]) * samples + n)
                for source in range(space) for n in range(samples)
            ]
            block = lax.ppermute(block, axes, pairs)
        channels_in, two, flat_cells = block.shape
        block = block.reshape(channels_in, two, HEIGHT, WIDTH).transpose(0, 2, 1, 3)
        x.append(block.reshape(channels_in * two * HEIGHT, WIDTH))
    pick, k1t, ogt, act_grad = prepare(k1, k2, out_grad)
    cells = act_grad.shape[1]
    rows = -(-TERM_ROWS // (devices * 2)) * 2
    act, terms = call(
        layer_kernel,
        [array((128, cells)), array((devices * rows, LANES))],
        (jnp.stack([sources[step] for step in steps]), *x, pick, k1t, ogt, act_grad),
        scratch=[pltpu.VMEM((768, cells), jnp.bfloat16), pltpu.VMEM((256, cells), jnp.bfloat16), pltpu.VMEM((4 * cells, 128), jnp.bfloat16)],
        flops=2 * 128 * 4096 * cells,
    )
    blocks = terms.reshape(devices, rows // 2, 2, LANES)
    mine = lax.all_to_all(blocks, axes, split_axis=0, concat_axis=0, tiled=True)
    (features,) = call(
        features_kernel,
        [array((2 * channels_out, planes * 32))],
        (act, k2),
        scratch=[pltpu.VMEM((128, 1152), jnp.bfloat16)],
        flops=2 * 128 * 1152 * cells,
    )
    features = features.reshape(2, channels_out, planes, 32).transpose(1, 2, 0, 3).reshape(out_grad.shape)
    add = functools.partial(add_kernel, rows)
    (spread,) = call(add, [array(terms.shape)], (mine.reshape(terms.shape),))
    spread = spread.reshape(blocks.shape)
    whole = lax.all_to_all(spread, axes, split_axis=0, concat_axis=0, tiled=True)
    shapes = [(3, 3, 3) + kernel.shape[1::-1] for kernel in (first_kernel, second_kernel)]
    first, second = pl.pallas_call(
        unpack_kernel,
        out_shape=[array(shape, jnp.float32) for shape in shapes],
        in_specs=[pl.BlockSpec(memory_space=pltpu.VMEM)],
        out_specs=[pl.BlockSpec(memory_space=pl.ANY)] * 2,
        scratch_shapes=[pltpu.VMEM(shape, jnp.float32) for shape in shapes] + [pltpu.SemaphoreType.DMA((2, 3))],
        compiler_params=pltpu.CompilerParams(vmem_limit_bytes=VMEM_BYTES),
    )(whole.reshape(terms.shape))
    return (features, jnp.transpose(first, (4, 3, 0, 1, 2)), jnp.transpose(second, (4, 3, 0, 1, 2)))


def solution(mesh):
    placed = (P("sample", None, "space", None), P(), P(), P(("sample", "space"), None, None, None))
    return jax.shard_map(
        body,
        mesh=mesh,
        in_specs=placed,
        out_specs=(P(("sample", "space"), None, None, None), P(), P()),
        check_vma=False,
    )
```

```python
import functools
import math

import jax
import jax.numpy as jnp
from jax import lax
from jax.experimental import pallas as pl
from jax.experimental.pallas import tpu as pltpu
from jax.sharding import PartitionSpec as P

HEIGHT = 8
WIDTH = 128
LANES = 128
VMEM_BYTES = 16 * 1024 * 1024
TERM_ROWS = 576


def iota(shape, dim):
    return lax.broadcasted_iota(jnp.int32, shape, dim)


def dot(left, right, dims=((1,), (0,))):
    return lax.dot_general(left, right, (dims, ((), ())), preferred_element_type=jnp.float32)


def ones_where(mask):
    return jnp.where(mask, 1.0, 0.0).astype(jnp.bfloat16)


def band_of_second(k2_ref, k2t_ref):
    channels_mid, channels_out = k2_ref.shape[3:]
    empty = jnp.zeros((channels_mid, channels_out), jnp.bfloat16)
    for ad in range(3):
        for aw in range(3):
            tap = [k2_ref[ad, ah, aw] for ah in range(3)]
            band = ((tap[1], empty), (tap[2], tap[0]), (empty, tap[1]), (empty, tap[2]))
            start = (ad * 3 + aw) * 2 * channels_out
            for hh in range(4):
                k2t_ref[hh * channels_mid:(hh + 1) * channels_mid, start:start + 2 * channels_out] = (
                    jnp.concatenate(band[hh], axis=1))


def upsampling(ad, aw, beyond=0):
    row, col = iota((128, 512), 0), iota((128, 512), 1)
    target = ((row >> 5) << 7) + ((row & 31) << 1) + (64 * (ad - 1) + aw - 1 + 128 * beyond)
    keep = col == target
    if aw == 0:
        keep = keep & ((row & 31) > 0)
    return ones_where(keep)


def prepare_kernel(k1_ref, k2_ref, og_ref, pick_ref, k1t_ref, ogt_ref, ag_ref, k2t_ref, ogu_ref):
    channels_in, channels_mid = k1_ref.shape[3:]
    row, col = iota((2 * WIDTH, 2 * 64), 0), iota((2 * WIDTH, 2 * 64), 1)
    for aw in range(3):
        same = (row >> 7) == (col >> 6)
        tap = (row & 127) == 2 * (col & 63) + aw - 1
        pick_ref[:, aw * 128:(aw + 1) * 128] = ones_where(same & tap)
    shape = (9 * channels_in, channels_in * 2 * HEIGHT)
    row, col = iota(shape, 0), iota(shape, 1)
    tap = row >> 4
    ad = jnp.where(tap >= 6, 2, jnp.where(tap >= 3, 1, 0))
    ah, i = tap - 3 * ad, row & 15
    same = i == col >> 4
    h, d = (col >> 1) & 7, col & 1
    taps = []
    for aw in range(3):
        parts = [k1_ref[a, b, aw] for a in range(3) for b in range(3)]
        taps.append(jnp.concatenate(parts, axis=0).astype(jnp.float32).T.astype(jnp.bfloat16))
    for following in range(2):
        plane = (ad == 0) & (d == 1) if following else (ad == d + 1)
        for hh in range(4):
            place = ones_where(same & plane & (h == 2 * hh + ah - 1))
            start = (following * 4 + hh) * channels_mid
            for aw in range(3):
                block = dot(taps[aw], place).astype(jnp.bfloat16)
                k1t_ref[start:start + channels_mid, aw * shape[1]:(aw + 1) * shape[1]] = block
    band_of_second(k2_ref, k2t_ref)
    groups = og_ref.shape[1] // 128
    for ad in range(3):
        for aw in range(3):
            t = ad * 3 + aw
            up = upsampling(ad, aw)
            for g in range(groups):
                value = dot(og_ref[:, g * 128:(g + 1) * 128], up)
                if ad == 0 and g + 1 < groups:
                    value = value + dot(og_ref[:, (g + 1) * 128:(g + 2) * 128], upsampling(ad, aw, 4))
                ogu_ref[t * 128:(t + 1) * 128, g * 512:(g + 1) * 512] = value.astype(jnp.bfloat16)
                ogt_ref[g * 512:(g + 1) * 512, t * 128:(t + 1) * 128] = value.T.astype(jnp.bfloat16)
    for g in range(groups):
        lanes = slice(g * 512, (g + 1) * 512)
        ag_ref[:, lanes] = dot(k2t_ref[...], ogu_ref[:, lanes]).astype(jnp.bfloat16)


def layer_kernel(steps, *refs):
    cells = refs[-6].shape[1]
    blocks = cells // 64
    pick_ref, k1t_ref, ogt_ref, ag_ref, act_ref, terms_ref, y_scr, pg_scr, x_ref = refs[blocks:]
    rows = 256
    position = lax.axis_index("space")
    for place, step in enumerate(steps):
        source = lax.bitwise_xor(position, jnp.int32(step))
        x_ref[pl.ds(pl.multiple_of(source * rows, rows), rows), :] = refs[place][...]
    for q in range(cells // 128):
        start = q * 2 * rows
        pair = jnp.concatenate([x_ref[start:start + rows, :], x_ref[start + rows:start + 2 * rows, :]], axis=1)
        y = dot(pair, pick_ref[...]).astype(jnp.bfloat16)
        for aw in range(3):
            y_scr[aw * rows:(aw + 1) * rows, q * 128:(q + 1) * 128] = y[:, aw * 128:(aw + 1) * 128]
    both = dot(k1t_ref[...], y_scr[...])
    lane = iota((128, cells), 1)
    from_last = jnp.where(lane < 64, 0.0, pltpu.roll(both[128:], 64, 1))
    pre = both[:128] + from_last
    sigma = jax.nn.sigmoid(pre)
    act = (pre * sigma).astype(jnp.bfloat16)
    act_ref[...] = act
    slope = sigma * (1.0 + pre * (1.0 - sigma))
    grad = (ag_ref[...].astype(jnp.float32) * slope).astype(jnp.bfloat16)
    pg_scr[:128, :] = grad
    to_last = pltpu.roll(grad.astype(jnp.float32), cells - 64, 1)
    pg_scr[128:, :] = jnp.where(lane < cells - 64, to_last, 0.0).astype(jnp.bfloat16)

    second = dot(act, ogt_ref[...])
    lane = iota((32, 128), 1)
    held = None
    for t in range(9):
        tile = second[:, t * 128:(t + 1) * 128]
        turned = pltpu.roll(tile, 64, 1)
        mixed = jnp.where(lane < 64, tile[0:32] + turned[64:96], turned[32:64] + tile[96:128])
        terms_ref[t * 32:(t + 1) * 32, :] = mixed.astype(jnp.bfloat16)
        if t % 2 == 0:
            held = jnp.where(lane < 64, turned[32:64], 0.0)
        else:
            held = jnp.where(lane < 64, held, tile[32:64])
        if t % 2 == 1:
            start = 288 + (t // 2) * 32
            terms_ref[start:start + 32, :] = held.astype(jnp.bfloat16)
    terms_ref[416:432, :] = jnp.where(lane[:16] < 64, held[:16], pltpu.roll(held[16:], 64, 1)).astype(jnp.bfloat16)

    first = dot(y_scr[...], pg_scr[...], ((1,), (1,))).astype(jnp.bfloat16)
    shape = (rows, 256)
    h, hh = (iota(shape, 0) >> 1) & 7, (iota(shape, 1) >> 5) & 3
    even, odd = ones_where((h >> 1) == hh), ones_where(((h & 1) == 1) & ((h + 1) >> 1 == hh))
    rank, index = iota((64, rows), 0), iota((64, rows), 1)
    same = ((rank & 15) == index >> 4) & (((rank >> 4) & 1) == (index & 1))
    later_taps = ones_where(same & ((rank >> 5) == ((index >> 1) & 1)))
    first_tap = ones_where(same[:32] & (((index[:32] >> 1) & 1) == 1))
    lane = iota((16, 128), 1)
    for aw in range(3):
        tile = first[aw * rows:(aw + 1) * rows]
        total = jnp.concatenate([dot(first_tap, tile * odd), dot(later_taps, tile * even)], axis=0)
        start = 432 + aw * 48
        for ad in range(3):
            side = slice(128, 256) if ad == 0 else slice(0, 128)
            d = 0 if ad == 1 else 1
            packed = None
            for ah in range(3):
                part = total[ah * 32 + d * 16:ah * 32 + d * 16 + 16, side]
                part = part + pltpu.roll(part, 64, 1)
                part = part + pltpu.roll(part, 32, 1)
                packed = part if packed is None else jnp.where(lane >= ah * 32, part, packed)
            terms_ref[start + ad * 16:start + (ad + 1) * 16, :] = packed.astype(jnp.bfloat16)
    rest = terms_ref.shape[0] - TERM_ROWS
    if rest > 0:
        terms_ref[TERM_ROWS:, :] = jnp.zeros((rest, 128), jnp.bfloat16)


def features_kernel(act_ref, k2_ref, out_ref, k2t_ref):
    band_of_second(k2_ref, k2t_ref)
    groups = out_ref.shape[1] // 128
    for g in range(groups):
        total = jnp.zeros((128, 128), jnp.float32)
        for t in range(9):
            taken = dot(act_ref[:, g * 512:(g + 1) * 512], upsampling(t // 3, t % 3), ((1,), (1,)))
            if t < 3 and g > 0:
                last = act_ref[:, (g - 1) * 512:g * 512]
                taken = taken + dot(last, upsampling(0, t, 4), ((1,), (1,)))
            band = k2t_ref[:, t * 128:(t + 1) * 128]
            total = total + dot(band, taken.astype(jnp.bfloat16), ((0,), (0,)))
        out_ref[:, g * 128:(g + 1) * 128] = total.astype(jnp.bfloat16)


def add_kernel(rows, mine_ref, out_ref):
    count = mine_ref.shape[0]
    unit = rows * 16 // math.gcd(rows, 16)
    total = mine_ref[0:unit, :].astype(jnp.float32)
    for start in range(unit, count, unit):
        total = total + mine_ref[start:start + unit, :].astype(jnp.float32)
    apart = (iota((unit, unit), 0) - iota((unit, unit), 1)).astype(jnp.float32)
    same = ones_where(jnp.round(apart * (1.0 / rows)) * rows == apart)
    high = total.astype(jnp.bfloat16)
    low = (total - high.astype(jnp.float32)).astype(jnp.bfloat16)
    spread = (dot(same, high) + dot(same, low)).astype(jnp.bfloat16)
    for start in range(0, count, unit):
        out_ref[start:start + unit, :] = spread


def unpack_kernel(whole_ref, first_ref, second_ref, first_scr, second_scr, sems):
    copies = []
    for ad in range(3):
        for aw in range(3):
            t = ad * 3 + aw
            pair = whole_ref[t * 32:(t + 1) * 32, :].astype(jnp.float32)
            second_scr[ad, 1, aw] = pair[:, :64]
            second_scr[ad, 2, aw] = pair[:, 64:]
            if t == 8:
                lone = whole_ref[416:432, :].astype(jnp.float32)
                second_scr[ad, 0, aw] = jnp.concatenate([lone[:, :64], lone[:, 64:]], axis=0)
            else:
                start = 288 + (t // 2) * 32
                lone = whole_ref[start:start + 32, :].astype(jnp.float32)
                second_scr[ad, 0, aw] = lone[:, :64] if t % 2 == 0 else lone[:, 64:]
        copies.append(pltpu.make_async_copy(second_scr.at[ad], second_ref.at[ad], sems.at[0, ad]))
        copies[-1].start()
    for ad in range(3):
        for aw in range(3):
            start = 432 + aw * 48 + ad * 16
            tile = whole_ref[start:start + 16, :].astype(jnp.float32)
            for ah in range(3):
                first_scr[ad, ah, aw] = tile[:, ah * 32:(ah + 1) * 32]
        copies.append(pltpu.make_async_copy(first_scr.at[ad], first_ref.at[ad], sems.at[1, ad]))
        copies[-1].start()
    for copy in copies:
        copy.wait()


def call(kernel, outs, args, scratch=(), flops=0):
    whole = pl.BlockSpec(memory_space=pltpu.VMEM)
    scalar = pl.BlockSpec(memory_space=pltpu.SMEM)
    size = sum(a.size * a.dtype.itemsize for a in list(args) + list(outs))
    return pl.pallas_call(
        kernel,
        out_shape=tuple(outs),
        in_specs=[scalar if a.dtype == jnp.int32 else whole for a in args],
        out_specs=(whole,) * len(outs),
        scratch_shapes=list(scratch),
        compiler_params=pltpu.CompilerParams(vmem_limit_bytes=VMEM_BYTES),
        cost_estimate=pl.CostEstimate(flops=flops, bytes_accessed=size, transcendentals=0),
    )(*args)


def array(shape, dtype=jnp.bfloat16):
    return jax.ShapeDtypeStruct(shape, dtype)


def by_tap(kernel):
    return jnp.transpose(kernel, (2, 3, 4, 1, 0))


def prepare(k1, k2, out_grad):
    c0, c1 = k1.shape[3:]
    c2 = k2.shape[4]
    planes = out_grad.shape[2]
    cells = planes * 2 * 64
    og = out_grad.reshape(c2, planes, 2, 32).transpose(2, 0, 1, 3).reshape(2 * c2, planes * 32)
    outs = [
        array((256, 384)),
        array((2 * 4 * c1, 3 * c0 * 16)),
        array((cells, 9 * 2 * c2)),
        array((4 * c1, cells)),
    ]
    scratch = [pltpu.VMEM((4 * c1, 9 * 2 * c2), jnp.bfloat16), pltpu.VMEM((9 * 2 * c2, cells), jnp.bfloat16)]
    return call(prepare_kernel, outs, (k1, k2, og), scratch, flops=2 * 128 * 1152 * cells * 2)


def body(crops, first_kernel, second_kernel, out_grad):
    axes = ("space", "sample")
    devices = lax.axis_size(axes)
    channels_out, planes = out_grad.shape[1:3]
    space = lax.axis_size("space")
    assert space & (space - 1) == 0
    position = lax.axis_index("space").astype(jnp.int32)
    across, near = range(space - 1, space // 2 - 1, -1), range(1, space // 2)
    order = [step for two in zip(across, near) for step in two] + [space // 2]
    early, late = order[:space // 2], order[space // 2:]
    steps = [0] + late[::-1] + early
    k1, k2 = by_tap(first_kernel), by_tap(second_kernel)
    x = []
    cut = [lax.dynamic_index_in_dim(crops, position ^ step, 0, keepdims=False) for step in early]
    rest, cut = lax.optimization_barrier((crops, cut))
    for step in steps:
        if step in early:
            block = cut[early.index(step)]
        else:
            block = lax.dynamic_index_in_dim(rest, position ^ step, 0, keepdims=False)
        if step > 0:
            block = lax.ppermute(block, "space", [(source, source ^ step) for source in range(space)])
        channels_in, two, flat_cells = block.shape
        block = block.reshape(channels_in, two, HEIGHT, WIDTH).transpose(0, 2, 1, 3)
        x.append(block.reshape(channels_in * two * HEIGHT, WIDTH))
    pick, k1t, ogt, act_grad = prepare(k1, k2, out_grad)
    cells = act_grad.shape[1]
    rows = -(-TERM_ROWS // (devices * 2)) * 2
    act, terms = call(
        functools.partial(layer_kernel, steps),
        [array((128, cells)), array((devices * rows, LANES))],
        (*x, pick, k1t, ogt, act_grad),
        scratch=[pltpu.VMEM((768, cells), jnp.bfloat16), pltpu.VMEM((256, cells), jnp.bfloat16), pltpu.VMEM((4 * cells, 128), jnp.bfloat16)],
        flops=2 * 128 * 4096 * cells,
    )
    blocks = terms.reshape(devices, rows // 2, 2, LANES)
    mine = lax.all_to_all(blocks, axes, split_axis=0, concat_axis=0, tiled=True)
    (features,) = call(
        features_kernel,
        [array((2 * channels_out, planes * 32))],
        (act, k2),
        scratch=[pltpu.VMEM((128, 1152), jnp.bfloat16)],
        flops=2 * 128 * 1152 * cells,
    )
    features = features.reshape(2, channels_out, planes, 32).transpose(1, 2, 0, 3).reshape(out_grad.shape)
    add = functools.partial(add_kernel, rows)
    (spread,) = call(add, [array(terms.shape)], (mine.reshape(terms.shape),))
    spread = spread.reshape(blocks.shape)
    whole = lax.all_to_all(spread, axes, split_axis=0, concat_axis=0, tiled=True)
    shapes = [(3, 3, 3) + kernel.shape[1::-1] for kernel in (first_kernel, second_kernel)]
    first, second = pl.pallas_call(
        unpack_kernel,
        out_shape=[array(shape, jnp.float32) for shape in shapes],
        in_specs=[pl.BlockSpec(memory_space=pltpu.VMEM)],
        out_specs=[pl.BlockSpec(memory_space=pl.ANY)] * 2,
        scratch_shapes=[pltpu.VMEM(shape, jnp.float32) for shape in shapes] + [pltpu.SemaphoreType.DMA((2, 3))],
        compiler_params=pltpu.CompilerParams(vmem_limit_bytes=VMEM_BYTES),
    )(whole.reshape(terms.shape))
    return (features, jnp.transpose(first, (4, 3, 0, 1, 2)), jnp.transpose(second, (4, 3, 0, 1, 2)))


def solution(mesh):
    placed = (P("sample", None, "space", None), P(), P(), P(("sample", "space"), None, None, None))
    return jax.shard_map(
        body,
        mesh=mesh,
        in_specs=placed,
        out_specs=(P(("sample", "space"), None, None, None), P(), P()),
        check_vma=False,
    )
```

```python
import functools
import math

import jax
import jax.numpy as jnp
from jax import lax
from jax.experimental import pallas as pl
from jax.experimental.pallas import tpu as pltpu
from jax.sharding import PartitionSpec as P

HEIGHT = 8
WIDTH = 128
LANES = 128
VMEM_BYTES = 16 * 1024 * 1024
TERM_ROWS = 576


def iota(shape, dim):
    return lax.broadcasted_iota(jnp.int32, shape, dim)


def dot(left, right, dims=((1,), (0,))):
    return lax.dot_general(left, right, (dims, ((), ())), preferred_element_type=jnp.float32)


def ones_where(mask):
    return jnp.where(mask, 1.0, 0.0).astype(jnp.bfloat16)


def band_of_second(k2_ref, k2t_ref):
    channels_mid, channels_out = k2_ref.shape[3:]
    empty = jnp.zeros((channels_mid, channels_out), jnp.bfloat16)
    for ad in range(3):
        for aw in range(3):
            tap = [k2_ref[ad, ah, aw] for ah in range(3)]
            band = ((tap[1], empty), (tap[2], tap[0]), (empty, tap[1]), (empty, tap[2]))
            start = (ad * 3 + aw) * 2 * channels_out
            for hh in range(4):
                k2t_ref[hh * channels_mid:(hh + 1) * channels_mid, start:start + 2 * channels_out] = (
                    jnp.concatenate(band[hh], axis=1))


def upsampling(ad, aw, beyond=0):
    row, col = iota((128, 512), 0), iota((128, 512), 1)
    target = ((row >> 5) << 7) + ((row & 31) << 1) + (64 * (ad - 1) + aw - 1 + 128 * beyond)
    keep = col == target
    if aw == 0:
        keep = keep & ((row & 31) > 0)
    return ones_where(keep)


def prepare_kernel(k1_ref, k2_ref, og_ref, pick_ref, k1t_ref, ogt_ref, ag_ref, k2t_ref, ogu_ref):
    channels_in, channels_mid = k1_ref.shape[3:]
    row, col = iota((3 * WIDTH, 2 * 64), 0), iota((3 * WIDTH, 2 * 64), 1)
    for aw in range(3):
        same = ((row >> 7) & 1) == (col >> 6)
        tap = (row & 127) == 2 * (col & 63) + aw - 1
        pick_ref[:, aw * 128:(aw + 1) * 128] = ones_where(same & tap)
    shape = (9 * channels_in, channels_in * 2 * HEIGHT)
    row, col = iota(shape, 0), iota(shape, 1)
    tap = row >> 4
    ad = jnp.where(tap >= 6, 2, jnp.where(tap >= 3, 1, 0))
    ah, i = tap - 3 * ad, row & 15
    same = i == col >> 4
    h, d = (col >> 1) & 7, col & 1
    taps = []
    for aw in range(3):
        parts = [k1_ref[a, b, aw] for a in range(3) for b in range(3)]
        taps.append(jnp.concatenate(parts, axis=0).astype(jnp.float32).T.astype(jnp.bfloat16))
    for following in range(2):
        plane = (ad == 0) & (d == 1) if following else (ad == d + 1)
        for hh in range(4):
            place = ones_where(same & plane & (h == 2 * hh + ah - 1))
            start = (following * 4 + hh) * channels_mid
            for aw in range(3):
                block = dot(taps[aw], place).astype(jnp.bfloat16)
                k1t_ref[start:start + channels_mid, aw * shape[1]:(aw + 1) * shape[1]] = block
    band_of_second(k2_ref, k2t_ref)
    groups = og_ref.shape[1] // 128
    for ad in range(3):
        for aw in range(3):
            t = ad * 3 + aw
            up = upsampling(ad, aw)
            for g in range(groups):
                value = dot(og_ref[:, g * 128:(g + 1) * 128], up)
                if ad == 0 and g + 1 < groups:
                    value = value + dot(og_ref[:, (g + 1) * 128:(g + 2) * 128], upsampling(ad, aw, 4))
                ogu_ref[t * 128:(t + 1) * 128, g * 512:(g + 1) * 512] = value.astype(jnp.bfloat16)
                ogt_ref[g * 512:(g + 1) * 512, t * 128:(t + 1) * 128] = value.T.astype(jnp.bfloat16)
    for g in range(groups):
        lanes = slice(g * 512, (g + 1) * 512)
        ag_ref[:, lanes] = dot(k2t_ref[...], ogu_ref[:, lanes]).astype(jnp.bfloat16)


def taps_of_pair(first_ref, second_ref, pick_ref):
    parity = lax.axis_index("space") & 1
    pick = pick_ref[pl.ds(pl.multiple_of(parity * WIDTH, WIDTH), 2 * WIDTH), :]
    pair = jnp.concatenate([first_ref[...], second_ref[...]], axis=1)
    return dot(pair, pick).astype(jnp.bfloat16)


def taps_kernel(pairs, given, *refs):
    pick_ref, out_ref = refs[-2:]
    for place, m in enumerate(pairs):
        y = taps_of_pair(refs[given.index(2 * m)], refs[given.index(2 * m + 1)], pick_ref)
        for aw in range(3):
            out_ref[aw * 256:(aw + 1) * 256, place * 128:(place + 1) * 128] = y[:, aw * 128:(aw + 1) * 128]


def layer_kernel(pairs, y_ref, first_ref, second_ref, pick_ref, k1t_ref, ogt_ref, ag_ref, act_ref, terms_ref, y_scr, pg_scr):
    cells = ag_ref.shape[1]
    rows = 256
    here = lax.axis_index("space") >> 1
    for place, m in enumerate(pairs):
        lanes = pl.ds(pl.multiple_of(lax.bitwise_xor(here, jnp.int32(m)) * 128, 128), 128)
        if place + 1 < len(pairs):
            y_scr[:, lanes] = y_ref[:, place * 128:(place + 1) * 128]
            continue
        y = taps_of_pair(first_ref, second_ref, pick_ref)
        for aw in range(3):
            y_scr[aw * rows:(aw + 1) * rows, lanes] = y[:, aw * 128:(aw + 1) * 128]
    both = dot(k1t_ref[...], y_scr[...])
    lane = iota((128, cells), 1)
    from_last = jnp.where(lane < 64, 0.0, pltpu.roll(both[128:], 64, 1))
    pre = both[:128] + from_last
    sigma = jax.nn.sigmoid(pre)
    act = (pre * sigma).astype(jnp.bfloat16)
    act_ref[...] = act
    slope = sigma * (1.0 + pre * (1.0 - sigma))
    grad = (ag_ref[...].astype(jnp.float32) * slope).astype(jnp.bfloat16)
    pg_scr[:128, :] = grad
    to_last = pltpu.roll(grad.astype(jnp.float32), cells - 64, 1)
    pg_scr[128:, :] = jnp.where(lane < cells - 64, to_last, 0.0).astype(jnp.bfloat16)

    second = dot(act, ogt_ref[...])
    lane = iota((32, 128), 1)
    held = None
    for t in range(9):
        tile = second[:, t * 128:(t + 1) * 128]
        turned = pltpu.roll(tile, 64, 1)
        mixed = jnp.where(lane < 64, tile[0:32] + turned[64:96], turned[32:64] + tile[96:128])
        terms_ref[t * 32:(t + 1) * 32, :] = mixed.astype(jnp.bfloat16)
        if t % 2 == 0:
            held = jnp.where(lane < 64, turned[32:64], 0.0)
        else:
            held = jnp.where(lane < 64, held, tile[32:64])
        if t % 2 == 1:
            start = 288 + (t // 2) * 32
            terms_ref[start:start + 32, :] = held.astype(jnp.bfloat16)
    terms_ref[416:432, :] = jnp.where(lane[:16] < 64, held[:16], pltpu.roll(held[16:], 64, 1)).astype(jnp.bfloat16)

    first = dot(y_scr[...], pg_scr[...], ((1,), (1,))).astype(jnp.bfloat16)
    shape = (rows, 256)
    h, hh = (iota(shape, 0) >> 1) & 7, (iota(shape, 1) >> 5) & 3
    even, odd = ones_where((h >> 1) == hh), ones_where(((h & 1) == 1) & ((h + 1) >> 1 == hh))
    rank, index = iota((64, rows), 0), iota((64, rows), 1)
    same = ((rank & 15) == index >> 4) & (((rank >> 4) & 1) == (index & 1))
    later_taps = ones_where(same & ((rank >> 5) == ((index >> 1) & 1)))
    first_tap = ones_where(same[:32] & (((index[:32] >> 1) & 1) == 1))
    lane = iota((16, 128), 1)
    for aw in range(3):
        tile = first[aw * rows:(aw + 1) * rows]
        total = jnp.concatenate([dot(first_tap, tile * odd), dot(later_taps, tile * even)], axis=0)
        start = 432 + aw * 48
        for ad in range(3):
            side = slice(128, 256) if ad == 0 else slice(0, 128)
            d = 0 if ad == 1 else 1
            packed = None
            for ah in range(3):
                part = total[ah * 32 + d * 16:ah * 32 + d * 16 + 16, side]
                part = part + pltpu.roll(part, 64, 1)
                part = part + pltpu.roll(part, 32, 1)
                packed = part if packed is None else jnp.where(lane >= ah * 32, part, packed)
            terms_ref[start + ad * 16:start + (ad + 1) * 16, :] = packed.astype(jnp.bfloat16)
    rest = terms_ref.shape[0] - TERM_ROWS
    if rest > 0:
        terms_ref[TERM_ROWS:, :] = jnp.zeros((rest, 128), jnp.bfloat16)


def features_kernel(act_ref, k2_ref, out_ref, k2t_ref):
    band_of_second(k2_ref, k2t_ref)
    groups = out_ref.shape[1] // 128
    for g in range(groups):
        total = jnp.zeros((128, 128), jnp.float32)
        for t in range(9):
            taken = dot(act_ref[:, g * 512:(g + 1) * 512], upsampling(t // 3, t % 3), ((1,), (1,)))
            if t < 3 and g > 0:
                last = act_ref[:, (g - 1) * 512:g * 512]
                taken = taken + dot(last, upsampling(0, t, 4), ((1,), (1,)))
            band = k2t_ref[:, t * 128:(t + 1) * 128]
            total = total + dot(band, taken.astype(jnp.bfloat16), ((0,), (0,)))
        out_ref[:, g * 128:(g + 1) * 128] = total.astype(jnp.bfloat16)


def add_kernel(rows, mine_ref, out_ref):
    count = mine_ref.shape[0]
    unit = rows * 16 // math.gcd(rows, 16)
    total = mine_ref[0:unit, :].astype(jnp.float32)
    for start in range(unit, count, unit):
        total = total + mine_ref[start:start + unit, :].astype(jnp.float32)
    if unit % (2 * rows) == 0 and (unit // 2) % 8 == 0:
        total = total[:unit // 2] + total[unit // 2:]
    parts = [total[start:start + rows] for start in range(0, total.shape[0], rows)]
    total = functools.reduce(jnp.add, parts)
    spread = jnp.concatenate([total] * (unit // rows), axis=0).astype(jnp.bfloat16)
    for start in range(0, count, unit):
        out_ref[start:start + unit, :] = spread


def unpack_kernel(whole_ref, first_ref, second_ref, first_scr, second_scr, sems):
    copies = []
    for ad in range(3):
        for aw in range(3):
            t = ad * 3 + aw
            pair = whole_ref[t * 32:(t + 1) * 32, :].astype(jnp.float32)
            second_scr[ad, 1, aw] = pair[:, :64]
            second_scr[ad, 2, aw] = pair[:, 64:]
            if t == 8:
                lone = whole_ref[416:432, :].astype(jnp.float32)
                second_scr[ad, 0, aw] = jnp.concatenate([lone[:, :64], lone[:, 64:]], axis=0)
            else:
                start = 288 + (t // 2) * 32
                lone = whole_ref[start:start + 32, :].astype(jnp.float32)
                second_scr[ad, 0, aw] = lone[:, :64] if t % 2 == 0 else lone[:, 64:]
        copies.append(pltpu.make_async_copy(second_scr.at[ad], second_ref.at[ad], sems.at[0, ad]))
        copies[-1].start()
    for ad in range(3):
        for aw in range(3):
            start = 432 + aw * 48 + ad * 16
            tile = whole_ref[start:start + 16, :].astype(jnp.float32)
            for ah in range(3):
                first_scr[ad, ah, aw] = tile[:, ah * 32:(ah + 1) * 32]
        copies.append(pltpu.make_async_copy(first_scr.at[ad], first_ref.at[ad], sems.at[1, ad]))
        copies[-1].start()
    for copy in copies:
        copy.wait()


def call(kernel, outs, args, scratch=(), flops=0):
    whole = pl.BlockSpec(memory_space=pltpu.VMEM)
    scalar = pl.BlockSpec(memory_space=pltpu.SMEM)
    size = sum(a.size * a.dtype.itemsize for a in list(args) + list(outs))
    return pl.pallas_call(
        kernel,
        out_shape=tuple(outs),
        in_specs=[scalar if a.dtype == jnp.int32 else whole for a in args],
        out_specs=(whole,) * len(outs),
        scratch_shapes=list(scratch),
        compiler_params=pltpu.CompilerParams(vmem_limit_bytes=VMEM_BYTES),
        cost_estimate=pl.CostEstimate(flops=flops, bytes_accessed=size, transcendentals=0),
    )(*args)


def array(shape, dtype=jnp.bfloat16):
    return jax.ShapeDtypeStruct(shape, dtype)


def by_tap(kernel):
    return jnp.transpose(kernel, (2, 3, 4, 1, 0))


def prepare(k1, k2, out_grad):
    c0, c1 = k1.shape[3:]
    c2 = k2.shape[4]
    planes = out_grad.shape[2]
    cells = planes * 2 * 64
    og = out_grad.reshape(c2, planes, 2, 32).transpose(2, 0, 1, 3).reshape(2 * c2, planes * 32)
    outs = [
        array((384, 384)),
        array((2 * 4 * c1, 3 * c0 * 16)),
        array((cells, 9 * 2 * c2)),
        array((4 * c1, cells)),
    ]
    scratch = [pltpu.VMEM((4 * c1, 9 * 2 * c2), jnp.bfloat16), pltpu.VMEM((9 * 2 * c2, cells), jnp.bfloat16)]
    return call(prepare_kernel, outs, (k1, k2, og), scratch, flops=2 * 128 * 1152 * cells * 2)


def body(crops, first_kernel, second_kernel, out_grad):
    axes = ("space", "sample")
    devices = lax.axis_size(axes)
    channels_out, planes = out_grad.shape[1:3]
    space = lax.axis_size("space")
    assert space & (space - 1) == 0
    position = lax.axis_index("space").astype(jnp.int32)
    across, near = list(range(space - 1, space // 2 - 1, -1)), list(range(1, space // 2))
    order = [step for two in zip(across[:-2], near[:-1]) for step in two] + near[-1:] + across[-2:]
    early, late = order[:space // 2], order[space // 2:]
    last = space // 4
    pairs = [m for m in range(space // 2) if m != last] + [last]
    k1, k2 = by_tap(first_kernel), by_tap(second_kernel)
    x = {}
    cut = [lax.dynamic_index_in_dim(crops, position ^ step, 0, keepdims=False) for step in early]
    rest, cut = lax.optimization_barrier((crops, cut))
    for step in [0] + late[::-1] + early:
        if step in early:
            block = cut[early.index(step)]
        else:
            block = lax.dynamic_index_in_dim(rest, position ^ step, 0, keepdims=False)
        if step > 0:
            block = lax.ppermute(block, "space", [(source, source ^ step) for source in range(space)])
        channels_in, two, flat_cells = block.shape
        block = block.reshape(channels_in, two, HEIGHT, WIDTH).transpose(0, 2, 1, 3)
        x[step] = block.reshape(channels_in * two * HEIGHT, WIDTH)
    pick, k1t, ogt, act_grad = prepare(k1, k2, out_grad)
    cells = act_grad.shape[1]
    given = early + [step for step in x if step not in early and step // 2 != last]
    (y,) = call(
        functools.partial(taps_kernel, pairs[:-1], given),
        [array((768, cells - 128))],
        [x[step] for step in given] + [pick],
        flops=2 * 256 * 384 * cells,
    )
    rows = -(-TERM_ROWS // (devices * 2)) * 2
    act, terms = call(
        functools.partial(layer_kernel, pairs),
        [array((128, cells)), array((devices * rows, LANES))],
        (y, x[2 * last], x[2 * last + 1], pick, k1t, ogt, act_grad),
        scratch=[pltpu.VMEM((768, cells), jnp.bfloat16), pltpu.VMEM((256, cells), jnp.bfloat16)],
        flops=2 * 128 * 4096 * cells,
    )
    blocks = terms.reshape(devices, rows // 2, 2, LANES)
    mine = lax.all_to_all(blocks, axes, split_axis=0, concat_axis=0, tiled=True)
    (features,) = call(
        features_kernel,
        [array((2 * channels_out, planes * 32))],
        (act, k2),
        scratch=[pltpu.VMEM((128, 1152), jnp.bfloat16)],
        flops=2 * 128 * 1152 * cells,
    )
    features = features.reshape(2, channels_out, planes, 32).transpose(1, 2, 0, 3).reshape(out_grad.shape)
    add = functools.partial(add_kernel, rows)
    (spread,) = call(add, [array(terms.shape)], (mine.reshape(terms.shape),))
    spread = spread.reshape(blocks.shape)
    whole = lax.all_to_all(spread, axes, split_axis=0, concat_axis=0, tiled=True)
    shapes = [(3, 3, 3) + kernel.shape[1::-1] for kernel in (first_kernel, second_kernel)]
    first, second = pl.pallas_call(
        unpack_kernel,
        out_shape=[array(shape, jnp.float32) for shape in shapes],
        in_specs=[pl.BlockSpec(memory_space=pltpu.VMEM)],
        out_specs=[pl.BlockSpec(memory_space=pl.ANY)] * 2,
        scratch_shapes=[pltpu.VMEM(shape, jnp.float32) for shape in shapes] + [pltpu.SemaphoreType.DMA((2, 3))],
        compiler_params=pltpu.CompilerParams(vmem_limit_bytes=VMEM_BYTES),
    )(whole.reshape(terms.shape))
    return (features, jnp.transpose(first, (4, 3, 0, 1, 2)), jnp.transpose(second, (4, 3, 0, 1, 2)))


def solution(mesh):
    placed = (P("sample", None, "space", None), P(), P(), P(("sample", "space"), None, None, None))
    return jax.shard_map(
        body,
        mesh=mesh,
        in_specs=placed,
        out_specs=(P(("sample", "space"), None, None, None), P(), P()),
        check_vma=False,
    )
```

```python
import functools
import math

import jax
import jax.numpy as jnp
from jax import lax
from jax.experimental import pallas as pl
from jax.experimental.pallas import tpu as pltpu
from jax.sharding import PartitionSpec as P

HEIGHT = 8
WIDTH = 128
LANES = 128
VMEM_BYTES = 16 * 1024 * 1024
TERM_ROWS = 576


def iota(shape, dim):
    return lax.broadcasted_iota(jnp.int32, shape, dim)


def dot(left, right, dims=((1,), (0,))):
    return lax.dot_general(left, right, (dims, ((), ())), preferred_element_type=jnp.float32)


def ones_where(mask):
    return jnp.where(mask, 1.0, 0.0).astype(jnp.bfloat16)


def band_of_second(k2_ref, k2t_ref):
    channels_mid, channels_out = k2_ref.shape[3:]
    empty = jnp.zeros((channels_mid, channels_out), jnp.bfloat16)
    for ad in range(3):
        for aw in range(3):
            tap = [k2_ref[ad, ah, aw] for ah in range(3)]
            band = ((tap[1], empty), (tap[2], tap[0]), (empty, tap[1]), (empty, tap[2]))
            start = (ad * 3 + aw) * 2 * channels_out
            for hh in range(4):
                k2t_ref[hh * channels_mid:(hh + 1) * channels_mid, start:start + 2 * channels_out] = (
                    jnp.concatenate(band[hh], axis=1))


def upsampling(ad, aw, beyond=0):
    row, col = iota((128, 512), 0), iota((128, 512), 1)
    target = ((row >> 5) << 7) + ((row & 31) << 1) + (64 * (ad - 1) + aw - 1 + 128 * beyond)
    keep = col == target
    if aw == 0:
        keep = keep & ((row & 31) > 0)
    return ones_where(keep)


def prepare_kernel(k1_ref, k2_ref, og_ref, pick_ref, k1t_ref, ogt_ref, ag_ref, k2t_ref, ogu_ref):
    channels_in, channels_mid = k1_ref.shape[3:]
    row, col = iota((3 * WIDTH, 2 * 64), 0), iota((3 * WIDTH, 2 * 64), 1)
    for aw in range(3):
        same = ((row >> 7) & 1) == (col >> 6)
        tap = (row & 127) == 2 * (col & 63) + aw - 1
        pick_ref[:, aw * 128:(aw + 1) * 128] = ones_where(same & tap)
    shape = (9 * channels_in, channels_in * 2 * HEIGHT)
    row, col = iota(shape, 0), iota(shape, 1)
    tap = row >> 4
    ad = jnp.where(tap >= 6, 2, jnp.where(tap >= 3, 1, 0))
    ah, i = tap - 3 * ad, row & 15
    same = i == col >> 4
    h, d = (col >> 1) & 7, col & 1
    taps = []
    for aw in range(3):
        parts = [k1_ref[a, b, aw] for a in range(3) for b in range(3)]
        taps.append(jnp.concatenate(parts, axis=0).astype(jnp.float32).T.astype(jnp.bfloat16))
    for following in range(2):
        plane = (ad == 0) & (d == 1) if following else (ad == d + 1)
        for hh in range(4):
            place = ones_where(same & plane & (h == 2 * hh + ah - 1))
            start = (following * 4 + hh) * channels_mid
            for aw in range(3):
                block = dot(taps[aw], place).astype(jnp.bfloat16)
                k1t_ref[start:start + channels_mid, aw * shape[1]:(aw + 1) * shape[1]] = block
    band_of_second(k2_ref, k2t_ref)
    groups = og_ref.shape[1] // 128
    for ad in range(3):
        for aw in range(3):
            t = ad * 3 + aw
            up = upsampling(ad, aw)
            for g in range(groups):
                value = dot(og_ref[:, g * 128:(g + 1) * 128], up)
                if ad == 0 and g + 1 < groups:
                    value = value + dot(og_ref[:, (g + 1) * 128:(g + 2) * 128], upsampling(ad, aw, 4))
                ogu_ref[t * 128:(t + 1) * 128, g * 512:(g + 1) * 512] = value.astype(jnp.bfloat16)
                ogt_ref[g * 512:(g + 1) * 512, t * 128:(t + 1) * 128] = value.T.astype(jnp.bfloat16)
    for g in range(groups):
        lanes = slice(g * 512, (g + 1) * 512)
        ag_ref[:, lanes] = dot(k2t_ref[...], ogu_ref[:, lanes]).astype(jnp.bfloat16)


def taps_of_pair(first_ref, second_ref, pick_ref):
    parity = lax.axis_index("space") & 1
    pick = pick_ref[pl.ds(pl.multiple_of(parity * WIDTH, WIDTH), 2 * WIDTH), :]
    pair = jnp.concatenate([first_ref[...], second_ref[...]], axis=1)
    return dot(pair, pick).astype(jnp.bfloat16)


def taps_kernel(pairs, given, *refs):
    pick_ref, out_ref = refs[-2:]
    for place, m in enumerate(pairs):
        y = taps_of_pair(refs[given.index(2 * m)], refs[given.index(2 * m + 1)], pick_ref)
        for aw in range(3):
            out_ref[aw * 256:(aw + 1) * 256, place * 128:(place + 1) * 128] = y[:, aw * 128:(aw + 1) * 128]


def layer_kernel(pairs, y_ref, first_ref, second_ref, pick_ref, k1t_ref, ogt_ref, ag_ref, act_ref, terms_ref, y_scr, pg_scr):
    cells = ag_ref.shape[1]
    rows = 256
    here = lax.axis_index("space") >> 1
    for place, m in enumerate(pairs):
        lanes = pl.ds(pl.multiple_of(lax.bitwise_xor(here, jnp.int32(m)) * 128, 128), 128)
        if place + 1 < len(pairs):
            y_scr[:, lanes] = y_ref[:, place * 128:(place + 1) * 128]
            continue
        y = taps_of_pair(first_ref, second_ref, pick_ref)
        for aw in range(3):
            y_scr[aw * rows:(aw + 1) * rows, lanes] = y[:, aw * 128:(aw + 1) * 128]
    both = dot(k1t_ref[...], y_scr[...])
    lane = iota((128, cells), 1)
    from_last = jnp.where(lane < 64, 0.0, pltpu.roll(both[128:], 64, 1))
    pre = both[:128] + from_last
    sigma = jax.nn.sigmoid(pre)
    act = (pre * sigma).astype(jnp.bfloat16)
    act_ref[...] = act
    slope = sigma * (1.0 + pre * (1.0 - sigma))
    grad = (ag_ref[...].astype(jnp.float32) * slope).astype(jnp.bfloat16)
    pg_scr[:128, :] = grad
    to_last = pltpu.roll(grad.astype(jnp.float32), cells - 64, 1)
    pg_scr[128:, :] = jnp.where(lane < cells - 64, to_last, 0.0).astype(jnp.bfloat16)

    second = dot(act, ogt_ref[...])
    lane = iota((32, 128), 1)
    held = None
    for t in range(9):
        tile = second[:, t * 128:(t + 1) * 128]
        turned = pltpu.roll(tile, 64, 1)
        mixed = jnp.where(lane < 64, tile[0:32] + turned[64:96], turned[32:64] + tile[96:128])
        terms_ref[t * 32:(t + 1) * 32, :] = mixed.astype(jnp.bfloat16)
        if t % 2 == 0:
            held = jnp.where(lane < 64, turned[32:64], 0.0)
        else:
            held = jnp.where(lane < 64, held, tile[32:64])
        if t % 2 == 1:
            start = 288 + (t // 2) * 32
            terms_ref[start:start + 32, :] = held.astype(jnp.bfloat16)
    terms_ref[416:432, :] = jnp.where(lane[:16] < 64, held[:16], pltpu.roll(held[16:], 64, 1)).astype(jnp.bfloat16)

    first = dot(y_scr[...], pg_scr[...], ((1,), (1,))).astype(jnp.bfloat16)
    shape = (rows, 256)
    h, hh = (iota(shape, 0) >> 1) & 7, (iota(shape, 1) >> 5) & 3
    even, odd = ones_where((h >> 1) == hh), ones_where(((h & 1) == 1) & ((h + 1) >> 1 == hh))
    rank, index = iota((64, rows), 0), iota((64, rows), 1)
    same = ((rank & 15) == index >> 4) & (((rank >> 4) & 1) == (index & 1))
    later_taps = ones_where(same & ((rank >> 5) == ((index >> 1) & 1)))
    first_tap = ones_where(same[:32] & (((index[:32] >> 1) & 1) == 1))
    lane = iota((16, 128), 1)
    for aw in range(3):
        tile = first[aw * rows:(aw + 1) * rows]
        total = jnp.concatenate([dot(first_tap, tile * odd), dot(later_taps, tile * even)], axis=0)
        start = 432 + aw * 48
        for ad in range(3):
            side = slice(128, 256) if ad == 0 else slice(0, 128)
            d = 0 if ad == 1 else 1
            packed = None
            for ah in range(3):
                part = total[ah * 32 + d * 16:ah * 32 + d * 16 + 16, side]
                part = part + pltpu.roll(part, 64, 1)
                part = part + pltpu.roll(part, 32, 1)
                packed = part if packed is None else jnp.where(lane >= ah * 32, part, packed)
            terms_ref[start + ad * 16:start + (ad + 1) * 16, :] = packed.astype(jnp.bfloat16)
    rest = terms_ref.shape[0] - TERM_ROWS
    if rest > 0:
        terms_ref[TERM_ROWS:, :] = jnp.zeros((rest, 128), jnp.bfloat16)


def features_kernel(act_ref, k2_ref, out_ref, k2t_ref):
    band_of_second(k2_ref, k2t_ref)
    groups = out_ref.shape[1] // 128
    for g in range(groups):
        total = jnp.zeros((128, 128), jnp.float32)
        for t in range(9):
            taken = dot(act_ref[:, g * 512:(g + 1) * 512], upsampling(t // 3, t % 3), ((1,), (1,)))
            if t < 3 and g > 0:
                last = act_ref[:, (g - 1) * 512:g * 512]
                taken = taken + dot(last, upsampling(0, t, 4), ((1,), (1,)))
            band = k2t_ref[:, t * 128:(t + 1) * 128]
            total = total + dot(band, taken.astype(jnp.bfloat16), ((0,), (0,)))
        out_ref[:, g * 128:(g + 1) * 128] = total.astype(jnp.bfloat16)


def add_kernel(rows, mine_ref, out_ref):
    count = mine_ref.shape[0]
    unit = rows * 16 // math.gcd(rows, 16)
    total = mine_ref[0:unit, :].astype(jnp.float32)
    for start in range(unit, count, unit):
        total = total + mine_ref[start:start + unit, :].astype(jnp.float32)
    if unit % (2 * rows) == 0 and (unit // 2) % 8 == 0:
        total = total[:unit // 2] + total[unit // 2:]
    parts = [total[start:start + rows] for start in range(0, total.shape[0], rows)]
    total = functools.reduce(jnp.add, parts)
    spread = jnp.concatenate([total] * (unit // rows), axis=0).astype(jnp.bfloat16)
    for start in range(0, count, unit):
        out_ref[start:start + unit, :] = spread


def unpack_kernel(whole_ref, first_ref, second_ref, first_scr, second_scr, sems):
    copies = []
    for ad in range(3):
        for aw in range(3):
            t = ad * 3 + aw
            pair = whole_ref[t * 32:(t + 1) * 32, :].astype(jnp.float32)
            second_scr[ad, 1, aw] = pair[:, :64]
            second_scr[ad, 2, aw] = pair[:, 64:]
            if t == 8:
                lone = whole_ref[416:432, :].astype(jnp.float32)
                second_scr[ad, 0, aw] = jnp.concatenate([lone[:, :64], lone[:, 64:]], axis=0)
            else:
                start = 288 + (t // 2) * 32
                lone = whole_ref[start:start + 32, :].astype(jnp.float32)
                second_scr[ad, 0, aw] = lone[:, :64] if t % 2 == 0 else lone[:, 64:]
        copies.append(pltpu.make_async_copy(second_scr.at[ad], second_ref.at[ad], sems.at[0, ad]))
        copies[-1].start()
    for ad in range(3):
        for aw in range(3):
            start = 432 + aw * 48 + ad * 16
            tile = whole_ref[start:start + 16, :].astype(jnp.float32)
            for ah in range(3):
                first_scr[ad, ah, aw] = tile[:, ah * 32:(ah + 1) * 32]
        copies.append(pltpu.make_async_copy(first_scr.at[ad], first_ref.at[ad], sems.at[1, ad]))
        copies[-1].start()
    for copy in copies:
        copy.wait()


def call(kernel, outs, args, scratch=(), flops=0):
    whole = pl.BlockSpec(memory_space=pltpu.VMEM)
    scalar = pl.BlockSpec(memory_space=pltpu.SMEM)
    size = sum(a.size * a.dtype.itemsize for a in list(args) + list(outs))
    return pl.pallas_call(
        kernel,
        out_shape=tuple(outs),
        in_specs=[scalar if a.dtype == jnp.int32 else whole for a in args],
        out_specs=(whole,) * len(outs),
        scratch_shapes=list(scratch),
        compiler_params=pltpu.CompilerParams(vmem_limit_bytes=VMEM_BYTES),
        cost_estimate=pl.CostEstimate(flops=flops, bytes_accessed=size, transcendentals=0),
    )(*args)


def array(shape, dtype=jnp.bfloat16):
    return jax.ShapeDtypeStruct(shape, dtype)


def by_tap(kernel):
    return jnp.transpose(kernel, (2, 3, 4, 1, 0))


def prepare(k1, k2, out_grad):
    c0, c1 = k1.shape[3:]
    c2 = k2.shape[4]
    planes = out_grad.shape[2]
    cells = planes * 2 * 64
    og = out_grad.reshape(c2, planes, 2, 32).transpose(2, 0, 1, 3).reshape(2 * c2, planes * 32)
    outs = [
        array((384, 384)),
        array((2 * 4 * c1, 3 * c0 * 16)),
        array((cells, 9 * 2 * c2)),
        array((4 * c1, cells)),
    ]
    scratch = [pltpu.VMEM((4 * c1, 9 * 2 * c2), jnp.bfloat16), pltpu.VMEM((9 * 2 * c2, cells), jnp.bfloat16)]
    return call(prepare_kernel, outs, (k1, k2, og), scratch, flops=2 * 128 * 1152 * cells * 2)


def body(crops, first_kernel, second_kernel, out_grad):
    axes = ("space", "sample")
    devices = lax.axis_size(axes)
    channels_out, planes = out_grad.shape[1:3]
    space = lax.axis_size("space")
    assert space & (space - 1) == 0
    position = lax.axis_index("space").astype(jnp.int32)
    across = list(range(space - 1, space // 2 - 1, -1))
    order = across[:1] + [1] + across[1:] + list(range(4, space // 2)) + [2, 3]
    early, late = order[:space // 2], order[space // 2:]
    last = 1
    pairs = [m for m in range(space // 2) if m != last] + [last]
    k1, k2 = by_tap(first_kernel), by_tap(second_kernel)
    x = {}
    cut = [lax.dynamic_index_in_dim(crops, position ^ step, 0, keepdims=False) for step in early]
    rest, cut = lax.optimization_barrier((crops, cut))
    for step in [0] + late[::-1] + early:
        if step in early:
            block = cut[early.index(step)]
        else:
            block = lax.dynamic_index_in_dim(rest, position ^ step, 0, keepdims=False)
        if step > 0:
            block = lax.ppermute(block, "space", [(source, source ^ step) for source in range(space)])
        channels_in, two, flat_cells = block.shape
        block = block.reshape(channels_in, two, HEIGHT, WIDTH).transpose(0, 2, 1, 3)
        x[step] = block.reshape(channels_in * two * HEIGHT, WIDTH)
    pick, k1t, ogt, act_grad = prepare(k1, k2, out_grad)
    cells = act_grad.shape[1]
    given = early + [step for step in x if step not in early and step // 2 != last]
    (y,) = call(
        functools.partial(taps_kernel, pairs[:-1], given),
        [array((768, cells - 128))],
        [x[step] for step in given] + [pick],
        flops=2 * 256 * 384 * cells,
    )
    rows = -(-TERM_ROWS // (devices * 2)) * 2
    act, terms = call(
        functools.partial(layer_kernel, pairs),
        [array((128, cells)), array((devices * rows, LANES))],
        (y, x[2 * last], x[2 * last + 1], pick, k1t, ogt, act_grad),
        scratch=[pltpu.VMEM((768, cells), jnp.bfloat16), pltpu.VMEM((256, cells), jnp.bfloat16)],
        flops=2 * 128 * 4096 * cells,
    )
    blocks = terms.reshape(devices, rows // 2, 2, LANES)
    mine = lax.all_to_all(blocks, axes, split_axis=0, concat_axis=0, tiled=True)
    (features,) = call(
        features_kernel,
        [array((2 * channels_out, planes * 32))],
        (act, k2),
        scratch=[pltpu.VMEM((128, 1152), jnp.bfloat16)],
        flops=2 * 128 * 1152 * cells,
    )
    features = features.reshape(2, channels_out, planes, 32).transpose(1, 2, 0, 3).reshape(out_grad.shape)
    add = functools.partial(add_kernel, rows)
    (spread,) = call(add, [array(terms.shape)], (mine.reshape(terms.shape),))
    spread = spread.reshape(blocks.shape)
    whole = lax.all_to_all(spread, axes, split_axis=0, concat_axis=0, tiled=True)
    shapes = [(3, 3, 3) + kernel.shape[1::-1] for kernel in (first_kernel, second_kernel)]
    first, second = pl.pallas_call(
        unpack_kernel,
        out_shape=[array(shape, jnp.float32) for shape in shapes],
        in_specs=[pl.BlockSpec(memory_space=pltpu.VMEM)],
        out_specs=[pl.BlockSpec(memory_space=pl.ANY)] * 2,
        scratch_shapes=[pltpu.VMEM(shape, jnp.float32) for shape in shapes] + [pltpu.SemaphoreType.DMA((2, 3))],
        compiler_params=pltpu.CompilerParams(vmem_limit_bytes=VMEM_BYTES),
    )(whole.reshape(terms.shape))
    return (features, jnp.transpose(first, (4, 3, 0, 1, 2)), jnp.transpose(second, (4, 3, 0, 1, 2)))


def solution(mesh):
    placed = (P("sample", None, "space", None), P(), P(), P(("sample", "space"), None, None, None))
    return jax.shard_map(
        body,
        mesh=mesh,
        in_specs=placed,
        out_specs=(P(("sample", "space"), None, None, None), P(), P()),
        check_vma=False,
    )
```

```python
import functools
import math

import jax
import jax.numpy as jnp
from jax import lax
from jax.experimental import pallas as pl
from jax.experimental.pallas import tpu as pltpu
from jax.sharding import PartitionSpec as P

HEIGHT = 8
WIDTH = 128
LANES = 128
VMEM_BYTES = 16 * 1024 * 1024
TERM_ROWS = 576


def iota(shape, dim):
    return lax.broadcasted_iota(jnp.int32, shape, dim)


def dot(left, right, dims=((1,), (0,))):
    return lax.dot_general(left, right, (dims, ((), ())), preferred_element_type=jnp.float32)


def ones_where(mask):
    return jnp.where(mask, 1.0, 0.0).astype(jnp.bfloat16)


def band_of_second(k2_ref, k2t_ref):
    channels_mid, channels_out = k2_ref.shape[3:]
    empty = jnp.zeros((channels_mid, channels_out), jnp.bfloat16)
    for ad in range(3):
        for aw in range(3):
            tap = [k2_ref[ad, ah, aw] for ah in range(3)]
            band = ((tap[1], empty), (tap[2], tap[0]), (empty, tap[1]), (empty, tap[2]))
            start = (ad * 3 + aw) * 2 * channels_out
            for hh in range(4):
                k2t_ref[hh * channels_mid:(hh + 1) * channels_mid, start:start + 2 * channels_out] = (
                    jnp.concatenate(band[hh], axis=1))


def upsampling(ad, aw, beyond=0):
    row, col = iota((128, 512), 0), iota((128, 512), 1)
    target = ((row >> 5) << 7) + ((row & 31) << 1) + (64 * (ad - 1) + aw - 1 + 128 * beyond)
    keep = col == target
    if aw == 0:
        keep = keep & ((row & 31) > 0)
    return ones_where(keep)


def prepare_kernel(k1_ref, k2_ref, og_ref, pick_ref, k1t_ref, ogt_ref, ag_ref, k2t_ref, ogu_ref):
    channels_in, channels_mid = k1_ref.shape[3:]
    row, col = iota((3 * WIDTH, 2 * 64), 0), iota((3 * WIDTH, 2 * 64), 1)
    for aw in range(3):
        same = ((row >> 7) & 1) == (col >> 6)
        tap = (row & 127) == 2 * (col & 63) + aw - 1
        pick_ref[:, aw * 128:(aw + 1) * 128] = ones_where(same & tap)
    shape = (9 * channels_in, channels_in * 2 * HEIGHT)
    row, col = iota(shape, 0), iota(shape, 1)
    tap = row >> 4
    ad = jnp.where(tap >= 6, 2, jnp.where(tap >= 3, 1, 0))
    ah, i = tap - 3 * ad, row & 15
    same = i == col >> 4
    h, d = (col >> 1) & 7, col & 1
    taps = []
    for aw in range(3):
        parts = [k1_ref[a, b, aw] for a in range(3) for b in range(3)]
        taps.append(jnp.concatenate(parts, axis=0).astype(jnp.float32).T.astype(jnp.bfloat16))
    for following in range(2):
        plane = (ad == 0) & (d == 1) if following else (ad == d + 1)
        for hh in range(4):
            place = ones_where(same & plane & (h == 2 * hh + ah - 1))
            start = (following * 4 + hh) * channels_mid
            for aw in range(3):
                block = dot(taps[aw], place).astype(jnp.bfloat16)
                k1t_ref[start:start + channels_mid, aw * shape[1]:(aw + 1) * shape[1]] = block
    band_of_second(k2_ref, k2t_ref)
    groups = og_ref.shape[1] // 128
    for ad in range(3):
        for aw in range(3):
            t = ad * 3 + aw
            up = upsampling(ad, aw)
            for g in range(groups):
                value = dot(og_ref[:, g * 128:(g + 1) * 128], up)
                if ad == 0 and g + 1 < groups:
                    value = value + dot(og_ref[:, (g + 1) * 128:(g + 2) * 128], upsampling(ad, aw, 4))
                ogu_ref[t * 128:(t + 1) * 128, g * 512:(g + 1) * 512] = value.astype(jnp.bfloat16)
                ogt_ref[g * 512:(g + 1) * 512, t * 128:(t + 1) * 128] = value.T.astype(jnp.bfloat16)
    for g in range(groups):
        lanes = slice(g * 512, (g + 1) * 512)
        ag_ref[:, lanes] = dot(k2t_ref[...], ogu_ref[:, lanes]).astype(jnp.bfloat16)


def taps_of_pair(first_ref, second_ref, pick_ref):
    parity = lax.axis_index("space") & 1
    pick = pick_ref[pl.ds(pl.multiple_of(parity * WIDTH, WIDTH), 2 * WIDTH), :]
    pair = jnp.concatenate([first_ref[...], second_ref[...]], axis=1)
    return dot(pair, pick).astype(jnp.bfloat16)


def taps_kernel(pairs, given, *refs):
    pick_ref, out_ref = refs[-2:]
    for place, m in enumerate(pairs):
        y = taps_of_pair(refs[given.index(2 * m)], refs[given.index(2 * m + 1)], pick_ref)
        for aw in range(3):
            out_ref[aw * 256:(aw + 1) * 256, place * 128:(place + 1) * 128] = y[:, aw * 128:(aw + 1) * 128]


def layer_kernel(first, last, given, y_ref, *refs):
    pick_ref, k1t_ref, ogt_ref, ag_ref, act_ref, terms_ref, y_scr, pg_scr = refs[len(given):]
    cells = ag_ref.shape[1]
    rows = 256
    here = lax.axis_index("space") >> 1

    def lanes(m):
        return pl.ds(pl.multiple_of(lax.bitwise_xor(here, jnp.int32(m)) * 128, 128), 128)

    for place, m in enumerate(first):
        y_scr[:, lanes(m)] = y_ref[:, place * 128:(place + 1) * 128]
    for m in last:
        y = taps_of_pair(refs[given.index(2 * m)], refs[given.index(2 * m + 1)], pick_ref)
        for aw in range(3):
            y_scr[aw * rows:(aw + 1) * rows, lanes(m)] = y[:, aw * 128:(aw + 1) * 128]
    both = dot(k1t_ref[...], y_scr[...])
    lane = iota((128, cells), 1)
    from_last = jnp.where(lane < 64, 0.0, pltpu.roll(both[128:], 64, 1))
    pre = both[:128] + from_last
    sigma = jax.nn.sigmoid(pre)
    act = (pre * sigma).astype(jnp.bfloat16)
    act_ref[...] = act
    slope = sigma * (1.0 + pre * (1.0 - sigma))
    grad = (ag_ref[...].astype(jnp.float32) * slope).astype(jnp.bfloat16)
    pg_scr[:128, :] = grad
    to_last = pltpu.roll(grad.astype(jnp.float32), cells - 64, 1)
    pg_scr[128:, :] = jnp.where(lane < cells - 64, to_last, 0.0).astype(jnp.bfloat16)

    second = dot(act, ogt_ref[...])
    lane = iota((32, 128), 1)
    held = None
    for t in range(9):
        tile = second[:, t * 128:(t + 1) * 128]
        turned = pltpu.roll(tile, 64, 1)
        mixed = jnp.where(lane < 64, tile[0:32] + turned[64:96], turned[32:64] + tile[96:128])
        terms_ref[t * 32:(t + 1) * 32, :] = mixed.astype(jnp.bfloat16)
        if t % 2 == 0:
            held = jnp.where(lane < 64, turned[32:64], 0.0)
        else:
            held = jnp.where(lane < 64, held, tile[32:64])
        if t % 2 == 1:
            start = 288 + (t // 2) * 32
            terms_ref[start:start + 32, :] = held.astype(jnp.bfloat16)
    terms_ref[416:432, :] = jnp.where(lane[:16] < 64, held[:16], pltpu.roll(held[16:], 64, 1)).astype(jnp.bfloat16)

    first = dot(y_scr[...], pg_scr[...], ((1,), (1,))).astype(jnp.bfloat16)
    shape = (rows, 256)
    h, hh = (iota(shape, 0) >> 1) & 7, (iota(shape, 1) >> 5) & 3
    even, odd = ones_where((h >> 1) == hh), ones_where(((h & 1) == 1) & ((h + 1) >> 1 == hh))
    rank, index = iota((64, rows), 0), iota((64, rows), 1)
    same = ((rank & 15) == index >> 4) & (((rank >> 4) & 1) == (index & 1))
    later_taps = ones_where(same & ((rank >> 5) == ((index >> 1) & 1)))
    first_tap = ones_where(same[:32] & (((index[:32] >> 1) & 1) == 1))
    lane = iota((16, 128), 1)
    for aw in range(3):
        tile = first[aw * rows:(aw + 1) * rows]
        total = jnp.concatenate([dot(first_tap, tile * odd), dot(later_taps, tile * even)], axis=0)
        start = 432 + aw * 48
        for ad in range(3):
            side = slice(128, 256) if ad == 0 else slice(0, 128)
            d = 0 if ad == 1 else 1
            packed = None
            for ah in range(3):
                part = total[ah * 32 + d * 16:ah * 32 + d * 16 + 16, side]
                part = part + pltpu.roll(part, 64, 1)
                part = part + pltpu.roll(part, 32, 1)
                packed = part if packed is None else jnp.where(lane >= ah * 32, part, packed)
            terms_ref[start + ad * 16:start + (ad + 1) * 16, :] = packed.astype(jnp.bfloat16)
    rest = terms_ref.shape[0] - TERM_ROWS
    if rest > 0:
        terms_ref[TERM_ROWS:, :] = jnp.zeros((rest, 128), jnp.bfloat16)


def features_kernel(act_ref, k2_ref, out_ref, k2t_ref):
    band_of_second(k2_ref, k2t_ref)
    groups = out_ref.shape[1] // 128
    for g in range(groups):
        total = jnp.zeros((128, 128), jnp.float32)
        for t in range(9):
            taken = dot(act_ref[:, g * 512:(g + 1) * 512], upsampling(t // 3, t % 3), ((1,), (1,)))
            if t < 3 and g > 0:
                last = act_ref[:, (g - 1) * 512:g * 512]
                taken = taken + dot(last, upsampling(0, t, 4), ((1,), (1,)))
            band = k2t_ref[:, t * 128:(t + 1) * 128]
            total = total + dot(band, taken.astype(jnp.bfloat16), ((0,), (0,)))
        out_ref[:, g * 128:(g + 1) * 128] = total.astype(jnp.bfloat16)


def add_kernel(rows, mine_ref, out_ref):
    count = mine_ref.shape[0]
    unit = rows * 16 // math.gcd(rows, 16)
    total = mine_ref[0:unit, :].astype(jnp.float32)
    for start in range(unit, count, unit):
        total = total + mine_ref[start:start + unit, :].astype(jnp.float32)
    if unit % (2 * rows) == 0 and (unit // 2) % 8 == 0:
        total = total[:unit // 2] + total[unit // 2:]
    parts = [total[start:start + rows] for start in range(0, total.shape[0], rows)]
    total = functools.reduce(jnp.add, parts)
    spread = jnp.concatenate([total] * (unit // rows), axis=0).astype(jnp.bfloat16)
    for start in range(0, count, unit):
        out_ref[start:start + unit, :] = spread


def unpack_kernel(whole_ref, first_ref, second_ref, first_scr, second_scr, sems):
    copies = []
    for ad in range(3):
        for aw in range(3):
            t = ad * 3 + aw
            pair = whole_ref[t * 32:(t + 1) * 32, :].astype(jnp.float32)
            second_scr[ad, 1, aw] = pair[:, :64]
            second_scr[ad, 2, aw] = pair[:, 64:]
            if t == 8:
                lone = whole_ref[416:432, :].astype(jnp.float32)
                second_scr[ad, 0, aw] = jnp.concatenate([lone[:, :64], lone[:, 64:]], axis=0)
            else:
                start = 288 + (t // 2) * 32
                lone = whole_ref[start:start + 32, :].astype(jnp.float32)
                second_scr[ad, 0, aw] = lone[:, :64] if t % 2 == 0 else lone[:, 64:]
        copies.append(pltpu.make_async_copy(second_scr.at[ad], second_ref.at[ad], sems.at[0, ad]))
        copies[-1].start()
    for ad in range(3):
        for aw in range(3):
            start = 432 + aw * 48 + ad * 16
            tile = whole_ref[start:start + 16, :].astype(jnp.float32)
            for ah in range(3):
                first_scr[ad, ah, aw] = tile[:, ah * 32:(ah + 1) * 32]
        copies.append(pltpu.make_async_copy(first_scr.at[ad], first_ref.at[ad], sems.at[1, ad]))
        copies[-1].start()
    for copy in copies:
        copy.wait()


def call(kernel, outs, args, scratch=(), flops=0):
    whole = pl.BlockSpec(memory_space=pltpu.VMEM)
    scalar = pl.BlockSpec(memory_space=pltpu.SMEM)
    size = sum(a.size * a.dtype.itemsize for a in list(args) + list(outs))
    return pl.pallas_call(
        kernel,
        out_shape=tuple(outs),
        in_specs=[scalar if a.dtype == jnp.int32 else whole for a in args],
        out_specs=(whole,) * len(outs),
        scratch_shapes=list(scratch),
        compiler_params=pltpu.CompilerParams(vmem_limit_bytes=VMEM_BYTES),
        cost_estimate=pl.CostEstimate(flops=flops, bytes_accessed=size, transcendentals=0),
    )(*args)


def array(shape, dtype=jnp.bfloat16):
    return jax.ShapeDtypeStruct(shape, dtype)


def by_tap(kernel):
    return jnp.transpose(kernel, (2, 3, 4, 1, 0))


def prepare(k1, k2, out_grad):
    c0, c1 = k1.shape[3:]
    c2 = k2.shape[4]
    planes = out_grad.shape[2]
    cells = planes * 2 * 64
    og = out_grad.reshape(c2, planes, 2, 32).transpose(2, 0, 1, 3).reshape(2 * c2, planes * 32)
    outs = [
        array((384, 384)),
        array((2 * 4 * c1, 3 * c0 * 16)),
        array((cells, 9 * 2 * c2)),
        array((4 * c1, cells)),
    ]
    scratch = [pltpu.VMEM((4 * c1, 9 * 2 * c2), jnp.bfloat16), pltpu.VMEM((9 * 2 * c2, cells), jnp.bfloat16)]
    return call(prepare_kernel, outs, (k1, k2, og), scratch, flops=2 * 128 * 1152 * cells * 2)


def body(crops, first_kernel, second_kernel, out_grad):
    axes = ("space", "sample")
    devices = lax.axis_size(axes)
    channels_out, planes = out_grad.shape[1:3]
    space = lax.axis_size("space")
    assert space & (space - 1) == 0
    position = lax.axis_index("space").astype(jnp.int32)
    across, near = range(space - 1, space // 2 - 1, -1), range(1, space // 2)
    order = [step for two in zip(across, near) for step in two] + [space // 2]
    early, late = order[:space // 2], order[space // 2:]
    last = sorted({step // 2 for step in order[-3:]})
    first = [m for m in range(space // 2) if m not in last]
    k1, k2 = by_tap(first_kernel), by_tap(second_kernel)
    x = {}
    cut = [lax.dynamic_index_in_dim(crops, position ^ step, 0, keepdims=False) for step in early]
    rest, cut = lax.optimization_barrier((crops, cut))
    for step in [0] + late[::-1] + early:
        if step in early:
            block = cut[early.index(step)]
        else:
            block = lax.dynamic_index_in_dim(rest, position ^ step, 0, keepdims=False)
        if step > 0:
            block = lax.ppermute(block, "space", [(source, source ^ step) for source in range(space)])
        channels_in, two, flat_cells = block.shape
        block = block.reshape(channels_in, two, HEIGHT, WIDTH).transpose(0, 2, 1, 3)
        x[step] = block.reshape(channels_in * two * HEIGHT, WIDTH)
    pick, k1t, ogt, act_grad = prepare(k1, k2, out_grad)
    cells = act_grad.shape[1]
    given = [step for step in order + [0] if step // 2 in first]
    (y,) = call(
        functools.partial(taps_kernel, first, given),
        [array((768, len(first) * 128))],
        [x[step] for step in given] + [pick],
        flops=2 * 256 * 384 * cells,
    )
    given = [step for step in order[::-1] if step // 2 in last]
    rows = -(-TERM_ROWS // (devices * 2)) * 2
    act, terms = call(
        functools.partial(layer_kernel, first, last, given),
        [array((128, cells)), array((devices * rows, LANES))],
        (y, *[x[step] for step in given], pick, k1t, ogt, act_grad),
        scratch=[pltpu.VMEM((768, cells), jnp.bfloat16), pltpu.VMEM((256, cells), jnp.bfloat16)],
        flops=2 * 128 * 4096 * cells,
    )
    blocks = terms.reshape(devices, rows // 2, 2, LANES)
    mine = lax.all_to_all(blocks, axes, split_axis=0, concat_axis=0, tiled=True)
    (features,) = call(
        features_kernel,
        [array((2 * channels_out, planes * 32))],
        (act, k2),
        scratch=[pltpu.VMEM((128, 1152), jnp.bfloat16)],
        flops=2 * 128 * 1152 * cells,
    )
    features = features.reshape(2, channels_out, planes, 32).transpose(1, 2, 0, 3).reshape(out_grad.shape)
    add = functools.partial(add_kernel, rows)
    (spread,) = call(add, [array(terms.shape)], (mine.reshape(terms.shape),))
    spread = spread.reshape(blocks.shape)
    whole = lax.all_to_all(spread, axes, split_axis=0, concat_axis=0, tiled=True)
    shapes = [(3, 3, 3) + kernel.shape[1::-1] for kernel in (first_kernel, second_kernel)]
    first, second = pl.pallas_call(
        unpack_kernel,
        out_shape=[array(shape, jnp.float32) for shape in shapes],
        in_specs=[pl.BlockSpec(memory_space=pltpu.VMEM)],
        out_specs=[pl.BlockSpec(memory_space=pl.ANY)] * 2,
        scratch_shapes=[pltpu.VMEM(shape, jnp.float32) for shape in shapes] + [pltpu.SemaphoreType.DMA((2, 3))],
        compiler_params=pltpu.CompilerParams(vmem_limit_bytes=VMEM_BYTES),
    )(whole.reshape(terms.shape))
    return (features, jnp.transpose(first, (4, 3, 0, 1, 2)), jnp.transpose(second, (4, 3, 0, 1, 2)))


def solution(mesh):
    placed = (P("sample", None, "space", None), P(), P(), P(("sample", "space"), None, None, None))
    return jax.shard_map(
        body,
        mesh=mesh,
        in_specs=placed,
        out_specs=(P(("sample", "space"), None, None, None), P(), P()),
        check_vma=False,
    )
```

```python
import functools
import math

import jax
import jax.numpy as jnp
from jax import lax
from jax.experimental import pallas as pl
from jax.experimental.pallas import tpu as pltpu
from jax.sharding import PartitionSpec as P

HEIGHT = 8
WIDTH = 128
LANES = 128
VMEM_BYTES = 16 * 1024 * 1024
TERM_ROWS = 576


def iota(shape, dim):
    return lax.broadcasted_iota(jnp.int32, shape, dim)


def dot(left, right, dims=((1,), (0,))):
    return lax.dot_general(left, right, (dims, ((), ())), preferred_element_type=jnp.float32)


def ones_where(mask):
    return jnp.where(mask, 1.0, 0.0).astype(jnp.bfloat16)


def band_of_second(k2_ref, k2t_ref):
    channels_mid, channels_out = k2_ref.shape[3:]
    empty = jnp.zeros((channels_mid, channels_out), jnp.bfloat16)
    for ad in range(3):
        for aw in range(3):
            tap = [k2_ref[ad, ah, aw] for ah in range(3)]
            band = ((tap[1], empty), (tap[2], tap[0]), (empty, tap[1]), (empty, tap[2]))
            start = (ad * 3 + aw) * 2 * channels_out
            for hh in range(4):
                k2t_ref[hh * channels_mid:(hh + 1) * channels_mid, start:start + 2 * channels_out] = (
                    jnp.concatenate(band[hh], axis=1))


def upsampling(ad, aw, beyond=0):
    row, col = iota((128, 512), 0), iota((128, 512), 1)
    target = ((row >> 5) << 7) + ((row & 31) << 1) + (64 * (ad - 1) + aw - 1 + 128 * beyond)
    keep = col == target
    if aw == 0:
        keep = keep & ((row & 31) > 0)
    return ones_where(keep)


def prepare_kernel(k1_ref, k2_ref, og_ref, pick_ref, k1t_ref, ogt_ref, ag_ref, k2t_ref, ogu_ref):
    channels_in, channels_mid = k1_ref.shape[3:]
    row, col = iota((3 * WIDTH, 2 * 64), 0), iota((3 * WIDTH, 2 * 64), 1)
    for aw in range(3):
        same = ((row >> 7) & 1) == (col >> 6)
        tap = (row & 127) == 2 * (col & 63) + aw - 1
        pick_ref[:, aw * 128:(aw + 1) * 128] = ones_where(same & tap)
    shape = (9 * channels_in, channels_in * 2 * HEIGHT)
    row, col = iota(shape, 0), iota(shape, 1)
    tap = row >> 4
    ad = jnp.where(tap >= 6, 2, jnp.where(tap >= 3, 1, 0))
    ah, i = tap - 3 * ad, row & 15
    same = i == col >> 4
    h, d = (col >> 1) & 7, col & 1
    taps = []
    for aw in range(3):
        parts = [k1_ref[a, b, aw] for a in range(3) for b in range(3)]
        taps.append(jnp.concatenate(parts, axis=0).astype(jnp.float32).T.astype(jnp.bfloat16))
    for following in range(2):
        plane = (ad == 0) & (d == 1) if following else (ad == d + 1)
        for hh in range(4):
            place = ones_where(same & plane & (h == 2 * hh + ah - 1))
            start = (following * 4 + hh) * channels_mid
            for aw in range(3):
                block = dot(taps[aw], place).astype(jnp.bfloat16)
                k1t_ref[start:start + channels_mid, aw * shape[1]:(aw + 1) * shape[1]] = block
    band_of_second(k2_ref, k2t_ref)
    groups = og_ref.shape[1] // 128
    for ad in range(3):
        for aw in range(3):
            t = ad * 3 + aw
            up = upsampling(ad, aw)
            for g in range(groups):
                value = dot(og_ref[:, g * 128:(g + 1) * 128], up)
                if ad == 0 and g + 1 < groups:
                    value = value + dot(og_ref[:, (g + 1) * 128:(g + 2) * 128], upsampling(ad, aw, 4))
                ogu_ref[t * 128:(t + 1) * 128, g * 512:(g + 1) * 512] = value.astype(jnp.bfloat16)
                ogt_ref[g * 512:(g + 1) * 512, t * 128:(t + 1) * 128] = value.T.astype(jnp.bfloat16)
    for g in range(groups):
        lanes = slice(g * 512, (g + 1) * 512)
        ag_ref[:, lanes] = dot(k2t_ref[...], ogu_ref[:, lanes]).astype(jnp.bfloat16)


def taps_of_pair(first_ref, second_ref, pick_ref):
    parity = lax.axis_index("space") & 1
    pick = pick_ref[pl.ds(pl.multiple_of(parity * WIDTH, WIDTH), 2 * WIDTH), :]
    pair = jnp.concatenate([first_ref[...], second_ref[...]], axis=1)
    return dot(pair, pick).astype(jnp.bfloat16)


def taps_kernel(pairs, given, *refs):
    pick_ref, out_ref = refs[-2:]
    for place, m in enumerate(pairs):
        y = taps_of_pair(refs[given.index(2 * m)], refs[given.index(2 * m + 1)], pick_ref)
        for aw in range(3):
            out_ref[aw * 256:(aw + 1) * 256, place * 128:(place + 1) * 128] = y[:, aw * 128:(aw + 1) * 128]


def layer_kernel(first, last, given, y_ref, *refs):
    pick_ref, k1t_ref, ogt_ref, ag_ref, act_ref, terms_ref, y_scr, pg_scr = refs[len(given):]
    cells = ag_ref.shape[1]
    rows = 256
    here = lax.axis_index("space") >> 1

    def lanes(m):
        return pl.ds(pl.multiple_of(lax.bitwise_xor(here, jnp.int32(m)) * 128, 128), 128)

    for place, m in enumerate(first):
        y_scr[:, lanes(m)] = y_ref[:, place * 128:(place + 1) * 128]
    for m in last:
        y = taps_of_pair(refs[given.index(2 * m)], refs[given.index(2 * m + 1)], pick_ref)
        for aw in range(3):
            y_scr[aw * rows:(aw + 1) * rows, lanes(m)] = y[:, aw * 128:(aw + 1) * 128]
    both = dot(k1t_ref[...], y_scr[...])
    lane = iota((128, cells), 1)
    from_last = jnp.where(lane < 64, 0.0, pltpu.roll(both[128:], 64, 1))
    pre = both[:128] + from_last
    sigma = jax.nn.sigmoid(pre)
    act = (pre * sigma).astype(jnp.bfloat16)
    act_ref[...] = act
    slope = sigma * (1.0 + pre * (1.0 - sigma))
    grad = (ag_ref[...].astype(jnp.float32) * slope).astype(jnp.bfloat16)
    pg_scr[:128, :] = grad
    to_last = pltpu.roll(grad.astype(jnp.float32), cells - 64, 1)
    pg_scr[128:, :] = jnp.where(lane < cells - 64, to_last, 0.0).astype(jnp.bfloat16)

    second = dot(act, ogt_ref[...])
    lane = iota((32, 128), 1)
    held = None
    for t in range(9):
        tile = second[:, t * 128:(t + 1) * 128]
        turned = pltpu.roll(tile, 64, 1)
        mixed = jnp.where(lane < 64, tile[0:32] + turned[64:96], turned[32:64] + tile[96:128])
        terms_ref[t * 32:(t + 1) * 32, :] = mixed.astype(jnp.bfloat16)
        if t % 2 == 0:
            held = jnp.where(lane < 64, turned[32:64], 0.0)
        else:
            held = jnp.where(lane < 64, held, tile[32:64])
        if t % 2 == 1:
            start = 288 + (t // 2) * 32
            terms_ref[start:start + 32, :] = held.astype(jnp.bfloat16)
    terms_ref[416:432, :] = jnp.where(lane[:16] < 64, held[:16], pltpu.roll(held[16:], 64, 1)).astype(jnp.bfloat16)

    first = dot(y_scr[...], pg_scr[...], ((1,), (1,))).astype(jnp.bfloat16)
    shape = (rows, 256)
    h, hh = (iota(shape, 0) >> 1) & 7, (iota(shape, 1) >> 5) & 3
    even, odd = ones_where((h >> 1) == hh), ones_where(((h & 1) == 1) & ((h + 1) >> 1 == hh))
    rank, index = iota((64, rows), 0), iota((64, rows), 1)
    same = ((rank & 15) == index >> 4) & (((rank >> 4) & 1) == (index & 1))
    later_taps = ones_where(same & ((rank >> 5) == ((index >> 1) & 1)))
    first_tap = ones_where(same[:32] & (((index[:32] >> 1) & 1) == 1))
    lane = iota((16, 128), 1)
    for aw in range(3):
        tile = first[aw * rows:(aw + 1) * rows]
        total = jnp.concatenate([dot(first_tap, tile * odd), dot(later_taps, tile * even)], axis=0)
        start = 432 + aw * 48
        for ad in range(3):
            side = slice(128, 256) if ad == 0 else slice(0, 128)
            d = 0 if ad == 1 else 1
            packed = None
            for ah in range(3):
                part = total[ah * 32 + d * 16:ah * 32 + d * 16 + 16, side]
                part = part + pltpu.roll(part, 64, 1)
                part = part + pltpu.roll(part, 32, 1)
                packed = part if packed is None else jnp.where(lane >= ah * 32, part, packed)
            terms_ref[start + ad * 16:start + (ad + 1) * 16, :] = packed.astype(jnp.bfloat16)
    rest = terms_ref.shape[0] - TERM_ROWS
    if rest > 0:
        terms_ref[TERM_ROWS:, :] = jnp.zeros((rest, 128), jnp.bfloat16)


def features_kernel(act_ref, k2_ref, out_ref, k2t_ref):
    band_of_second(k2_ref, k2t_ref)
    groups = out_ref.shape[1] // 128
    for g in range(groups):
        total = jnp.zeros((128, 128), jnp.float32)
        for t in range(9):
            taken = dot(act_ref[:, g * 512:(g + 1) * 512], upsampling(t // 3, t % 3), ((1,), (1,)))
            if t < 3 and g > 0:
                last = act_ref[:, (g - 1) * 512:g * 512]
                taken = taken + dot(last, upsampling(0, t, 4), ((1,), (1,)))
            band = k2t_ref[:, t * 128:(t + 1) * 128]
            total = total + dot(band, taken.astype(jnp.bfloat16), ((0,), (0,)))
        out_ref[:, g * 128:(g + 1) * 128] = total.astype(jnp.bfloat16)


def add_kernel(rows, mine_ref, out_ref):
    count = mine_ref.shape[0]
    unit = rows * 16 // math.gcd(rows, 16)
    total = mine_ref[0:unit, :].astype(jnp.float32)
    for start in range(unit, count, unit):
        total = total + mine_ref[start:start + unit, :].astype(jnp.float32)
    if unit % (2 * rows) == 0 and (unit // 2) % 8 == 0:
        total = total[:unit // 2] + total[unit // 2:]
    parts = [total[start:start + rows] for start in range(0, total.shape[0], rows)]
    total = functools.reduce(jnp.add, parts)
    spread = jnp.concatenate([total] * (unit // rows), axis=0).astype(jnp.bfloat16)
    for start in range(0, count, unit):
        out_ref[start:start + unit, :] = spread


def unpack_kernel(whole_ref, first_ref, second_ref, first_scr, second_scr, sems):
    copies = []
    for ad in range(3):
        for aw in range(3):
            t = ad * 3 + aw
            pair = whole_ref[t * 32:(t + 1) * 32, :].astype(jnp.float32)
            second_scr[ad, 1, aw] = pair[:, :64]
            second_scr[ad, 2, aw] = pair[:, 64:]
            if t == 8:
                lone = whole_ref[416:432, :].astype(jnp.float32)
                second_scr[ad, 0, aw] = jnp.concatenate([lone[:, :64], lone[:, 64:]], axis=0)
            else:
                start = 288 + (t // 2) * 32
                lone = whole_ref[start:start + 32, :].astype(jnp.float32)
                second_scr[ad, 0, aw] = lone[:, :64] if t % 2 == 0 else lone[:, 64:]
        copies.append(pltpu.make_async_copy(second_scr.at[ad], second_ref.at[ad], sems.at[0, ad]))
        copies[-1].start()
    for ad in range(3):
        for aw in range(3):
            start = 432 + aw * 48 + ad * 16
            tile = whole_ref[start:start + 16, :].astype(jnp.float32)
            for ah in range(3):
                first_scr[ad, ah, aw] = tile[:, ah * 32:(ah + 1) * 32]
        copies.append(pltpu.make_async_copy(first_scr.at[ad], first_ref.at[ad], sems.at[1, ad]))
        copies[-1].start()
    for copy in copies:
        copy.wait()


def call(kernel, outs, args, scratch=(), flops=0):
    whole = pl.BlockSpec(memory_space=pltpu.VMEM)
    scalar = pl.BlockSpec(memory_space=pltpu.SMEM)
    size = sum(a.size * a.dtype.itemsize for a in list(args) + list(outs))
    return pl.pallas_call(
        kernel,
        out_shape=tuple(outs),
        in_specs=[scalar if a.dtype == jnp.int32 else whole for a in args],
        out_specs=(whole,) * len(outs),
        scratch_shapes=list(scratch),
        compiler_params=pltpu.CompilerParams(vmem_limit_bytes=VMEM_BYTES),
        cost_estimate=pl.CostEstimate(flops=flops, bytes_accessed=size, transcendentals=0),
    )(*args)


def array(shape, dtype=jnp.bfloat16):
    return jax.ShapeDtypeStruct(shape, dtype)


def by_tap(kernel):
    return jnp.transpose(kernel, (2, 3, 4, 1, 0))


def prepare(k1, k2, out_grad):
    c0, c1 = k1.shape[3:]
    c2 = k2.shape[4]
    planes = out_grad.shape[2]
    cells = planes * 2 * 64
    og = out_grad.reshape(c2, planes, 2, 32).transpose(2, 0, 1, 3).reshape(2 * c2, planes * 32)
    outs = [
        array((384, 384)),
        array((2 * 4 * c1, 3 * c0 * 16)),
        array((cells, 9 * 2 * c2)),
        array((4 * c1, cells)),
    ]
    scratch = [pltpu.VMEM((4 * c1, 9 * 2 * c2), jnp.bfloat16), pltpu.VMEM((9 * 2 * c2, cells), jnp.bfloat16)]
    return call(prepare_kernel, outs, (k1, k2, og), scratch, flops=2 * 128 * 1152 * cells * 2)


def body(crops, first_kernel, second_kernel, out_grad):
    axes = ("space", "sample")
    devices = lax.axis_size(axes)
    channels_out, planes = out_grad.shape[1:3]
    space = lax.axis_size("space")
    assert space & (space - 1) == 0
    position = lax.axis_index("space").astype(jnp.int32)
    across, near = range(space - 1, space // 2 - 1, -1), range(1, space // 2)
    order = [step for two in zip(across, near) for step in two] + [space // 2]
    early, late = order[:2], order[2:]
    last = sorted({step // 2 for step in order[-3:]})
    first = [m for m in range(space // 2) if m not in last]
    k1, k2 = by_tap(first_kernel), by_tap(second_kernel)
    x = {}
    cut = [lax.dynamic_index_in_dim(crops, position ^ step, 0, keepdims=False) for step in early]
    rest, cut = lax.optimization_barrier((crops, cut))
    for step in [0] + late[::-1] + early:
        if step in early:
            block = cut[early.index(step)]
        else:
            block = lax.dynamic_index_in_dim(rest, position ^ step, 0, keepdims=False)
        if step > 0:
            block = lax.ppermute(block, "space", [(source, source ^ step) for source in range(space)])
        channels_in, two, flat_cells = block.shape
        block = block.reshape(channels_in, two, HEIGHT, WIDTH).transpose(0, 2, 1, 3)
        x[step] = block.reshape(channels_in * two * HEIGHT, WIDTH)
    pick, k1t, ogt, act_grad = prepare(k1, k2, out_grad)
    cells = act_grad.shape[1]
    given = [step for step in order + [0] if step // 2 in first]
    (y,) = call(
        functools.partial(taps_kernel, first, given),
        [array((768, len(first) * 128))],
        [x[step] for step in given] + [pick],
        flops=2 * 256 * 384 * cells,
    )
    given = [step for step in order[::-1] if step // 2 in last]
    rows = -(-TERM_ROWS // (devices * 2)) * 2
    act, terms = call(
        functools.partial(layer_kernel, first, last, given),
        [array((128, cells)), array((devices * rows, LANES))],
        (y, *[x[step] for step in given], pick, k1t, ogt, act_grad),
        scratch=[pltpu.VMEM((768, cells), jnp.bfloat16), pltpu.VMEM((256, cells), jnp.bfloat16)],
        flops=2 * 128 * 4096 * cells,
    )
    blocks = terms.reshape(devices, rows // 2, 2, LANES)
    mine = lax.all_to_all(blocks, axes, split_axis=0, concat_axis=0, tiled=True)
    (features,) = call(
        features_kernel,
        [array((2 * channels_out, planes * 32))],
        (act, k2),
        scratch=[pltpu.VMEM((128, 1152), jnp.bfloat16)],
        flops=2 * 128 * 1152 * cells,
    )
    features = features.reshape(2, channels_out, planes, 32).transpose(1, 2, 0, 3).reshape(out_grad.shape)
    add = functools.partial(add_kernel, rows)
    (spread,) = call(add, [array(terms.shape)], (mine.reshape(terms.shape),))
    spread = spread.reshape(blocks.shape)
    whole = lax.all_to_all(spread, axes, split_axis=0, concat_axis=0, tiled=True)
    shapes = [(3, 3, 3) + kernel.shape[1::-1] for kernel in (first_kernel, second_kernel)]
    first, second = pl.pallas_call(
        unpack_kernel,
        out_shape=[array(shape, jnp.float32) for shape in shapes],
        in_specs=[pl.BlockSpec(memory_space=pltpu.VMEM)],
        out_specs=[pl.BlockSpec(memory_space=pl.ANY)] * 2,
        scratch_shapes=[pltpu.VMEM(shape, jnp.float32) for shape in shapes] + [pltpu.SemaphoreType.DMA((2, 3))],
        compiler_params=pltpu.CompilerParams(vmem_limit_bytes=VMEM_BYTES),
    )(whole.reshape(terms.shape))
    return (features, jnp.transpose(first, (4, 3, 0, 1, 2)), jnp.transpose(second, (4, 3, 0, 1, 2)))


def solution(mesh):
    placed = (P("sample", None, "space", None), P(), P(), P(("sample", "space"), None, None, None))
    return jax.shard_map(
        body,
        mesh=mesh,
        in_specs=placed,
        out_specs=(P(("sample", "space"), None, None, None), P(), P()),
        check_vma=False,
    )
```

```python
import functools
import math

import jax
import jax.numpy as jnp
from jax import lax
from jax.experimental import pallas as pl
from jax.experimental.pallas import tpu as pltpu
from jax.sharding import PartitionSpec as P

HEIGHT = 8
WIDTH = 128
LANES = 128
VMEM_BYTES = 16 * 1024 * 1024
TERM_ROWS = 576


def iota(shape, dim):
    return lax.broadcasted_iota(jnp.int32, shape, dim)


def dot(left, right, dims=((1,), (0,))):
    return lax.dot_general(left, right, (dims, ((), ())), preferred_element_type=jnp.float32)


def ones_where(mask):
    return jnp.where(mask, 1.0, 0.0).astype(jnp.bfloat16)


def band_of_second(k2_ref, k2t_ref):
    channels_mid, channels_out = k2_ref.shape[3:]
    empty = jnp.zeros((channels_mid, channels_out), jnp.bfloat16)
    for ad in range(3):
        for aw in range(3):
            tap = [k2_ref[ad, ah, aw] for ah in range(3)]
            band = ((tap[1], empty), (tap[2], tap[0]), (empty, tap[1]), (empty, tap[2]))
            start = (ad * 3 + aw) * 2 * channels_out
            for hh in range(4):
                k2t_ref[hh * channels_mid:(hh + 1) * channels_mid, start:start + 2 * channels_out] = (
                    jnp.concatenate(band[hh], axis=1))


def upsampling(ad, aw, beyond=0):
    row, col = iota((128, 512), 0), iota((128, 512), 1)
    target = ((row >> 5) << 7) + ((row & 31) << 1) + (64 * (ad - 1) + aw - 1 + 128 * beyond)
    keep = col == target
    if aw == 0:
        keep = keep & ((row & 31) > 0)
    return ones_where(keep)


def prepare_kernel(k1_ref, k2_ref, og_ref, pick_ref, k1t_ref, ogt_ref, ag_ref, k2t_ref, ogu_ref):
    channels_in, channels_mid = k1_ref.shape[3:]
    row, col = iota((3 * WIDTH, 2 * 64), 0), iota((3 * WIDTH, 2 * 64), 1)
    for aw in range(3):
        same = ((row >> 7) & 1) == (col >> 6)
        tap = (row & 127) == 2 * (col & 63) + aw - 1
        pick_ref[:, aw * 128:(aw + 1) * 128] = ones_where(same & tap)
    shape = (9 * channels_in, channels_in * 2 * HEIGHT)
    row, col = iota(shape, 0), iota(shape, 1)
    tap = row >> 4
    ad = jnp.where(tap >= 6, 2, jnp.where(tap >= 3, 1, 0))
    ah, i = tap - 3 * ad, row & 15
    same = i == col >> 4
    h, d = (col >> 1) & 7, col & 1
    taps = []
    for aw in range(3):
        parts = [k1_ref[a, b, aw] for a in range(3) for b in range(3)]
        taps.append(jnp.concatenate(parts, axis=0).astype(jnp.float32).T.astype(jnp.bfloat16))
    for following in range(2):
        plane = (ad == 0) & (d == 1) if following else (ad == d + 1)
        for hh in range(4):
            place = ones_where(same & plane & (h == 2 * hh + ah - 1))
            start = (following * 4 + hh) * channels_mid
            for aw in range(3):
                block = dot(taps[aw], place).astype(jnp.bfloat16)
                k1t_ref[start:start + channels_mid, aw * shape[1]:(aw + 1) * shape[1]] = block
    band_of_second(k2_ref, k2t_ref)
    groups = og_ref.shape[1] // 128
    for ad in range(3):
        for aw in range(3):
            t = ad * 3 + aw
            up = upsampling(ad, aw)
            for g in range(groups):
                value = dot(og_ref[:, g * 128:(g + 1) * 128], up)
                if ad == 0 and g + 1 < groups:
                    value = value + dot(og_ref[:, (g + 1) * 128:(g + 2) * 128], upsampling(ad, aw, 4))
                ogu_ref[t * 128:(t + 1) * 128, g * 512:(g + 1) * 512] = value.astype(jnp.bfloat16)
                ogt_ref[g * 512:(g + 1) * 512, t * 128:(t + 1) * 128] = value.T.astype(jnp.bfloat16)
    for g in range(groups):
        lanes = slice(g * 512, (g + 1) * 512)
        ag_ref[:, lanes] = dot(k2t_ref[...], ogu_ref[:, lanes]).astype(jnp.bfloat16)


def taps_of_pair(first_ref, second_ref, pick_ref):
    parity = lax.axis_index("space") & 1
    pick = pick_ref[pl.ds(pl.multiple_of(parity * WIDTH, WIDTH), 2 * WIDTH), :]
    pair = jnp.concatenate([first_ref[...], second_ref[...]], axis=1)
    return dot(pair, pick).astype(jnp.bfloat16)


def taps_kernel(pairs, given, *refs):
    pick_ref, out_ref = refs[-2:]
    for place, m in enumerate(pairs):
        y = taps_of_pair(refs[given.index(2 * m)], refs[given.index(2 * m + 1)], pick_ref)
        for aw in range(3):
            out_ref[aw * 256:(aw + 1) * 256, place * 128:(place + 1) * 128] = y[:, aw * 128:(aw + 1) * 128]


def layer_kernel(first, last, given, y_ref, *refs):
    pick_ref, k1t_ref, ogt_ref, ag_ref, act_ref, terms_ref, y_scr, pg_scr = refs[len(given):]
    cells = ag_ref.shape[1]
    rows = 256
    here = lax.axis_index("space") >> 1

    def lanes(m):
        return pl.ds(pl.multiple_of(lax.bitwise_xor(here, jnp.int32(m)) * 128, 128), 128)

    for place, m in enumerate(first):
        y_scr[:, lanes(m)] = y_ref[:, place * 128:(place + 1) * 128]
    for m in last:
        y = taps_of_pair(refs[given.index(2 * m)], refs[given.index(2 * m + 1)], pick_ref)
        for aw in range(3):
            y_scr[aw * rows:(aw + 1) * rows, lanes(m)] = y[:, aw * 128:(aw + 1) * 128]
    both = dot(k1t_ref[...], y_scr[...])
    lane = iota((128, cells), 1)
    from_last = jnp.where(lane < 64, 0.0, pltpu.roll(both[128:], 64, 1))
    pre = both[:128] + from_last
    sigma = jax.nn.sigmoid(pre)
    act = (pre * sigma).astype(jnp.bfloat16)
    act_ref[...] = act
    slope = sigma * (1.0 + pre * (1.0 - sigma))
    grad = (ag_ref[...].astype(jnp.float32) * slope).astype(jnp.bfloat16)
    pg_scr[:128, :] = grad
    to_last = pltpu.roll(grad.astype(jnp.float32), cells - 64, 1)
    pg_scr[128:, :] = jnp.where(lane < cells - 64, to_last, 0.0).astype(jnp.bfloat16)

    second = dot(act, ogt_ref[...])
    lane = iota((32, 128), 1)
    held = None
    for t in range(9):
        tile = second[:, t * 128:(t + 1) * 128]
        turned = pltpu.roll(tile, 64, 1)
        mixed = jnp.where(lane < 64, tile[0:32] + turned[64:96], turned[32:64] + tile[96:128])
        terms_ref[t * 32:(t + 1) * 32, :] = mixed.astype(jnp.bfloat16)
        if t % 2 == 0:
            held = jnp.where(lane < 64, turned[32:64], 0.0)
        else:
            held = jnp.where(lane < 64, held, tile[32:64])
        if t % 2 == 1:
            start = 288 + (t // 2) * 32
            terms_ref[start:start + 32, :] = held.astype(jnp.bfloat16)
    terms_ref[416:432, :] = jnp.where(lane[:16] < 64, held[:16], pltpu.roll(held[16:], 64, 1)).astype(jnp.bfloat16)

    first = dot(y_scr[...], pg_scr[...], ((1,), (1,))).astype(jnp.bfloat16)
    shape = (rows, 256)
    h, hh = (iota(shape, 0) >> 1) & 7, (iota(shape, 1) >> 5) & 3
    even, odd = ones_where((h >> 1) == hh), ones_where(((h & 1) == 1) & ((h + 1) >> 1 == hh))
    rank, index = iota((64, rows), 0), iota((64, rows), 1)
    same = ((rank & 15) == index >> 4) & (((rank >> 4) & 1) == (index & 1))
    later_taps = ones_where(same & ((rank >> 5) == ((index >> 1) & 1)))
    first_tap = ones_where(same[:32] & (((index[:32] >> 1) & 1) == 1))
    lane = iota((16, 128), 1)
    for aw in range(3):
        tile = first[aw * rows:(aw + 1) * rows]
        total = jnp.concatenate([dot(first_tap, tile * odd), dot(later_taps, tile * even)], axis=0)
        start = 432 + aw * 48
        for ad in range(3):
            side = slice(128, 256) if ad == 0 else slice(0, 128)
            d = 0 if ad == 1 else 1
            packed = None
            for ah in range(3):
                part = total[ah * 32 + d * 16:ah * 32 + d * 16 + 16, side]
                part = part + pltpu.roll(part, 64, 1)
                part = part + pltpu.roll(part, 32, 1)
                packed = part if packed is None else jnp.where(lane >= ah * 32, part, packed)
            terms_ref[start + ad * 16:start + (ad + 1) * 16, :] = packed.astype(jnp.bfloat16)
    rest = terms_ref.shape[0] - TERM_ROWS
    if rest > 0:
        terms_ref[TERM_ROWS:, :] = jnp.zeros((rest, 128), jnp.bfloat16)


def features_kernel(act_ref, k2_ref, out_ref, k2t_ref):
    band_of_second(k2_ref, k2t_ref)
    groups = out_ref.shape[1] // 128
    for g in range(groups):
        total = jnp.zeros((128, 128), jnp.float32)
        for t in range(9):
            taken = dot(act_ref[:, g * 512:(g + 1) * 512], upsampling(t // 3, t % 3), ((1,), (1,)))
            if t < 3 and g > 0:
                last = act_ref[:, (g - 1) * 512:g * 512]
                taken = taken + dot(last, upsampling(0, t, 4), ((1,), (1,)))
            band = k2t_ref[:, t * 128:(t + 1) * 128]
            total = total + dot(band, taken.astype(jnp.bfloat16), ((0,), (0,)))
        out_ref[:, g * 128:(g + 1) * 128] = total.astype(jnp.bfloat16)


def add_kernel(rows, mine_ref, out_ref):
    count = mine_ref.shape[0]
    unit = rows * 16 // math.gcd(rows, 16)
    total = mine_ref[0:unit, :].astype(jnp.float32)
    for start in range(unit, count, unit):
        total = total + mine_ref[start:start + unit, :].astype(jnp.float32)
    if unit % (2 * rows) == 0 and (unit // 2) % 8 == 0:
        total = total[:unit // 2] + total[unit // 2:]
    parts = [total[start:start + rows] for start in range(0, total.shape[0], rows)]
    total = functools.reduce(jnp.add, parts)
    spread = jnp.concatenate([total] * (unit // rows), axis=0).astype(jnp.bfloat16)
    for start in range(0, count, unit):
        out_ref[start:start + unit, :] = spread


def unpack_kernel(whole_ref, first_ref, second_ref, first_scr, second_scr, sems):
    copies = []
    for ad in range(3):
        for aw in range(3):
            t = ad * 3 + aw
            pair = whole_ref[t * 32:(t + 1) * 32, :].astype(jnp.float32)
            second_scr[ad, 1, aw] = pair[:, :64]
            second_scr[ad, 2, aw] = pair[:, 64:]
            if t == 8:
                lone = whole_ref[416:432, :].astype(jnp.float32)
                second_scr[ad, 0, aw] = jnp.concatenate([lone[:, :64], lone[:, 64:]], axis=0)
            else:
                start = 288 + (t // 2) * 32
                lone = whole_ref[start:start + 32, :].astype(jnp.float32)
                second_scr[ad, 0, aw] = lone[:, :64] if t % 2 == 0 else lone[:, 64:]
        copies.append(pltpu.make_async_copy(second_scr.at[ad], second_ref.at[ad], sems.at[0, ad]))
        copies[-1].start()
    for ad in range(3):
        for aw in range(3):
            start = 432 + aw * 48 + ad * 16
            tile = whole_ref[start:start + 16, :].astype(jnp.float32)
            for ah in range(3):
                first_scr[ad, ah, aw] = tile[:, ah * 32:(ah + 1) * 32]
        copies.append(pltpu.make_async_copy(first_scr.at[ad], first_ref.at[ad], sems.at[1, ad]))
        copies[-1].start()
    for copy in copies:
        copy.wait()


def call(kernel, outs, args, scratch=(), flops=0):
    whole = pl.BlockSpec(memory_space=pltpu.VMEM)
    scalar = pl.BlockSpec(memory_space=pltpu.SMEM)
    size = sum(a.size * a.dtype.itemsize for a in list(args) + list(outs))
    return pl.pallas_call(
        kernel,
        out_shape=tuple(outs),
        in_specs=[scalar if a.dtype == jnp.int32 else whole for a in args],
        out_specs=(whole,) * len(outs),
        scratch_shapes=list(scratch),
        compiler_params=pltpu.CompilerParams(vmem_limit_bytes=VMEM_BYTES),
        cost_estimate=pl.CostEstimate(flops=flops, bytes_accessed=size, transcendentals=0),
    )(*args)


def array(shape, dtype=jnp.bfloat16):
    return jax.ShapeDtypeStruct(shape, dtype)


def by_tap(kernel):
    return jnp.transpose(kernel, (2, 3, 4, 1, 0))


def prepare(k1, k2, out_grad):
    c0, c1 = k1.shape[3:]
    c2 = k2.shape[4]
    planes = out_grad.shape[2]
    cells = planes * 2 * 64
    og = out_grad.reshape(c2, planes, 2, 32).transpose(2, 0, 1, 3).reshape(2 * c2, planes * 32)
    outs = [
        array((384, 384)),
        array((2 * 4 * c1, 3 * c0 * 16)),
        array((cells, 9 * 2 * c2)),
        array((4 * c1, cells)),
    ]
    scratch = [pltpu.VMEM((4 * c1, 9 * 2 * c2), jnp.bfloat16), pltpu.VMEM((9 * 2 * c2, cells), jnp.bfloat16)]
    return call(prepare_kernel, outs, (k1, k2, og), scratch, flops=2 * 128 * 1152 * cells * 2)


def body(crops, first_kernel, second_kernel, out_grad):
    axes = ("space", "sample")
    devices = lax.axis_size(axes)
    channels_out, planes = out_grad.shape[1:3]
    space = lax.axis_size("space")
    assert space & (space - 1) == 0
    position = lax.axis_index("space").astype(jnp.int32)
    across, near = range(space - 1, space // 2 - 1, -1), range(1, space // 2)
    order = [step for two in zip(across, near) for step in two] + [space // 2]
    early, late = order[:2], order[2:]
    last = sorted({step // 2 for step in order[-3:]})
    first = [m for m in range(space // 2) if m not in last]
    k1, k2 = by_tap(first_kernel), by_tap(second_kernel)
    x = {}
    cut = [lax.dynamic_index_in_dim(crops, position ^ step, 0, keepdims=False) for step in early]
    rest, cut = lax.optimization_barrier((crops, cut))
    for step in [0] + late[::-1] + early:
        if step in early:
            block = cut[early.index(step)]
        else:
            block = lax.dynamic_index_in_dim(rest, position ^ step, 0, keepdims=False)
        if step > 0:
            block = lax.ppermute(block, "space", [(source, source ^ step) for source in range(space)])
        channels_in, two, flat_cells = block.shape
        block = block.reshape(channels_in, two, HEIGHT, WIDTH).transpose(0, 2, 1, 3)
        x[step] = block.reshape(channels_in * two * HEIGHT, WIDTH)
    pick, k1t, ogt, act_grad = prepare(k1, k2, out_grad)
    cells = act_grad.shape[1]
    given = [step for step in order + [0] if step // 2 in first]
    (y,) = call(
        functools.partial(taps_kernel, first, given),
        [array((768, len(first) * 128))],
        [x[step] for step in given] + [pick],
        flops=2 * 256 * 384 * cells,
    )
    given = [step for step in order[-2:] + order[-3::-1] if step // 2 in last]
    rows = -(-TERM_ROWS // (devices * 2)) * 2
    act, terms = call(
        functools.partial(layer_kernel, first, last, given),
        [array((128, cells)), array((devices * rows, LANES))],
        (y, *[x[step] for step in given], pick, k1t, ogt, act_grad),
        scratch=[pltpu.VMEM((768, cells), jnp.bfloat16), pltpu.VMEM((256, cells), jnp.bfloat16)],
        flops=2 * 128 * 4096 * cells,
    )
    blocks = terms.reshape(devices, rows // 2, 2, LANES)
    mine = lax.all_to_all(blocks, axes, split_axis=0, concat_axis=0, tiled=True)
    (features,) = call(
        features_kernel,
        [array((2 * channels_out, planes * 32))],
        (act, k2),
        scratch=[pltpu.VMEM((128, 1152), jnp.bfloat16)],
        flops=2 * 128 * 1152 * cells,
    )
    features = features.reshape(2, channels_out, planes, 32).transpose(1, 2, 0, 3).reshape(out_grad.shape)
    add = functools.partial(add_kernel, rows)
    (spread,) = call(add, [array(terms.shape)], (mine.reshape(terms.shape),))
    spread = spread.reshape(blocks.shape)
    whole = lax.all_to_all(spread, axes, split_axis=0, concat_axis=0, tiled=True)
    shapes = [(3, 3, 3) + kernel.shape[1::-1] for kernel in (first_kernel, second_kernel)]
    first, second = pl.pallas_call(
        unpack_kernel,
        out_shape=[array(shape, jnp.float32) for shape in shapes],
        in_specs=[pl.BlockSpec(memory_space=pltpu.VMEM)],
        out_specs=[pl.BlockSpec(memory_space=pl.ANY)] * 2,
        scratch_shapes=[pltpu.VMEM(shape, jnp.float32) for shape in shapes] + [pltpu.SemaphoreType.DMA((2, 3))],
        compiler_params=pltpu.CompilerParams(vmem_limit_bytes=VMEM_BYTES),
    )(whole.reshape(terms.shape))
    return (features, jnp.transpose(first, (4, 3, 0, 1, 2)), jnp.transpose(second, (4, 3, 0, 1, 2)))


def solution(mesh):
    placed = (P("sample", None, "space", None), P(), P(), P(("sample", "space"), None, None, None))
    return jax.shard_map(
        body,
        mesh=mesh,
        in_specs=placed,
        out_specs=(P(("sample", "space"), None, None, None), P(), P()),
        check_vma=False,
    )
```

```python
import functools
import math

import jax
import jax.numpy as jnp
from jax import lax
from jax.experimental import pallas as pl
from jax.experimental.pallas import tpu as pltpu
from jax.sharding import PartitionSpec as P

HEIGHT = 8
WIDTH = 128
LANES = 128
VMEM_BYTES = 16 * 1024 * 1024
TERM_ROWS = 576


def iota(shape, dim):
    return lax.broadcasted_iota(jnp.int32, shape, dim)


def dot(left, right, dims=((1,), (0,))):
    return lax.dot_general(left, right, (dims, ((), ())), preferred_element_type=jnp.float32)


def ones_where(mask):
    return jnp.where(mask, 1.0, 0.0).astype(jnp.bfloat16)


def band_of_second(k2_ref, k2t_ref):
    channels_mid, channels_out = k2_ref.shape[3:]
    empty = jnp.zeros((channels_mid, channels_out), jnp.bfloat16)
    for ad in range(3):
        for aw in range(3):
            tap = [k2_ref[ad, ah, aw] for ah in range(3)]
            band = ((tap[1], empty), (tap[2], tap[0]), (empty, tap[1]), (empty, tap[2]))
            start = (ad * 3 + aw) * 2 * channels_out
            for hh in range(4):
                k2t_ref[hh * channels_mid:(hh + 1) * channels_mid, start:start + 2 * channels_out] = (
                    jnp.concatenate(band[hh], axis=1))


def upsampling(ad, aw, beyond=0):
    row, col = iota((128, 512), 0), iota((128, 512), 1)
    target = ((row >> 5) << 7) + ((row & 31) << 1) + (64 * (ad - 1) + aw - 1 + 128 * beyond)
    keep = col == target
    if aw == 0:
        keep = keep & ((row & 31) > 0)
    return ones_where(keep)


def prepare_kernel(k1_ref, k2_ref, og_ref, pick_ref, k1t_ref, ogt_ref, ag_ref, k2t_ref, ogu_ref):
    channels_in, channels_mid = k1_ref.shape[3:]
    row, col = iota((3 * WIDTH, 2 * 64), 0), iota((3 * WIDTH, 2 * 64), 1)
    for aw in range(3):
        same = ((row >> 7) & 1) == (col >> 6)
        tap = (row & 127) == 2 * (col & 63) + aw - 1
        pick_ref[:, aw * 128:(aw + 1) * 128] = ones_where(same & tap)
    shape = (9 * channels_in, channels_in * 2 * HEIGHT)
    row, col = iota(shape, 0), iota(shape, 1)
    tap = row >> 4
    ad = jnp.where(tap >= 6, 2, jnp.where(tap >= 3, 1, 0))
    ah, i = tap - 3 * ad, row & 15
    same = i == col >> 4
    h, d = (col >> 1) & 7, col & 1
    taps = []
    for aw in range(3):
        parts = [k1_ref[a, b, aw] for a in range(3) for b in range(3)]
        taps.append(jnp.concatenate(parts, axis=0).astype(jnp.float32).T.astype(jnp.bfloat16))
    for following in range(2):
        plane = (ad == 0) & (d == 1) if following else (ad == d + 1)
        for hh in range(4):
            place = ones_where(same & plane & (h == 2 * hh + ah - 1))
            start = (following * 4 + hh) * channels_mid
            for aw in range(3):
                block = dot(taps[aw], place).astype(jnp.bfloat16)
                k1t_ref[start:start + channels_mid, aw * shape[1]:(aw + 1) * shape[1]] = block
    band_of_second(k2_ref, k2t_ref)
    groups = og_ref.shape[1] // 128
    for ad in range(3):
        for aw in range(3):
            t = ad * 3 + aw
            up = upsampling(ad, aw)
            for g in range(groups):
                value = dot(og_ref[:, g * 128:(g + 1) * 128], up)
                if ad == 0 and g + 1 < groups:
                    value = value + dot(og_ref[:, (g + 1) * 128:(g + 2) * 128], upsampling(ad, aw, 4))
                ogu_ref[t * 128:(t + 1) * 128, g * 512:(g + 1) * 512] = value.astype(jnp.bfloat16)
                ogt_ref[g * 512:(g + 1) * 512, t * 128:(t + 1) * 128] = value.T.astype(jnp.bfloat16)
    for g in range(groups):
        lanes = slice(g * 512, (g + 1) * 512)
        ag_ref[:, lanes] = dot(k2t_ref[...], ogu_ref[:, lanes]).astype(jnp.bfloat16)


def taps_of_pair(first_ref, second_ref, pick_ref):
    parity = lax.axis_index("space") & 1
    pick = pick_ref[pl.ds(pl.multiple_of(parity * WIDTH, WIDTH), 2 * WIDTH), :]
    pair = jnp.concatenate([first_ref[...], second_ref[...]], axis=1)
    return dot(pair, pick).astype(jnp.bfloat16)


def taps_kernel(pairs, given, *refs):
    pick_ref, out_ref = refs[-2:]
    for place, m in enumerate(pairs):
        y = taps_of_pair(refs[given.index(2 * m)], refs[given.index(2 * m + 1)], pick_ref)
        for aw in range(3):
            out_ref[aw * 256:(aw + 1) * 256, place * 128:(place + 1) * 128] = y[:, aw * 128:(aw + 1) * 128]


def layer_kernel(first, last, given, y_ref, *refs):
    pick_ref, k1t_ref, ogt_ref, ag_ref, act_ref, terms_ref, y_scr, pg_scr = refs[len(given):]
    cells = ag_ref.shape[1]
    rows = 256
    here = lax.axis_index("space") >> 1

    def lanes(m):
        return pl.ds(pl.multiple_of(lax.bitwise_xor(here, jnp.int32(m)) * 128, 128), 128)

    for place, m in enumerate(first):
        y_scr[:, lanes(m)] = y_ref[:, place * 128:(place + 1) * 128]
    for m in last:
        y = taps_of_pair(refs[given.index(2 * m)], refs[given.index(2 * m + 1)], pick_ref)
        for aw in range(3):
            y_scr[aw * rows:(aw + 1) * rows, lanes(m)] = y[:, aw * 128:(aw + 1) * 128]
    both = dot(k1t_ref[...], y_scr[...])
    lane = iota((128, cells), 1)
    from_last = jnp.where(lane < 64, 0.0, pltpu.roll(both[128:], 64, 1))
    pre = both[:128] + from_last
    sigma = jax.nn.sigmoid(pre)
    act = (pre * sigma).astype(jnp.bfloat16)
    act_ref[...] = act
    slope = sigma * (1.0 + pre * (1.0 - sigma))
    grad = (ag_ref[...].astype(jnp.float32) * slope).astype(jnp.bfloat16)
    pg_scr[:128, :] = grad
    to_last = pltpu.roll(grad.astype(jnp.float32), cells - 64, 1)
    pg_scr[128:, :] = jnp.where(lane < cells - 64, to_last, 0.0).astype(jnp.bfloat16)

    second = dot(act, ogt_ref[...])
    lane = iota((32, 128), 1)
    held = None
    for t in range(9):
        tile = second[:, t * 128:(t + 1) * 128]
        turned = pltpu.roll(tile, 64, 1)
        mixed = jnp.where(lane < 64, tile[0:32] + turned[64:96], turned[32:64] + tile[96:128])
        terms_ref[t * 32:(t + 1) * 32, :] = mixed.astype(jnp.bfloat16)
        if t % 2 == 0:
            held = jnp.where(lane < 64, turned[32:64], 0.0)
        else:
            held = jnp.where(lane < 64, held, tile[32:64])
        if t % 2 == 1:
            start = 288 + (t // 2) * 32
            terms_ref[start:start + 32, :] = held.astype(jnp.bfloat16)
    terms_ref[416:432, :] = jnp.where(lane[:16] < 64, held[:16], pltpu.roll(held[16:], 64, 1)).astype(jnp.bfloat16)

    first = dot(y_scr[...], pg_scr[...], ((1,), (1,))).astype(jnp.bfloat16)
    shape = (rows, 256)
    h, hh = (iota(shape, 0) >> 1) & 7, (iota(shape, 1) >> 5) & 3
    even, odd = ones_where((h >> 1) == hh), ones_where(((h & 1) == 1) & ((h + 1) >> 1 == hh))
    rank, index = iota((64, rows), 0), iota((64, rows), 1)
    same = ((rank & 15) == index >> 4) & (((rank >> 4) & 1) == (index & 1))
    later_taps = ones_where(same & ((rank >> 5) == ((index >> 1) & 1)))
    first_tap = ones_where(same[:32] & (((index[:32] >> 1) & 1) == 1))
    lane = iota((16, 128), 1)
    for aw in range(3):
        tile = first[aw * rows:(aw + 1) * rows]
        total = jnp.concatenate([dot(first_tap, tile * odd), dot(later_taps, tile * even)], axis=0)
        start = 432 + aw * 48
        for ad in range(3):
            side = slice(128, 256) if ad == 0 else slice(0, 128)
            d = 0 if ad == 1 else 1
            packed = None
            for ah in range(3):
                part = total[ah * 32 + d * 16:ah * 32 + d * 16 + 16, side]
                part = part + pltpu.roll(part, 64, 1)
                part = part + pltpu.roll(part, 32, 1)
                packed = part if packed is None else jnp.where(lane >= ah * 32, part, packed)
            terms_ref[start + ad * 16:start + (ad + 1) * 16, :] = packed.astype(jnp.bfloat16)
    rest = terms_ref.shape[0] - TERM_ROWS
    if rest > 0:
        terms_ref[TERM_ROWS:, :] = jnp.zeros((rest, 128), jnp.bfloat16)


def features_kernel(act_ref, k2_ref, out_ref, k2t_ref):
    band_of_second(k2_ref, k2t_ref)
    groups = out_ref.shape[1] // 128
    for g in range(groups):
        total = jnp.zeros((128, 128), jnp.float32)
        for t in range(9):
            taken = dot(act_ref[:, g * 512:(g + 1) * 512], upsampling(t // 3, t % 3), ((1,), (1,)))
            if t < 3 and g > 0:
                last = act_ref[:, (g - 1) * 512:g * 512]
                taken = taken + dot(last, upsampling(0, t, 4), ((1,), (1,)))
            band = k2t_ref[:, t * 128:(t + 1) * 128]
            total = total + dot(band, taken.astype(jnp.bfloat16), ((0,), (0,)))
        out_ref[:, g * 128:(g + 1) * 128] = total.astype(jnp.bfloat16)


def add_kernel(rows, mine_ref, out_ref):
    count = mine_ref.shape[0]
    unit = rows * 16 // math.gcd(rows, 16)
    total = mine_ref[0:unit, :].astype(jnp.float32)
    for start in range(unit, count, unit):
        total = total + mine_ref[start:start + unit, :].astype(jnp.float32)
    if unit % (2 * rows) == 0 and (unit // 2) % 8 == 0:
        total = total[:unit // 2] + total[unit // 2:]
    parts = [total[start:start + rows] for start in range(0, total.shape[0], rows)]
    total = functools.reduce(jnp.add, parts)
    spread = jnp.concatenate([total] * (unit // rows), axis=0).astype(jnp.bfloat16)
    for start in range(0, count, unit):
        out_ref[start:start + unit, :] = spread


def unpack_kernel(whole_ref, first_ref, second_ref, first_scr, second_scr, sems):
    copies = []
    for ad in range(3):
        for aw in range(3):
            t = ad * 3 + aw
            pair = whole_ref[t * 32:(t + 1) * 32, :].astype(jnp.float32)
            second_scr[ad, 1, aw] = pair[:, :64]
            second_scr[ad, 2, aw] = pair[:, 64:]
            if t == 8:
                lone = whole_ref[416:432, :].astype(jnp.float32)
                second_scr[ad, 0, aw] = jnp.concatenate([lone[:, :64], lone[:, 64:]], axis=0)
            else:
                start = 288 + (t // 2) * 32
                lone = whole_ref[start:start + 32, :].astype(jnp.float32)
                second_scr[ad, 0, aw] = lone[:, :64] if t % 2 == 0 else lone[:, 64:]
        copies.append(pltpu.make_async_copy(second_scr.at[ad], second_ref.at[ad], sems.at[0, ad]))
        copies[-1].start()
    for ad in range(3):
        for aw in range(3):
            start = 432 + aw * 48 + ad * 16
            tile = whole_ref[start:start + 16, :].astype(jnp.float32)
            for ah in range(3):
                first_scr[ad, ah, aw] = tile[:, ah * 32:(ah + 1) * 32]
        copies.append(pltpu.make_async_copy(first_scr.at[ad], first_ref.at[ad], sems.at[1, ad]))
        copies[-1].start()
    for copy in copies:
        copy.wait()


def call(kernel, outs, args, scratch=(), flops=0):
    whole = pl.BlockSpec(memory_space=pltpu.VMEM)
    scalar = pl.BlockSpec(memory_space=pltpu.SMEM)
    size = sum(a.size * a.dtype.itemsize for a in list(args) + list(outs))
    return pl.pallas_call(
        kernel,
        out_shape=tuple(outs),
        in_specs=[scalar if a.dtype == jnp.int32 else whole for a in args],
        out_specs=(whole,) * len(outs),
        scratch_shapes=list(scratch),
        compiler_params=pltpu.CompilerParams(vmem_limit_bytes=VMEM_BYTES),
        cost_estimate=pl.CostEstimate(flops=flops, bytes_accessed=size, transcendentals=0),
    )(*args)


def array(shape, dtype=jnp.bfloat16):
    return jax.ShapeDtypeStruct(shape, dtype)


def by_tap(kernel):
    return jnp.transpose(kernel, (2, 3, 4, 1, 0))


def prepare(k1, k2, out_grad):
    c0, c1 = k1.shape[3:]
    c2 = k2.shape[4]
    planes = out_grad.shape[2]
    cells = planes * 2 * 64
    og = out_grad.reshape(c2, planes, 2, 32).transpose(2, 0, 1, 3).reshape(2 * c2, planes * 32)
    outs = [
        array((384, 384)),
        array((2 * 4 * c1, 3 * c0 * 16)),
        array((cells, 9 * 2 * c2)),
        array((4 * c1, cells)),
    ]
    scratch = [pltpu.VMEM((4 * c1, 9 * 2 * c2), jnp.bfloat16), pltpu.VMEM((9 * 2 * c2, cells), jnp.bfloat16)]
    return call(prepare_kernel, outs, (k1, k2, og), scratch, flops=2 * 128 * 1152 * cells * 2)


def body(crops, first_kernel, second_kernel, out_grad):
    axes = ("space", "sample")
    devices = lax.axis_size(axes)
    channels_out, planes = out_grad.shape[1:3]
    space = lax.axis_size("space")
    assert space & (space - 1) == 0
    position = lax.axis_index("space").astype(jnp.int32)
    across, near = range(space - 1, space // 2 - 1, -1), range(1, space // 2)
    order = [step for two in zip(across, near) for step in two] + [space // 2]
    early, late = order[:2], order[2:]
    last = sorted({step // 2 for step in order[-3:]})
    first = [m for m in range(space // 2) if m not in last]
    k1, k2 = by_tap(first_kernel), by_tap(second_kernel)
    x = {}
    cut = [lax.dynamic_index_in_dim(crops, position ^ step, 0, keepdims=False) for step in early]
    rest, cut = lax.optimization_barrier((crops, cut))
    for step in [0] + late[::-1] + early:
        if step in early:
            block = cut[early.index(step)]
        else:
            block = lax.dynamic_index_in_dim(rest, position ^ step, 0, keepdims=False)
        if step > 0:
            block = lax.ppermute(block, "space", [(source, source ^ step) for source in range(space)])
        channels_in, two, flat_cells = block.shape
        block = block.reshape(channels_in, two, HEIGHT, WIDTH).transpose(0, 2, 1, 3)
        x[step] = block.reshape(channels_in * two * HEIGHT, WIDTH)
    pick, k1t, ogt, act_grad = prepare(k1, k2, out_grad)
    cells = act_grad.shape[1]
    given = [step for step in order + [0] if step // 2 in first]
    (y,) = call(
        functools.partial(taps_kernel, first, given),
        [array((768, len(first) * 128))],
        [x[step] for step in given] + [pick],
        flops=2 * 256 * 384 * cells,
    )
    given = [step for step in sorted(order) if step // 2 in last]
    rows = -(-TERM_ROWS // (devices * 2)) * 2
    act, terms = call(
        functools.partial(layer_kernel, first, last, given),
        [array((128, cells)), array((devices * rows, LANES))],
        (y, *[x[step] for step in given], pick, k1t, ogt, act_grad),
        scratch=[pltpu.VMEM((768, cells), jnp.bfloat16), pltpu.VMEM((256, cells), jnp.bfloat16)],
        flops=2 * 128 * 4096 * cells,
    )
    blocks = terms.reshape(devices, rows // 2, 2, LANES)
    mine = lax.all_to_all(blocks, axes, split_axis=0, concat_axis=0, tiled=True)
    (features,) = call(
        features_kernel,
        [array((2 * channels_out, planes * 32))],
        (act, k2),
        scratch=[pltpu.VMEM((128, 1152), jnp.bfloat16)],
        flops=2 * 128 * 1152 * cells,
    )
    features = features.reshape(2, channels_out, planes, 32).transpose(1, 2, 0, 3).reshape(out_grad.shape)
    add = functools.partial(add_kernel, rows)
    (spread,) = call(add, [array(terms.shape)], (mine.reshape(terms.shape),))
    spread = spread.reshape(blocks.shape)
    whole = lax.all_to_all(spread, axes, split_axis=0, concat_axis=0, tiled=True)
    shapes = [(3, 3, 3) + kernel.shape[1::-1] for kernel in (first_kernel, second_kernel)]
    first, second = pl.pallas_call(
        unpack_kernel,
        out_shape=[array(shape, jnp.float32) for shape in shapes],
        in_specs=[pl.BlockSpec(memory_space=pltpu.VMEM)],
        out_specs=[pl.BlockSpec(memory_space=pl.ANY)] * 2,
        scratch_shapes=[pltpu.VMEM(shape, jnp.float32) for shape in shapes] + [pltpu.SemaphoreType.DMA((2, 3))],
        compiler_params=pltpu.CompilerParams(vmem_limit_bytes=VMEM_BYTES),
    )(whole.reshape(terms.shape))
    return (features, jnp.transpose(first, (4, 3, 0, 1, 2)), jnp.transpose(second, (4, 3, 0, 1, 2)))


def solution(mesh):
    placed = (P("sample", None, "space", None), P(), P(), P(("sample", "space"), None, None, None))
    return jax.shard_map(
        body,
        mesh=mesh,
        in_specs=placed,
        out_specs=(P(("sample", "space"), None, None, None), P(), P()),
        check_vma=False,
    )
```

```python
import functools
import math

import jax
import jax.numpy as jnp
from jax import lax
from jax.experimental import pallas as pl
from jax.experimental.pallas import tpu as pltpu
from jax.sharding import PartitionSpec as P

HEIGHT = 8
WIDTH = 128
LANES = 128
VMEM_BYTES = 16 * 1024 * 1024
TERM_ROWS = 576


def iota(shape, dim):
    return lax.broadcasted_iota(jnp.int32, shape, dim)


def dot(left, right, dims=((1,), (0,))):
    return lax.dot_general(left, right, (dims, ((), ())), preferred_element_type=jnp.float32)


def ones_where(mask):
    return jnp.where(mask, 1.0, 0.0).astype(jnp.bfloat16)


def band_of_second(k2_ref, k2t_ref):
    channels_mid, channels_out = k2_ref.shape[3:]
    empty = jnp.zeros((channels_mid, channels_out), jnp.bfloat16)
    for ad in range(3):
        for aw in range(3):
            tap = [k2_ref[ad, ah, aw] for ah in range(3)]
            band = ((tap[1], empty), (tap[2], tap[0]), (empty, tap[1]), (empty, tap[2]))
            start = (ad * 3 + aw) * 2 * channels_out
            for hh in range(4):
                k2t_ref[hh * channels_mid:(hh + 1) * channels_mid, start:start + 2 * channels_out] = (
                    jnp.concatenate(band[hh], axis=1))


def upsampling(ad, aw, beyond=0):
    row, col = iota((128, 512), 0), iota((128, 512), 1)
    target = ((row >> 5) << 7) + ((row & 31) << 1) + (64 * (ad - 1) + aw - 1 + 128 * beyond)
    keep = col == target
    if aw == 0:
        keep = keep & ((row & 31) > 0)
    return ones_where(keep)


def prepare_kernel(k1_ref, k2_ref, og_ref, pick_ref, k1t_ref, ogt_ref, ag_ref, k2t_ref, ogu_ref):
    channels_in, channels_mid = k1_ref.shape[3:]
    row, col = iota((3 * WIDTH, 2 * 64), 0), iota((3 * WIDTH, 2 * 64), 1)
    for aw in range(3):
        same = ((row >> 7) & 1) == (col >> 6)
        tap = (row & 127) == 2 * (col & 63) + aw - 1
        pick_ref[:, aw * 128:(aw + 1) * 128] = ones_where(same & tap)
    shape = (9 * channels_in, channels_in * 2 * HEIGHT)
    row, col = iota(shape, 0), iota(shape, 1)
    tap = row >> 4
    ad = jnp.where(tap >= 6, 2, jnp.where(tap >= 3, 1, 0))
    ah, i = tap - 3 * ad, row & 15
    same = i == col >> 4
    h, d = (col >> 1) & 7, col & 1
    taps = []
    for aw in range(3):
        parts = [k1_ref[a, b, aw] for a in range(3) for b in range(3)]
        taps.append(jnp.concatenate(parts, axis=0).astype(jnp.float32).T.astype(jnp.bfloat16))
    for following in range(2):
        plane = (ad == 0) & (d == 1) if following else (ad == d + 1)
        for hh in range(4):
            place = ones_where(same & plane & (h == 2 * hh + ah - 1))
            start = (following * 4 + hh) * channels_mid
            for aw in range(3):
                block = dot(taps[aw], place).astype(jnp.bfloat16)
                k1t_ref[start:start + channels_mid, aw * shape[1]:(aw + 1) * shape[1]] = block
    band_of_second(k2_ref, k2t_ref)
    groups = og_ref.shape[1] // 128
    for ad in range(3):
        for aw in range(3):
            t = ad * 3 + aw
            up = upsampling(ad, aw)
            for g in range(groups):
                value = dot(og_ref[:, g * 128:(g + 1) * 128], up)
                if ad == 0 and g + 1 < groups:
                    value = value + dot(og_ref[:, (g + 1) * 128:(g + 2) * 128], upsampling(ad, aw, 4))
                ogu_ref[t * 128:(t + 1) * 128, g * 512:(g + 1) * 512] = value.astype(jnp.bfloat16)
                ogt_ref[g * 512:(g + 1) * 512, t * 128:(t + 1) * 128] = value.T.astype(jnp.bfloat16)
    for g in range(groups):
        lanes = slice(g * 512, (g + 1) * 512)
        ag_ref[:, lanes] = dot(k2t_ref[...], ogu_ref[:, lanes]).astype(jnp.bfloat16)


def taps_of_pair(first_ref, second_ref, pick_ref):
    parity = lax.axis_index("space") & 1
    pick = pick_ref[pl.ds(pl.multiple_of(parity * WIDTH, WIDTH), 2 * WIDTH), :]
    pair = jnp.concatenate([first_ref[...], second_ref[...]], axis=1)
    return dot(pair, pick).astype(jnp.bfloat16)


def taps_kernel(pairs, given, *refs):
    pick_ref, out_ref = refs[-2:]
    for place, m in enumerate(pairs):
        y = taps_of_pair(refs[given.index(2 * m)], refs[given.index(2 * m + 1)], pick_ref)
        for aw in range(3):
            out_ref[aw * 256:(aw + 1) * 256, place * 128:(place + 1) * 128] = y[:, aw * 128:(aw + 1) * 128]


def layer_kernel(first, last, given, y_ref, *refs):
    pick_ref, k1t_ref, ogt_ref, ag_ref, act_ref, terms_ref, y_scr, pg_scr = refs[len(given):]
    cells = ag_ref.shape[1]
    rows = 256
    here = lax.axis_index("space") >> 1

    def lanes(m):
        return pl.ds(pl.multiple_of(lax.bitwise_xor(here, jnp.int32(m)) * 128, 128), 128)

    for place, m in enumerate(first):
        y_scr[:, lanes(m)] = y_ref[:, place * 128:(place + 1) * 128]
    for m in last:
        y = taps_of_pair(refs[given.index(2 * m)], refs[given.index(2 * m + 1)], pick_ref)
        for aw in range(3):
            y_scr[aw * rows:(aw + 1) * rows, lanes(m)] = y[:, aw * 128:(aw + 1) * 128]
    both = dot(k1t_ref[...], y_scr[...])
    lane = iota((128, cells), 1)
    from_last = jnp.where(lane < 64, 0.0, pltpu.roll(both[128:], 64, 1))
    pre = both[:128] + from_last
    sigma = jax.nn.sigmoid(pre)
    act = (pre * sigma).astype(jnp.bfloat16)
    act_ref[...] = act
    slope = sigma * (1.0 + pre * (1.0 - sigma))
    grad = (ag_ref[...].astype(jnp.float32) * slope).astype(jnp.bfloat16)
    pg_scr[:128, :] = grad
    to_last = pltpu.roll(grad.astype(jnp.float32), cells - 64, 1)
    pg_scr[128:, :] = jnp.where(lane < cells - 64, to_last, 0.0).astype(jnp.bfloat16)

    second = dot(act, ogt_ref[...])
    lane = iota((32, 128), 1)
    held = None
    for t in range(9):
        tile = second[:, t * 128:(t + 1) * 128]
        turned = pltpu.roll(tile, 64, 1)
        mixed = jnp.where(lane < 64, tile[0:32] + turned[64:96], turned[32:64] + tile[96:128])
        terms_ref[t * 32:(t + 1) * 32, :] = mixed.astype(jnp.bfloat16)
        if t % 2 == 0:
            held = jnp.where(lane < 64, turned[32:64], 0.0)
        else:
            held = jnp.where(lane < 64, held, tile[32:64])
        if t % 2 == 1:
            start = 288 + (t // 2) * 32
            terms_ref[start:start + 32, :] = held.astype(jnp.bfloat16)
    terms_ref[416:432, :] = jnp.where(lane[:16] < 64, held[:16], pltpu.roll(held[16:], 64, 1)).astype(jnp.bfloat16)

    first = dot(y_scr[...], pg_scr[...], ((1,), (1,))).astype(jnp.bfloat16)
    shape = (rows, 256)
    h, hh = (iota(shape, 0) >> 1) & 7, (iota(shape, 1) >> 5) & 3
    even, odd = ones_where((h >> 1) == hh), ones_where(((h & 1) == 1) & ((h + 1) >> 1 == hh))
    rank, index = iota((64, rows), 0), iota((64, rows), 1)
    same = ((rank & 15) == index >> 4) & (((rank >> 4) & 1) == (index & 1))
    later_taps = ones_where(same & ((rank >> 5) == ((index >> 1) & 1)))
    first_tap = ones_where(same[:32] & (((index[:32] >> 1) & 1) == 1))
    lane = iota((16, 128), 1)
    for aw in range(3):
        tile = first[aw * rows:(aw + 1) * rows]
        total = jnp.concatenate([dot(first_tap, tile * odd), dot(later_taps, tile * even)], axis=0)
        start = 432 + aw * 48
        for ad in range(3):
            side = slice(128, 256) if ad == 0 else slice(0, 128)
            d = 0 if ad == 1 else 1
            packed = None
            for ah in range(3):
                part = total[ah * 32 + d * 16:ah * 32 + d * 16 + 16, side]
                part = part + pltpu.roll(part, 64, 1)
                part = part + pltpu.roll(part, 32, 1)
                packed = part if packed is None else jnp.where(lane >= ah * 32, part, packed)
            terms_ref[start + ad * 16:start + (ad + 1) * 16, :] = packed.astype(jnp.bfloat16)
    rest = terms_ref.shape[0] - TERM_ROWS
    if rest > 0:
        terms_ref[TERM_ROWS:, :] = jnp.zeros((rest, 128), jnp.bfloat16)


def features_kernel(act_ref, k2_ref, out_ref, k2t_ref):
    band_of_second(k2_ref, k2t_ref)
    groups = out_ref.shape[1] // 128
    for g in range(groups):
        total = jnp.zeros((128, 128), jnp.float32)
        for t in range(9):
            taken = dot(act_ref[:, g * 512:(g + 1) * 512], upsampling(t // 3, t % 3), ((1,), (1,)))
            if t < 3 and g > 0:
                last = act_ref[:, (g - 1) * 512:g * 512]
                taken = taken + dot(last, upsampling(0, t, 4), ((1,), (1,)))
            band = k2t_ref[:, t * 128:(t + 1) * 128]
            total = total + dot(band, taken.astype(jnp.bfloat16), ((0,), (0,)))
        out_ref[:, g * 128:(g + 1) * 128] = total.astype(jnp.bfloat16)


def add_kernel(rows, mine_ref, out_ref):
    count = mine_ref.shape[0]
    unit = rows * 16 // math.gcd(rows, 16)
    total = mine_ref[0:unit, :].astype(jnp.float32)
    for start in range(unit, count, unit):
        total = total + mine_ref[start:start + unit, :].astype(jnp.float32)
    shift = unit // 2
    while shift >= rows:
        total = total + pltpu.roll(total, shift, 0)
        shift //= 2
    spread = total.astype(jnp.bfloat16)
    for start in range(0, count, unit):
        out_ref[start:start + unit, :] = spread


def unpack_kernel(whole_ref, first_ref, second_ref, first_scr, second_scr, sems):
    copies = []
    for ad in range(3):
        for aw in range(3):
            t = ad * 3 + aw
            pair = whole_ref[t * 32:(t + 1) * 32, :].astype(jnp.float32)
            second_scr[ad, 1, aw] = pair[:, :64]
            second_scr[ad, 2, aw] = pair[:, 64:]
            if t == 8:
                lone = whole_ref[416:432, :].astype(jnp.float32)
                second_scr[ad, 0, aw] = jnp.concatenate([lone[:, :64], lone[:, 64:]], axis=0)
            else:
                start = 288 + (t // 2) * 32
                lone = whole_ref[start:start + 32, :].astype(jnp.float32)
                second_scr[ad, 0, aw] = lone[:, :64] if t % 2 == 0 else lone[:, 64:]
        copies.append(pltpu.make_async_copy(second_scr.at[ad], second_ref.at[ad], sems.at[0, ad]))
        copies[-1].start()
    for ad in range(3):
        for aw in range(3):
            start = 432 + aw * 48 + ad * 16
            tile = whole_ref[start:start + 16, :].astype(jnp.float32)
            for ah in range(3):
                first_scr[ad, ah, aw] = tile[:, ah * 32:(ah + 1) * 32]
        copies.append(pltpu.make_async_copy(first_scr.at[ad], first_ref.at[ad], sems.at[1, ad]))
        copies[-1].start()
    for copy in copies:
        copy.wait()


def call(kernel, outs, args, scratch=(), flops=0):
    whole = pl.BlockSpec(memory_space=pltpu.VMEM)
    scalar = pl.BlockSpec(memory_space=pltpu.SMEM)
    size = sum(a.size * a.dtype.itemsize for a in list(args) + list(outs))
    return pl.pallas_call(
        kernel,
        out_shape=tuple(outs),
        in_specs=[scalar if a.dtype == jnp.int32 else whole for a in args],
        out_specs=(whole,) * len(outs),
        scratch_shapes=list(scratch),
        compiler_params=pltpu.CompilerParams(vmem_limit_bytes=VMEM_BYTES),
        cost_estimate=pl.CostEstimate(flops=flops, bytes_accessed=size, transcendentals=0),
    )(*args)


def array(shape, dtype=jnp.bfloat16):
    return jax.ShapeDtypeStruct(shape, dtype)


def by_tap(kernel):
    return jnp.transpose(kernel, (2, 3, 4, 1, 0))


def prepare(k1, k2, out_grad):
    c0, c1 = k1.shape[3:]
    c2 = k2.shape[4]
    planes = out_grad.shape[2]
    cells = planes * 2 * 64
    og = out_grad.reshape(c2, planes, 2, 32).transpose(2, 0, 1, 3).reshape(2 * c2, planes * 32)
    outs = [
        array((384, 384)),
        array((2 * 4 * c1, 3 * c0 * 16)),
        array((cells, 9 * 2 * c2)),
        array((4 * c1, cells)),
    ]
    scratch = [pltpu.VMEM((4 * c1, 9 * 2 * c2), jnp.bfloat16), pltpu.VMEM((9 * 2 * c2, cells), jnp.bfloat16)]
    return call(prepare_kernel, outs, (k1, k2, og), scratch, flops=2 * 128 * 1152 * cells * 2)


def body(crops, first_kernel, second_kernel, out_grad):
    axes = ("space", "sample")
    devices = lax.axis_size(axes)
    channels_out, planes = out_grad.shape[1:3]
    space = lax.axis_size("space")
    assert space & (space - 1) == 0
    position = lax.axis_index("space").astype(jnp.int32)
    across, near = range(space - 1, space // 2 - 1, -1), range(1, space // 2)
    order = [step for two in zip(across, near) for step in two] + [space // 2]
    early, late = order[:2], order[2:]
    last = sorted({step // 2 for step in order[-3:]})
    first = [m for m in range(space // 2) if m not in last]
    k1, k2 = by_tap(first_kernel), by_tap(second_kernel)
    x = {}
    cut = [lax.dynamic_index_in_dim(crops, position ^ step, 0, keepdims=False) for step in early]
    rest, cut = lax.optimization_barrier((crops, cut))
    for step in [0] + late[::-1] + early:
        if step in early:
            block = cut[early.index(step)]
        else:
            block = lax.dynamic_index_in_dim(rest, position ^ step, 0, keepdims=False)
        if step > 0:
            block = lax.ppermute(block, "space", [(source, source ^ step) for source in range(space)])
        channels_in, two, flat_cells = block.shape
        block = block.reshape(channels_in, two, HEIGHT, WIDTH).transpose(0, 2, 1, 3)
        x[step] = block.reshape(channels_in * two * HEIGHT, WIDTH)
    pick, k1t, ogt, act_grad = prepare(k1, k2, out_grad)
    cells = act_grad.shape[1]
    given = [step for step in order + [0] if step // 2 in first]
    (y,) = call(
        functools.partial(taps_kernel, first, given),
        [array((768, len(first) * 128))],
        [x[step] for step in given] + [pick],
        flops=2 * 256 * 384 * cells,
    )
    given = [step for step in order[::-1] if step // 2 in last]
    rows = -(-TERM_ROWS // (devices * 2)) * 2
    act, terms = call(
        functools.partial(layer_kernel, first, last, given),
        [array((128, cells)), array((devices * rows, LANES))],
        (y, *[x[step] for step in given], pick, k1t, ogt, act_grad),
        scratch=[pltpu.VMEM((768, cells), jnp.bfloat16), pltpu.VMEM((256, cells), jnp.bfloat16)],
        flops=2 * 128 * 4096 * cells,
    )
    blocks = terms.reshape(devices, rows // 2, 2, LANES)
    mine = lax.all_to_all(blocks, axes, split_axis=0, concat_axis=0, tiled=True)
    (features,) = call(
        features_kernel,
        [array((2 * channels_out, planes * 32))],
        (act, k2),
        scratch=[pltpu.VMEM((128, 1152), jnp.bfloat16)],
        flops=2 * 128 * 1152 * cells,
    )
    features = features.reshape(2, channels_out, planes, 32).transpose(1, 2, 0, 3).reshape(out_grad.shape)
    add = functools.partial(add_kernel, rows)
    (spread,) = call(add, [array(terms.shape)], (mine.reshape(terms.shape),))
    spread = spread.reshape(blocks.shape)
    whole = lax.all_to_all(spread, axes, split_axis=0, concat_axis=0, tiled=True)
    shapes = [(3, 3, 3) + kernel.shape[1::-1] for kernel in (first_kernel, second_kernel)]
    first, second = pl.pallas_call(
        unpack_kernel,
        out_shape=[array(shape, jnp.float32) for shape in shapes],
        in_specs=[pl.BlockSpec(memory_space=pltpu.VMEM)],
        out_specs=[pl.BlockSpec(memory_space=pl.ANY)] * 2,
        scratch_shapes=[pltpu.VMEM(shape, jnp.float32) for shape in shapes] + [pltpu.SemaphoreType.DMA((2, 3))],
        compiler_params=pltpu.CompilerParams(vmem_limit_bytes=VMEM_BYTES),
    )(whole.reshape(terms.shape))
    return (features, jnp.transpose(first, (4, 3, 0, 1, 2)), jnp.transpose(second, (4, 3, 0, 1, 2)))


def solution(mesh):
    placed = (P("sample", None, "space", None), P(), P(), P(("sample", "space"), None, None, None))
    return jax.shard_map(
        body,
        mesh=mesh,
        in_specs=placed,
        out_specs=(P(("sample", "space"), None, None, None), P(), P()),
        check_vma=False,
    )
```
